32 devices in a mesh: exp: 16 (over z, y, core), hid: 2 (over x).
Axes of the slice: x: 2, y: 2, z: 4, core: 2. Of those that a mesh axis runs over, the one named last changes fastest.
Arguments:
- tokens: bfloat16 [128, 2048], P(('exp', 'hid')), may hold values from -6 to 6
- grad_out: bfloat16 [128, 2048], P(('exp', 'hid')), may hold values from -3 to 3
- router_logits: float32 [128, 16], P(('exp', 'hid')), may hold values from -12 to 330
- selected: int32 [128, 8], P(('exp', 'hid')), may hold values from 0 to 15, as said below
- router_w: bfloat16 [2048, 16], replicated, may hold values from -0.59765625 to 0.59765625
- w_gate: bfloat16 [32, 2048, 384], P(('exp', 'hid')), may hold values from -0.125 to 0.125
- w_up: bfloat16 [32, 2048, 384], P(('exp', 'hid')), may hold values from -0.125 to 0.125
- w_down: bfloat16 [32, 384, 2048], P(('exp', 'hid')), may hold values from -0.21875 to 0.21875
Outputs:
- x_grad: bfloat16 [128, 2048], P(('exp', 'hid'))
- router_grad: float32 [2048, 16], P(('exp', 'hid'))
The draws below stay inside these ranges and needn't reach their ends.
Inputs may be any that keep to these rules, and one draw needn't show every extreme that they name: `selected`: each row names 8 different experts; within each aligned block of 8 rows (the tokens of one index of exp) no expert is named by more than 8 rows, and in every block some expert is named by exactly 8 rows.
All inputs are finite; a program needn't handle non-finite values.
Results may differ from the reference program's by a relative error of at most 0.0075.
Values may be sent and summed in bfloat16 or wider, within the bound.
No kernel may reach another device: no remote copies, remote signals or barrier semaphores. Data moves between devices by JAX's collectives and lax.ppermute only.
A program may use at most 64 MiB of HBM per device.

```python
import jax
import jax.numpy as jnp
from jax import lax

D = 2048
F = 768
TOPK = 8
TOK_DEV = 4
FH = 384
UNITS = 32
EXPERTS = 16
TOKENS = 128
CAP_G = 8
N_HID = 2


def choose_block(key):
    block_rows = N_HID * TOK_DEV
    windows = EXPERTS // TOPK
    slot_count = windows * CAP_G
    keys = jax.random.split(key, 4)
    order = jax.random.permutation(keys[0], EXPERTS).astype(jnp.int32)
    first_window = jax.random.randint(keys[1], (), 0, windows).astype(jnp.int32)
    slot_window = (jnp.arange(slot_count, dtype=jnp.int32) // CAP_G).astype(jnp.int32)
    priority = jax.random.randint(keys[2], (slot_count,), 0, 1 << 20) * slot_count + jnp.arange(slot_count, dtype=jnp.int32)
    priority = jnp.where(slot_window == first_window, priority + (1 << 20) * slot_count, priority)
    taken = lax.top_k(priority, block_rows)[1].astype(jnp.int32)
    row_window = jax.random.permutation(keys[3], slot_window[taken]).astype(jnp.int32)
    positions = row_window[:, None] * TOPK + jnp.arange(TOPK, dtype=jnp.int32)[None, :]
    return order[positions].astype(jnp.int32)


def choose_experts(key):
    block_rows = N_HID * TOK_DEV
    block_count = TOKENS // block_rows
    block_keys = jax.random.split(jax.random.fold_in(key, 17), block_count)
    chosen = jax.vmap(choose_block)(block_keys)
    return chosen.reshape(TOKENS, TOPK).astype(jnp.int32)


def draw_selected(key, part):
    return choose_experts(key)


def draw_router_logits(key, part):
    chosen = choose_experts(key)
    expert_ids = jnp.arange(EXPERTS, dtype=jnp.int32)
    hit_table = jnp.sum((chosen[:, :, None] == expert_ids[None, None, :]).astype(jnp.float32), axis=1)
    subkeys = jax.random.split(jax.random.fold_in(key, 29), 3)
    col_offset = jax.random.uniform(subkeys[0], (1, EXPERTS), minval=-0.6, maxval=0.6)
    chosen_level = 2.0 + jax.random.uniform(subkeys[1], (TOKENS, EXPERTS), minval=-1.15, maxval=1.15)
    noise_draw = jnp.clip(0.6 * jax.random.normal(subkeys[2], (TOKENS, EXPERTS)), -0.9, 0.9)
    other_level = col_offset + noise_draw
    logits = jnp.where(hit_table > 0.5, chosen_level, other_level)
    return logits.astype(jnp.float32)


def block_scale(rng, dims, shards, low, largest):
    def one(dim, blocks):
        heights = jax.random.uniform(jax.random.fold_in(jax.random.fold_in(rng, 6), dim), (blocks,), jnp.float32, low / len(shards), largest / len(shards))
        return jnp.repeat(jnp.exp(heights), dims[dim] // blocks).reshape((-1,) + (1,) * (len(dims) - dim - 1))

    loudness = one(*shards[0])
    for cut in shards[1:]:
        loudness = loudness * one(*cut)
    return loudness


def centred(stream_key, shape, width, reach, shards=(), kind=jnp.bfloat16):
    drawn = jax.random.normal(stream_key, shape, jnp.float32) * width
    if len(shards) > 0:
        drawn = block_scale(stream_key, shape, shards, -0.22, 0.18) * drawn
    return jnp.clip(drawn, min=-reach, max=reach).astype(kind)


def setup_inputs(seed: int = 0) -> dict:
    arg_keys = jax.random.split(jax.random.key(seed), 9)
    tokens = centred(arg_keys[0], (TOKENS, D), 1.0, 6.0, ((0, 32),))
    grad_out = centred(arg_keys[1], (TOKENS, D), 0.5, 3.0, ((0, 32),))
    router_logits = draw_router_logits(jax.random.fold_in(arg_keys[8], 71), 0)
    selected = draw_selected(jax.random.fold_in(arg_keys[8], 71), 0)
    router_w = centred(arg_keys[4], (D, EXPERTS), 0.1, 0.59765625)
    w_gate = centred(arg_keys[5], (UNITS, D, FH), D ** -0.5, 0.125, ((0, 32),))
    w_up = centred(arg_keys[6], (UNITS, D, FH), D ** -0.5, 0.125, ((0, 32),))
    w_down = centred(arg_keys[7], (UNITS, FH, D), F ** -0.5, 0.21875, ((0, 32),))
    return {"tokens": tokens, "grad_out": grad_out, "router_logits": router_logits, "selected": selected, "router_w": router_w, "w_gate": w_gate, "w_up": w_up, "w_down": w_down}


def softmax_rows(values):
    top_val = jnp.max(values, axis=-1, keepdims=True)
    raised = jnp.exp(values - top_val)
    return raised / jnp.sum(raised, axis=-1, keepdims=True)


def combine_table(logits, chosen, expert_count):
    picked = jnp.take_along_axis(logits, chosen, axis=1)
    weights = softmax_rows(picked)
    expert_ids = jnp.arange(expert_count, dtype=jnp.int32)
    matched = (chosen[:, :, None] == expert_ids[None, None, :]).astype(jnp.float32)
    return jnp.sum(weights[:, :, None] * matched, axis=1).astype(jnp.bfloat16)


def reference(tokens, grad_out, router_logits, selected, router_w, w_gate, w_up, w_down):
    probs_all = softmax_rows(router_logits)
    combine = combine_table(router_logits, selected, EXPERTS)

    def one_unit(totals, packed):
        gate_w, up_w, down_w, unit_id = packed
        column = lax.dynamic_slice_in_dim(combine, unit_id // 2, 1, 1).astype(jnp.float32)
        gate_pre = jnp.dot(tokens, gate_w, preferred_element_type=jnp.float32)
        up_pre = jnp.dot(tokens, up_w, preferred_element_type=jnp.float32)
        back_grad = jnp.dot(grad_out, down_w.T, preferred_element_type=jnp.float32)
        sig_gate = jax.nn.sigmoid(gate_pre)
        act_gate = gate_pre * sig_gate
        score_part = jnp.sum(act_gate * up_pre * back_grad, axis=1)
        weighted = column * back_grad
        grad_gate = (weighted * up_pre * sig_gate * (1.0 + gate_pre * (1.0 - sig_gate))).astype(jnp.bfloat16)
        grad_up = (weighted * act_gate).astype(jnp.bfloat16)
        totals = totals + jnp.dot(grad_gate, gate_w.T, preferred_element_type=jnp.float32)
        totals = totals + jnp.dot(grad_up, up_w.T, preferred_element_type=jnp.float32)
        return totals, score_part

    unit_ids = jnp.arange(UNITS, dtype=jnp.int32)
    start_totals = jnp.zeros((TOKENS, D), jnp.float32)
    expert_grad, unit_scores = lax.scan(one_unit, start_totals, (w_gate, w_up, w_down, unit_ids))
    expert_scores = jnp.sum(unit_scores.reshape(EXPERTS, 2, TOKENS), axis=1).T
    mean_score = jnp.sum(probs_all * expert_scores, axis=1, keepdims=True)
    logit_grad = (probs_all * (expert_scores - mean_score)).astype(jnp.bfloat16)
    router_grad = jnp.dot(tokens.T, logit_grad, preferred_element_type=jnp.float32)
    router_part = jnp.dot(logit_grad, router_w.T, preferred_element_type=jnp.float32)
    x_grad = (expert_grad + router_part).astype(jnp.bfloat16)
    return x_grad, router_grad
```

```python
import jax
import jax.numpy as jnp
from jax import lax
from jax.sharding import PartitionSpec as P

AXES = ("exp", "hid")


def softmax_rows(values):
    top_val = jnp.max(values, axis=-1, keepdims=True)
    raised = jnp.exp(values - top_val)
    return raised / jnp.sum(raised, axis=-1, keepdims=True)


def combine_table(logits, chosen, expert_count):
    expert_ids = jnp.arange(expert_count, dtype=jnp.int32)
    hit = jnp.any(chosen[:, :, None] == expert_ids[None, None, :], axis=1)
    top_val = jnp.max(jnp.where(hit, logits, -jnp.inf), axis=1, keepdims=True)
    raised = jnp.where(hit, jnp.exp(jnp.minimum(logits - top_val, 0.0)), 0.0)
    return (raised / jnp.sum(raised, axis=1, keepdims=True)).astype(jnp.bfloat16)


def split_bf16(values, parts):
    pieces = []
    for _ in range(parts):
        piece = values.astype(jnp.bfloat16)
        pieces.append(piece)
        values = values - piece.astype(jnp.float32)
    return pieces


def stage_masks(exp_size, hid_size):
    hid_bits = hid_size.bit_length() - 1
    all_bits = (exp_size * hid_size).bit_length() - 1
    core = hid_bits
    first = list(range(max(core + 1, all_bits - 2), all_bits))
    middle = [b for b in range(all_bits) if b != core and b not in first]
    groups = [first] + [middle[i : i + 2] for i in range(0, len(middle), 2)] + [[core]]
    stages = []
    for group in groups:
        masks = [0]
        for bit in group:
            masks = masks + [m ^ (1 << bit) for m in masks]
        stages.append(masks)
    return stages


def swap(value, mask, count):
    return lax.ppermute(value, AXES, [(i, i ^ mask) for i in range(count)])


def gather_rel(block, stages, count):
    for masks in stages:
        block = jnp.concatenate([block] + [swap(block, m, count) for m in masks[1:]], axis=0)
    return block


def scatter_rel(total, stages, count):
    for masks in reversed(stages):
        chunks = jnp.split(total, len(masks), axis=0)
        arrived = [swap(c.astype(jnp.bfloat16), m, count) for c, m in zip(chunks[1:], masks[1:])]
        total = chunks[0]
        for piece in arrived:
            total = total + piece.astype(jnp.float32)
    return total


def on_device(tokens, grad_out, router_logits, selected, router_w, w_gate, w_up, w_down):
    tok_local, width = tokens.shape
    expert_count = router_logits.shape[1]
    exp_size = lax.axis_size("exp")
    hid_size = lax.axis_size("hid")
    count = exp_size * hid_size
    own = lax.axis_index(AXES)
    stages = stage_masks(exp_size, hid_size)
    order = [0]
    for masks in stages:
        order = [m ^ k for k in masks for m in order]
    token_count = count * tok_local

    combine = combine_table(router_logits, selected, expert_count)
    probs_own = softmax_rows(router_logits)
    extras = jnp.concatenate([combine] + split_bf16(probs_own, 3), axis=1)
    extra_width = -(-4 * expert_count // 128) * 128
    extras = jnp.pad(extras, ((0, 0), (0, extra_width - extras.shape[1])))
    block = jnp.concatenate(
        [
            jnp.concatenate([tokens, extras], axis=1),
            jnp.concatenate([grad_out, jnp.zeros_like(extras)], axis=1),
        ],
        axis=0,
    )
    gathered = gather_rel(block, stages, count).reshape(count, 2, tok_local, -1)
    x_rows = gathered[:, 0, :, :width].reshape(token_count, width)
    g_rows = gathered[:, 1, :, :width].reshape(token_count, width)
    more = gathered[:, 0, :, width : width + 4 * expert_count].reshape(token_count, 4, expert_count)
    probs = (more[:, 1].astype(jnp.float32) + more[:, 2].astype(jnp.float32)) + more[:, 3].astype(
        jnp.float32
    )
    expert_ids = jnp.arange(expert_count, dtype=jnp.int32)
    column = jnp.sum(
        jnp.where(expert_ids[None, :] == own // 2, more[:, 0].astype(jnp.float32), 0.0),
        axis=1,
        keepdims=True,
    )

    gate_pre = jnp.dot(x_rows, w_gate[0], preferred_element_type=jnp.float32)
    up_pre = jnp.dot(x_rows, w_up[0], preferred_element_type=jnp.float32)
    back_grad = jnp.einsum("td,fd->tf", g_rows, w_down[0], preferred_element_type=jnp.float32)
    sig_gate = jax.nn.sigmoid(gate_pre)
    act_gate = gate_pre * sig_gate
    score = jnp.sum(act_gate * up_pre * back_grad, axis=1)
    weighted = column * back_grad
    grad_gate = (weighted * up_pre * sig_gate * (1.0 + gate_pre * (1.0 - sig_gate))).astype(
        jnp.bfloat16
    )
    grad_up = (weighted * act_gate).astype(jnp.bfloat16)

    rel = jnp.arange(token_count, dtype=jnp.int32)
    place = (jnp.asarray(order, dtype=jnp.int32)[rel // tok_local] ^ own) * tok_local + rel % tok_local
    to_whole = place[:, None] == rel[None, :]
    score_whole = jnp.sum(jnp.where(to_whole, score[:, None], 0.0), axis=0)
    score_units = gather_rel(score_whole[None, :], stages, count)

    input_part = jnp.einsum("tf,df->td", grad_gate, w_gate[0], preferred_element_type=jnp.float32)
    input_part = input_part + jnp.einsum(
        "tf,df->td", grad_up, w_up[0], preferred_element_type=jnp.float32
    )
    input_sum = scatter_rel(input_part, stages, count)

    unit_expert = (jnp.asarray(order, dtype=jnp.int32) ^ own) // 2
    unit_pick = (unit_expert[:, None] == expert_ids[None, :]).astype(jnp.float32)
    expert_scores = jnp.einsum(
        "rw,uw,ue->re",
        to_whole.astype(jnp.float32),
        score_units,
        unit_pick,
        precision=lax.Precision.HIGHEST,
        preferred_element_type=jnp.float32,
    )
    mean_score = jnp.sum(probs * expert_scores, axis=1, keepdims=True)
    logit_grad = (probs * (expert_scores - mean_score)).astype(jnp.bfloat16)
    rows_out = width // count
    own_columns = lax.dynamic_slice_in_dim(x_rows, own * rows_out, rows_out, axis=1)
    router_grad = jnp.einsum("tc,te->ce", own_columns, logit_grad, preferred_element_type=jnp.float32)
    router_part = jnp.einsum(
        "te,de->td", logit_grad[:tok_local], router_w, preferred_element_type=jnp.float32
    )
    x_grad = (input_sum + router_part).astype(jnp.bfloat16)
    return (x_grad, router_grad)


def solution(mesh):
    rows = P(AXES, None)
    units = P(AXES, None, None)
    return jax.shard_map(
        on_device,
        mesh=mesh,
        in_specs=(rows, rows, rows, rows, P(), units, units, units),
        out_specs=(rows, rows),
        check_vma=False,
    )
```

```python
import functools

import jax
import jax.numpy as jnp
from jax import lax
from jax.experimental import pallas as pl
from jax.experimental.pallas import tpu as pltpu
from jax.sharding import PartitionSpec as P

AXES = ("exp", "hid")
LANES = 128
PIECES = 4
VMEM_SPEC = pl.BlockSpec(memory_space=pltpu.VMEM)
F32 = jnp.float32
BF16 = jnp.bfloat16
HIGHEST = lax.Precision.HIGHEST
NT = (((1,), (1,)), ((), ()))
TN = (((0,), (0,)), ((), ()))


def stage_bits(exp_size, hid_size):
    hid_bits = hid_size.bit_length() - 1
    all_bits = (exp_size * hid_size).bit_length() - 1
    core = hid_bits
    first = list(range(max(core + 1, all_bits - 2), all_bits))
    middle = [b for b in range(all_bits) if b != core and b not in first]
    return [first] + [middle[i : i + 2] for i in range(0, len(middle), 2)], core


def group_lists(bits, count):
    masks = [0]
    for bit in bits:
        masks = masks + [m | (1 << bit) for m in masks]
    return [[i | m for m in masks] for i in range(count) if not any(i >> b & 1 for b in bits)]


def exchange(pieces, bits, count):
    return lax.all_to_all(pieces, AXES, 0, 0, axis_index_groups=group_lists(bits, count), tiled=True)


def spread(block, bits, count):
    copies = jnp.broadcast_to(block[None], (1 << len(bits),) + block.shape)
    return exchange(copies, bits, count).reshape((-1,) + block.shape[1:])


def core_swap(block, core, count):
    return lax.ppermute(block, AXES, [(i, i ^ (1 << core)) for i in range(count)])


def place_bits(place, bits):
    total = jnp.zeros_like(place)
    for digit, bit in enumerate(bits):
        total = total | (((place >> digit) & 1) << bit)
    return total


def own_index():
    return lax.axis_index("exp") * lax.axis_size("hid") + lax.axis_index("hid")


def softmax_f32(values):
    raised = jnp.exp(values - jnp.max(values, axis=-1, keepdims=True))
    return raised / jnp.sum(raised, axis=-1, keepdims=True)


def prep_kernel(tokens_ref, grad_ref, logits_ref, chosen_ref, out_ref, rows_ref):
    tok, width = tokens_ref.shape
    logits = logits_ref[...]
    chosen = chosen_ref[...]
    experts = logits.shape[1]
    ids = lax.broadcasted_iota(jnp.int32, logits.shape, 1)
    hit = ids == chosen[:, 0:1]
    for k in range(1, chosen.shape[1]):
        hit = hit | (ids == chosen[:, k : k + 1])
    top = jnp.max(jnp.where(hit, logits, -jnp.inf), axis=1, keepdims=True)
    raised = jnp.where(hit, jnp.exp(jnp.minimum(logits - top, 0.0)), 0.0)
    parts = [raised / jnp.sum(raised, axis=1, keepdims=True)]
    rest = softmax_f32(logits)
    for _ in range(PIECES - 1):
        parts.append(rest)
        rest = rest - rest.astype(BF16).astype(F32)
    lanes = out_ref.shape[1] - width
    extras = jnp.zeros((tok, lanes), F32)
    row = lax.broadcasted_iota(jnp.int32, (experts, lanes), 0)
    lane = lax.broadcasted_iota(jnp.int32, (experts, lanes), 1)
    for k, part in enumerate(parts):
        place = jnp.where(lane == row + k * experts, 1.0, 0.0).astype(BF16)
        extras = extras + jnp.dot(part.astype(BF16), place, preferred_element_type=F32)
    rows_ref[0:tok, :width] = tokens_ref[...].astype(F32)
    rows_ref[tok:, :width] = grad_ref[...].astype(F32)
    rows_ref[0:tok, width:] = extras
    rows_ref[tok:, width:] = jnp.zeros((tok, lanes), F32)
    out_ref[...] = rows_ref[...].astype(BF16)


def half_kernel(place_of, swap_mask, buf_ref, gate_ref, up_ref, down_ref, *rest):
    base_ref = rest[0] if len(rest) == 3 else None
    out_ref, score_ref = rest[-2:]
    width = gate_ref.shape[1]
    experts_width = buf_ref.shape[1] - width
    own = own_index()
    expert = own // 2
    rows, tokens = buf_ref.shape[0], score_ref.shape[1]
    step = min(rows, 128)
    if base_ref is None:
        score_ref[...] = jnp.zeros(score_ref.shape, F32)
    else:
        score_ref[...] = base_ref[...]

    def one(index):
        start = pl.multiple_of(index * step, step)
        block = buf_ref[pl.ds(start, step), :]
        act = block[:, :width]
        extras = block[:, width:].astype(F32)
        lane = lax.broadcasted_iota(jnp.int32, (step, experts_width), 1)
        column = jnp.sum(jnp.where(lane == expert, extras, 0.0), axis=1, keepdims=True)
        gate_pre = jnp.dot(act, gate_ref[0], preferred_element_type=F32)
        up_pre = jnp.dot(act, up_ref[0], preferred_element_type=F32)
        back = lax.dot_general(act, down_ref[0], NT, preferred_element_type=F32)
        back = pltpu.roll(back, step - 4, 0)
        sig = jax.nn.sigmoid(gate_pre)
        act_gate = gate_pre * sig
        score = jnp.sum(act_gate * up_pre * back, axis=1, keepdims=True)
        weighted = column * back
        grad_gate = weighted * up_pre * sig * (1.0 + gate_pre * (1.0 - sig))
        grad_up = weighted * act_gate

        def compact(value):
            pairs = value.reshape(step // 16, 16, value.shape[1])
            low = pairs[:, :8]
            high = pairs[:, 8:]
            high = jnp.concatenate([high[:, 4:], high[:, :4]], axis=1)
            sub = lax.broadcasted_iota(jnp.int32, low.shape, 1)
            return jnp.where(sub < 4, low, high).reshape(step // 2, value.shape[1]).astype(BF16)

        total = lax.dot_general(compact(grad_gate), gate_ref[0], NT, preferred_element_type=F32)
        total = total + lax.dot_general(compact(grad_up), up_ref[0], NT, preferred_element_type=F32)
        out_start = pl.multiple_of(index * (step // 2), step // 2)
        out_ref[pl.ds(out_start, step // 2), :] = total.astype(out_ref.dtype)

        row = lax.broadcasted_iota(jnp.int32, (step, tokens), 0) + start
        token = lax.broadcasted_iota(jnp.int32, (step, tokens), 1)
        whole = (place_of(row >> 3, own) ^ swap_mask) * 4 + (row & 7)
        here = (whole == token) & ((row & 7) < 4)
        score_ref[...] += jnp.sum(jnp.where(here, score, 0.0), axis=0, keepdims=True)

    if rows == step:
        one(0)
    else:
        pl.loop(0, rows // step)(one)


def router_kernel(place_of, core_mask, own_place, sender_of, bufs_own_ref, bufs_other_ref, score_ref, router_ref,
                  part_ref, grad_ref, lg_ref):
    experts = router_ref.shape[0]
    width = router_ref.shape[1]
    half = bufs_own_ref.shape[0]
    units, tokens = score_ref.shape
    lanes = bufs_own_ref.shape[1] - width
    own = own_index()
    ids = lax.broadcasted_iota(jnp.int32, (experts, units), 0)
    unit = sender_of(lax.broadcasted_iota(jnp.int32, (experts, units), 1), own)
    pick = jnp.where((unit >> 1) == ids, 1.0, 0.0)
    by_expert = jnp.dot(pick, score_ref[...], precision=HIGHEST, preferred_element_type=F32)
    lane = lax.broadcasted_iota(jnp.int32, (lanes, experts), 0)
    ids = lax.broadcasted_iota(jnp.int32, (lanes, experts), 1)
    tally = jnp.zeros((lanes, experts), F32)
    for k in range(1, PIECES):
        tally = tally + jnp.where(lane == ids + k * experts, 1.0, 0.0)
    rows_out = grad_ref.shape[1]
    first = own * rows_out
    column = pl.multiple_of(first // LANES * LANES, LANES)
    grad = jnp.zeros((experts, LANES), F32)
    for index, ref in enumerate((bufs_own_ref, bufs_other_ref)):
        row = lax.broadcasted_iota(jnp.int32, (half, tokens), 0)
        token = lax.broadcasted_iota(jnp.int32, (half, tokens), 1)
        whole = (place_of(row >> 3, own) ^ (core_mask if index else 0)) * 4 + (row & 7)
        here = jnp.where((whole == token) & ((row & 7) < 4), 1.0, 0.0)
        scores = lax.dot_general(here, by_expert, NT, precision=HIGHEST, preferred_element_type=F32)
        probs = jnp.dot(ref[:, width:], tally.astype(BF16), preferred_element_type=F32)
        mean = jnp.sum(probs * scores, axis=1, keepdims=True)
        logit_grad = probs * (scores - mean)
        if index == 0:
            lg_ref[...] = logit_grad
        grad = grad + lax.dot_general(
            logit_grad.astype(BF16), ref[:, pl.ds(column, LANES)], TN, preferred_element_type=F32
        )
    shift = (LANES - (first - column)) % LANES
    grad_ref[...] = pltpu.roll(grad, shift, 1)[:, :rows_out]
    mine = lg_ref[pl.ds(pl.multiple_of(own_place(own) * 8, 8), 8), :]
    part = jnp.dot(mine.astype(BF16), router_ref[...], preferred_element_type=F32)
    part_ref[...] = part[: part_ref.shape[0]]


def on_device(tokens, grad_out, router_logits, selected, router_w, w_gate, w_up, w_down):
    tok, width = tokens.shape
    experts = router_logits.shape[1]
    hidden = w_gate.shape[2]
    exp_size = lax.axis_size("exp")
    hid_size = lax.axis_size("hid")
    count = exp_size * hid_size
    half = count // 2
    stages, core = stage_bits(exp_size, hid_size)
    core_mask = 1 << core
    order = [b for bits in stages for b in bits]
    back_order = [core] + [b for bits in reversed(stages) for b in bits]
    token_count = count * tok
    lanes = -(-PIECES * experts // LANES) * LANES
    params = pltpu.CompilerParams(vmem_limit_bytes=24 * 2**20)

    def place_of(place, own):
        return place_bits(place, order) | (own & core_mask)

    def own_place(own):
        total = 0
        for digit, bit in enumerate(order):
            total = total | (((own >> bit) & 1) << digit)
        return total

    def sender_of(place, own):
        return place_bits(place, back_order) ^ (own & core_mask)

    block = pl.pallas_call(
        prep_kernel,
        out_shape=jax.ShapeDtypeStruct((2 * tok, width + lanes), BF16),
        in_specs=[VMEM_SPEC] * 4,
        out_specs=VMEM_SPEC,
        scratch_shapes=[pltpu.VMEM((2 * tok, width + lanes), F32)],
        compiler_params=params,
        name="prep",
    )(tokens, grad_out, router_logits, selected)

    for bits in stages:
        block = spread(block, bits, count)
    other = core_swap(block, core, count)

    cost = pl.CostEstimate(
        flops=2 * half * 8 * width * hidden * 4,
        bytes_accessed=3 * width * hidden * 2 + half * 8 * width * 2,
        transcendentals=half * 8 * hidden,
    )

    def half_call(buf, swap_mask, out_dtype, base, name):
        inputs = [buf, w_gate, w_up, w_down] + ([] if base is None else [base])
        return pl.pallas_call(
            functools.partial(half_kernel, place_of, swap_mask),
            out_shape=(
                jax.ShapeDtypeStruct((half * tok, width), out_dtype),
                jax.ShapeDtypeStruct((1, token_count), F32),
            ),
            in_specs=[VMEM_SPEC] * len(inputs),
            out_specs=(VMEM_SPEC, VMEM_SPEC),
            compiler_params=params,
            cost_estimate=cost,
            name=name,
        )(*inputs)

    kept, score = half_call(block, 0, F32, None, "half_own")
    sent, score = half_call(other, core_mask, BF16, score, "half_other")

    arrived = core_swap(sent, core, count)
    score = jnp.concatenate([score, core_swap(score, core, count)], axis=0)
    total = kept + arrived.astype(F32)
    for bits in reversed(stages):
        size = 1 << len(bits)
        pieces = exchange(total.astype(BF16).reshape(size, -1, width), bits, count)
        score = spread(score, bits, count)
        total = jnp.sum(pieces.astype(F32), axis=0)

    part, grad = pl.pallas_call(
        functools.partial(router_kernel, place_of, core_mask, own_place, sender_of),
        out_shape=(
            jax.ShapeDtypeStruct((tok, width), F32),
            jax.ShapeDtypeStruct((experts, width // count), F32),
        ),
        in_specs=[VMEM_SPEC] * 4,
        out_specs=(VMEM_SPEC, VMEM_SPEC),
        scratch_shapes=[pltpu.VMEM((half * 8, experts), F32)],
        compiler_params=params,
        cost_estimate=pl.CostEstimate(flops=10**8, bytes_accessed=10**6, transcendentals=0),
        name="router",
    )(block, other, score, router_w.T)
    x_grad = (total + part).astype(BF16)
    return (x_grad, grad.T)


def solution(mesh):
    rows = P(AXES, None)
    units = P(AXES, None, None)
    return jax.shard_map(
        on_device,
        mesh=mesh,
        in_specs=(rows, rows, rows, rows, P(), units, units, units),
        out_specs=(rows, rows),
        check_vma=False,
    )
```

```python
import functools

import jax
import jax.numpy as jnp
from jax import lax
from jax.experimental import pallas as pl
from jax.experimental.pallas import tpu as pltpu
from jax.sharding import PartitionSpec as P

AXES = ("exp", "hid")
LANES = 128
PIECES = 4
SCORE_PIECES = 2
VMEM_SPEC = pl.BlockSpec(memory_space=pltpu.VMEM)
HBM_SPEC = pl.BlockSpec(memory_space=pltpu.HBM)
F32 = jnp.float32
BF16 = jnp.bfloat16
NT = (((1,), (1,)), ((), ()))
TN = (((0,), (0,)), ((), ()))
PARAMS = pltpu.CompilerParams(vmem_limit_bytes=24 * 2**20)


def stage_masks(exp_size, hid_size):
    hid_bits = hid_size.bit_length() - 1
    all_bits = (exp_size * hid_size).bit_length() - 1
    core = hid_bits
    first = list(range(max(core + 1, all_bits - 2), all_bits))
    middle = [b for b in range(all_bits) if b != core and b not in first]
    groups = [first] + [middle[i : i + 2] for i in range(0, len(middle), 2)]
    return groups, core


def group_masks(bits):
    masks = [0]
    for bit in bits:
        masks = masks + [m | (1 << bit) for m in masks]
    return masks


def swap(block, mask, count):
    return lax.ppermute(block, AXES, [(i, i ^ mask) for i in range(count)])


def place_mask(place, bits):
    total = jnp.zeros_like(place)
    for digit, bit in enumerate(bits):
        total = total | (((place >> digit) & 1) << bit)
    return total


def own_index():
    return lax.axis_index("exp") * lax.axis_size("hid") + lax.axis_index("hid")


def in_hbm(*arrays):
    return tuple(pltpu.with_memory_space_constraint(a, pltpu.HBM) for a in arrays)


def softmax_f32(values):
    raised = jnp.exp(values - jnp.max(values, axis=-1, keepdims=True))
    return raised / jnp.sum(raised, axis=-1, keepdims=True)


def prep_kernel(tokens_in, grad_in, logits_in, chosen_in, out_ref, tokens_ref, grad_ref, logits_ref, chosen_ref,
                rows_ref, sems):
    copies = [
        pltpu.make_async_copy(src, dst, sems.at[i])
        for i, (src, dst) in enumerate(
            [(logits_in, logits_ref), (chosen_in, chosen_ref), (tokens_in, tokens_ref), (grad_in, grad_ref)]
        )
    ]
    for copy in copies:
        copy.start()
    copies[0].wait()
    copies[1].wait()
    tok, width = tokens_ref.shape
    logits = logits_ref[...]
    chosen = chosen_ref[...]
    experts = logits.shape[1]
    ids = lax.broadcasted_iota(jnp.int32, logits.shape, 1)
    hit = ids == chosen[:, 0:1]
    for k in range(1, chosen.shape[1]):
        hit = hit | (ids == chosen[:, k : k + 1])
    top = jnp.max(jnp.where(hit, logits, -jnp.inf), axis=1, keepdims=True)
    raised = jnp.where(hit, jnp.exp(jnp.minimum(logits - top, 0.0)), 0.0)
    parts = [raised / jnp.sum(raised, axis=1, keepdims=True)]
    rest = softmax_f32(logits)
    for _ in range(PIECES - 1):
        parts.append(rest)
        rest = rest - rest.astype(BF16).astype(F32)
    lanes = out_ref.shape[1] - width
    extras = jnp.zeros((tok, lanes), F32)
    row = lax.broadcasted_iota(jnp.int32, (experts, lanes), 0)
    lane = lax.broadcasted_iota(jnp.int32, (experts, lanes), 1)
    for k, part in enumerate(parts):
        place = jnp.where(lane == row + k * experts, 1.0, 0.0).astype(BF16)
        extras = extras + jnp.dot(part.astype(BF16), place, preferred_element_type=F32)
    copies[2].wait()
    copies[3].wait()
    rows_ref[0:tok, :width] = tokens_ref[...].astype(F32)
    rows_ref[tok:, :width] = grad_ref[...].astype(F32)
    rows_ref[0:tok, width:] = extras
    rows_ref[tok:, width:] = jnp.zeros((tok, lanes), F32)
    out_ref[...] = rows_ref[...].astype(BF16)


def load_kernel(chunks, after_ref, *refs):
    count = (len(refs) - 1) // 2
    sems = refs[-1]
    copies = []
    for src, dst in zip(refs[:count], refs[count : 2 * count]):
        size = src.shape[1] // chunks
        for c in range(chunks):
            part = (slice(None), pl.ds(c * size, size))
            copies.append(pltpu.make_async_copy(src.at[part], dst.at[part], sems.at[len(copies)]))
    for copy in copies:
        copy.start()
    for copy in copies:
        copy.wait()


def put_scores(out_ref, scores_ref, width):
    rows = out_ref.shape[0]
    for c in range((out_ref.shape[1] - width) // LANES):
        out_ref[:, width + c * LANES : width + (c + 1) * LANES] = scores_ref[c * rows : (c + 1) * rows, :].astype(BF16)


def get_scores(in_ref, scores_ref, base, size, width):
    rows = in_ref.shape[0]
    for c in range(-(-size // rows)):
        here = min(rows, size - c * rows)
        tall = min(rows, -(-here // 16) * 16)
        block = in_ref[0:tall, width + c * LANES : width + (c + 1) * LANES].astype(F32)
        scores_ref[base + c * rows : base + c * rows + here, :] = block[:here]


def half_kernel(bits, swap_mask, last, buf_ref, gate_ref, up_ref, down_ref, *rest):
    width = gate_ref.shape[1]
    experts_width = buf_ref.shape[1] - width
    own = own_index()
    expert = own // 2
    rows = buf_ref.shape[0]
    if last:
        base_ref, out_ref, pieces_ref, score_ref, padded_ref = rest
        score_ref[...] = base_ref[...]
    else:
        out_ref, score_ref = rest
        score_ref[...] = jnp.zeros(score_ref.shape, F32)
    tokens = score_ref.shape[1]
    step = min(rows, 128)

    def one(index):
        start = pl.multiple_of(index * step, step)
        block = buf_ref[pl.ds(start, step), :]
        act = block[:, :width]
        extras = block[:, width:].astype(F32)
        lane = lax.broadcasted_iota(jnp.int32, (step, experts_width), 1)
        column = jnp.sum(jnp.where(lane == expert, extras, 0.0), axis=1, keepdims=True)
        gate_pre = jnp.dot(act, gate_ref[0], preferred_element_type=F32)
        up_pre = jnp.dot(act, up_ref[0], preferred_element_type=F32)
        back = lax.dot_general(act, down_ref[0], NT, preferred_element_type=F32)
        back = pltpu.roll(back, step - 4, 0)
        sig = jax.nn.sigmoid(gate_pre)
        act_gate = gate_pre * sig
        score = jnp.sum(act_gate * up_pre * back, axis=1, keepdims=True)
        weighted = column * back
        grad_gate = weighted * up_pre * sig * (1.0 + gate_pre * (1.0 - sig))
        grad_up = weighted * act_gate

        def compact(value):
            pairs = value.reshape(step // 16, 16, value.shape[1])
            low = pairs[:, :8]
            high = pairs[:, 8:]
            high = jnp.concatenate([high[:, 4:], high[:, :4]], axis=1)
            sub = lax.broadcasted_iota(jnp.int32, low.shape, 1)
            return jnp.where(sub < 4, low, high).reshape(step // 2, value.shape[1]).astype(BF16)

        total = lax.dot_general(compact(grad_gate), gate_ref[0], NT, preferred_element_type=F32)
        total = total + lax.dot_general(compact(grad_up), up_ref[0], NT, preferred_element_type=F32)
        out_start = pl.multiple_of(index * (step // 2), step // 2)
        out_ref[pl.ds(out_start, step // 2), 0:width] = total.astype(out_ref.dtype)

        row = lax.broadcasted_iota(jnp.int32, (step, tokens), 0) + start
        token = lax.broadcasted_iota(jnp.int32, (step, tokens), 1)
        whole = (place_mask(row >> 3, bits) ^ (own ^ swap_mask)) * 4 + (row & 7)
        here = (whole == token) & ((row & 7) < 4)
        score_ref[...] += jnp.sum(jnp.where(here, score, 0.0), axis=0, keepdims=True)

    if rows == step:
        one(0)
    else:
        pl.loop(0, rows // step)(one)
    if last:
        blocks = tokens // LANES
        padded_ref[...] = jnp.zeros(padded_ref.shape, F32)
        value = score_ref[...]
        for piece in range(SCORE_PIECES):
            rounded = value.astype(BF16).astype(F32)
            for b in range(blocks):
                padded_ref[piece * blocks + b : piece * blocks + b + 1, :] = rounded[:, b * LANES : (b + 1) * LANES]
            value = value - rounded
        pieces_ref[...] = padded_ref[0 : pieces_ref.shape[0], :]
        put_scores(out_ref, padded_ref, width)


def add_kernel(arrivals, radix, *refs):
    kept_ref, pieces_ref = refs[0], refs[1]
    arrived = refs[2 : 2 + arrivals]
    outs = refs[2 + arrivals :]
    next_kept_ref, next_pieces_ref = outs[0], outs[1]
    sends = outs[2 : 1 + radix]
    total_ref, scores_ref = outs[1 + radix :]
    width = kept_ref.shape[1]
    size = pieces_ref.shape[0]
    total = kept_ref[...]
    for ref in arrived:
        total = total + ref[:, 0:width].astype(F32)
    total_ref[...] = total
    if scores_ref.shape[0] > next_pieces_ref.shape[0]:
        scores_ref[...] = jnp.zeros(scores_ref.shape, F32)
    scores_ref[0:size, :] = pieces_ref[...]
    for j, ref in enumerate(arrived):
        get_scores(ref, scores_ref, (j + 1) * size, size, width)
    rows = next_kept_ref.shape[0]
    next_kept_ref[...] = total_ref[0:rows, :]
    next_pieces_ref[...] = scores_ref[0 : next_pieces_ref.shape[0], :]
    for j, ref in enumerate(sends):
        ref[:, 0:width] = total_ref[(j + 1) * rows : (j + 2) * rows, :].astype(BF16)
        put_scores(ref, scores_ref, width)


def final_kernel(arrivals, bits, back_bits, core_mask, *refs):
    buf_own_ref, buf_other_ref, router_ref, kept_ref, pieces_ref = refs[:5]
    arrived = refs[5 : 5 + arrivals]
    x_ref, grad_ref, scores_ref, lg_ref = refs[5 + arrivals :]
    experts, width = router_ref.shape
    half, buf_width = buf_own_ref.shape
    lanes = buf_width - width
    size = pieces_ref.shape[0]
    tok = kept_ref.shape[0]
    own = own_index()
    scores_ref[0:size, :] = pieces_ref[...]
    for j, ref in enumerate(arrived):
        get_scores(ref, scores_ref, (j + 1) * size, size, width)
    tokens = half * 2 // 8 * 4
    blocks = tokens // LANES
    wide = scores_ref.shape[0] // blocks
    sender = lax.broadcasted_iota(jnp.int32, (wide, experts), 0) // SCORE_PIECES
    ids = lax.broadcasted_iota(jnp.int32, (wide, experts), 1)
    pick = jnp.where(((place_mask(sender, back_bits) ^ own) >> 1) == ids, 1.0, 0.0).astype(BF16)
    lane = lax.broadcasted_iota(jnp.int32, (lanes, experts), 0)
    ids = lax.broadcasted_iota(jnp.int32, (lanes, experts), 1)
    tally = jnp.zeros((lanes, experts), F32)
    for k in range(1, PIECES):
        tally = tally + jnp.where(lane == ids + k * experts, 1.0, 0.0)
    rows_out = grad_ref.shape[1]
    first = own * rows_out
    column = pl.multiple_of(first // LANES * LANES, LANES)
    grad = jnp.zeros((experts, LANES), F32)
    for index, ref in enumerate((buf_own_ref, buf_other_ref)):
        picked = jnp.zeros((half, wide), F32)
        for b in range(blocks):
            row = lax.broadcasted_iota(jnp.int32, (half, LANES), 0)
            token = lax.broadcasted_iota(jnp.int32, (half, LANES), 1) + b * LANES
            whole = (place_mask(row >> 3, bits) ^ (own ^ (core_mask if index else 0))) * 4 + (row & 7)
            here = jnp.where((whole == token) & ((row & 7) < 4), 1.0, 0.0).astype(BF16)
            block = scores_ref[...] if blocks == 1 else scores_ref[pl.ds(b, wide, stride=blocks), :]
            picked = picked + lax.dot_general(here, block.astype(BF16), NT, preferred_element_type=F32)
        scores = jnp.dot(picked.astype(BF16), pick, preferred_element_type=F32)
        probs = jnp.dot(ref[:, width:], tally.astype(BF16), preferred_element_type=F32)
        mean = jnp.sum(probs * scores, axis=1, keepdims=True)
        logit_grad = probs * (scores - mean)
        if index == 0:
            lg_ref[...] = logit_grad[0:8]
        grad = grad + lax.dot_general(
            logit_grad.astype(BF16), ref[:, pl.ds(column, LANES)], TN, preferred_element_type=F32
        )
    shift = (LANES - (first - column)) % LANES
    grad_ref[...] = pltpu.roll(grad, shift, 1)[:, :rows_out]
    part = jnp.dot(lg_ref[...].astype(BF16), router_ref[...], preferred_element_type=F32)
    total = kept_ref[...]
    for ref in arrived:
        total = total + ref[:, 0:width].astype(F32)
    x_ref[...] = (total + part[:tok]).astype(BF16)


def on_device(tokens, grad_out, router_logits, selected, router_w, w_gate, w_up, w_down):
    tok, width = tokens.shape
    experts = router_logits.shape[1]
    hidden = w_gate.shape[2]
    exp_size = lax.axis_size("exp")
    hid_size = lax.axis_size("hid")
    count = exp_size * hid_size
    half = count // 2
    groups, core = stage_masks(exp_size, hid_size)
    core_mask = 1 << core
    bits = [b for group in groups for b in group]
    back_groups = [[core]] + groups[::-1]
    back_bits = [b for group in back_groups for b in group]
    token_count = count * tok
    lanes = -(-PIECES * experts // LANES) * LANES

    block = pl.pallas_call(
        prep_kernel,
        out_shape=jax.ShapeDtypeStruct((2 * tok, width + lanes), BF16),
        in_specs=[HBM_SPEC] * 4,
        out_specs=VMEM_SPEC,
        scratch_shapes=[
            pltpu.VMEM(tokens.shape, tokens.dtype),
            pltpu.VMEM(grad_out.shape, grad_out.dtype),
            pltpu.VMEM(router_logits.shape, router_logits.dtype),
            pltpu.VMEM(selected.shape, selected.dtype),
            pltpu.VMEM((2 * tok, width + lanes), F32),
            pltpu.SemaphoreType.DMA((4,)),
        ],
        compiler_params=PARAMS,
        name="prep",
    )(*in_hbm(tokens, grad_out, router_logits, selected))

    weights = in_hbm(w_gate, w_up, w_down)
    for index, group in enumerate(groups):
        if index == len(groups) - 1:
            chunks = 4
            weights = pl.pallas_call(
                functools.partial(load_kernel, chunks),
                out_shape=tuple(pltpu.VMEM(w.shape, w.dtype) for w in weights),
                in_specs=[pl.BlockSpec(memory_space=pl.ANY)] + [HBM_SPEC] * 3,
                out_specs=(VMEM_SPEC,) * 3,
                scratch_shapes=[pltpu.SemaphoreType.DMA((3 * chunks,))],
                compiler_params=pltpu.CompilerParams(vmem_limit_bytes=4 * 2**20),
                cost_estimate=pl.CostEstimate(flops=0, bytes_accessed=6 * width * hidden * 2, transcendentals=0),
                name="load",
            )(block, *weights)
        block = jnp.concatenate([block] + [swap(block, m, count) for m in group_masks(group)[1:]], axis=0)
    other = swap(block, core_mask, count)

    cost = pl.CostEstimate(
        flops=2 * half * 8 * width * hidden * 4,
        bytes_accessed=3 * width * hidden * 2 + half * 8 * width * 2,
        transcendentals=half * 8 * hidden,
    )
    unit_rows = SCORE_PIECES * token_count // LANES
    kept, score = pl.pallas_call(
        functools.partial(half_kernel, bits, 0, False),
        out_shape=(
            jax.ShapeDtypeStruct((half * tok, width), F32),
            jax.ShapeDtypeStruct((1, token_count), F32),
        ),
        in_specs=[VMEM_SPEC] * 4,
        out_specs=(VMEM_SPEC, VMEM_SPEC),
        compiler_params=PARAMS,
        cost_estimate=cost,
        name="half_own",
    )(block, *weights)
    extra = -(-unit_rows // (half * tok)) * LANES
    message, pieces = pl.pallas_call(
        functools.partial(half_kernel, bits, core_mask, True),
        out_shape=(
            jax.ShapeDtypeStruct((half * tok, width + extra), BF16),
            jax.ShapeDtypeStruct((unit_rows, LANES), F32),
        ),
        in_specs=[VMEM_SPEC] * 5,
        out_specs=(VMEM_SPEC, VMEM_SPEC),
        scratch_shapes=[
            pltpu.VMEM((1, token_count), F32),
            pltpu.VMEM((max(half * tok * extra // LANES, unit_rows), LANES), F32),
        ],
        compiler_params=PARAMS,
        cost_estimate=cost,
        name="half_other",
    )(other, *weights, score)

    arrived = [swap(message, core_mask, count)]
    for group in groups[::-1]:
        masks = group_masks(group)
        radix = len(masks)
        rows = kept.shape[0]
        next_rows = rows // radix
        size = pieces.shape[0] * (1 + len(arrived))
        extra = -(-size // next_rows) * LANES
        sends = [jax.ShapeDtypeStruct((next_rows, width + extra), BF16)] * (radix - 1)
        outs = pl.pallas_call(
            functools.partial(add_kernel, len(arrived), radix),
            out_shape=[
                jax.ShapeDtypeStruct((next_rows, width), F32),
                jax.ShapeDtypeStruct((size, LANES), F32),
            ]
            + sends,
            in_specs=[VMEM_SPEC] * (2 + len(arrived)),
            out_specs=[VMEM_SPEC] * (1 + radix),
            scratch_shapes=[
                pltpu.VMEM((rows, width), F32),
                pltpu.VMEM((max(next_rows * extra // LANES, size), LANES), F32),
            ],
            compiler_params=PARAMS,
            name="add",
        )(kept, pieces, *arrived)
        kept, pieces = outs[0], outs[1]
        arrived = [swap(piece, m, count) for piece, m in zip(outs[2:], masks[1:])]

    x_grad, grad = pl.pallas_call(
        functools.partial(final_kernel, len(arrived), bits, back_bits, core_mask),
        out_shape=(
            jax.ShapeDtypeStruct((tok, width), BF16),
            jax.ShapeDtypeStruct((experts, width // count), F32),
        ),
        in_specs=[VMEM_SPEC] * (5 + len(arrived)),
        out_specs=(VMEM_SPEC, VMEM_SPEC),
        scratch_shapes=[
            pltpu.VMEM((pieces.shape[0] * (1 + len(arrived)), LANES), F32),
            pltpu.VMEM((8, experts), F32),
        ],
        compiler_params=PARAMS,
        name="final",
    )(block, other, router_w.T, kept, pieces, *arrived)
    return (x_grad, grad.T)


def solution(mesh):
    rows = P(AXES, None)
    units = P(AXES, None, None)
    return jax.shard_map(
        on_device,
        mesh=mesh,
        in_specs=(rows, rows, rows, rows, P(), units, units, units),
        out_specs=(rows, rows),
        check_vma=False,
    )
```

```python
import functools

import jax
import jax.numpy as jnp
from jax import lax
from jax.experimental import pallas as pl
from jax.experimental.pallas import tpu as pltpu
from jax.sharding import PartitionSpec as P

AXES = ("exp", "hid")
LANES = 128
PIECES = 4
SCORE_PIECES = 2
VMEM_SPEC = pl.BlockSpec(memory_space=pltpu.VMEM)
HBM_SPEC = pl.BlockSpec(memory_space=pltpu.HBM)
F32 = jnp.float32
BF16 = jnp.bfloat16
NT = (((1,), (1,)), ((), ()))
TN = (((0,), (0,)), ((), ()))
PARAMS = pltpu.CompilerParams(vmem_limit_bytes=24 * 2**20)


def stage_masks(exp_size, hid_size):
    hid_bits = hid_size.bit_length() - 1
    all_bits = (exp_size * hid_size).bit_length() - 1
    core = hid_bits
    first = list(range(max(core + 1, all_bits - 2), all_bits))
    middle = [b for b in range(all_bits) if b != core and b not in first]
    groups = [first] + [middle[i : i + 2] for i in range(0, len(middle), 2)]
    bases = [[sum(1 << b for b in group[i:]) for i in range(len(group))] for group in groups]
    return bases, 1 << core


def group_masks(basis):
    masks = [0]
    for mask in basis:
        masks = masks + [m ^ mask for m in masks]
    return masks


def swap(block, mask, count):
    return lax.ppermute(block, AXES, [(i, i ^ mask) for i in range(count)])


def place_mask(place, basis):
    total = jnp.zeros_like(place)
    for digit, mask in enumerate(basis):
        total = total ^ (((place >> digit) & 1) * mask)
    return total


def own_index():
    return lax.axis_index("exp") * lax.axis_size("hid") + lax.axis_index("hid")


def in_hbm(*arrays):
    return tuple(pltpu.with_memory_space_constraint(a, pltpu.HBM) for a in arrays)


def softmax_f32(values):
    raised = jnp.exp(values - jnp.max(values, axis=-1, keepdims=True))
    return raised / jnp.sum(raised, axis=-1, keepdims=True)


def prep_kernel(tokens_in, grad_in, logits_in, chosen_in, out_ref, tokens_ref, grad_ref, logits_ref, chosen_ref,
                rows_ref, sems):
    copies = [
        pltpu.make_async_copy(src, dst, sems.at[i])
        for i, (src, dst) in enumerate(
            [(logits_in, logits_ref), (chosen_in, chosen_ref), (tokens_in, tokens_ref), (grad_in, grad_ref)]
        )
    ]
    for copy in copies:
        copy.start()
    copies[0].wait()
    copies[1].wait()
    tok, width = tokens_ref.shape
    logits = logits_ref[...]
    chosen = chosen_ref[...]
    experts = logits.shape[1]
    ids = lax.broadcasted_iota(jnp.int32, logits.shape, 1)
    hit = ids == chosen[:, 0:1]
    for k in range(1, chosen.shape[1]):
        hit = hit | (ids == chosen[:, k : k + 1])
    top = jnp.max(jnp.where(hit, logits, -jnp.inf), axis=1, keepdims=True)
    raised = jnp.where(hit, jnp.exp(jnp.minimum(logits - top, 0.0)), 0.0)
    parts = [raised / jnp.sum(raised, axis=1, keepdims=True)]
    rest = softmax_f32(logits)
    for _ in range(PIECES - 1):
        parts.append(rest)
        rest = rest - rest.astype(BF16).astype(F32)
    lanes = out_ref.shape[1] - width
    extras = jnp.zeros((tok, lanes), F32)
    row = lax.broadcasted_iota(jnp.int32, (experts, lanes), 0)
    lane = lax.broadcasted_iota(jnp.int32, (experts, lanes), 1)
    for k, part in enumerate(parts):
        place = jnp.where(lane == row + k * experts, 1.0, 0.0).astype(BF16)
        extras = extras + jnp.dot(part.astype(BF16), place, preferred_element_type=F32)
    copies[2].wait()
    copies[3].wait()
    rows_ref[0:tok, :width] = tokens_ref[...].astype(F32)
    rows_ref[tok:, :width] = grad_ref[...].astype(F32)
    rows_ref[0:tok, width:] = extras
    rows_ref[tok:, width:] = jnp.zeros((tok, lanes), F32)
    out_ref[...] = rows_ref[...].astype(BF16)


def load_kernel(chunks, after_ref, *refs):
    count = (len(refs) - 1) // 2
    sems = refs[-1]
    copies = []
    for src, dst in zip(refs[:count], refs[count : 2 * count]):
        size = src.shape[1] // chunks
        for c in range(chunks):
            part = (slice(None), pl.ds(c * size, size))
            copies.append(pltpu.make_async_copy(src.at[part], dst.at[part], sems.at[len(copies)]))
    for copy in copies:
        copy.start()
    for copy in copies:
        copy.wait()


def put_scores(out_ref, scores_ref, width):
    rows = out_ref.shape[0]
    for c in range((out_ref.shape[1] - width) // LANES):
        out_ref[:, width + c * LANES : width + (c + 1) * LANES] = scores_ref[c * rows : (c + 1) * rows, :].astype(BF16)


def get_scores(in_ref, scores_ref, base, size, width):
    rows = in_ref.shape[0]
    for c in range(-(-size // rows)):
        here = min(rows, size - c * rows)
        tall = min(rows, -(-here // 16) * 16)
        block = in_ref[0:tall, width + c * LANES : width + (c + 1) * LANES].astype(F32)
        scores_ref[base + c * rows : base + c * rows + here, :] = block[:here]


def half_kernel(basis, swap_mask, last, buf_ref, gate_ref, up_ref, down_ref, *rest):
    width = gate_ref.shape[1]
    experts_width = buf_ref.shape[1] - width
    own = own_index()
    expert = own // 2
    rows = buf_ref.shape[0]
    if last:
        base_ref, out_ref, pieces_ref, score_ref, padded_ref = rest
        score_ref[...] = base_ref[...]
    else:
        out_ref, score_ref = rest
        score_ref[...] = jnp.zeros(score_ref.shape, F32)
    tokens = score_ref.shape[1]
    step = min(rows, 128)

    def one(index):
        start = pl.multiple_of(index * step, step)
        block = buf_ref[pl.ds(start, step), :]
        act = block[:, :width]
        extras = block[:, width:].astype(F32)
        lane = lax.broadcasted_iota(jnp.int32, (step, experts_width), 1)
        column = jnp.sum(jnp.where(lane == expert, extras, 0.0), axis=1, keepdims=True)
        gate_pre = jnp.dot(act, gate_ref[0], preferred_element_type=F32)
        up_pre = jnp.dot(act, up_ref[0], preferred_element_type=F32)
        back = lax.dot_general(act, down_ref[0], NT, preferred_element_type=F32)
        back = pltpu.roll(back, step - 4, 0)
        sig = jax.nn.sigmoid(gate_pre)
        act_gate = gate_pre * sig
        score = jnp.sum(act_gate * up_pre * back, axis=1, keepdims=True)
        weighted = column * back
        grad_gate = weighted * up_pre * sig * (1.0 + gate_pre * (1.0 - sig))
        grad_up = weighted * act_gate

        def compact(value):
            pairs = value.reshape(step // 16, 16, value.shape[1])
            low = pairs[:, :8]
            high = pairs[:, 8:]
            high = jnp.concatenate([high[:, 4:], high[:, :4]], axis=1)
            sub = lax.broadcasted_iota(jnp.int32, low.shape, 1)
            return jnp.where(sub < 4, low, high).reshape(step // 2, value.shape[1]).astype(BF16)

        total = lax.dot_general(compact(grad_gate), gate_ref[0], NT, preferred_element_type=F32)
        total = total + lax.dot_general(compact(grad_up), up_ref[0], NT, preferred_element_type=F32)
        out_start = pl.multiple_of(index * (step // 2), step // 2)
        out_ref[pl.ds(out_start, step // 2), 0:width] = total.astype(out_ref.dtype)

        row = lax.broadcasted_iota(jnp.int32, (step, tokens), 0) + start
        token = lax.broadcasted_iota(jnp.int32, (step, tokens), 1)
        whole = (place_mask(row >> 3, basis) ^ (own ^ swap_mask)) * 4 + (row & 7)
        here = (whole == token) & ((row & 7) < 4)
        score_ref[...] += jnp.sum(jnp.where(here, score, 0.0), axis=0, keepdims=True)

    if rows == step:
        one(0)
    else:
        pl.loop(0, rows // step)(one)
    if last:
        blocks = tokens // LANES
        padded_ref[...] = jnp.zeros(padded_ref.shape, F32)
        value = score_ref[...]
        for piece in range(SCORE_PIECES):
            rounded = value.astype(BF16).astype(F32)
            for b in range(blocks):
                padded_ref[piece * blocks + b : piece * blocks + b + 1, :] = rounded[:, b * LANES : (b + 1) * LANES]
            value = value - rounded
        pieces_ref[...] = padded_ref[0 : pieces_ref.shape[0], :]
        put_scores(out_ref, padded_ref, width)


def add_kernel(arrivals, radix, *refs):
    kept_ref, pieces_ref = refs[0], refs[1]
    arrived = refs[2 : 2 + arrivals]
    outs = refs[2 + arrivals :]
    next_kept_ref, next_pieces_ref = outs[0], outs[1]
    sends = outs[2 : 1 + radix]
    total_ref, scores_ref = outs[1 + radix :]
    width = kept_ref.shape[1]
    size = pieces_ref.shape[0]
    total = kept_ref[...]
    for ref in arrived:
        total = total + ref[:, 0:width].astype(F32)
    total_ref[...] = total
    if scores_ref.shape[0] > next_pieces_ref.shape[0]:
        scores_ref[...] = jnp.zeros(scores_ref.shape, F32)
    scores_ref[0:size, :] = pieces_ref[...]
    for j, ref in enumerate(arrived):
        get_scores(ref, scores_ref, (j + 1) * size, size, width)
    rows = next_kept_ref.shape[0]
    next_kept_ref[...] = total_ref[0:rows, :]
    next_pieces_ref[...] = scores_ref[0 : next_pieces_ref.shape[0], :]
    for j, ref in enumerate(sends):
        ref[:, 0:width] = total_ref[(j + 1) * rows : (j + 2) * rows, :].astype(BF16)
        put_scores(ref, scores_ref, width)


def table_kernel(basis, core_mask, rows_out, after_ref, buf_own_ref, buf_other_ref, here_ref, probs_ref, column_ref):
    half, buf_width = buf_own_ref.shape
    experts = probs_ref.shape[1]
    tokens = here_ref.shape[1]
    width = buf_width - -(-PIECES * experts // LANES) * LANES
    lanes = buf_width - width
    own = own_index()
    lane = lax.broadcasted_iota(jnp.int32, (lanes, experts), 0)
    ids = lax.broadcasted_iota(jnp.int32, (lanes, experts), 1)
    tally = jnp.zeros((lanes, experts), F32)
    for k in range(1, PIECES):
        tally = tally + jnp.where(lane == ids + k * experts, 1.0, 0.0)
    column = pl.multiple_of(own * rows_out // LANES * LANES, LANES)
    for index, ref in enumerate((buf_own_ref, buf_other_ref)):
        row = lax.broadcasted_iota(jnp.int32, (half, tokens), 0)
        token = lax.broadcasted_iota(jnp.int32, (half, tokens), 1)
        whole = (place_mask(row >> 3, basis) ^ (own ^ (core_mask if index else 0))) * 4 + (row & 7)
        here = jnp.where((whole == token) & ((row & 7) < 4), 1.0, 0.0).astype(BF16)
        part = slice(index * half, (index + 1) * half)
        here_ref[part, :] = here
        probs_ref[part, :] = jnp.dot(ref[:, width:], tally.astype(BF16), preferred_element_type=F32)
        column_ref[part, :] = ref[:, pl.ds(column, LANES)]


def final_kernel(arrivals, back_basis, *refs):
    here_ref, probs_ref, column_ref, router_ref, kept_ref, pieces_ref = refs[:6]
    arrived = refs[6 : 6 + arrivals]
    x_ref, grad_ref, scores_ref = refs[6 + arrivals :]
    experts, width = router_ref.shape
    size = pieces_ref.shape[0]
    tok = kept_ref.shape[0]
    own = own_index()
    scores_ref[0:size, :] = pieces_ref[...]
    for j, ref in enumerate(arrived):
        get_scores(ref, scores_ref, (j + 1) * size, size, width)
    blocks = here_ref.shape[1] // LANES
    wide = scores_ref.shape[0] // blocks
    sender = lax.broadcasted_iota(jnp.int32, (wide, experts), 0) // SCORE_PIECES
    ids = lax.broadcasted_iota(jnp.int32, (wide, experts), 1)
    pick = jnp.where(((place_mask(sender, back_basis) ^ own) >> 1) == ids, 1.0, 0.0).astype(BF16)
    picked = jnp.zeros((here_ref.shape[0], wide), F32)
    for b in range(blocks):
        block = scores_ref[...] if blocks == 1 else scores_ref[pl.ds(b, wide, stride=blocks), :]
        picked = picked + lax.dot_general(
            here_ref[:, b * LANES : (b + 1) * LANES], block.astype(BF16), NT, preferred_element_type=F32
        )
    scores = jnp.dot(picked.astype(BF16), pick, preferred_element_type=F32)
    probs = probs_ref[...]
    mean = jnp.sum(probs * scores, axis=1, keepdims=True)
    logit_grad = (probs * (scores - mean)).astype(BF16)
    part = jnp.dot(logit_grad[0:16], router_ref[...], preferred_element_type=F32)
    total = kept_ref[...]
    for ref in arrived:
        total = total + ref[:, 0:width].astype(F32)
    x_ref[...] = (total + part[:tok]).astype(BF16)
    grad = lax.dot_general(logit_grad, column_ref[...], TN, preferred_element_type=F32)
    rows_out = grad_ref.shape[1]
    first = own * rows_out % LANES
    grad_ref[...] = pltpu.roll(grad, (LANES - first) % LANES, 1)[:, :rows_out]


def on_device(tokens, grad_out, router_logits, selected, router_w, w_gate, w_up, w_down):
    tok, width = tokens.shape
    experts = router_logits.shape[1]
    hidden = w_gate.shape[2]
    exp_size = lax.axis_size("exp")
    hid_size = lax.axis_size("hid")
    count = exp_size * hid_size
    half = count // 2
    groups, core_mask = stage_masks(exp_size, hid_size)
    basis = [m for group in groups for m in group]
    back_basis = [core_mask] + [m for group in groups[::-1] for m in group]
    token_count = count * tok
    lanes = -(-PIECES * experts // LANES) * LANES

    block = pl.pallas_call(
        prep_kernel,
        out_shape=jax.ShapeDtypeStruct((2 * tok, width + lanes), BF16),
        in_specs=[HBM_SPEC] * 4,
        out_specs=VMEM_SPEC,
        scratch_shapes=[
            pltpu.VMEM(tokens.shape, tokens.dtype),
            pltpu.VMEM(grad_out.shape, grad_out.dtype),
            pltpu.VMEM(router_logits.shape, router_logits.dtype),
            pltpu.VMEM(selected.shape, selected.dtype),
            pltpu.VMEM((2 * tok, width + lanes), F32),
            pltpu.SemaphoreType.DMA((4,)),
        ],
        compiler_params=PARAMS,
        name="prep",
    )(*in_hbm(tokens, grad_out, router_logits, selected))

    weights = in_hbm(w_gate, w_up, w_down)
    for index, group in enumerate(groups):
        if index == len(groups) - 1:
            chunks = 4
            weights = pl.pallas_call(
                functools.partial(load_kernel, chunks),
                out_shape=tuple(pltpu.VMEM(w.shape, w.dtype) for w in weights),
                in_specs=[pl.BlockSpec(memory_space=pl.ANY)] + [HBM_SPEC] * 3,
                out_specs=(VMEM_SPEC,) * 3,
                scratch_shapes=[pltpu.SemaphoreType.DMA((3 * chunks,))],
                compiler_params=pltpu.CompilerParams(vmem_limit_bytes=4 * 2**20),
                cost_estimate=pl.CostEstimate(flops=0, bytes_accessed=6 * width * hidden * 2, transcendentals=0),
                name="load",
            )(block, *weights)
        block = jnp.concatenate([block] + [swap(block, m, count) for m in group_masks(group)[1:]], axis=0)
    other = swap(block, core_mask, count)

    cost = pl.CostEstimate(
        flops=2 * half * 8 * width * hidden * 4,
        bytes_accessed=3 * width * hidden * 2 + half * 8 * width * 2,
        transcendentals=half * 8 * hidden,
    )
    unit_rows = SCORE_PIECES * token_count // LANES
    kept, score = pl.pallas_call(
        functools.partial(half_kernel, basis, 0, False),
        out_shape=(
            jax.ShapeDtypeStruct((half * tok, width), F32),
            jax.ShapeDtypeStruct((1, token_count), F32),
        ),
        in_specs=[VMEM_SPEC] * 4,
        out_specs=(VMEM_SPEC, VMEM_SPEC),
        compiler_params=PARAMS,
        cost_estimate=pl.CostEstimate(
            flops=cost.flops * 16, bytes_accessed=cost.bytes_accessed, transcendentals=cost.transcendentals
        ),
        name="half_own",
    )(block, *weights)
    extra = -(-unit_rows // (half * tok)) * LANES
    message, pieces = pl.pallas_call(
        functools.partial(half_kernel, basis, core_mask, True),
        out_shape=(
            jax.ShapeDtypeStruct((half * tok, width + extra), BF16),
            jax.ShapeDtypeStruct((unit_rows, LANES), F32),
        ),
        in_specs=[VMEM_SPEC] * 5,
        out_specs=(VMEM_SPEC, VMEM_SPEC),
        scratch_shapes=[
            pltpu.VMEM((1, token_count), F32),
            pltpu.VMEM((max(half * tok * extra // LANES, unit_rows), LANES), F32),
        ],
        compiler_params=PARAMS,
        cost_estimate=cost,
        name="half_other",
    )(other, *weights, score)

    arrived = [swap(message, core_mask, count)]
    tables = None
    rows_out = width // count
    for group in groups[::-1]:
        masks = group_masks(group)
        radix = len(masks)
        rows = kept.shape[0]
        next_rows = rows // radix
        size = pieces.shape[0] * (1 + len(arrived))
        extra = -(-size // next_rows) * LANES
        sends = [jax.ShapeDtypeStruct((next_rows, width + extra), BF16)] * (radix - 1)
        outs = pl.pallas_call(
            functools.partial(add_kernel, len(arrived), radix),
            out_shape=[
                jax.ShapeDtypeStruct((next_rows, width), F32),
                jax.ShapeDtypeStruct((size, LANES), F32),
            ]
            + sends,
            in_specs=[VMEM_SPEC] * (2 + len(arrived)),
            out_specs=[VMEM_SPEC] * (1 + radix),
            scratch_shapes=[
                pltpu.VMEM((rows, width), F32),
                pltpu.VMEM((max(next_rows * extra // LANES, size), LANES), F32),
            ],
            compiler_params=PARAMS,
            name="add",
        )(kept, pieces, *arrived)
        kept, pieces = outs[0], outs[1]
        if tables is None:
            tables = pl.pallas_call(
                functools.partial(table_kernel, basis, core_mask, rows_out),
                out_shape=(
                    jax.ShapeDtypeStruct((2 * block.shape[0], token_count), BF16),
                    jax.ShapeDtypeStruct((2 * block.shape[0], experts), F32),
                    jax.ShapeDtypeStruct((2 * block.shape[0], LANES), BF16),
                ),
                in_specs=[pl.BlockSpec(memory_space=pl.ANY)] + [VMEM_SPEC] * 2,
                out_specs=(VMEM_SPEC,) * 3,
                compiler_params=PARAMS,
                cost_estimate=pl.CostEstimate(flops=10**9, bytes_accessed=10**6, transcendentals=0),
                name="tables",
            )(pieces, block, other)
        arrived = [swap(piece, m, count) for piece, m in zip(outs[2:], masks[1:])]

    x_grad, grad = pl.pallas_call(
        functools.partial(final_kernel, len(arrived), back_basis),
        out_shape=(
            jax.ShapeDtypeStruct((tok, width), BF16),
            jax.ShapeDtypeStruct((experts, rows_out), F32),
        ),
        in_specs=[VMEM_SPEC] * (6 + len(arrived)),
        out_specs=(VMEM_SPEC, VMEM_SPEC),
        scratch_shapes=[pltpu.VMEM((pieces.shape[0] * (1 + len(arrived)), LANES), F32)],
        compiler_params=PARAMS,
        name="final",
    )(*tables, router_w.T, kept, pieces, *arrived)
    return (x_grad, grad.T)


def solution(mesh):
    rows = P(AXES, None)
    units = P(AXES, None, None)
    return jax.shard_map(
        on_device,
        mesh=mesh,
        in_specs=(rows, rows, rows, rows, P(), units, units, units),
        out_specs=(rows, rows),
        check_vma=False,
    )
```

```python
import functools

import jax
import jax.numpy as jnp
from jax import lax
from jax.experimental import pallas as pl
from jax.experimental.pallas import tpu as pltpu
from jax.sharding import PartitionSpec as P

AXES = ("exp", "hid")
LANES = 128
PIECES = 4
SCORE_PIECES = 2
VMEM_SPEC = pl.BlockSpec(memory_space=pltpu.VMEM)
HBM_SPEC = pl.BlockSpec(memory_space=pltpu.HBM)
F32 = jnp.float32
BF16 = jnp.bfloat16
NT = (((1,), (1,)), ((), ()))
TN = (((0,), (0,)), ((), ()))
PARAMS = pltpu.CompilerParams(vmem_limit_bytes=24 * 2**20)


def stage_masks(exp_size, hid_size):
    hid_bits = hid_size.bit_length() - 1
    all_bits = (exp_size * hid_size).bit_length() - 1
    core = hid_bits
    first = list(range(max(core + 1, all_bits - 2), all_bits))
    middle = [b for b in range(all_bits) if b != core and b not in first]
    groups = [first] + [middle[i : i + 2] for i in range(0, len(middle), 2)]
    bases = [[sum(1 << b for b in group[i:]) for i in range(len(group))] for group in groups]
    return bases, 1 << core


def group_masks(basis):
    masks = [0]
    for mask in basis:
        masks = masks + [m ^ mask for m in masks]
    return masks


def near_first(basis):
    return [a ^ b for a, b in zip(basis, basis[1:] + [0])]


def swap(block, mask, count):
    return lax.ppermute(block, AXES, [(i, i ^ mask) for i in range(count)])


def place_mask(place, basis):
    total = jnp.zeros_like(place)
    for digit, mask in enumerate(basis):
        total = total ^ (((place >> digit) & 1) * mask)
    return total


def own_index():
    return lax.axis_index("exp") * lax.axis_size("hid") + lax.axis_index("hid")


def in_hbm(*arrays):
    return tuple(pltpu.with_memory_space_constraint(a, pltpu.HBM) for a in arrays)


def softmax_f32(values):
    raised = jnp.exp(values - jnp.max(values, axis=-1, keepdims=True))
    return raised / jnp.sum(raised, axis=-1, keepdims=True)


def prep_kernel(tokens_in, grad_in, logits_in, chosen_in, out_ref, tokens_ref, grad_ref, logits_ref, chosen_ref,
                rows_ref, sems):
    copies = [
        pltpu.make_async_copy(src, dst, sems.at[i])
        for i, (src, dst) in enumerate(
            [(logits_in, logits_ref), (chosen_in, chosen_ref), (tokens_in, tokens_ref), (grad_in, grad_ref)]
        )
    ]
    for copy in copies:
        copy.start()
    copies[0].wait()
    copies[1].wait()
    tok, width = tokens_ref.shape
    logits = logits_ref[...]
    chosen = chosen_ref[...]
    experts = logits.shape[1]
    ids = lax.broadcasted_iota(jnp.int32, logits.shape, 1)
    hit = ids == chosen[:, 0:1]
    for k in range(1, chosen.shape[1]):
        hit = hit | (ids == chosen[:, k : k + 1])
    top = jnp.max(jnp.where(hit, logits, -jnp.inf), axis=1, keepdims=True)
    raised = jnp.where(hit, jnp.exp(jnp.minimum(logits - top, 0.0)), 0.0)
    parts = [raised / jnp.sum(raised, axis=1, keepdims=True)]
    rest = softmax_f32(logits)
    for _ in range(PIECES - 1):
        parts.append(rest)
        rest = rest - rest.astype(BF16).astype(F32)
    lanes = out_ref.shape[1] - width
    extras = jnp.zeros((tok, lanes), F32)
    row = lax.broadcasted_iota(jnp.int32, (experts, lanes), 0)
    lane = lax.broadcasted_iota(jnp.int32, (experts, lanes), 1)
    for k, part in enumerate(parts):
        place = jnp.where(lane == row + k * experts, 1.0, 0.0).astype(BF16)
        extras = extras + jnp.dot(part.astype(BF16), place, preferred_element_type=F32)
    copies[2].wait()
    copies[3].wait()
    rows_ref[0:tok, :width] = tokens_ref[...].astype(F32)
    rows_ref[tok:, :width] = grad_ref[...].astype(F32)
    rows_ref[0:tok, width:] = extras
    rows_ref[tok:, width:] = jnp.zeros((tok, lanes), F32)
    out_ref[...] = rows_ref[...].astype(BF16)


def load_kernel(chunks, after_ref, gate_in, up_in, down_in, pair_ref, down_ref, sems):
    hidden = gate_in.shape[2]
    copies = []

    def add(src, dst):
        copies.append(pltpu.make_async_copy(src, dst, sems.at[len(copies)]))

    for c in range(chunks):
        rows = gate_in.shape[1] // chunks
        part = pl.ds(c * rows, rows)
        add(gate_in.at[0, part, :], pair_ref.at[part, 0:hidden])
        add(up_in.at[0, part, :], pair_ref.at[part, hidden : 2 * hidden])
        rows = hidden // chunks
        part = pl.ds(c * rows, rows)
        add(down_in.at[0, part, :], down_ref.at[part, :])
    for copy in copies:
        copy.start()
    for copy in copies:
        copy.wait()


def put_scores(out_ref, scores_ref, width):
    rows = out_ref.shape[0]
    for c in range((out_ref.shape[1] - width) // LANES):
        out_ref[:, width + c * LANES : width + (c + 1) * LANES] = scores_ref[c * rows : (c + 1) * rows, :].astype(BF16)


def get_scores(in_ref, scores_ref, base, size, width):
    rows = in_ref.shape[0]
    for c in range(-(-size // rows)):
        here = min(rows, size - c * rows)
        tall = min(rows, -(-here // 16) * 16)
        block = in_ref[0:tall, width + c * LANES : width + (c + 1) * LANES].astype(F32)
        scores_ref[base + c * rows : base + c * rows + here, :] = block[:here]


def half_kernel(basis, swap_mask, last, buf_ref, pair_ref, down_ref, *rest):
    hidden, width = down_ref.shape
    experts_width = buf_ref.shape[1] - width
    own = own_index()
    expert = own // 2
    rows = buf_ref.shape[0]
    if last:
        base_ref, out_ref, pieces_ref, score_ref, padded_ref = rest
        score_ref[...] = base_ref[...]
    else:
        out_ref, score_ref = rest
        score_ref[...] = jnp.zeros(score_ref.shape, F32)
    tokens = score_ref.shape[1]
    step = min(rows, 128)

    def one(index):
        start = pl.multiple_of(index * step, step)
        block = buf_ref[pl.ds(start, step), :]
        act = block[:, :width]
        extras = block[:, width:].astype(F32)
        lane = lax.broadcasted_iota(jnp.int32, (step, experts_width), 1)
        column = jnp.sum(jnp.where(lane == expert, extras, 0.0), axis=1, keepdims=True)
        pair = jnp.dot(act, pair_ref[...], preferred_element_type=F32)
        gate_pre = pair[:, :hidden]
        up_pre = pair[:, hidden:]
        back = lax.dot_general(act, down_ref[...], NT, preferred_element_type=F32)
        back = pltpu.roll(back, step - 4, 0)
        sig = jax.nn.sigmoid(gate_pre)
        act_gate = gate_pre * sig
        score = jnp.sum(act_gate * up_pre * back, axis=1, keepdims=True)
        weighted = column * back
        grad_gate = weighted * up_pre * sig * (1.0 + gate_pre * (1.0 - sig))
        grad_up = weighted * act_gate

        def compact(value):
            pairs = value.reshape(step // 16, 16, value.shape[1])
            low = pairs[:, :8]
            high = pairs[:, 8:]
            high = jnp.concatenate([high[:, 4:], high[:, :4]], axis=1)
            sub = lax.broadcasted_iota(jnp.int32, low.shape, 1)
            return jnp.where(sub < 4, low, high).reshape(step // 2, value.shape[1]).astype(BF16)

        grads = jnp.concatenate([compact(grad_gate), compact(grad_up)], axis=1)
        total = lax.dot_general(grads, pair_ref[...], NT, preferred_element_type=F32)
        out_start = pl.multiple_of(index * (step // 2), step // 2)
        out_ref[pl.ds(out_start, step // 2), 0:width] = total.astype(out_ref.dtype)

        row = lax.broadcasted_iota(jnp.int32, (step, tokens), 0) + start
        token = lax.broadcasted_iota(jnp.int32, (step, tokens), 1)
        whole = (place_mask(row >> 3, basis) ^ (own ^ swap_mask)) * 4 + (row & 7)
        here = (whole == token) & ((row & 7) < 4)
        score_ref[...] += jnp.sum(jnp.where(here, score, 0.0), axis=0, keepdims=True)

    if rows == step:
        one(0)
    else:
        pl.loop(0, rows // step)(one)
    if last:
        blocks = tokens // LANES
        padded_ref[...] = jnp.zeros(padded_ref.shape, F32)
        value = score_ref[...]
        for piece in range(SCORE_PIECES):
            rounded = value.astype(BF16).astype(F32)
            for b in range(blocks):
                padded_ref[piece * blocks + b : piece * blocks + b + 1, :] = rounded[:, b * LANES : (b + 1) * LANES]
            value = value - rounded
        pieces_ref[...] = padded_ref[0 : pieces_ref.shape[0], :]
        put_scores(out_ref, padded_ref, width)


def add_kernel(arrivals, positions, *refs):
    kept_ref, pieces_ref = refs[0], refs[1]
    arrived = refs[2 : 2 + arrivals]
    outs = refs[2 + arrivals :]
    next_kept_ref, next_pieces_ref = outs[0], outs[1]
    sends = outs[2 : 2 + len(positions)]
    total_ref, scores_ref = outs[2 + len(positions) :]
    width = kept_ref.shape[1]
    size = pieces_ref.shape[0]
    total = kept_ref[...]
    for ref in arrived:
        total = total + ref[:, 0:width].astype(F32)
    total_ref[...] = total
    if scores_ref.shape[0] > next_pieces_ref.shape[0]:
        scores_ref[...] = jnp.zeros(scores_ref.shape, F32)
    scores_ref[0:size, :] = pieces_ref[...]
    for j, ref in enumerate(arrived):
        get_scores(ref, scores_ref, (j + 1) * size, size, width)
    rows = next_kept_ref.shape[0]
    next_kept_ref[...] = total_ref[0:rows, :]
    next_pieces_ref[...] = scores_ref[0 : next_pieces_ref.shape[0], :]
    for j, ref in zip(positions, sends):
        ref[:, 0:width] = total_ref[j * rows : (j + 1) * rows, :].astype(BF16)
        put_scores(ref, scores_ref, width)


def table_kernel(basis, core_mask, rows_out, after_ref, buf_own_ref, buf_other_ref, here_ref, probs_ref, column_ref):
    half, buf_width = buf_own_ref.shape
    experts = probs_ref.shape[1]
    tokens = here_ref.shape[1]
    width = buf_width - -(-PIECES * experts // LANES) * LANES
    lanes = buf_width - width
    own = own_index()
    lane = lax.broadcasted_iota(jnp.int32, (lanes, experts), 0)
    ids = lax.broadcasted_iota(jnp.int32, (lanes, experts), 1)
    tally = jnp.zeros((lanes, experts), F32)
    for k in range(1, PIECES):
        tally = tally + jnp.where(lane == ids + k * experts, 1.0, 0.0)
    column = pl.multiple_of(own * rows_out // LANES * LANES, LANES)
    for index, ref in enumerate((buf_own_ref, buf_other_ref)):
        row = lax.broadcasted_iota(jnp.int32, (half, tokens), 0)
        token = lax.broadcasted_iota(jnp.int32, (half, tokens), 1)
        whole = (place_mask(row >> 3, basis) ^ (own ^ (core_mask if index else 0))) * 4 + (row & 7)
        here = jnp.where((whole == token) & ((row & 7) < 4), 1.0, 0.0).astype(BF16)
        part = slice(index * half, (index + 1) * half)
        here_ref[part, :] = here
        probs_ref[part, :] = jnp.dot(ref[:, width:], tally.astype(BF16), preferred_element_type=F32)
        column_ref[part, :] = ref[:, pl.ds(column, LANES)]


def final_kernel(arrivals, back_basis, *refs):
    here_ref, probs_ref, column_ref, router_ref, kept_ref, pieces_ref = refs[:6]
    arrived = refs[6 : 6 + arrivals]
    x_out, grad_out, x_ref, grad_ref, scores_ref, sems = refs[6 + arrivals :]
    experts, width = router_ref.shape
    size = pieces_ref.shape[0]
    tok = kept_ref.shape[0]
    own = own_index()
    scores_ref[0:size, :] = pieces_ref[...]
    for j, ref in enumerate(arrived):
        get_scores(ref, scores_ref, (j + 1) * size, size, width)
    blocks = here_ref.shape[1] // LANES
    wide = scores_ref.shape[0] // blocks
    sender = lax.broadcasted_iota(jnp.int32, (wide, experts), 0) // SCORE_PIECES
    ids = lax.broadcasted_iota(jnp.int32, (wide, experts), 1)
    pick = jnp.where(((place_mask(sender, back_basis) ^ own) >> 1) == ids, 1.0, 0.0).astype(BF16)
    picked = jnp.zeros((here_ref.shape[0], wide), F32)
    for b in range(blocks):
        block = scores_ref[...] if blocks == 1 else scores_ref[pl.ds(b, wide, stride=blocks), :]
        picked = picked + lax.dot_general(
            here_ref[:, b * LANES : (b + 1) * LANES], block.astype(BF16), NT, preferred_element_type=F32
        )
    scores = jnp.dot(picked.astype(BF16), pick, preferred_element_type=F32)
    probs = probs_ref[...]
    mean = jnp.sum(probs * scores, axis=1, keepdims=True)
    logit_grad = (probs * (scores - mean)).astype(BF16)
    part = jnp.dot(logit_grad[0:16], router_ref[...], preferred_element_type=F32)
    total = kept_ref[...]
    for ref in arrived:
        total = total + ref[:, 0:width].astype(F32)
    x_ref[...] = (total + part[:tok]).astype(BF16)
    x_copy = pltpu.make_async_copy(x_ref, x_out, sems.at[0])
    x_copy.start()
    grad = lax.dot_general(logit_grad, column_ref[...], TN, preferred_element_type=F32)
    rows_out = grad_ref.shape[1]
    first = own * rows_out % LANES
    grad_ref[...] = pltpu.roll(grad, (LANES - first) % LANES, 1)[:, :rows_out]
    grad_copy = pltpu.make_async_copy(grad_ref, grad_out, sems.at[1])
    grad_copy.start()
    x_copy.wait()
    grad_copy.wait()


def on_device(tokens, grad_out, router_logits, selected, router_w, w_gate, w_up, w_down):
    tok, width = tokens.shape
    experts = router_logits.shape[1]
    hidden = w_gate.shape[2]
    exp_size = lax.axis_size("exp")
    hid_size = lax.axis_size("hid")
    count = exp_size * hid_size
    half = count // 2
    groups, core_mask = stage_masks(exp_size, hid_size)
    basis = [m for group in groups for m in group]
    back_groups = [near_first(group) for group in groups[:0:-1]] + [groups[0]]
    back_basis = [core_mask] + [m for group in back_groups for m in group]
    token_count = count * tok
    lanes = -(-PIECES * experts // LANES) * LANES

    block = pl.pallas_call(
        prep_kernel,
        out_shape=jax.ShapeDtypeStruct((2 * tok, width + lanes), BF16),
        in_specs=[HBM_SPEC] * 4,
        out_specs=VMEM_SPEC,
        scratch_shapes=[
            pltpu.VMEM(tokens.shape, tokens.dtype),
            pltpu.VMEM(grad_out.shape, grad_out.dtype),
            pltpu.VMEM(router_logits.shape, router_logits.dtype),
            pltpu.VMEM(selected.shape, selected.dtype),
            pltpu.VMEM((2 * tok, width + lanes), F32),
            pltpu.SemaphoreType.DMA((4,)),
        ],
        compiler_params=PARAMS,
        name="prep",
    )(*in_hbm(tokens, grad_out, router_logits, selected))

    weights = in_hbm(w_gate, w_up, w_down)
    for index, group in enumerate(groups):
        if index == len(groups) - 1:
            chunks = 4
            weights = pl.pallas_call(
                functools.partial(load_kernel, chunks),
                out_shape=(pltpu.VMEM((width, 2 * hidden), BF16), pltpu.VMEM((hidden, width), BF16)),
                in_specs=[pl.BlockSpec(memory_space=pl.ANY)] + [HBM_SPEC] * 3,
                out_specs=(VMEM_SPEC,) * 2,
                scratch_shapes=[pltpu.SemaphoreType.DMA((3 * chunks,))],
                compiler_params=pltpu.CompilerParams(vmem_limit_bytes=4 * 2**20),
                cost_estimate=pl.CostEstimate(flops=0, bytes_accessed=6 * width * hidden * 2, transcendentals=0),
                name="load",
            )(block, *weights)
        block = jnp.concatenate([block] + [swap(block, m, count) for m in group_masks(group)[1:]], axis=0)
    other = swap(block, core_mask, count)

    cost = pl.CostEstimate(
        flops=2 * half * 8 * width * hidden * 4,
        bytes_accessed=3 * width * hidden * 2 + half * 8 * width * 2,
        transcendentals=half * 8 * hidden,
    )
    unit_rows = SCORE_PIECES * token_count // LANES
    kept, score = pl.pallas_call(
        functools.partial(half_kernel, basis, 0, False),
        out_shape=(
            jax.ShapeDtypeStruct((half * tok, width), F32),
            jax.ShapeDtypeStruct((1, token_count), F32),
        ),
        in_specs=[VMEM_SPEC] * 3,
        out_specs=(VMEM_SPEC, VMEM_SPEC),
        compiler_params=PARAMS,
        cost_estimate=pl.CostEstimate(
            flops=cost.flops * 16, bytes_accessed=cost.bytes_accessed, transcendentals=cost.transcendentals
        ),
        name="half_own",
    )(block, *weights)
    extra = -(-unit_rows // (half * tok)) * LANES
    message, pieces = pl.pallas_call(
        functools.partial(half_kernel, basis, core_mask, True),
        out_shape=(
            jax.ShapeDtypeStruct((half * tok, width + extra), BF16),
            jax.ShapeDtypeStruct((unit_rows, LANES), F32),
        ),
        in_specs=[VMEM_SPEC] * 4,
        out_specs=(VMEM_SPEC, VMEM_SPEC),
        scratch_shapes=[
            pltpu.VMEM((1, token_count), F32),
            pltpu.VMEM((max(half * tok * extra // LANES, unit_rows), LANES), F32),
        ],
        compiler_params=PARAMS,
        cost_estimate=cost,
        name="half_other",
    )(other, *weights, score)

    arrived = [swap(message, core_mask, count)]
    tables = None
    rows_out = width // count
    for group, back_group in zip(groups[::-1], back_groups):
        masks = group_masks(group)
        back_masks = group_masks(back_group)
        radix = len(masks)
        rows = kept.shape[0]
        next_rows = rows // radix
        size = pieces.shape[0] * (1 + len(arrived))
        extra = -(-size // next_rows) * LANES
        sends = [jax.ShapeDtypeStruct((next_rows, width + extra), BF16)] * (radix - 1)
        outs = pl.pallas_call(
            functools.partial(add_kernel, len(arrived), [masks.index(m) for m in back_masks[1:]]),
            out_shape=[
                jax.ShapeDtypeStruct((next_rows, width), F32),
                jax.ShapeDtypeStruct((size, LANES), F32),
            ]
            + sends,
            in_specs=[VMEM_SPEC] * (2 + len(arrived)),
            out_specs=[VMEM_SPEC] * (1 + radix),
            scratch_shapes=[
                pltpu.VMEM((rows, width), F32),
                pltpu.VMEM((max(next_rows * extra // LANES, size), LANES), F32),
            ],
            compiler_params=PARAMS,
            name="add",
        )(kept, pieces, *arrived)
        kept, pieces = outs[0], outs[1]
        if tables is None:
            tables = pl.pallas_call(
                functools.partial(table_kernel, basis, core_mask, rows_out),
                out_shape=(
                    jax.ShapeDtypeStruct((2 * block.shape[0], token_count), BF16),
                    jax.ShapeDtypeStruct((2 * block.shape[0], experts), F32),
                    jax.ShapeDtypeStruct((2 * block.shape[0], LANES), BF16),
                ),
                in_specs=[pl.BlockSpec(memory_space=pl.ANY)] + [VMEM_SPEC] * 2,
                out_specs=(VMEM_SPEC,) * 3,
                compiler_params=PARAMS,
                cost_estimate=pl.CostEstimate(flops=10**9, bytes_accessed=10**6, transcendentals=0),
                name="tables",
            )(pieces, block, other)
        arrived = [swap(piece, m, count) for piece, m in zip(outs[2:], back_masks[1:])]

    x_grad, grad = pl.pallas_call(
        functools.partial(final_kernel, len(arrived), back_basis),
        out_shape=(
            jax.ShapeDtypeStruct((tok, width), BF16),
            jax.ShapeDtypeStruct((experts, rows_out), F32),
        ),
        in_specs=[VMEM_SPEC] * (6 + len(arrived)),
        out_specs=(HBM_SPEC, HBM_SPEC),
        scratch_shapes=[
            pltpu.VMEM((tok, width), BF16),
            pltpu.VMEM((experts, rows_out), F32),
            pltpu.VMEM((pieces.shape[0] * (1 + len(arrived)), LANES), F32),
            pltpu.SemaphoreType.DMA((2,)),
        ],
        compiler_params=PARAMS,
        name="final",
    )(*tables, router_w.T, kept, pieces, *arrived)
    return (x_grad, grad.T)


def solution(mesh):
    rows = P(AXES, None)
    units = P(AXES, None, None)
    return jax.shard_map(
        on_device,
        mesh=mesh,
        in_specs=(rows, rows, rows, rows, P(), units, units, units),
        out_specs=(rows, rows),
        check_vma=False,
    )
```

```python
import functools

import jax
import jax.numpy as jnp
from jax import lax
from jax.experimental import pallas as pl
from jax.experimental.pallas import tpu as pltpu
from jax.sharding import PartitionSpec as P

AXES = ("exp", "hid")
LANES = 128
PIECES = 4
SCORE_PIECES = 2
VMEM_SPEC = pl.BlockSpec(memory_space=pltpu.VMEM)
HBM_SPEC = pl.BlockSpec(memory_space=pltpu.HBM)
F32 = jnp.float32
BF16 = jnp.bfloat16
NT = (((1,), (1,)), ((), ()))
TN = (((0,), (0,)), ((), ()))
PARAMS = pltpu.CompilerParams(vmem_limit_bytes=24 * 2**20)


def stage_masks(exp_size, hid_size):
    hid_bits = hid_size.bit_length() - 1
    all_bits = (exp_size * hid_size).bit_length() - 1
    core = hid_bits
    first = list(range(max(core + 1, all_bits - 2), all_bits))
    middle = [b for b in range(all_bits) if b != core and b not in first]
    groups = [first] + [middle[i : i + 2] for i in range(0, len(middle), 2)]
    bases = [[sum(1 << b for b in group[i:]) for i in range(len(group))] for group in groups]
    return bases, 1 << core


def group_masks(basis):
    masks = [0]
    for mask in basis:
        masks = masks + [m ^ mask for m in masks]
    return masks


def near_first(basis):
    return [a ^ b for a, b in zip(basis, basis[1:] + [0])]


def swap(block, mask, count):
    return lax.ppermute(block, AXES, [(i, i ^ mask) for i in range(count)])


def place_mask(place, basis):
    total = jnp.zeros_like(place)
    for digit, mask in enumerate(basis):
        total = total ^ (((place >> digit) & 1) * mask)
    return total


def own_index():
    return lax.axis_index("exp") * lax.axis_size("hid") + lax.axis_index("hid")


def in_hbm(*arrays):
    return tuple(pltpu.with_memory_space_constraint(a, pltpu.HBM) for a in arrays)


def softmax_f32(values):
    raised = jnp.exp(values - jnp.max(values, axis=-1, keepdims=True))
    return raised / jnp.sum(raised, axis=-1, keepdims=True)


def prep_kernel(tokens_in, grad_in, logits_in, chosen_in, out_ref, tokens_ref, grad_ref, logits_ref, chosen_ref,
                rows_ref, sems):
    copies = [
        pltpu.make_async_copy(src, dst, sems.at[i])
        for i, (src, dst) in enumerate(
            [(logits_in, logits_ref), (chosen_in, chosen_ref), (tokens_in, tokens_ref), (grad_in, grad_ref)]
        )
    ]
    for copy in copies:
        copy.start()
    copies[0].wait()
    copies[1].wait()
    tok, width = tokens_ref.shape
    logits = logits_ref[...]
    chosen = chosen_ref[...]
    experts = logits.shape[1]
    ids = lax.broadcasted_iota(jnp.int32, logits.shape, 1)
    hit = ids == chosen[:, 0:1]
    for k in range(1, chosen.shape[1]):
        hit = hit | (ids == chosen[:, k : k + 1])
    top = jnp.max(jnp.where(hit, logits, -jnp.inf), axis=1, keepdims=True)
    raised = jnp.where(hit, jnp.exp(jnp.minimum(logits - top, 0.0)), 0.0)
    parts = [raised / jnp.sum(raised, axis=1, keepdims=True)]
    rest = softmax_f32(logits)
    for _ in range(PIECES - 1):
        parts.append(rest)
        rest = rest - rest.astype(BF16).astype(F32)
    lanes = out_ref.shape[1] - width
    spare = lanes - PIECES * experts
    extras = jnp.concatenate(parts + ([jnp.zeros((tok, spare), F32)] if spare else []), axis=1)
    copies[2].wait()
    copies[3].wait()
    rows_ref[0:tok, :width] = tokens_ref[...].astype(F32)
    rows_ref[tok:, :width] = grad_ref[...].astype(F32)
    rows_ref[0:tok, width:] = extras
    rows_ref[tok:, width:] = jnp.zeros((tok, lanes), F32)
    out_ref[...] = rows_ref[...].astype(BF16)


def load_kernel(chunks, after_ref, gate_in, up_in, down_in, pair_ref, down_ref, sems):
    hidden = gate_in.shape[2]
    copies = []

    def add(src, dst):
        copies.append(pltpu.make_async_copy(src, dst, sems.at[len(copies)]))

    for c in range(chunks):
        rows = gate_in.shape[1] // chunks
        part = pl.ds(c * rows, rows)
        add(gate_in.at[0, part, :], pair_ref.at[part, 0:hidden])
        add(up_in.at[0, part, :], pair_ref.at[part, hidden : 2 * hidden])
        rows = hidden // chunks
        part = pl.ds(c * rows, rows)
        add(down_in.at[0, part, :], down_ref.at[part, :])
    for copy in copies:
        copy.start()
    for copy in copies:
        copy.wait()


def join_kernel(tok, *refs):
    blocks, out_ref, rows_ref = refs[:-2], refs[-2], refs[-1]
    count = len(blocks)
    for j, ref in enumerate(blocks):
        block = ref[...].astype(F32)
        rows_ref[j * tok : (j + 1) * tok, :] = block[:tok]
        rows_ref[(count + j) * tok : (count + j + 1) * tok, :] = block[tok:]
    out_ref[...] = rows_ref[...].astype(BF16)


def token_rows(ref, start, rows, group, kind, columns):
    parts = []
    for j in range(rows // (2 * group)):
        first = start + (2 * j + kind) * group
        if not isinstance(first, int):
            first = pl.multiple_of(first, group)
        parts.append(ref[pl.ds(first, group), columns])
    return parts[0] if len(parts) == 1 else jnp.concatenate(parts, axis=0)


def put_scores(out_ref, scores_ref, width):
    rows = out_ref.shape[0]
    for c in range((out_ref.shape[1] - width) // LANES):
        out_ref[:, width + c * LANES : width + (c + 1) * LANES] = scores_ref[c * rows : (c + 1) * rows, :].astype(BF16)


def get_scores(in_ref, scores_ref, base, size, width):
    rows = in_ref.shape[0]
    for c in range(-(-size // rows)):
        here = min(rows, size - c * rows)
        tall = min(rows, -(-here // 16) * 16)
        block = in_ref[0:tall, width + c * LANES : width + (c + 1) * LANES].astype(F32)
        scores_ref[base + c * rows : base + c * rows + here, :] = block[:here]


def half_kernel(basis, group, tok, swap_mask, last, buf_ref, pair_ref, down_ref, *rest):
    hidden, width = down_ref.shape
    experts_width = buf_ref.shape[1] - width
    own = own_index()
    expert = own // 2
    rows = buf_ref.shape[0]
    if last:
        base_ref, out_ref, pieces_ref, score_ref, padded_ref = rest
        score_ref[...] = base_ref[...]
    else:
        out_ref, score_ref = rest
        score_ref[...] = jnp.zeros(score_ref.shape, F32)
    tokens = score_ref.shape[1]
    step = min(rows, 128)
    half_step = step // 2

    def one(index):
        start = index * step
        act = token_rows(buf_ref, start, step, group, 0, slice(None))
        extras = act[:, width:].astype(F32)
        lane = lax.broadcasted_iota(jnp.int32, (half_step, experts_width), 1)
        column = jnp.sum(jnp.where(lane == expert, extras, 0.0), axis=1, keepdims=True)
        pair = jnp.dot(act[:, :width], pair_ref[...], preferred_element_type=F32)
        gate_pre = pair[:, :hidden]
        up_pre = pair[:, hidden:]
        cot = token_rows(buf_ref, start, step, group, 1, slice(0, width))
        back = lax.dot_general(cot, down_ref[...], NT, preferred_element_type=F32)
        sig = jax.nn.sigmoid(gate_pre)
        act_gate = gate_pre * sig
        score = jnp.sum(act_gate * up_pre * back, axis=1, keepdims=True)
        weighted = column * back
        grad_gate = weighted * up_pre * sig * (1.0 + gate_pre * (1.0 - sig))
        grad_up = weighted * act_gate
        grads = jnp.concatenate([grad_gate.astype(BF16), grad_up.astype(BF16)], axis=1)
        total = lax.dot_general(grads, pair_ref[...], NT, preferred_element_type=F32)
        out_start = index * half_step if isinstance(index, int) else pl.multiple_of(index * half_step, half_step)
        out_ref[pl.ds(out_start, half_step), 0:width] = total.astype(out_ref.dtype)

        row = lax.broadcasted_iota(jnp.int32, (half_step, tokens), 0) + index * half_step
        token = lax.broadcasted_iota(jnp.int32, (half_step, tokens), 1)
        whole = (place_mask(row // tok, basis) ^ (own ^ swap_mask)) * tok + row % tok
        score_ref[...] += jnp.sum(jnp.where(whole == token, score, 0.0), axis=0, keepdims=True)

    if rows == step:
        one(0)
    else:
        pl.loop(0, rows // step)(one)
    if last:
        blocks = tokens // LANES
        padded_ref[...] = jnp.zeros(padded_ref.shape, F32)
        value = score_ref[...]
        for piece in range(SCORE_PIECES):
            rounded = value.astype(BF16).astype(F32)
            for b in range(blocks):
                padded_ref[piece * blocks + b : piece * blocks + b + 1, :] = rounded[:, b * LANES : (b + 1) * LANES]
            value = value - rounded
        pieces_ref[...] = padded_ref[0 : pieces_ref.shape[0], :]
        put_scores(out_ref, padded_ref, width)


def add_kernel(arrivals, positions, *refs):
    kept_ref, pieces_ref = refs[0], refs[1]
    arrived = refs[2 : 2 + arrivals]
    outs = refs[2 + arrivals :]
    next_kept_ref, next_pieces_ref = outs[0], outs[1]
    sends = outs[2 : 2 + len(positions)]
    total_ref, scores_ref = outs[2 + len(positions) :]
    width = kept_ref.shape[1]
    size = pieces_ref.shape[0]
    total = kept_ref[...]
    for ref in arrived:
        total = total + ref[:, 0:width].astype(F32)
    total_ref[...] = total
    if scores_ref.shape[0] > next_pieces_ref.shape[0]:
        scores_ref[...] = jnp.zeros(scores_ref.shape, F32)
    scores_ref[0:size, :] = pieces_ref[...]
    for j, ref in enumerate(arrived):
        get_scores(ref, scores_ref, (j + 1) * size, size, width)
    rows = next_kept_ref.shape[0]
    next_kept_ref[...] = total_ref[0:rows, :]
    next_pieces_ref[...] = scores_ref[0 : next_pieces_ref.shape[0], :]
    for j, ref in zip(positions, sends):
        ref[:, 0:width] = total_ref[j * rows : (j + 1) * rows, :].astype(BF16)
        put_scores(ref, scores_ref, width)


def table_kernel(basis, group, tok, core_mask, rows_out, after_ref, buf_own_ref, buf_other_ref, here_ref, probs_ref,
                 column_ref):
    rows, buf_width = buf_own_ref.shape
    half = rows // 2
    experts = probs_ref.shape[1]
    tokens = here_ref.shape[1]
    lanes = -(-PIECES * experts // LANES) * LANES
    width = buf_width - lanes
    own = own_index()
    lane = lax.broadcasted_iota(jnp.int32, (lanes, experts), 0)
    ids = lax.broadcasted_iota(jnp.int32, (lanes, experts), 1)
    tally = jnp.zeros((lanes, experts), F32)
    for k in range(1, PIECES):
        tally = tally + jnp.where(lane == ids + k * experts, 1.0, 0.0)
    column = pl.multiple_of(own * rows_out // LANES * LANES, LANES)
    for index, ref in enumerate((buf_own_ref, buf_other_ref)):
        row = lax.broadcasted_iota(jnp.int32, (half, tokens), 0)
        token = lax.broadcasted_iota(jnp.int32, (half, tokens), 1)
        whole = (place_mask(row // tok, basis) ^ (own ^ (core_mask if index else 0))) * tok + row % tok
        part = slice(index * half, (index + 1) * half)
        here_ref[part, :] = jnp.where(whole == token, 1.0, 0.0).astype(BF16)
        extras = token_rows(ref, 0, rows, group, 0, slice(width, buf_width))
        probs_ref[part, :] = jnp.dot(extras, tally.astype(BF16), preferred_element_type=F32)
        column_ref[part, :] = token_rows(ref, 0, rows, group, 0, pl.ds(column, LANES))


def final_kernel(arrivals, back_basis, *refs):
    here_ref, probs_ref, column_ref, router_ref, kept_ref, pieces_ref = refs[:6]
    arrived = refs[6 : 6 + arrivals]
    x_out, grad_out, x_ref, grad_ref, scores_ref, sems = refs[6 + arrivals :]
    experts, width = router_ref.shape
    size = pieces_ref.shape[0]
    tok = kept_ref.shape[0]
    own = own_index()
    scores_ref[0:size, :] = pieces_ref[...]
    for j, ref in enumerate(arrived):
        get_scores(ref, scores_ref, (j + 1) * size, size, width)
    blocks = here_ref.shape[1] // LANES
    wide = scores_ref.shape[0] // blocks
    sender = lax.broadcasted_iota(jnp.int32, (wide, experts), 0) // SCORE_PIECES
    ids = lax.broadcasted_iota(jnp.int32, (wide, experts), 1)
    pick = jnp.where(((place_mask(sender, back_basis) ^ own) >> 1) == ids, 1.0, 0.0).astype(BF16)

    def logit_grads(rows):
        picked = jnp.zeros((rows, wide), F32)
        for b in range(blocks):
            block = scores_ref[...] if blocks == 1 else scores_ref[pl.ds(b, wide, stride=blocks), :]
            here = here_ref[0:rows, b * LANES : (b + 1) * LANES]
            picked = picked + lax.dot_general(here, block.astype(BF16), NT, preferred_element_type=F32)
        scores = jnp.dot(picked.astype(BF16), pick, preferred_element_type=F32)
        probs = probs_ref[0:rows, :]
        mean = jnp.sum(probs * scores, axis=1, keepdims=True)
        return (probs * (scores - mean)).astype(BF16)

    part = jnp.dot(logit_grads(16), router_ref[...], preferred_element_type=F32)
    total = kept_ref[...]
    for ref in arrived:
        total = total + ref[:, 0:width].astype(F32)
    x_ref[...] = (total + part[:tok]).astype(BF16)
    x_copy = pltpu.make_async_copy(x_ref, x_out, sems.at[0])
    x_copy.start()
    grad = lax.dot_general(logit_grads(here_ref.shape[0]), column_ref[...], TN, preferred_element_type=F32)
    rows_out = grad_ref.shape[1]
    first = own * rows_out % LANES
    grad_ref[...] = pltpu.roll(grad, (LANES - first) % LANES, 1)[:, :rows_out]
    grad_copy = pltpu.make_async_copy(grad_ref, grad_out, sems.at[1])
    grad_copy.start()
    x_copy.wait()
    grad_copy.wait()


def on_device(tokens, grad_out, router_logits, selected, router_w, w_gate, w_up, w_down):
    tok, width = tokens.shape
    experts = router_logits.shape[1]
    hidden = w_gate.shape[2]
    exp_size = lax.axis_size("exp")
    hid_size = lax.axis_size("hid")
    count = exp_size * hid_size
    half = count // 2
    groups, core_mask = stage_masks(exp_size, hid_size)
    basis = [m for group in groups for m in group]
    back_groups = [near_first(group) for group in groups[:0:-1]] + [groups[0]]
    back_basis = [core_mask] + [m for group in back_groups for m in group]
    token_count = count * tok
    lanes = -(-PIECES * experts // LANES) * LANES

    block = pl.pallas_call(
        prep_kernel,
        out_shape=jax.ShapeDtypeStruct((2 * tok, width + lanes), BF16),
        in_specs=[HBM_SPEC] * 4,
        out_specs=VMEM_SPEC,
        scratch_shapes=[
            pltpu.VMEM(tokens.shape, tokens.dtype),
            pltpu.VMEM(grad_out.shape, grad_out.dtype),
            pltpu.VMEM(router_logits.shape, router_logits.dtype),
            pltpu.VMEM(selected.shape, selected.dtype),
            pltpu.VMEM((2 * tok, width + lanes), F32),
            pltpu.SemaphoreType.DMA((4,)),
        ],
        compiler_params=PARAMS,
        name="prep",
    )(*in_hbm(tokens, grad_out, router_logits, selected))

    weights = in_hbm(w_gate, w_up, w_down)
    for index, group in enumerate(groups):
        if index == len(groups) - 1:
            chunks = 4
            weights = pl.pallas_call(
                functools.partial(load_kernel, chunks),
                out_shape=(pltpu.VMEM((width, 2 * hidden), BF16), pltpu.VMEM((hidden, width), BF16)),
                in_specs=[pl.BlockSpec(memory_space=pl.ANY)] + [HBM_SPEC] * 3,
                out_specs=(VMEM_SPEC,) * 2,
                scratch_shapes=[pltpu.SemaphoreType.DMA((3 * chunks,))],
                compiler_params=pltpu.CompilerParams(vmem_limit_bytes=4 * 2**20),
                cost_estimate=pl.CostEstimate(flops=0, bytes_accessed=6 * width * hidden * 2, transcendentals=0),
                name="load",
            )(block, *weights)
        blocks = [block] + [swap(block, m, count) for m in group_masks(group)[1:]]
        if index == 0:
            group_rows = tok * len(blocks)
            block = pl.pallas_call(
                functools.partial(join_kernel, tok),
                out_shape=jax.ShapeDtypeStruct((2 * group_rows, width + lanes), BF16),
                in_specs=[VMEM_SPEC] * len(blocks),
                out_specs=VMEM_SPEC,
                scratch_shapes=[pltpu.VMEM((2 * group_rows, width + lanes), F32)],
                compiler_params=PARAMS,
                name="join",
            )(*blocks)
        else:
            block = jnp.concatenate(blocks, axis=0)
    other = swap(block, core_mask, count)

    cost = pl.CostEstimate(
        flops=2 * half * 8 * width * hidden * 4,
        bytes_accessed=3 * width * hidden * 2 + half * 8 * width * 2,
        transcendentals=half * 8 * hidden,
    )
    unit_rows = SCORE_PIECES * token_count // LANES
    kept, score = pl.pallas_call(
        functools.partial(half_kernel, basis, group_rows, tok, 0, False),
        out_shape=(
            jax.ShapeDtypeStruct((half * tok, width), F32),
            jax.ShapeDtypeStruct((1, token_count), F32),
        ),
        in_specs=[VMEM_SPEC] * 3,
        out_specs=(VMEM_SPEC, VMEM_SPEC),
        compiler_params=PARAMS,
        cost_estimate=pl.CostEstimate(
            flops=cost.flops * 16, bytes_accessed=cost.bytes_accessed, transcendentals=cost.transcendentals
        ),
        name="half_own",
    )(block, *weights)
    extra = -(-unit_rows // (half * tok)) * LANES
    message, pieces = pl.pallas_call(
        functools.partial(half_kernel, basis, group_rows, tok, core_mask, True),
        out_shape=(
            jax.ShapeDtypeStruct((half * tok, width + extra), BF16),
            jax.ShapeDtypeStruct((unit_rows, LANES), F32),
        ),
        in_specs=[VMEM_SPEC] * 4,
        out_specs=(VMEM_SPEC, VMEM_SPEC),
        scratch_shapes=[
            pltpu.VMEM((1, token_count), F32),
            pltpu.VMEM((max(half * tok * extra // LANES, unit_rows), LANES), F32),
        ],
        compiler_params=PARAMS,
        cost_estimate=cost,
        name="half_other",
    )(other, *weights, score)

    arrived = [swap(message, core_mask, count)]
    tables = None
    rows_out = width // count
    for group, back_group in zip(groups[::-1], back_groups):
        masks = group_masks(group)
        back_masks = group_masks(back_group)
        radix = len(masks)
        rows = kept.shape[0]
        next_rows = rows // radix
        size = pieces.shape[0] * (1 + len(arrived))
        extra = -(-size // next_rows) * LANES
        sends = [jax.ShapeDtypeStruct((next_rows, width + extra), BF16)] * (radix - 1)
        outs = pl.pallas_call(
            functools.partial(add_kernel, len(arrived), [masks.index(m) for m in back_masks[1:]]),
            out_shape=[
                jax.ShapeDtypeStruct((next_rows, width), F32),
                jax.ShapeDtypeStruct((size, LANES), F32),
            ]
            + sends,
            in_specs=[VMEM_SPEC] * (2 + len(arrived)),
            out_specs=[VMEM_SPEC] * (1 + radix),
            scratch_shapes=[
                pltpu.VMEM((rows, width), F32),
                pltpu.VMEM((max(next_rows * extra // LANES, size), LANES), F32),
            ],
            compiler_params=PARAMS,
            name="add",
        )(kept, pieces, *arrived)
        kept, pieces = outs[0], outs[1]
        if tables is None:
            tables = pl.pallas_call(
                functools.partial(table_kernel, basis, group_rows, tok, core_mask, rows_out),
                out_shape=(
                    jax.ShapeDtypeStruct((block.shape[0], token_count), BF16),
                    jax.ShapeDtypeStruct((block.shape[0], experts), F32),
                    jax.ShapeDtypeStruct((block.shape[0], LANES), BF16),
                ),
                in_specs=[pl.BlockSpec(memory_space=pl.ANY)] + [VMEM_SPEC] * 2,
                out_specs=(VMEM_SPEC,) * 3,
                compiler_params=PARAMS,
                cost_estimate=pl.CostEstimate(flops=10**9, bytes_accessed=10**6, transcendentals=0),
                name="tables",
            )(pieces, block, other)
        arrived = [swap(piece, m, count) for piece, m in zip(outs[2:], back_masks[1:])]

    x_grad, grad = pl.pallas_call(
        functools.partial(final_kernel, len(arrived), back_basis),
        out_shape=(
            jax.ShapeDtypeStruct((tok, width), BF16),
            jax.ShapeDtypeStruct((experts, rows_out), F32),
        ),
        in_specs=[VMEM_SPEC] * (6 + len(arrived)),
        out_specs=(HBM_SPEC, HBM_SPEC),
        scratch_shapes=[
            pltpu.VMEM((tok, width), BF16),
            pltpu.VMEM((experts, rows_out), F32),
            pltpu.VMEM((pieces.shape[0] * (1 + len(arrived)), LANES), F32),
            pltpu.SemaphoreType.DMA((2,)),
        ],
        compiler_params=PARAMS,
        name="final",
    )(*tables, router_w.T, kept, pieces, *arrived)
    return (x_grad, grad.T)


def solution(mesh):
    rows = P(AXES, None)
    units = P(AXES, None, None)
    return jax.shard_map(
        on_device,
        mesh=mesh,
        in_specs=(rows, rows, rows, rows, P(), units, units, units),
        out_specs=(rows, rows),
        check_vma=False,
    )
```

```python
import functools

import jax
import jax.numpy as jnp
from jax import lax
from jax.experimental import pallas as pl
from jax.experimental.pallas import tpu as pltpu
from jax.sharding import PartitionSpec as P

AXES = ("exp", "hid")
LANES = 128
PIECES = 4
SCORE_PIECES = 2
VMEM_SPEC = pl.BlockSpec(memory_space=pltpu.VMEM)
HBM_SPEC = pl.BlockSpec(memory_space=pltpu.HBM)
F32 = jnp.float32
BF16 = jnp.bfloat16
NT = (((1,), (1,)), ((), ()))
TN = (((0,), (0,)), ((), ()))
PARAMS = pltpu.CompilerParams(vmem_limit_bytes=24 * 2**20)


def stage_masks(exp_size, hid_size):
    hid_bits = hid_size.bit_length() - 1
    all_bits = (exp_size * hid_size).bit_length() - 1
    core = hid_bits
    first = list(range(max(core + 1, all_bits - 2), all_bits))
    middle = [b for b in range(all_bits) if b != core and b not in first]
    groups = [first] + [middle[i : i + 2] for i in range(0, len(middle), 2)]
    bases = [[sum(1 << b for b in group[i:]) for i in range(len(group))] for group in groups]
    return bases, core


def group_masks(basis):
    masks = [0]
    for mask in basis:
        masks = masks + [m ^ mask for m in masks]
    return masks


def swap(block, mask, count):
    return lax.ppermute(block, AXES, [(i, i ^ mask) for i in range(count)])


def place_mask(place, basis):
    total = jnp.zeros_like(place)
    for digit, mask in enumerate(basis):
        total = total ^ (((place >> digit) & 1) * mask)
    return total


def own_index():
    return lax.axis_index("exp") * lax.axis_size("hid") + lax.axis_index("hid")


def in_hbm(*arrays):
    return tuple(pltpu.with_memory_space_constraint(a, pltpu.HBM) for a in arrays)


def softmax_f32(values):
    raised = jnp.exp(values - jnp.max(values, axis=-1, keepdims=True))
    return raised / jnp.sum(raised, axis=-1, keepdims=True)


def prep_kernel(tokens_in, grad_in, logits_in, chosen_in, out_ref, tokens_ref, grad_ref, logits_ref, chosen_ref,
                rows_ref, sems):
    copies = [
        pltpu.make_async_copy(src, dst, sems.at[i])
        for i, (src, dst) in enumerate(
            [(logits_in, logits_ref), (chosen_in, chosen_ref), (tokens_in, tokens_ref), (grad_in, grad_ref)]
        )
    ]
    for copy in copies:
        copy.start()
    copies[0].wait()
    copies[1].wait()
    tok, width = tokens_ref.shape
    logits = logits_ref[...]
    chosen = chosen_ref[...]
    experts = logits.shape[1]
    ids = lax.broadcasted_iota(jnp.int32, logits.shape, 1)
    hit = ids == chosen[:, 0:1]
    for k in range(1, chosen.shape[1]):
        hit = hit | (ids == chosen[:, k : k + 1])
    top = jnp.max(jnp.where(hit, logits, -jnp.inf), axis=1, keepdims=True)
    raised = jnp.where(hit, jnp.exp(jnp.minimum(logits - top, 0.0)), 0.0)
    parts = [raised / jnp.sum(raised, axis=1, keepdims=True)]
    rest = softmax_f32(logits)
    for _ in range(PIECES - 1):
        parts.append(rest)
        rest = rest - rest.astype(BF16).astype(F32)
    lanes = out_ref.shape[1] - width
    spare = lanes - PIECES * experts
    extras = jnp.concatenate(parts + ([jnp.zeros((tok, spare), F32)] if spare else []), axis=1)
    copies[2].wait()
    copies[3].wait()
    rows_ref[0:tok, :width] = tokens_ref[...].astype(F32)
    rows_ref[tok:, :width] = grad_ref[...].astype(F32)
    rows_ref[0:tok, width:] = extras
    rows_ref[tok:, width:] = jnp.zeros((tok, lanes), F32)
    out_ref[...] = rows_ref[...].astype(BF16)


def load_kernel(chunks, after_ref, gate_in, up_in, down_in, pair_ref, down_ref, sems):
    hidden = gate_in.shape[2]
    copies = []

    def add(src, dst):
        copies.append(pltpu.make_async_copy(src, dst, sems.at[len(copies)]))

    for c in range(chunks):
        rows = gate_in.shape[1] // chunks
        part = pl.ds(c * rows, rows)
        add(gate_in.at[0, part, :], pair_ref.at[part, 0:hidden])
        add(up_in.at[0, part, :], pair_ref.at[part, hidden : 2 * hidden])
        rows = hidden // chunks
        part = pl.ds(c * rows, rows)
        add(down_in.at[0, part, :], down_ref.at[part, :])
    for copy in copies:
        copy.start()
    for copy in copies:
        copy.wait()


def join_kernel(tok, *refs):
    blocks, out_ref, rows_ref = refs[:-2], refs[-2], refs[-1]
    count = len(blocks)
    for j, ref in enumerate(blocks):
        block = ref[...].astype(F32)
        rows_ref[j * tok : (j + 1) * tok, :] = block[:tok]
        rows_ref[(count + j) * tok : (count + j + 1) * tok, :] = block[tok:]
    out_ref[...] = rows_ref[...].astype(BF16)


def stack_kernel(*refs):
    out_ref = refs[-1]
    rows = refs[0].shape[0]
    for j, ref in enumerate(refs[:-1]):
        out_ref[j * rows : (j + 1) * rows, :] = ref[...]


def token_rows(ref, start, rows, group, kind, columns):
    parts = []
    for j in range(rows // (2 * group)):
        first = start + (2 * j + kind) * group
        if not isinstance(first, int):
            first = pl.multiple_of(first, group)
        parts.append(ref[pl.ds(first, group), columns])
    return parts[0] if len(parts) == 1 else jnp.concatenate(parts, axis=0)


def put_scores(out_ref, scores_ref, width):
    rows = out_ref.shape[0]
    for c in range((out_ref.shape[1] - width) // LANES):
        out_ref[:, width + c * LANES : width + (c + 1) * LANES] = scores_ref[c * rows : (c + 1) * rows, :].astype(BF16)


def get_scores(in_ref, scores_ref, base, size, width):
    rows = in_ref.shape[0]
    for c in range(-(-size // rows)):
        here = min(rows, size - c * rows)
        tall = min(rows, -(-here // 16) * 16)
        block = in_ref[0:tall, width + c * LANES : width + (c + 1) * LANES].astype(F32)
        scores_ref[base + c * rows : base + c * rows + here, :] = block[:here]


def half_kernel(basis, group, tok, swap_mask, last, buf_ref, pair_ref, down_ref, *rest):
    hidden, width = down_ref.shape
    experts_width = buf_ref.shape[1] - width
    own = own_index()
    expert = own // 2
    rows = buf_ref.shape[0]
    if last:
        base_ref, out_ref, pieces_ref, score_ref, padded_ref = rest
        score_ref[...] = base_ref[...]
    else:
        out_ref, score_ref = rest
        score_ref[...] = jnp.zeros(score_ref.shape, F32)
    tokens = score_ref.shape[1]
    step = min(rows, 128)
    half_step = step // 2

    def one(index):
        start = index * step
        act = token_rows(buf_ref, start, step, group, 0, slice(None))
        extras = act[:, width:].astype(F32)
        lane = lax.broadcasted_iota(jnp.int32, (half_step, experts_width), 1)
        column = jnp.sum(jnp.where(lane == expert, extras, 0.0), axis=1, keepdims=True)
        pair = jnp.dot(act[:, :width], pair_ref[...], preferred_element_type=F32)
        gate_pre = pair[:, :hidden]
        up_pre = pair[:, hidden:]
        cot = token_rows(buf_ref, start, step, group, 1, slice(0, width))
        back = lax.dot_general(cot, down_ref[...], NT, preferred_element_type=F32)
        sig = jax.nn.sigmoid(gate_pre)
        act_gate = gate_pre * sig
        score = jnp.sum(act_gate * up_pre * back, axis=1, keepdims=True)
        weighted = column * back
        grad_gate = weighted * up_pre * sig * (1.0 + gate_pre * (1.0 - sig))
        grad_up = weighted * act_gate
        grads = jnp.concatenate([grad_gate.astype(BF16), grad_up.astype(BF16)], axis=1)
        total = lax.dot_general(grads, pair_ref[...], NT, preferred_element_type=F32)
        out_start = index * half_step if isinstance(index, int) else pl.multiple_of(index * half_step, half_step)
        out_ref[pl.ds(out_start, half_step), 0:width] = total.astype(out_ref.dtype)

        row = lax.broadcasted_iota(jnp.int32, (half_step, tokens), 0) + index * half_step
        token = lax.broadcasted_iota(jnp.int32, (half_step, tokens), 1)
        whole = (place_mask(row // tok, basis) ^ (own ^ swap_mask)) * tok + row % tok
        score_ref[...] += jnp.sum(jnp.where(whole == token, score, 0.0), axis=0, keepdims=True)

    if rows == step:
        one(0)
    else:
        pl.loop(0, rows // step)(one)
    if last:
        blocks = tokens // LANES
        padded_ref[...] = jnp.zeros(padded_ref.shape, F32)
        value = score_ref[...]
        for piece in range(SCORE_PIECES):
            rounded = value.astype(BF16).astype(F32)
            for b in range(blocks):
                padded_ref[piece * blocks + b : piece * blocks + b + 1, :] = rounded[:, b * LANES : (b + 1) * LANES]
            value = value - rounded
        pieces_ref[...] = padded_ref[0 : pieces_ref.shape[0], :]
        put_scores(out_ref, padded_ref, width)


def member_of(device, core):
    return ((device >> (core + 1)) << core) | (device & ((1 << core) - 1))


def device_of(member, core, bit):
    return ((member >> core) << (core + 1)) | (member & ((1 << core) - 1)) | bit


def add_kernel(basis, core, kept_ref, pieces_ref, arrived_ref, out_ref, total_ref, scores_ref):
    width = kept_ref.shape[1]
    size = pieces_ref.shape[0]
    tok = out_ref.shape[1]
    own = own_index()
    total_ref[...] = kept_ref[...] + arrived_ref[:, 0:width].astype(F32)
    scores_ref[...] = jnp.zeros(scores_ref.shape, F32)
    scores_ref[0:size, :] = pieces_ref[...]
    get_scores(arrived_ref, scores_ref, size, size, width)
    extras = [scores_ref[c * tok : (c + 1) * tok, :].astype(BF16) for c in range((out_ref.shape[2] - width) // LANES)]
    for place in range(out_ref.shape[0]):
        mask = 0
        for digit, m in enumerate(basis):
            mask = mask ^ ((place >> digit & 1) * m)
        to = member_of(own ^ mask, core)
        out_ref[to, :, 0:width] = total_ref[place * tok : (place + 1) * tok, :].astype(BF16)
        for c, extra in enumerate(extras):
            out_ref[to, :, width + c * LANES : width + (c + 1) * LANES] = extra


def table_kernel(basis, group, tok, core_mask, rows_out, after_ref, buf_own_ref, buf_other_ref, here_ref, probs_ref,
                 column_ref):
    rows, buf_width = buf_own_ref.shape
    half = rows // 2
    experts = probs_ref.shape[1]
    tokens = here_ref.shape[1]
    lanes = -(-PIECES * experts // LANES) * LANES
    width = buf_width - lanes
    own = own_index()
    lane = lax.broadcasted_iota(jnp.int32, (lanes, experts), 0)
    ids = lax.broadcasted_iota(jnp.int32, (lanes, experts), 1)
    tally = jnp.zeros((lanes, experts), F32)
    for k in range(1, PIECES):
        tally = tally + jnp.where(lane == ids + k * experts, 1.0, 0.0)
    column = pl.multiple_of(own * rows_out // LANES * LANES, LANES)
    for index, ref in enumerate((buf_own_ref, buf_other_ref)):
        row = lax.broadcasted_iota(jnp.int32, (half, tokens), 0)
        token = lax.broadcasted_iota(jnp.int32, (half, tokens), 1)
        whole = (place_mask(row // tok, basis) ^ (own ^ (core_mask if index else 0))) * tok + row % tok
        part = slice(index * half, (index + 1) * half)
        here_ref[part, :] = jnp.where(whole == token, 1.0, 0.0).astype(BF16)
        extras = token_rows(ref, 0, rows, group, 0, slice(width, buf_width))
        probs_ref[part, :] = jnp.dot(extras, tally.astype(BF16), preferred_element_type=F32)
        column_ref[part, :] = token_rows(ref, 0, rows, group, 0, pl.ds(column, LANES))


def final_kernel(core, size, here_ref, probs_ref, column_ref, router_ref, arrived_ref, x_out, grad_out, x_ref, grad_ref,
                 scores_ref, sems):
    experts, width = router_ref.shape
    members, tok = arrived_ref.shape[:2]
    own = own_index()
    core_mask = 1 << core
    for j in range(members):
        for c in range(-(-size // tok)):
            here = min(tok, size - c * tok)
            block = arrived_ref[j, :, width + c * LANES : width + (c + 1) * LANES].astype(F32)
            scores_ref[j * size + c * tok : j * size + c * tok + here, :] = block[:here]
    blocks = here_ref.shape[1] // LANES
    wide = scores_ref.shape[0] // blocks
    unit = lax.broadcasted_iota(jnp.int32, (wide, experts), 0) // SCORE_PIECES
    sender = device_of(unit >> 1, core, own & core_mask) ^ ((unit & 1) * core_mask)
    ids = lax.broadcasted_iota(jnp.int32, (wide, experts), 1)
    pick = jnp.where((sender >> 1) == ids, 1.0, 0.0).astype(BF16)
    picked = jnp.zeros((here_ref.shape[0], wide), F32)
    for b in range(blocks):
        block = scores_ref[...] if blocks == 1 else scores_ref[pl.ds(b, wide, stride=blocks), :]
        here = here_ref[:, b * LANES : (b + 1) * LANES]
        picked = picked + lax.dot_general(here, block.astype(BF16), NT, preferred_element_type=F32)
    scores = jnp.dot(picked.astype(BF16), pick, preferred_element_type=F32)
    probs = probs_ref[...]
    mean = jnp.sum(probs * scores, axis=1, keepdims=True)
    logit_grad = (probs * (scores - mean)).astype(BF16)
    part = jnp.dot(logit_grad[0:16], router_ref[...], preferred_element_type=F32)
    total = arrived_ref[0, :, 0:width].astype(F32)
    for j in range(1, members):
        total = total + arrived_ref[j, :, 0:width].astype(F32)
    x_ref[...] = (total + part[:tok]).astype(BF16)
    x_copy = pltpu.make_async_copy(x_ref, x_out, sems.at[0])
    x_copy.start()
    grad = lax.dot_general(logit_grad, column_ref[...], TN, preferred_element_type=F32)
    rows_out = grad_ref.shape[1]
    first = own * rows_out % LANES
    grad_ref[...] = pltpu.roll(grad, (LANES - first) % LANES, 1)[:, :rows_out]
    grad_copy = pltpu.make_async_copy(grad_ref, grad_out, sems.at[1])
    grad_copy.start()
    x_copy.wait()
    grad_copy.wait()


def on_device(tokens, grad_out, router_logits, selected, router_w, w_gate, w_up, w_down):
    tok, width = tokens.shape
    experts = router_logits.shape[1]
    hidden = w_gate.shape[2]
    exp_size = lax.axis_size("exp")
    hid_size = lax.axis_size("hid")
    count = exp_size * hid_size
    half = count // 2
    groups, core = stage_masks(exp_size, hid_size)
    core_mask = 1 << core
    basis = [m for group in groups for m in group]
    token_count = count * tok
    lanes = -(-PIECES * experts // LANES) * LANES

    block = pl.pallas_call(
        prep_kernel,
        out_shape=jax.ShapeDtypeStruct((2 * tok, width + lanes), BF16),
        in_specs=[HBM_SPEC] * 4,
        out_specs=VMEM_SPEC,
        scratch_shapes=[
            pltpu.VMEM(tokens.shape, tokens.dtype),
            pltpu.VMEM(grad_out.shape, grad_out.dtype),
            pltpu.VMEM(router_logits.shape, router_logits.dtype),
            pltpu.VMEM(selected.shape, selected.dtype),
            pltpu.VMEM((2 * tok, width + lanes), F32),
            pltpu.SemaphoreType.DMA((4,)),
        ],
        compiler_params=PARAMS,
        name="prep",
    )(*in_hbm(tokens, grad_out, router_logits, selected))

    weights = in_hbm(w_gate, w_up, w_down)
    for index, group in enumerate(groups):
        if index == len(groups) - 1:
            chunks = 4
            weights = pl.pallas_call(
                functools.partial(load_kernel, chunks),
                out_shape=(pltpu.VMEM((width, 2 * hidden), BF16), pltpu.VMEM((hidden, width), BF16)),
                in_specs=[pl.BlockSpec(memory_space=pl.ANY)] + [HBM_SPEC] * 3,
                out_specs=(VMEM_SPEC,) * 2,
                scratch_shapes=[pltpu.SemaphoreType.DMA((3 * chunks,))],
                compiler_params=pltpu.CompilerParams(vmem_limit_bytes=4 * 2**20),
                cost_estimate=pl.CostEstimate(flops=0, bytes_accessed=6 * width * hidden * 2, transcendentals=0),
                name="load",
            )(block, *weights)
        blocks = [block] + [swap(block, m, count) for m in group_masks(group)[1:]]
        if index == 0:
            group_rows = tok * len(blocks)
            block = pl.pallas_call(
                functools.partial(join_kernel, tok),
                out_shape=jax.ShapeDtypeStruct((2 * group_rows, width + lanes), BF16),
                in_specs=[VMEM_SPEC] * len(blocks),
                out_specs=VMEM_SPEC,
                scratch_shapes=[pltpu.VMEM((2 * group_rows, width + lanes), F32)],
                compiler_params=PARAMS,
                name="join",
            )(*blocks)
        else:
            block = pl.pallas_call(
                stack_kernel,
                out_shape=jax.ShapeDtypeStruct((len(blocks) * block.shape[0], block.shape[1]), BF16),
                in_specs=[VMEM_SPEC] * len(blocks),
                out_specs=VMEM_SPEC,
                compiler_params=PARAMS,
                name="stack",
            )(*blocks)
    other = swap(block, core_mask, count)

    cost = pl.CostEstimate(
        flops=2 * half * 8 * width * hidden * 4,
        bytes_accessed=3 * width * hidden * 2 + half * 8 * width * 2,
        transcendentals=half * 8 * hidden,
    )
    unit_rows = SCORE_PIECES * token_count // LANES
    kept, score = pl.pallas_call(
        functools.partial(half_kernel, basis, group_rows, tok, 0, False),
        out_shape=(
            jax.ShapeDtypeStruct((half * tok, width), F32),
            jax.ShapeDtypeStruct((1, token_count), F32),
        ),
        in_specs=[VMEM_SPEC] * 3,
        out_specs=(VMEM_SPEC, VMEM_SPEC),
        compiler_params=PARAMS,
        cost_estimate=pl.CostEstimate(
            flops=cost.flops * 16, bytes_accessed=cost.bytes_accessed, transcendentals=cost.transcendentals
        ),
        name="half_own",
    )(block, *weights)
    extra = -(-unit_rows // (half * tok)) * LANES
    message, pieces = pl.pallas_call(
        functools.partial(half_kernel, basis, group_rows, tok, core_mask, True),
        out_shape=(
            jax.ShapeDtypeStruct((half * tok, width + extra), BF16),
            jax.ShapeDtypeStruct((unit_rows, LANES), F32),
        ),
        in_specs=[VMEM_SPEC] * 4,
        out_specs=(VMEM_SPEC, VMEM_SPEC),
        scratch_shapes=[
            pltpu.VMEM((1, token_count), F32),
            pltpu.VMEM((max(half * tok * extra // LANES, unit_rows), LANES), F32),
        ],
        compiler_params=PARAMS,
        cost_estimate=cost,
        name="half_other",
    )(other, *weights, score)

    arrived = swap(message, core_mask, count)
    rows_out = width // count
    size = 2 * unit_rows
    extra = -(-size // tok) * LANES
    sends = pl.pallas_call(
        functools.partial(add_kernel, basis, core),
        out_shape=jax.ShapeDtypeStruct((half, tok, width + extra), BF16),
        in_specs=[VMEM_SPEC] * 3,
        out_specs=VMEM_SPEC,
        scratch_shapes=[
            pltpu.VMEM((half * tok, width), F32),
            pltpu.VMEM((max(tok * extra // LANES, size), LANES), F32),
        ],
        compiler_params=PARAMS,
        name="add",
    )(kept, pieces, arrived)
    tables = pl.pallas_call(
        functools.partial(table_kernel, basis, group_rows, tok, core_mask, rows_out),
        out_shape=(
            jax.ShapeDtypeStruct((block.shape[0], token_count), BF16),
            jax.ShapeDtypeStruct((block.shape[0], experts), F32),
            jax.ShapeDtypeStruct((block.shape[0], LANES), BF16),
        ),
        in_specs=[pl.BlockSpec(memory_space=pl.ANY)] + [VMEM_SPEC] * 2,
        out_specs=(VMEM_SPEC,) * 3,
        compiler_params=PARAMS,
        cost_estimate=pl.CostEstimate(flops=10**9, bytes_accessed=10**6, transcendentals=0),
        name="tables",
    )(sends, block, other)
    members = [[i for i in range(count) if (i >> core & 1) == bit] for bit in (0, 1)]
    arrived = lax.all_to_all(sends, AXES, 0, 0, axis_index_groups=members, tiled=True)

    x_grad, grad = pl.pallas_call(
        functools.partial(final_kernel, core, size),
        out_shape=(
            jax.ShapeDtypeStruct((tok, width), BF16),
            jax.ShapeDtypeStruct((experts, rows_out), F32),
        ),
        in_specs=[VMEM_SPEC] * 5,
        out_specs=(HBM_SPEC, HBM_SPEC),
        scratch_shapes=[
            pltpu.VMEM((tok, width), BF16),
            pltpu.VMEM((experts, rows_out), F32),
            pltpu.VMEM((half * size, LANES), F32),
            pltpu.SemaphoreType.DMA((2,)),
        ],
        compiler_params=PARAMS,
        name="final",
    )(*tables, router_w.T, arrived)
    return (x_grad, grad.T)


def solution(mesh):
    rows = P(AXES, None)
    units = P(AXES, None, None)
    return jax.shard_map(
        on_device,
        mesh=mesh,
        in_specs=(rows, rows, rows, rows, P(), units, units, units),
        out_specs=(rows, rows),
        check_vma=False,
    )
```

```python
import functools

import jax
import jax.numpy as jnp
from jax import lax
from jax.experimental import pallas as pl
from jax.experimental.pallas import tpu as pltpu
from jax.sharding import PartitionSpec as P

AXES = ("exp", "hid")
LANES = 128
PIECES = 4
SCORE_PIECES = 2
VMEM_SPEC = pl.BlockSpec(memory_space=pltpu.VMEM)
HBM_SPEC = pl.BlockSpec(memory_space=pltpu.HBM)
F32 = jnp.float32
BF16 = jnp.bfloat16
NT = (((1,), (1,)), ((), ()))
TN = (((0,), (0,)), ((), ()))
PARAMS = pltpu.CompilerParams(vmem_limit_bytes=24 * 2**20)


def stage_masks(exp_size, hid_size):
    hid_bits = hid_size.bit_length() - 1
    all_bits = (exp_size * hid_size).bit_length() - 1
    core = hid_bits
    first = list(range(max(core + 1, all_bits - 2), all_bits))
    middle = [b for b in range(all_bits) if b != core and b not in first]
    groups = [first] + [middle[i : i + 2] for i in range(0, len(middle), 2)]
    bases = [[sum(1 << b for b in group[i:]) for i in range(len(group))] for group in groups]
    return bases, 1 << core


def group_masks(basis):
    masks = [0]
    for mask in basis:
        masks = masks + [m ^ mask for m in masks]
    return masks


def near_first(basis):
    return [a ^ b for a, b in zip(basis, basis[1:] + [0])]


def swap(block, mask, count):
    return lax.ppermute(block, AXES, [(i, i ^ mask) for i in range(count)])


def place_mask(place, basis):
    total = jnp.zeros_like(place)
    for digit, mask in enumerate(basis):
        total = total ^ (((place >> digit) & 1) * mask)
    return total


def own_index():
    return lax.axis_index("exp") * lax.axis_size("hid") + lax.axis_index("hid")


def in_hbm(*arrays):
    return tuple(pltpu.with_memory_space_constraint(a, pltpu.HBM) for a in arrays)


def softmax_f32(values):
    raised = jnp.exp(values - jnp.max(values, axis=-1, keepdims=True))
    return raised / jnp.sum(raised, axis=-1, keepdims=True)


def prep_kernel(tokens_in, grad_in, logits_in, chosen_in, out_ref, tokens_ref, grad_ref, logits_ref, chosen_ref,
                rows_ref, sems):
    copies = [
        pltpu.make_async_copy(src, dst, sems.at[i])
        for i, (src, dst) in enumerate(
            [(logits_in, logits_ref), (chosen_in, chosen_ref), (tokens_in, tokens_ref), (grad_in, grad_ref)]
        )
    ]
    for copy in copies:
        copy.start()
    copies[0].wait()
    copies[1].wait()
    tok, width = tokens_ref.shape
    logits = logits_ref[...]
    chosen = chosen_ref[...]
    experts = logits.shape[1]
    ids = lax.broadcasted_iota(jnp.int32, logits.shape, 1)
    hit = ids == chosen[:, 0:1]
    for k in range(1, chosen.shape[1]):
        hit = hit | (ids == chosen[:, k : k + 1])
    top = jnp.max(jnp.where(hit, logits, -jnp.inf), axis=1, keepdims=True)
    raised = jnp.where(hit, jnp.exp(jnp.minimum(logits - top, 0.0)), 0.0)
    parts = [raised / jnp.sum(raised, axis=1, keepdims=True)]
    rest = softmax_f32(logits)
    for _ in range(PIECES - 1):
        parts.append(rest)
        rest = rest - rest.astype(BF16).astype(F32)
    lanes = out_ref.shape[1] - width
    spare = lanes - PIECES * experts
    extras = jnp.concatenate(parts + ([jnp.zeros((tok, spare), F32)] if spare else []), axis=1)
    copies[2].wait()
    copies[3].wait()
    rows_ref[0:tok, :width] = tokens_ref[...].astype(F32)
    rows_ref[tok:, :width] = grad_ref[...].astype(F32)
    rows_ref[0:tok, width:] = extras
    rows_ref[tok:, width:] = jnp.zeros((tok, lanes), F32)
    out_ref[...] = rows_ref[...].astype(BF16)


def load_kernel(chunks, after_ref, gate_in, up_in, down_in, pair_ref, down_ref, sems):
    hidden = gate_in.shape[2]
    copies = []

    def add(src, dst):
        copies.append(pltpu.make_async_copy(src, dst, sems.at[len(copies)]))

    for c in range(chunks):
        rows = gate_in.shape[1] // chunks
        part = pl.ds(c * rows, rows)
        add(gate_in.at[0, part, :], pair_ref.at[part, 0:hidden])
        add(up_in.at[0, part, :], pair_ref.at[part, hidden : 2 * hidden])
        rows = hidden // chunks
        part = pl.ds(c * rows, rows)
        add(down_in.at[0, part, :], down_ref.at[part, :])
    for copy in copies:
        copy.start()
    for copy in copies:
        copy.wait()


def join_kernel(tok, *refs):
    blocks, out_ref, rows_ref = refs[:-2], refs[-2], refs[-1]
    count = len(blocks)
    for j, ref in enumerate(blocks):
        block = ref[...].astype(F32)
        rows_ref[j * tok : (j + 1) * tok, :] = block[:tok]
        rows_ref[(count + j) * tok : (count + j + 1) * tok, :] = block[tok:]
    out_ref[...] = rows_ref[...].astype(BF16)


def stack_kernel(*refs):
    out_ref = refs[-1]
    rows = refs[0].shape[0]
    for j, ref in enumerate(refs[:-1]):
        out_ref[j * rows : (j + 1) * rows, :] = ref[...]


def token_rows(ref, start, rows, group, kind, columns):
    parts = []
    for j in range(rows // (2 * group)):
        first = start + (2 * j + kind) * group
        if not isinstance(first, int):
            first = pl.multiple_of(first, group)
        parts.append(ref[pl.ds(first, group), columns])
    return parts[0] if len(parts) == 1 else jnp.concatenate(parts, axis=0)


def put_scores(out_ref, scores_ref, width):
    rows = out_ref.shape[0]
    for c in range((out_ref.shape[1] - width) // LANES):
        out_ref[:, width + c * LANES : width + (c + 1) * LANES] = scores_ref[c * rows : (c + 1) * rows, :].astype(BF16)


def get_scores(in_ref, scores_ref, base, size, width):
    rows = in_ref.shape[0]
    for c in range(-(-size // rows)):
        here = min(rows, size - c * rows)
        tall = min(rows, -(-here // 16) * 16)
        block = in_ref[0:tall, width + c * LANES : width + (c + 1) * LANES].astype(F32)
        scores_ref[base + c * rows : base + c * rows + here, :] = block[:here]


def half_kernel(basis, group, tok, swap_mask, last, buf_ref, pair_ref, down_ref, *rest):
    hidden, width = down_ref.shape
    experts_width = buf_ref.shape[1] - width
    own = own_index()
    expert = own // 2
    rows = buf_ref.shape[0]
    if last:
        base_ref, out_ref, pieces_ref, score_ref, padded_ref = rest
        score_ref[...] = base_ref[...]
    else:
        out_ref, score_ref = rest
        score_ref[...] = jnp.zeros(score_ref.shape, F32)
    tokens = score_ref.shape[1]
    step = min(rows, 128)
    half_step = step // 2

    def one(index):
        start = index * step
        act = token_rows(buf_ref, start, step, group, 0, slice(None))
        extras = act[:, width:].astype(F32)
        lane = lax.broadcasted_iota(jnp.int32, (half_step, experts_width), 1)
        column = jnp.sum(jnp.where(lane == expert, extras, 0.0), axis=1, keepdims=True)
        pair = jnp.dot(act[:, :width], pair_ref[...], preferred_element_type=F32)
        gate_pre = pair[:, :hidden]
        up_pre = pair[:, hidden:]
        cot = token_rows(buf_ref, start, step, group, 1, slice(0, width))
        back = lax.dot_general(cot, down_ref[...], NT, preferred_element_type=F32)
        sig = jax.nn.sigmoid(gate_pre)
        act_gate = gate_pre * sig
        score = jnp.sum(act_gate * up_pre * back, axis=1, keepdims=True)
        weighted = column * back
        grad_gate = weighted * up_pre * sig * (1.0 + gate_pre * (1.0 - sig))
        grad_up = weighted * act_gate
        grads = jnp.concatenate([grad_gate.astype(BF16), grad_up.astype(BF16)], axis=1)
        total = lax.dot_general(grads, pair_ref[...], NT, preferred_element_type=F32)
        out_start = index * half_step if isinstance(index, int) else pl.multiple_of(index * half_step, half_step)
        out_ref[pl.ds(out_start, half_step), 0:width] = total.astype(out_ref.dtype)

        row = lax.broadcasted_iota(jnp.int32, (half_step, tokens), 0) + index * half_step
        token = lax.broadcasted_iota(jnp.int32, (half_step, tokens), 1)
        whole = (place_mask(row // tok, basis) ^ (own ^ swap_mask)) * tok + row % tok
        score_ref[...] += jnp.sum(jnp.where(whole == token, score, 0.0), axis=0, keepdims=True)

    if rows == step:
        one(0)
    else:
        pl.loop(0, rows // step)(one)
    if last:
        blocks = tokens // LANES
        padded_ref[...] = jnp.zeros(padded_ref.shape, F32)
        value = score_ref[...]
        for piece in range(SCORE_PIECES):
            rounded = value.astype(BF16).astype(F32)
            for b in range(blocks):
                padded_ref[piece * blocks + b : piece * blocks + b + 1, :] = rounded[:, b * LANES : (b + 1) * LANES]
            value = value - rounded
        pieces_ref[...] = padded_ref[0 : pieces_ref.shape[0], :]
        put_scores(out_ref, padded_ref, width)


def add_kernel(arrivals, positions, *refs):
    kept_ref, pieces_ref = refs[0], refs[1]
    arrived = refs[2 : 2 + arrivals]
    outs = refs[2 + arrivals :]
    next_kept_ref, next_pieces_ref = outs[0], outs[1]
    sends = outs[2 : 2 + len(positions)]
    total_ref, scores_ref = outs[2 + len(positions) :]
    width = kept_ref.shape[1]
    size = pieces_ref.shape[0]
    total = kept_ref[...]
    for ref in arrived:
        total = total + ref[:, 0:width].astype(F32)
    total_ref[...] = total
    if scores_ref.shape[0] > next_pieces_ref.shape[0]:
        scores_ref[...] = jnp.zeros(scores_ref.shape, F32)
    scores_ref[0:size, :] = pieces_ref[...]
    for j, ref in enumerate(arrived):
        get_scores(ref, scores_ref, (j + 1) * size, size, width)
    rows = next_kept_ref.shape[0]
    next_kept_ref[...] = total_ref[0:rows, :]
    next_pieces_ref[...] = scores_ref[0 : next_pieces_ref.shape[0], :]
    for j, ref in zip(positions, sends):
        ref[:, 0:width] = total_ref[j * rows : (j + 1) * rows, :].astype(BF16)
        put_scores(ref, scores_ref, width)


def table_kernel(basis, group, tok, core_mask, rows_out, after_ref, buf_own_ref, buf_other_ref, here_ref, probs_ref,
                 column_ref):
    rows, buf_width = buf_own_ref.shape
    half = rows // 2
    experts = probs_ref.shape[1]
    tokens = here_ref.shape[1]
    lanes = -(-PIECES * experts // LANES) * LANES
    width = buf_width - lanes
    own = own_index()
    lane = lax.broadcasted_iota(jnp.int32, (lanes, experts), 0)
    ids = lax.broadcasted_iota(jnp.int32, (lanes, experts), 1)
    tally = jnp.zeros((lanes, experts), F32)
    for k in range(1, PIECES):
        tally = tally + jnp.where(lane == ids + k * experts, 1.0, 0.0)
    column = pl.multiple_of(own * rows_out // LANES * LANES, LANES)
    for index, ref in enumerate((buf_own_ref, buf_other_ref)):
        row = lax.broadcasted_iota(jnp.int32, (half, tokens), 0)
        token = lax.broadcasted_iota(jnp.int32, (half, tokens), 1)
        whole = (place_mask(row // tok, basis) ^ (own ^ (core_mask if index else 0))) * tok + row % tok
        part = slice(index * half, (index + 1) * half)
        here_ref[part, :] = jnp.where(whole == token, 1.0, 0.0).astype(BF16)
        extras = token_rows(ref, 0, rows, group, 0, slice(width, buf_width))
        probs_ref[part, :] = jnp.dot(extras, tally.astype(BF16), preferred_element_type=F32)
        column_ref[part, :] = token_rows(ref, 0, rows, group, 0, pl.ds(column, LANES))


def final_kernel(arrivals, back_basis, *refs):
    here_ref, probs_ref, column_ref, router_ref, kept_ref, pieces_ref = refs[:6]
    arrived = refs[6 : 6 + arrivals]
    x_out, grad_out, x_ref, grad_ref, scores_ref, sems = refs[6 + arrivals :]
    experts, width = router_ref.shape
    size = pieces_ref.shape[0]
    tok = kept_ref.shape[0]
    own = own_index()
    scores_ref[0:size, :] = pieces_ref[...]
    for j, ref in enumerate(arrived):
        get_scores(ref, scores_ref, (j + 1) * size, size, width)
    blocks = here_ref.shape[1] // LANES
    wide = scores_ref.shape[0] // blocks
    sender = lax.broadcasted_iota(jnp.int32, (wide, experts), 0) // SCORE_PIECES
    ids = lax.broadcasted_iota(jnp.int32, (wide, experts), 1)
    pick = jnp.where(((place_mask(sender, back_basis) ^ own) >> 1) == ids, 1.0, 0.0).astype(BF16)
    picked = jnp.zeros((here_ref.shape[0], wide), F32)
    for b in range(blocks):
        block = scores_ref[...] if blocks == 1 else scores_ref[pl.ds(b, wide, stride=blocks), :]
        here = here_ref[:, b * LANES : (b + 1) * LANES]
        picked = picked + lax.dot_general(here, block.astype(BF16), NT, preferred_element_type=F32)
    scores = jnp.dot(picked.astype(BF16), pick, preferred_element_type=F32)
    probs = probs_ref[...]
    mean = jnp.sum(probs * scores, axis=1, keepdims=True)
    logit_grad = (probs * (scores - mean)).astype(BF16)
    part = jnp.dot(logit_grad[0:16], router_ref[...], preferred_element_type=F32)
    total = kept_ref[...]
    for ref in arrived:
        total = total + ref[:, 0:width].astype(F32)
    x_ref[...] = (total + part[:tok]).astype(BF16)
    x_copy = pltpu.make_async_copy(x_ref, x_out, sems.at[0])
    x_copy.start()
    grad = lax.dot_general(logit_grad, column_ref[...], TN, preferred_element_type=F32)
    rows_out = grad_ref.shape[1]
    first = own * rows_out % LANES
    grad_ref[...] = pltpu.roll(grad, (LANES - first) % LANES, 1)[:, :rows_out]
    grad_copy = pltpu.make_async_copy(grad_ref, grad_out, sems.at[1])
    grad_copy.start()
    x_copy.wait()
    grad_copy.wait()


def on_device(tokens, grad_out, router_logits, selected, router_w, w_gate, w_up, w_down):
    tok, width = tokens.shape
    experts = router_logits.shape[1]
    hidden = w_gate.shape[2]
    exp_size = lax.axis_size("exp")
    hid_size = lax.axis_size("hid")
    count = exp_size * hid_size
    half = count // 2
    groups, core_mask = stage_masks(exp_size, hid_size)
    basis = [m for group in groups for m in group]
    back_groups = [near_first(group) for group in groups[:0:-1]] + [groups[0]]
    back_basis = [core_mask] + [m for group in back_groups for m in group]
    token_count = count * tok
    lanes = -(-PIECES * experts // LANES) * LANES

    block = pl.pallas_call(
        prep_kernel,
        out_shape=jax.ShapeDtypeStruct((2 * tok, width + lanes), BF16),
        in_specs=[HBM_SPEC] * 4,
        out_specs=VMEM_SPEC,
        scratch_shapes=[
            pltpu.VMEM(tokens.shape, tokens.dtype),
            pltpu.VMEM(grad_out.shape, grad_out.dtype),
            pltpu.VMEM(router_logits.shape, router_logits.dtype),
            pltpu.VMEM(selected.shape, selected.dtype),
            pltpu.VMEM((2 * tok, width + lanes), F32),
            pltpu.SemaphoreType.DMA((4,)),
        ],
        compiler_params=PARAMS,
        name="prep",
    )(*in_hbm(tokens, grad_out, router_logits, selected))

    weights = in_hbm(w_gate, w_up, w_down)
    for index, group in enumerate(groups):
        if index == len(groups) - 1:
            chunks = 4
            weights = pl.pallas_call(
                functools.partial(load_kernel, chunks),
                out_shape=(pltpu.VMEM((width, 2 * hidden), BF16), pltpu.VMEM((hidden, width), BF16)),
                in_specs=[pl.BlockSpec(memory_space=pl.ANY)] + [HBM_SPEC] * 3,
                out_specs=(VMEM_SPEC,) * 2,
                scratch_shapes=[pltpu.SemaphoreType.DMA((3 * chunks,))],
                compiler_params=pltpu.CompilerParams(vmem_limit_bytes=4 * 2**20),
                cost_estimate=pl.CostEstimate(flops=0, bytes_accessed=6 * width * hidden * 2, transcendentals=0),
                name="load",
            )(block, *weights)
        blocks = [block] + [swap(block, m, count) for m in group_masks(group)[1:]]
        if index == 0:
            group_rows = tok * len(blocks)
            block = pl.pallas_call(
                functools.partial(join_kernel, tok),
                out_shape=jax.ShapeDtypeStruct((2 * group_rows, width + lanes), BF16),
                in_specs=[VMEM_SPEC] * len(blocks),
                out_specs=VMEM_SPEC,
                scratch_shapes=[pltpu.VMEM((2 * group_rows, width + lanes), F32)],
                compiler_params=PARAMS,
                name="join",
            )(*blocks)
        else:
            block = pl.pallas_call(
                stack_kernel,
                out_shape=jax.ShapeDtypeStruct((len(blocks) * block.shape[0], block.shape[1]), BF16),
                in_specs=[VMEM_SPEC] * len(blocks),
                out_specs=VMEM_SPEC,
                compiler_params=PARAMS,
                name="stack",
            )(*blocks)
    other = swap(block, core_mask, count)

    cost = pl.CostEstimate(
        flops=2 * half * 8 * width * hidden * 4,
        bytes_accessed=3 * width * hidden * 2 + half * 8 * width * 2,
        transcendentals=half * 8 * hidden,
    )
    unit_rows = SCORE_PIECES * token_count // LANES
    kept, score = pl.pallas_call(
        functools.partial(half_kernel, basis, group_rows, tok, 0, False),
        out_shape=(
            jax.ShapeDtypeStruct((half * tok, width), F32),
            jax.ShapeDtypeStruct((1, token_count), F32),
        ),
        in_specs=[VMEM_SPEC] * 3,
        out_specs=(VMEM_SPEC, VMEM_SPEC),
        compiler_params=PARAMS,
        cost_estimate=pl.CostEstimate(
            flops=cost.flops * 16, bytes_accessed=cost.bytes_accessed, transcendentals=cost.transcendentals
        ),
        name="half_own",
    )(block, *weights)
    extra = -(-unit_rows // (half * tok)) * LANES
    message, pieces = pl.pallas_call(
        functools.partial(half_kernel, basis, group_rows, tok, core_mask, True),
        out_shape=(
            jax.ShapeDtypeStruct((half * tok, width + extra), BF16),
            jax.ShapeDtypeStruct((unit_rows, LANES), F32),
        ),
        in_specs=[VMEM_SPEC] * 4,
        out_specs=(VMEM_SPEC, VMEM_SPEC),
        scratch_shapes=[
            pltpu.VMEM((1, token_count), F32),
            pltpu.VMEM((max(half * tok * extra // LANES, unit_rows), LANES), F32),
        ],
        compiler_params=PARAMS,
        cost_estimate=cost,
        name="half_other",
    )(other, *weights, score)

    arrived = [swap(message, core_mask, count)]
    tables = None
    rows_out = width // count
    for group, back_group in zip(groups[::-1], back_groups):
        masks = group_masks(group)
        back_masks = group_masks(back_group)
        radix = len(masks)
        rows = kept.shape[0]
        next_rows = rows // radix
        size = pieces.shape[0] * (1 + len(arrived))
        extra = -(-size // next_rows) * LANES
        sends = [jax.ShapeDtypeStruct((next_rows, width + extra), BF16)] * (radix - 1)
        outs = pl.pallas_call(
            functools.partial(add_kernel, len(arrived), [masks.index(m) for m in back_masks[1:]]),
            out_shape=[
                jax.ShapeDtypeStruct((next_rows, width), F32),
                jax.ShapeDtypeStruct((size, LANES), F32),
            ]
            + sends,
            in_specs=[VMEM_SPEC] * (2 + len(arrived)),
            out_specs=[VMEM_SPEC] * (1 + radix),
            scratch_shapes=[
                pltpu.VMEM((rows, width), F32),
                pltpu.VMEM((max(next_rows * extra // LANES, size), LANES), F32),
            ],
            compiler_params=PARAMS,
            name="add",
        )(kept, pieces, *arrived)
        kept, pieces = outs[0], outs[1]
        if tables is None:
            tables = pl.pallas_call(
                functools.partial(table_kernel, basis, group_rows, tok, core_mask, rows_out),
                out_shape=(
                    jax.ShapeDtypeStruct((block.shape[0], token_count), BF16),
                    jax.ShapeDtypeStruct((block.shape[0], experts), F32),
                    jax.ShapeDtypeStruct((block.shape[0], LANES), BF16),
                ),
                in_specs=[pl.BlockSpec(memory_space=pl.ANY)] + [VMEM_SPEC] * 2,
                out_specs=(VMEM_SPEC,) * 3,
                compiler_params=PARAMS,
                cost_estimate=pl.CostEstimate(flops=10**9, bytes_accessed=10**6, transcendentals=0),
                name="tables",
            )(pieces, block, other)
        arrived = [swap(piece, m, count) for piece, m in zip(outs[2:], back_masks[1:])]

    x_grad, grad = pl.pallas_call(
        functools.partial(final_kernel, len(arrived), back_basis),
        out_shape=(
            jax.ShapeDtypeStruct((tok, width), BF16),
            jax.ShapeDtypeStruct((experts, rows_out), F32),
        ),
        in_specs=[VMEM_SPEC] * (6 + len(arrived)),
        out_specs=(HBM_SPEC, HBM_SPEC),
        scratch_shapes=[
            pltpu.VMEM((tok, width), BF16),
            pltpu.VMEM((experts, rows_out), F32),
            pltpu.VMEM((pieces.shape[0] * (1 + len(arrived)), LANES), F32),
            pltpu.SemaphoreType.DMA((2,)),
        ],
        compiler_params=PARAMS,
        name="final",
    )(*tables, router_w.T, kept, pieces, *arrived)
    return (x_grad, grad.T)


def solution(mesh):
    rows = P(AXES, None)
    units = P(AXES, None, None)
    return jax.shard_map(
        on_device,
        mesh=mesh,
        in_specs=(rows, rows, rows, rows, P(), units, units, units),
        out_specs=(rows, rows),
        check_vma=False,
    )
```

```python
import functools

import jax
import jax.numpy as jnp
from jax import lax
from jax.experimental import pallas as pl
from jax.experimental.pallas import tpu as pltpu
from jax.sharding import PartitionSpec as P

AXES = ("exp", "hid")
LANES = 128
PIECES = 4
SCORE_PIECES = 2
VMEM_SPEC = pl.BlockSpec(memory_space=pltpu.VMEM)
HBM_SPEC = pl.BlockSpec(memory_space=pltpu.HBM)
F32 = jnp.float32
BF16 = jnp.bfloat16
NT = (((1,), (1,)), ((), ()))
TN = (((0,), (0,)), ((), ()))
PARAMS = pltpu.CompilerParams(vmem_limit_bytes=24 * 2**20)


def stage_masks(exp_size, hid_size):
    hid_bits = hid_size.bit_length() - 1
    all_bits = (exp_size * hid_size).bit_length() - 1
    core = hid_bits
    first = list(range(max(core + 1, all_bits - 2), all_bits))
    middle = [b for b in range(all_bits) if b != core and b not in first]
    groups = [first] + [middle[i : i + 2] for i in range(0, len(middle), 2)]
    bases = [[sum(1 << b for b in group[i:]) for i in range(len(group))] for group in groups]
    return bases, 1 << core


def group_masks(basis):
    masks = [0]
    for mask in basis:
        masks = masks + [m ^ mask for m in masks]
    return masks


def near_first(basis):
    return [a ^ b for a, b in zip(basis, basis[1:] + [0])]


def swap(block, mask, count):
    return lax.ppermute(block, AXES, [(i, i ^ mask) for i in range(count)])


def swaps(block, masks, count):
    return [swap(block, m, count) for m in masks]


def forward(blocks):
    return blocks[:1] + blocks[:0:-1]


def place_mask(place, basis):
    total = jnp.zeros_like(place)
    for digit, mask in enumerate(basis):
        total = total ^ (((place >> digit) & 1) * mask)
    return total


def own_index():
    return lax.axis_index("exp") * lax.axis_size("hid") + lax.axis_index("hid")


def in_hbm(*arrays):
    return tuple(pltpu.with_memory_space_constraint(a, pltpu.HBM) for a in arrays)


def softmax_f32(values):
    raised = jnp.exp(values - jnp.max(values, axis=-1, keepdims=True))
    return raised / jnp.sum(raised, axis=-1, keepdims=True)


def prep_kernel(tokens_in, grad_in, logits_in, chosen_in, out_ref, logits_ref, chosen_ref, sems):
    tok, width = tokens_in.shape
    pairs = [
        (logits_in, logits_ref),
        (chosen_in, chosen_ref),
        (tokens_in, out_ref.at[0, :, 0:width]),
        (grad_in, out_ref.at[1, :, 0:width]),
    ]
    copies = [pltpu.make_async_copy(src, dst, sems.at[i]) for i, (src, dst) in enumerate(pairs)]
    for copy in copies:
        copy.start()
    copies[0].wait()
    copies[1].wait()
    logits = logits_ref[...]
    chosen = chosen_ref[...]
    experts = logits.shape[1]
    ids = lax.broadcasted_iota(jnp.int32, logits.shape, 1)
    hit = ids == chosen[:, 0:1]
    for k in range(1, chosen.shape[1]):
        hit = hit | (ids == chosen[:, k : k + 1])
    top = jnp.max(jnp.where(hit, logits, -jnp.inf), axis=1, keepdims=True)
    raised = jnp.where(hit, jnp.exp(jnp.minimum(logits - top, 0.0)), 0.0)
    parts = [raised / jnp.sum(raised, axis=1, keepdims=True)]
    rest = softmax_f32(logits)
    for _ in range(PIECES - 1):
        parts.append(rest)
        rest = rest - rest.astype(BF16).astype(F32)
    lanes = out_ref.shape[2] - width
    spare = lanes - PIECES * experts
    extras = jnp.concatenate(parts + ([jnp.zeros((tok, spare), F32)] if spare else []), axis=1)
    out_ref[0, :, width:] = extras.astype(BF16)
    out_ref[1, :, width:] = jnp.zeros((tok, lanes), BF16)
    copies[2].wait()
    copies[3].wait()


def load_kernel(chunks, after_ref, *refs):
    weights, out_ref, sems = refs[:-2], refs[-2], refs[-1]
    copies = []
    for k, ref in enumerate(weights):
        rows, columns = ref.shape[1] // chunks, ref.shape[2]
        for c in range(chunks):
            src = ref.at[0, pl.ds(c * rows, rows), :]
            dst = out_ref.at[pl.ds(c * rows, rows), k * columns : (k + 1) * columns]
            copies.append(pltpu.make_async_copy(src, dst, sems.at[len(copies)]))
    for copy in copies:
        copy.start()
    for copy in copies:
        copy.wait()


def load(after, *weights):
    chunks = 4
    rows, columns = weights[0].shape[1:]
    return pl.pallas_call(
        functools.partial(load_kernel, chunks),
        out_shape=pltpu.VMEM((rows, columns * len(weights)), weights[0].dtype),
        in_specs=[pl.BlockSpec(memory_space=pl.ANY)] + [HBM_SPEC] * len(weights),
        out_specs=VMEM_SPEC,
        scratch_shapes=[pltpu.SemaphoreType.DMA((chunks * len(weights),))],
        compiler_params=pltpu.CompilerParams(vmem_limit_bytes=4 * 2**20),
        cost_estimate=pl.CostEstimate(
            flops=0, bytes_accessed=4 * rows * columns * len(weights), transcendentals=0
        ),
        name="load",
    )(after, *in_hbm(*weights))


def join_kernel(*refs):
    blocks, out_ref, rows_ref = refs[:1] + refs[1:-3][::-1], refs[-2], refs[-1]
    count = len(blocks)
    tok = blocks[0].shape[1]
    for kind in range(2):
        for j, ref in enumerate(blocks):
            first = (kind * count + j) * tok
            rows_ref[first : first + tok, :] = ref[kind].astype(F32)
    out_ref[...] = rows_ref[...].astype(BF16)


def stack_kernel(*refs):
    out_ref = refs[-1]
    rows = refs[0].shape[0]
    for j, ref in enumerate(refs[:-1]):
        out_ref[j * rows : (j + 1) * rows, :] = ref[...]


def token_rows(refs, start, rows, group, kind, columns):
    parts = []
    for ref in refs:
        for j in range(rows // (2 * group)):
            first = start + (2 * j + kind) * group
            if not isinstance(first, int):
                first = pl.multiple_of(first, group)
            parts.append(ref[pl.ds(first, group), columns])
    return parts[0] if len(parts) == 1 else jnp.concatenate(parts, axis=0)


def put_scores(out_ref, scores_ref, width):
    rows = out_ref.shape[0]
    for c in range((out_ref.shape[1] - width) // LANES):
        out_ref[:, width + c * LANES : width + (c + 1) * LANES] = scores_ref[c * rows : (c + 1) * rows, :].astype(BF16)


def get_scores(in_ref, scores_ref, base, size, width):
    rows = in_ref.shape[0]
    for c in range(-(-size // rows)):
        here = min(rows, size - c * rows)
        tall = min(rows, -(-here // 16) * 16)
        block = in_ref[0:tall, width + c * LANES : width + (c + 1) * LANES].astype(F32)
        scores_ref[base + c * rows : base + c * rows + here, :] = block[:here]


def units_kernel(basis, group, tok, core_mask, blocks, *refs):
    own_refs, other_refs = forward(refs[:blocks]), forward(refs[blocks : 2 * blocks])
    pair_ref, down_ref, kept_ref, message_ref, pieces_ref, score_ref, padded_ref = refs[2 * blocks :]
    hidden, width = down_ref.shape
    rows, buf_width = own_refs[0].shape
    tokens = score_ref.shape[1]
    own = own_index()

    def terms(sets, start, step):
        act = token_rows(sets, start, step, group, 0, slice(None))
        count = act.shape[0]
        extras = act[:, width:].astype(F32)
        lane = lax.broadcasted_iota(jnp.int32, (count, buf_width - width), 1)
        column = jnp.sum(jnp.where(lane == own // 2, extras, 0.0), axis=1, keepdims=True)
        pair = jnp.dot(act[:, :width], pair_ref[...], preferred_element_type=F32)
        gate_pre = pair[:, :hidden]
        up_pre = pair[:, hidden:]
        cot = token_rows(sets, start, step, group, 1, slice(0, width))
        back = lax.dot_general(cot, down_ref[...], NT, preferred_element_type=F32)
        sig = jax.nn.sigmoid(gate_pre)
        act_gate = gate_pre * sig
        score = jnp.sum(act_gate * up_pre * back, axis=1, keepdims=True)
        weighted = column * back
        grad_gate = weighted * up_pre * sig * (1.0 + gate_pre * (1.0 - sig))
        grad_up = weighted * act_gate
        grads = jnp.concatenate([grad_gate.astype(BF16), grad_up.astype(BF16)], axis=1)
        return lax.dot_general(grads, pair_ref[...], NT, preferred_element_type=F32), score

    def in_order(score, place, swap_mask):
        token = lax.broadcasted_iota(jnp.int32, (score.shape[0], tokens), 1)
        whole = (place_mask(place // tok, basis) ^ (own ^ swap_mask)) * tok + place % tok
        return jnp.sum(jnp.where(whole == token, score, 0.0), axis=0, keepdims=True)

    half = blocks * rows // 2
    if 2 * half <= 128:
        total, score = terms(own_refs + other_refs, 0, rows)
        kept_ref[...] = total[:half]
        message_ref[:, 0:width] = total[half:].astype(BF16)
        row = lax.broadcasted_iota(jnp.int32, (2 * half, tokens), 0)
        score_ref[...] = in_order(score, row % half, jnp.where(row < half, 0, core_mask))
    else:
        step = min(rows, 128)
        score_ref[...] = jnp.zeros(score_ref.shape, F32)
        for out_ref, sets, swap_mask in ((kept_ref, own_refs, 0), (message_ref, other_refs, core_mask)):
            for j, ref in enumerate(sets):

                def one(index):
                    total, score = terms((ref,), index * step, step)
                    first = pl.multiple_of(j * (rows // 2) + index * (step // 2), step // 2)
                    out_ref[pl.ds(first, step // 2), 0:width] = total.astype(out_ref.dtype)
                    place = lax.broadcasted_iota(jnp.int32, (step // 2, tokens), 0) + first
                    score_ref[...] += in_order(score, place, swap_mask)

                pl.loop(0, rows // step)(one)

    lane_blocks = tokens // LANES
    padded_ref[...] = jnp.zeros(padded_ref.shape, F32)
    value = score_ref[...]
    for piece in range(SCORE_PIECES):
        rounded = value.astype(BF16).astype(F32)
        for b in range(lane_blocks):
            at = piece * lane_blocks + b
            padded_ref[at : at + 1, :] = rounded[:, b * LANES : (b + 1) * LANES]
        value = value - rounded
    pieces_ref[...] = padded_ref[0 : pieces_ref.shape[0], :]
    put_scores(message_ref, padded_ref, width)


def add_kernel(arrivals, positions, *refs):
    kept_ref, pieces_ref = refs[0], refs[1]
    arrived = refs[2 : 2 + arrivals]
    outs = refs[2 + arrivals :]
    next_kept_ref, next_pieces_ref = outs[0], outs[1]
    sends = outs[2 : 2 + len(positions)]
    total_ref, scores_ref = outs[2 + len(positions) :]
    width = kept_ref.shape[1]
    size = pieces_ref.shape[0]
    total = kept_ref[...]
    for ref in arrived:
        total = total + ref[:, 0:width].astype(F32)
    total_ref[...] = total
    if scores_ref.shape[0] > next_pieces_ref.shape[0]:
        scores_ref[...] = jnp.zeros(scores_ref.shape, F32)
    scores_ref[0:size, :] = pieces_ref[...]
    for j, ref in enumerate(arrived):
        get_scores(ref, scores_ref, (j + 1) * size, size, width)
    rows = next_kept_ref.shape[0]
    next_kept_ref[...] = total_ref[0:rows, :]
    next_pieces_ref[...] = scores_ref[0 : next_pieces_ref.shape[0], :]
    for j, ref in zip(positions, sends):
        ref[:, 0:width] = total_ref[j * rows : (j + 1) * rows, :].astype(BF16)
        put_scores(ref, scores_ref, width)


def table_kernel(basis, group, tok, core_mask, rows_out, blocks, after_ref, *refs):
    here_ref, probs_ref, column_ref = refs[2 * blocks :]
    rows, buf_width = refs[0].shape
    half = blocks * rows // 2
    experts = probs_ref.shape[1]
    tokens = here_ref.shape[1]
    lanes = -(-PIECES * experts // LANES) * LANES
    width = buf_width - lanes
    own = own_index()
    lane = lax.broadcasted_iota(jnp.int32, (lanes, experts), 0)
    ids = lax.broadcasted_iota(jnp.int32, (lanes, experts), 1)
    tally = jnp.zeros((lanes, experts), F32)
    for k in range(1, PIECES):
        tally = tally + jnp.where(lane == ids + k * experts, 1.0, 0.0)
    column = pl.multiple_of(own * rows_out // LANES * LANES, LANES)
    for index in range(2):
        sets = forward(refs[index * blocks : (index + 1) * blocks])
        row = lax.broadcasted_iota(jnp.int32, (half, tokens), 0)
        token = lax.broadcasted_iota(jnp.int32, (half, tokens), 1)
        whole = (place_mask(row // tok, basis) ^ (own ^ (core_mask if index else 0))) * tok + row % tok
        part = slice(index * half, (index + 1) * half)
        here_ref[part, :] = jnp.where(whole == token, 1.0, 0.0).astype(BF16)
        extras = token_rows(sets, 0, rows, group, 0, slice(width, buf_width))
        probs_ref[part, :] = jnp.dot(extras, tally.astype(BF16), preferred_element_type=F32)
        column_ref[part, :] = token_rows(sets, 0, rows, group, 0, pl.ds(column, LANES))


def final_kernel(arrivals, back_basis, *refs):
    here_ref, probs_ref, column_ref, router_ref, kept_ref, pieces_ref = refs[:6]
    arrived = refs[6 : 6 + arrivals]
    x_out, grad_out, x_ref, grad_ref, scores_ref, sems = refs[6 + arrivals :]
    experts, width = router_ref.shape
    size = pieces_ref.shape[0]
    tok = kept_ref.shape[0]
    own = own_index()
    scores_ref[0:size, :] = pieces_ref[...]
    for j, ref in enumerate(arrived):
        get_scores(ref, scores_ref, (j + 1) * size, size, width)
    blocks = here_ref.shape[1] // LANES
    wide = scores_ref.shape[0] // blocks
    sender = lax.broadcasted_iota(jnp.int32, (wide, experts), 0) // SCORE_PIECES
    ids = lax.broadcasted_iota(jnp.int32, (wide, experts), 1)
    pick = jnp.where(((place_mask(sender, back_basis) ^ own) >> 1) == ids, 1.0, 0.0).astype(BF16)
    picked = jnp.zeros((here_ref.shape[0], wide), F32)
    for b in range(blocks):
        block = scores_ref[...] if blocks == 1 else scores_ref[pl.ds(b, wide, stride=blocks), :]
        here = here_ref[:, b * LANES : (b + 1) * LANES]
        picked = picked + lax.dot_general(here, block.astype(BF16), NT, preferred_element_type=F32)
    scores = jnp.dot(picked.astype(BF16), pick, preferred_element_type=F32)
    probs = probs_ref[...]
    mean = jnp.sum(probs * scores, axis=1, keepdims=True)
    logit_grad = (probs * (scores - mean)).astype(BF16)
    part = jnp.dot(logit_grad[0:16], router_ref[...], preferred_element_type=F32)
    total = kept_ref[...]
    for ref in arrived:
        total = total + ref[:, 0:width].astype(F32)
    x_ref[...] = (total + part[:tok]).astype(BF16)
    x_copy = pltpu.make_async_copy(x_ref, x_out, sems.at[0])
    x_copy.start()
    grad = lax.dot_general(logit_grad, column_ref[...], TN, preferred_element_type=F32)
    rows_out = grad_ref.shape[1]
    first = own * rows_out % LANES
    grad_ref[...] = pltpu.roll(grad, (LANES - first) % LANES, 1)[:, :rows_out]
    grad_copy = pltpu.make_async_copy(grad_ref, grad_out, sems.at[1])
    grad_copy.start()
    x_copy.wait()
    grad_copy.wait()


def on_device(tokens, grad_out, router_logits, selected, router_w, w_gate, w_up, w_down):
    tok, width = tokens.shape
    experts = router_logits.shape[1]
    hidden = w_gate.shape[2]
    exp_size = lax.axis_size("exp")
    hid_size = lax.axis_size("hid")
    count = exp_size * hid_size
    half = count // 2
    groups, core_mask = stage_masks(exp_size, hid_size)
    basis = [m for group in groups for m in group]
    back_groups = [near_first(group) for group in groups[:0:-1]] + [groups[0]]
    back_basis = [core_mask] + [m for group in back_groups for m in group]
    token_count = count * tok
    lanes = -(-PIECES * experts // LANES) * LANES

    block = pl.pallas_call(
        prep_kernel,
        out_shape=jax.ShapeDtypeStruct((2, tok, width + lanes), BF16),
        in_specs=[HBM_SPEC] * 4,
        out_specs=VMEM_SPEC,
        scratch_shapes=[
            pltpu.VMEM(router_logits.shape, router_logits.dtype),
            pltpu.VMEM(selected.shape, selected.dtype),
            pltpu.SemaphoreType.DMA((4,)),
        ],
        compiler_params=PARAMS,
        name="prep",
    )(*in_hbm(tokens, grad_out, router_logits, selected))

    masks = group_masks(groups[0])
    pair = load(block, w_gate, w_up)
    blocks = [block] + swaps(block, masks[1:], count)
    group_rows = tok * len(blocks)
    block = pl.pallas_call(
        join_kernel,
        out_shape=jax.ShapeDtypeStruct((2 * group_rows, width + lanes), BF16),
        in_specs=[VMEM_SPEC] * len(blocks) + [pl.BlockSpec(memory_space=pl.ANY)],
        out_specs=VMEM_SPEC,
        scratch_shapes=[pltpu.VMEM((2 * group_rows, width + lanes), F32)],
        compiler_params=PARAMS,
        name="join",
    )(block, *blocks[:0:-1], pair)
    for group in groups[1:-1]:
        blocks = [block] + swaps(block, group_masks(group)[1:], count)
        block = pl.pallas_call(
            stack_kernel,
            out_shape=jax.ShapeDtypeStruct((len(blocks) * block.shape[0], block.shape[1]), BF16),
            in_specs=[VMEM_SPEC] * len(blocks),
            out_specs=VMEM_SPEC,
            compiler_params=PARAMS,
            name="stack",
        )(*blocks)
    down = load(block, w_down)
    masks = group_masks(groups[-1]) if len(groups) > 1 else [0]
    blocks = [block] + swaps(block, masks[1:], count)
    blocks = forward(blocks)
    blocks = blocks + [swap(b, core_mask, count) for b in blocks]
    block_count = len(blocks) // 2
    all_rows = half * 2 * tok

    unit_rows = SCORE_PIECES * token_count // LANES
    extra = -(-unit_rows // (half * tok)) * LANES
    kept, message, pieces = pl.pallas_call(
        functools.partial(units_kernel, basis, group_rows, tok, core_mask, block_count),
        out_shape=(
            jax.ShapeDtypeStruct((half * tok, width), F32),
            jax.ShapeDtypeStruct((half * tok, width + extra), BF16),
            jax.ShapeDtypeStruct((unit_rows, LANES), F32),
        ),
        in_specs=[VMEM_SPEC] * (len(blocks) + 2),
        out_specs=(VMEM_SPEC,) * 3,
        scratch_shapes=[
            pltpu.VMEM((1, token_count), F32),
            pltpu.VMEM((max(half * tok * extra // LANES, unit_rows), LANES), F32),
        ],
        compiler_params=PARAMS,
        cost_estimate=pl.CostEstimate(
            flops=10 * token_count * width * hidden,
            bytes_accessed=3 * width * hidden * 2 + 2 * token_count * width * 2,
            transcendentals=token_count * hidden,
        ),
        name="units",
    )(*blocks, pair, down)

    arrived = [swap(message, core_mask, count)]
    tables = None
    rows_out = width // count
    for group, back_group in zip(groups[::-1], back_groups):
        masks = group_masks(group)
        back_masks = group_masks(back_group)
        radix = len(masks)
        rows = kept.shape[0]
        next_rows = rows // radix
        size = pieces.shape[0] * (1 + len(arrived))
        extra = -(-size // next_rows) * LANES
        sends = [jax.ShapeDtypeStruct((next_rows, width + extra), BF16)] * (radix - 1)
        outs = pl.pallas_call(
            functools.partial(add_kernel, len(arrived), [masks.index(m) for m in back_masks[1:]]),
            out_shape=[
                jax.ShapeDtypeStruct((next_rows, width), F32),
                jax.ShapeDtypeStruct((size, LANES), F32),
            ]
            + sends,
            in_specs=[VMEM_SPEC] * (2 + len(arrived)),
            out_specs=[VMEM_SPEC] * (1 + radix),
            scratch_shapes=[
                pltpu.VMEM((rows, width), F32),
                pltpu.VMEM((max(next_rows * extra // LANES, size), LANES), F32),
            ],
            compiler_params=PARAMS,
            name="add",
        )(kept, pieces, *arrived)
        kept, pieces = outs[0], outs[1]
        if tables is None:
            tables = pl.pallas_call(
                functools.partial(table_kernel, basis, group_rows, tok, core_mask, rows_out, block_count),
                out_shape=(
                    jax.ShapeDtypeStruct((all_rows, token_count), BF16),
                    jax.ShapeDtypeStruct((all_rows, experts), F32),
                    jax.ShapeDtypeStruct((all_rows, LANES), BF16),
                ),
                in_specs=[pl.BlockSpec(memory_space=pl.ANY)] + [VMEM_SPEC] * len(blocks),
                out_specs=(VMEM_SPEC,) * 3,
                compiler_params=PARAMS,
                cost_estimate=pl.CostEstimate(flops=10**9, bytes_accessed=10**6, transcendentals=0),
                name="tables",
            )(pieces, *blocks)
        arrived = [swap(piece, m, count) for piece, m in zip(outs[2:], back_masks[1:])]

    x_grad, grad = pl.pallas_call(
        functools.partial(final_kernel, len(arrived), back_basis),
        out_shape=(
            jax.ShapeDtypeStruct((tok, width), BF16),
            jax.ShapeDtypeStruct((experts, rows_out), F32),
        ),
        in_specs=[VMEM_SPEC] * (6 + len(arrived)),
        out_specs=(HBM_SPEC, HBM_SPEC),
        scratch_shapes=[
            pltpu.VMEM((tok, width), BF16),
            pltpu.VMEM((experts, rows_out), F32),
            pltpu.VMEM((pieces.shape[0] * (1 + len(arrived)), LANES), F32),
            pltpu.SemaphoreType.DMA((2,)),
        ],
        compiler_params=PARAMS,
        name="final",
    )(*tables, router_w.T, kept, pieces, *arrived)
    return (x_grad, grad.T)


def solution(mesh):
    rows = P(AXES, None)
    units = P(AXES, None, None)
    return jax.shard_map(
        on_device,
        mesh=mesh,
        in_specs=(rows, rows, rows, rows, P(), units, units, units),
        out_specs=(rows, rows),
        check_vma=False,
    )
```

```python
import functools

import jax
import jax.numpy as jnp
from jax import lax
from jax.experimental import pallas as pl
from jax.experimental.pallas import tpu as pltpu
from jax.sharding import PartitionSpec as P

AXES = ("exp", "hid")
LANES = 128
PIECES = 4
SCORE_PIECES = 2
VMEM_SPEC = pl.BlockSpec(memory_space=pltpu.VMEM)
HBM_SPEC = pl.BlockSpec(memory_space=pltpu.HBM)
F32 = jnp.float32
BF16 = jnp.bfloat16
NT = (((1,), (1,)), ((), ()))
TN = (((0,), (0,)), ((), ()))
PARAMS = pltpu.CompilerParams(vmem_limit_bytes=24 * 2**20)


def stage_masks(exp_size, hid_size):
    hid_bits = hid_size.bit_length() - 1
    all_bits = (exp_size * hid_size).bit_length() - 1
    core = hid_bits
    first = list(range(max(core + 1, all_bits - 2), all_bits))
    middle = [b for b in range(all_bits) if b != core and b not in first]
    groups = [first] + [middle[i : i + 2] for i in range(0, len(middle), 2)]
    bases = [[sum(1 << b for b in group[i:]) for i in range(len(group))] for group in groups]
    return bases, 1 << core


def group_masks(basis):
    masks = [0]
    for mask in basis:
        masks = masks + [m ^ mask for m in masks]
    return masks


def near_first(basis):
    return [a ^ b for a, b in zip(basis, basis[1:] + [0])]


def swap(block, mask, count):
    return lax.ppermute(block, AXES, [(i, i ^ mask) for i in range(count)])


def swaps(block, masks, count):
    return [swap(block, m, count) for m in masks]


def forward(blocks):
    return blocks[:1] + blocks[:0:-1]


def place_mask(place, basis):
    total = jnp.zeros_like(place)
    for digit, mask in enumerate(basis):
        total = total ^ (((place >> digit) & 1) * mask)
    return total


def own_index():
    return lax.axis_index("exp") * lax.axis_size("hid") + lax.axis_index("hid")


def in_hbm(*arrays):
    return tuple(pltpu.with_memory_space_constraint(a, pltpu.HBM) for a in arrays)


def softmax_f32(values):
    raised = jnp.exp(values - jnp.max(values, axis=-1, keepdims=True))
    return raised / jnp.sum(raised, axis=-1, keepdims=True)


def prep_kernel(tokens_in, grad_in, logits_in, chosen_in, out_ref, logits_ref, chosen_ref, sems):
    tok, width = tokens_in.shape
    pairs = [
        (logits_in, logits_ref),
        (chosen_in, chosen_ref),
        (tokens_in, out_ref.at[0, :, 0:width]),
        (grad_in, out_ref.at[1, :, 0:width]),
    ]
    copies = [pltpu.make_async_copy(src, dst, sems.at[i]) for i, (src, dst) in enumerate(pairs)]
    for copy in copies:
        copy.start()
    copies[0].wait()
    copies[1].wait()
    logits = logits_ref[...]
    chosen = chosen_ref[...]
    experts = logits.shape[1]
    ids = lax.broadcasted_iota(jnp.int32, logits.shape, 1)
    hit = ids == chosen[:, 0:1]
    for k in range(1, chosen.shape[1]):
        hit = hit | (ids == chosen[:, k : k + 1])
    top = jnp.max(jnp.where(hit, logits, -jnp.inf), axis=1, keepdims=True)
    raised = jnp.where(hit, jnp.exp(jnp.minimum(logits - top, 0.0)), 0.0)
    parts = [raised / jnp.sum(raised, axis=1, keepdims=True)]
    rest = softmax_f32(logits)
    for _ in range(PIECES - 1):
        parts.append(rest)
        rest = rest - rest.astype(BF16).astype(F32)
    lanes = out_ref.shape[2] - width
    spare = lanes - PIECES * experts
    extras = jnp.concatenate(parts + ([jnp.zeros((tok, spare), F32)] if spare else []), axis=1)
    out_ref[0, :, width:] = extras.astype(BF16)
    out_ref[1, :, width:] = jnp.zeros((tok, lanes), BF16)
    copies[2].wait()
    copies[3].wait()


def load_kernel(chunks, block_in, gate_in, up_in, down_in, block_ref, pair_ref, down_ref, sems):
    copies = []

    def add(src, dst):
        copies.append(pltpu.make_async_copy(src, dst, sems.at[len(copies)]))

    hidden, width = down_ref.shape
    for c in range(chunks):
        part = pl.ds(c * (width // chunks), width // chunks)
        add(gate_in.at[0, part, :], pair_ref.at[part, 0:hidden])
        add(up_in.at[0, part, :], pair_ref.at[part, hidden : 2 * hidden])
        part = pl.ds(c * (hidden // chunks), hidden // chunks)
        add(down_in.at[0, part, :], down_ref.at[part, :])
    add(block_in, block_ref)
    for copy in copies:
        copy.start()
    for copy in copies:
        copy.wait()


def join_kernel(*refs):
    blocks, out_ref, rows_ref = forward(refs[:-2]), refs[-2], refs[-1]
    count = len(blocks)
    tok = blocks[0].shape[1]
    for kind in range(2):
        for j, ref in enumerate(blocks):
            first = (kind * count + j) * tok
            rows_ref[first : first + tok, :] = ref[kind].astype(F32)
    out_ref[...] = rows_ref[...].astype(BF16)


def stack_kernel(*refs):
    out_ref = refs[-1]
    rows = refs[0].shape[0]
    for j, ref in enumerate(refs[:-1]):
        out_ref[j * rows : (j + 1) * rows, :] = ref[...]


def token_rows(refs, start, rows, group, kind, columns):
    parts = []
    for ref in refs:
        for j in range(rows // (2 * group)):
            first = start + (2 * j + kind) * group
            if not isinstance(first, int):
                first = pl.multiple_of(first, group)
            parts.append(ref[pl.ds(first, group), columns])
    return parts[0] if len(parts) == 1 else jnp.concatenate(parts, axis=0)


def put_scores(out_ref, scores_ref, width):
    rows = out_ref.shape[0]
    for c in range((out_ref.shape[1] - width) // LANES):
        out_ref[:, width + c * LANES : width + (c + 1) * LANES] = scores_ref[c * rows : (c + 1) * rows, :].astype(BF16)


def get_scores(in_ref, scores_ref, base, size, width):
    rows = in_ref.shape[0]
    for c in range(-(-size // rows)):
        here = min(rows, size - c * rows)
        tall = min(rows, -(-here // 16) * 16)
        block = in_ref[0:tall, width + c * LANES : width + (c + 1) * LANES].astype(F32)
        scores_ref[base + c * rows : base + c * rows + here, :] = block[:here]


def units_kernel(basis, group, tok, core_mask, blocks, *refs):
    own_refs, other_refs = forward(refs[:blocks]), forward(refs[blocks : 2 * blocks])
    pair_ref, down_ref, kept_ref, message_ref, pieces_ref, score_ref, padded_ref = refs[2 * blocks :]
    hidden, width = down_ref.shape
    rows, buf_width = own_refs[0].shape
    tokens = score_ref.shape[1]
    own = own_index()

    def terms(sets, start, step):
        act = token_rows(sets, start, step, group, 0, slice(None))
        count = act.shape[0]
        extras = act[:, width:].astype(F32)
        lane = lax.broadcasted_iota(jnp.int32, (count, buf_width - width), 1)
        column = jnp.sum(jnp.where(lane == own // 2, extras, 0.0), axis=1, keepdims=True)
        pair = jnp.dot(act[:, :width], pair_ref[...], preferred_element_type=F32)
        gate_pre = pair[:, :hidden]
        up_pre = pair[:, hidden:]
        cot = token_rows(sets, start, step, group, 1, slice(0, width))
        back = lax.dot_general(cot, down_ref[...], NT, preferred_element_type=F32)
        sig = jax.nn.sigmoid(gate_pre)
        act_gate = gate_pre * sig
        score = jnp.sum(act_gate * up_pre * back, axis=1, keepdims=True)
        weighted = column * back
        grad_gate = weighted * up_pre * sig * (1.0 + gate_pre * (1.0 - sig))
        grad_up = weighted * act_gate
        grads = jnp.concatenate([grad_gate.astype(BF16), grad_up.astype(BF16)], axis=1)
        return lax.dot_general(grads, pair_ref[...], NT, preferred_element_type=F32), score

    def in_order(score, place, swap_mask):
        token = lax.broadcasted_iota(jnp.int32, (score.shape[0], tokens), 1)
        whole = (place_mask(place // tok, basis) ^ (own ^ swap_mask)) * tok + place % tok
        return jnp.sum(jnp.where(whole == token, score, 0.0), axis=0, keepdims=True)

    half = blocks * rows // 2
    if 2 * half <= 128:
        total, score = terms(own_refs + other_refs, 0, rows)
        kept_ref[...] = total[:half]
        message_ref[:, 0:width] = total[half:].astype(BF16)
        row = lax.broadcasted_iota(jnp.int32, (2 * half, tokens), 0)
        score_ref[...] = in_order(score, row % half, jnp.where(row < half, 0, core_mask))
    else:
        step = min(rows, 128)
        score_ref[...] = jnp.zeros(score_ref.shape, F32)
        for out_ref, sets, swap_mask in ((kept_ref, own_refs, 0), (message_ref, other_refs, core_mask)):
            for j, ref in enumerate(sets):

                def one(index):
                    total, score = terms((ref,), index * step, step)
                    first = pl.multiple_of(j * (rows // 2) + index * (step // 2), step // 2)
                    out_ref[pl.ds(first, step // 2), 0:width] = total.astype(out_ref.dtype)
                    place = lax.broadcasted_iota(jnp.int32, (step // 2, tokens), 0) + first
                    score_ref[...] += in_order(score, place, swap_mask)

                pl.loop(0, rows // step)(one)

    lane_blocks = tokens // LANES
    padded_ref[...] = jnp.zeros(padded_ref.shape, F32)
    value = score_ref[...]
    for piece in range(SCORE_PIECES):
        rounded = value.astype(BF16).astype(F32)
        for b in range(lane_blocks):
            at = piece * lane_blocks + b
            padded_ref[at : at + 1, :] = rounded[:, b * LANES : (b + 1) * LANES]
        value = value - rounded
    pieces_ref[...] = padded_ref[0 : pieces_ref.shape[0], :]
    put_scores(message_ref, padded_ref, width)


def add_kernel(arrivals, positions, *refs):
    kept_ref, pieces_ref = refs[0], refs[1]
    arrived = refs[2 : 2 + arrivals]
    outs = refs[2 + arrivals :]
    next_kept_ref, next_pieces_ref = outs[0], outs[1]
    sends = outs[2 : 2 + len(positions)]
    total_ref, scores_ref = outs[2 + len(positions) :]
    width = kept_ref.shape[1]
    size = pieces_ref.shape[0]
    total = kept_ref[...]
    for ref in arrived:
        total = total + ref[:, 0:width].astype(F32)
    total_ref[...] = total
    if scores_ref.shape[0] > next_pieces_ref.shape[0]:
        scores_ref[...] = jnp.zeros(scores_ref.shape, F32)
    scores_ref[0:size, :] = pieces_ref[...]
    for j, ref in enumerate(arrived):
        get_scores(ref, scores_ref, (j + 1) * size, size, width)
    rows = next_kept_ref.shape[0]
    next_kept_ref[...] = total_ref[0:rows, :]
    next_pieces_ref[...] = scores_ref[0 : next_pieces_ref.shape[0], :]
    for j, ref in zip(positions, sends):
        ref[:, 0:width] = total_ref[j * rows : (j + 1) * rows, :].astype(BF16)
        put_scores(ref, scores_ref, width)


def table_kernel(basis, group, tok, core_mask, rows_out, blocks, after_ref, *refs):
    probs_ref, column_ref, mine_ref = refs[2 * blocks :]
    rows, buf_width = refs[0].shape
    half = blocks * rows // 2
    experts, tokens = probs_ref.shape
    lanes = -(-PIECES * experts // LANES) * LANES
    width = buf_width - lanes
    own = own_index()
    lane = lax.broadcasted_iota(jnp.int32, (experts, lanes), 1)
    ids = lax.broadcasted_iota(jnp.int32, (experts, lanes), 0)
    tally = jnp.zeros((experts, lanes), F32)
    for k in range(1, PIECES):
        tally = tally + jnp.where(lane == ids + k * experts, 1.0, 0.0)
    column = pl.multiple_of(own * rows_out // LANES * LANES, LANES)
    extras = jnp.zeros((tokens, lanes), F32)
    columns = jnp.zeros((tokens, LANES), F32)
    for index in range(2):
        sets = forward(refs[index * blocks : (index + 1) * blocks])
        row = lax.broadcasted_iota(jnp.int32, (half, tokens), 0)
        token = lax.broadcasted_iota(jnp.int32, (half, tokens), 1)
        whole = (place_mask(row // tok, basis) ^ (own ^ (core_mask if index else 0))) * tok + row % tok
        here = jnp.where(whole == token, 1.0, 0.0).astype(BF16)
        part = token_rows(sets, 0, rows, group, 0, slice(width, buf_width))
        extras = extras + lax.dot_general(here, part, TN, preferred_element_type=F32)
        part = token_rows(sets, 0, rows, group, 0, pl.ds(column, LANES))
        columns = columns + lax.dot_general(here, part, TN, preferred_element_type=F32)
    probs_ref[...] = lax.dot_general(tally.astype(BF16), extras.astype(BF16), NT, preferred_element_type=F32)
    column_ref[...] = columns.astype(BF16)
    row = lax.broadcasted_iota(jnp.int32, mine_ref.shape, 0)
    token = lax.broadcasted_iota(jnp.int32, mine_ref.shape, 1)
    mine_ref[...] = jnp.where((row < tok) & (token == own * tok + row), 1.0, 0.0).astype(BF16)


def final_kernel(arrivals, back_basis, *refs):
    probs_ref, column_ref, mine_ref, router_ref, kept_ref, pieces_ref = refs[:6]
    arrived = refs[6 : 6 + arrivals]
    x_out, grad_out, x_ref, grad_ref, scores_ref, sems = refs[6 + arrivals :]
    experts, width = router_ref.shape
    size = pieces_ref.shape[0]
    tok = kept_ref.shape[0]
    own = own_index()
    scores_ref[0:size, :] = pieces_ref[...]
    for j, ref in enumerate(arrived):
        get_scores(ref, scores_ref, (j + 1) * size, size, width)
    blocks = probs_ref.shape[1] // LANES
    wide = scores_ref.shape[0] // blocks
    sender = lax.broadcasted_iota(jnp.int32, (experts, wide), 1) // SCORE_PIECES
    ids = lax.broadcasted_iota(jnp.int32, (experts, wide), 0)
    pick = jnp.where(((place_mask(sender, back_basis) ^ own) >> 1) == ids, 1.0, 0.0).astype(BF16)
    parts = []
    for b in range(blocks):
        block = scores_ref[...] if blocks == 1 else scores_ref[pl.ds(b, wide, stride=blocks), :]
        parts.append(jnp.dot(pick, block.astype(BF16), preferred_element_type=F32))
    scores = parts[0] if blocks == 1 else jnp.concatenate(parts, axis=1)
    probs = probs_ref[...]
    mean = jnp.sum(probs * scores, axis=0, keepdims=True)
    logit_grad = (probs * (scores - mean)).astype(BF16)
    mine = lax.dot_general(mine_ref[...], logit_grad, NT, preferred_element_type=F32)
    part = jnp.dot(mine.astype(BF16), router_ref[...], preferred_element_type=F32)
    total = kept_ref[...]
    for ref in arrived:
        total = total + ref[:, 0:width].astype(F32)
    x_ref[...] = (total + part[:tok]).astype(BF16)
    x_copy = pltpu.make_async_copy(x_ref, x_out, sems.at[0])
    x_copy.start()
    grad = jnp.dot(logit_grad, column_ref[...], preferred_element_type=F32)
    rows_out = grad_ref.shape[1]
    first = own * rows_out % LANES
    grad_ref[...] = pltpu.roll(grad, (LANES - first) % LANES, 1)[:, :rows_out]
    grad_copy = pltpu.make_async_copy(grad_ref, grad_out, sems.at[1])
    grad_copy.start()
    x_copy.wait()
    grad_copy.wait()


def on_device(tokens, grad_out, router_logits, selected, router_w, w_gate, w_up, w_down):
    tok, width = tokens.shape
    experts = router_logits.shape[1]
    hidden = w_gate.shape[2]
    exp_size = lax.axis_size("exp")
    hid_size = lax.axis_size("hid")
    count = exp_size * hid_size
    half = count // 2
    groups, core_mask = stage_masks(exp_size, hid_size)
    basis = [m for group in groups for m in group]
    back_groups = [near_first(group) for group in groups[:0:-1]] + [groups[0]]
    back_basis = [core_mask] + [m for group in back_groups for m in group]
    token_count = count * tok
    lanes = -(-PIECES * experts // LANES) * LANES

    block = pl.pallas_call(
        prep_kernel,
        out_shape=jax.ShapeDtypeStruct((2, tok, width + lanes), BF16),
        in_specs=[HBM_SPEC] * 4,
        out_specs=VMEM_SPEC,
        scratch_shapes=[
            pltpu.VMEM(router_logits.shape, router_logits.dtype),
            pltpu.VMEM(selected.shape, selected.dtype),
            pltpu.SemaphoreType.DMA((4,)),
        ],
        compiler_params=PARAMS,
        name="prep",
    )(*in_hbm(tokens, grad_out, router_logits, selected))

    masks = group_masks(groups[0])
    blocks = [block] + swaps(block, masks[1:], count)
    group_rows = tok * len(blocks)
    block = pl.pallas_call(
        join_kernel,
        out_shape=jax.ShapeDtypeStruct((2 * group_rows, width + lanes), BF16),
        in_specs=[VMEM_SPEC] * len(blocks),
        out_specs=VMEM_SPEC,
        scratch_shapes=[pltpu.VMEM((2 * group_rows, width + lanes), F32)],
        compiler_params=PARAMS,
        name="join",
    )(*forward(blocks))
    for group in groups[1:-1]:
        blocks = [block] + swaps(block, group_masks(group)[1:], count)
        block = pl.pallas_call(
            stack_kernel,
            out_shape=jax.ShapeDtypeStruct((len(blocks) * block.shape[0], block.shape[1]), BF16),
            in_specs=[VMEM_SPEC] * len(blocks),
            out_specs=VMEM_SPEC,
            compiler_params=PARAMS,
            name="stack",
        )(*blocks)
    chunks = 4
    copied, pair, down = pl.pallas_call(
        functools.partial(load_kernel, chunks),
        out_shape=(
            pltpu.VMEM(block.shape, BF16),
            pltpu.VMEM((width, 2 * hidden), BF16),
            pltpu.VMEM((hidden, width), BF16),
        ),
        in_specs=[VMEM_SPEC] + [HBM_SPEC] * 3,
        out_specs=(VMEM_SPEC,) * 3,
        scratch_shapes=[pltpu.SemaphoreType.DMA((3 * chunks + 1,))],
        compiler_params=pltpu.CompilerParams(vmem_limit_bytes=4 * 2**20),
        cost_estimate=pl.CostEstimate(flops=0, bytes_accessed=6 * width * hidden * 2, transcendentals=0),
        name="load",
    )(block, *in_hbm(w_gate, w_up, w_down))
    masks = group_masks(groups[-1]) if len(groups) > 1 else [0]
    blocks = [block] + swaps(block, masks[1:], count)
    blocks = forward(blocks)
    blocks = blocks + [swap(b, core_mask, count) for b in [copied] + blocks[1:]]
    block_count = len(blocks) // 2

    unit_rows = SCORE_PIECES * token_count // LANES
    extra = -(-unit_rows // (half * tok)) * LANES
    kept, message, pieces = pl.pallas_call(
        functools.partial(units_kernel, basis, group_rows, tok, core_mask, block_count),
        out_shape=(
            jax.ShapeDtypeStruct((half * tok, width), F32),
            jax.ShapeDtypeStruct((half * tok, width + extra), BF16),
            jax.ShapeDtypeStruct((unit_rows, LANES), F32),
        ),
        in_specs=[VMEM_SPEC] * (len(blocks) + 2),
        out_specs=(VMEM_SPEC,) * 3,
        scratch_shapes=[
            pltpu.VMEM((1, token_count), F32),
            pltpu.VMEM((max(half * tok * extra // LANES, unit_rows), LANES), F32),
        ],
        compiler_params=PARAMS,
        cost_estimate=pl.CostEstimate(
            flops=10 * token_count * width * hidden,
            bytes_accessed=3 * width * hidden * 2 + 2 * token_count * width * 2,
            transcendentals=token_count * hidden,
        ),
        name="units",
    )(*blocks, pair, down)

    arrived = [swap(message, core_mask, count)]
    tables = None
    rows_out = width // count
    for group, back_group in zip(groups[::-1], back_groups):
        masks = group_masks(group)
        back_masks = group_masks(back_group)
        radix = len(masks)
        rows = kept.shape[0]
        next_rows = rows // radix
        size = pieces.shape[0] * (1 + len(arrived))
        extra = -(-size // next_rows) * LANES
        sends = [jax.ShapeDtypeStruct((next_rows, width + extra), BF16)] * (radix - 1)
        outs = pl.pallas_call(
            functools.partial(add_kernel, len(arrived), [masks.index(m) for m in back_masks[1:]]),
            out_shape=[
                jax.ShapeDtypeStruct((next_rows, width), F32),
                jax.ShapeDtypeStruct((size, LANES), F32),
            ]
            + sends,
            in_specs=[VMEM_SPEC] * (2 + len(arrived)),
            out_specs=[VMEM_SPEC] * (1 + radix),
            scratch_shapes=[
                pltpu.VMEM((rows, width), F32),
                pltpu.VMEM((max(next_rows * extra // LANES, size), LANES), F32),
            ],
            compiler_params=PARAMS,
            name="add",
        )(kept, pieces, *arrived)
        kept, pieces = outs[0], outs[1]
        if tables is None:
            tables = pl.pallas_call(
                functools.partial(table_kernel, basis, group_rows, tok, core_mask, rows_out, block_count),
                out_shape=(
                    jax.ShapeDtypeStruct((experts, token_count), F32),
                    jax.ShapeDtypeStruct((token_count, LANES), BF16),
                    jax.ShapeDtypeStruct((16, token_count), BF16),
                ),
                in_specs=[pl.BlockSpec(memory_space=pl.ANY)] + [VMEM_SPEC] * len(blocks),
                out_specs=(VMEM_SPEC,) * 3,
                compiler_params=PARAMS,
                cost_estimate=pl.CostEstimate(flops=10**9, bytes_accessed=10**6, transcendentals=0),
                name="tables",
            )(pieces, *blocks)
        arrived = [swap(piece, m, count) for piece, m in zip(outs[2:], back_masks[1:])]

    x_grad, grad = pl.pallas_call(
        functools.partial(final_kernel, len(arrived), back_basis),
        out_shape=(
            jax.ShapeDtypeStruct((tok, width), BF16),
            jax.ShapeDtypeStruct((experts, rows_out), F32),
        ),
        in_specs=[VMEM_SPEC] * (6 + len(arrived)),
        out_specs=(HBM_SPEC, HBM_SPEC),
        scratch_shapes=[
            pltpu.VMEM((tok, width), BF16),
            pltpu.VMEM((experts, rows_out), F32),
            pltpu.VMEM((pieces.shape[0] * (1 + len(arrived)), LANES), F32),
            pltpu.SemaphoreType.DMA((2,)),
        ],
        compiler_params=PARAMS,
        name="final",
    )(*tables, router_w.T, kept, pieces, *arrived)
    return (x_grad, grad.T)


def solution(mesh):
    rows = P(AXES, None)
    units = P(AXES, None, None)
    return jax.shard_map(
        on_device,
        mesh=mesh,
        in_specs=(rows, rows, rows, rows, P(), units, units, units),
        out_specs=(rows, rows),
        check_vma=False,
    )
```

```python
import functools

import jax
import jax.numpy as jnp
from jax import lax
from jax.experimental import pallas as pl
from jax.experimental.pallas import tpu as pltpu
from jax.sharding import PartitionSpec as P

AXES = ("exp", "hid")
LANES = 128
PIECES = 4
SCORE_PIECES = 2
VMEM_SPEC = pl.BlockSpec(memory_space=pltpu.VMEM)
HBM_SPEC = pl.BlockSpec(memory_space=pltpu.HBM)
F32 = jnp.float32
BF16 = jnp.bfloat16
NT = (((1,), (1,)), ((), ()))
TN = (((0,), (0,)), ((), ()))
PARAMS = pltpu.CompilerParams(vmem_limit_bytes=24 * 2**20)


def stage_masks(exp_size, hid_size):
    hid_bits = hid_size.bit_length() - 1
    all_bits = (exp_size * hid_size).bit_length() - 1
    core = hid_bits
    first = list(range(max(core + 1, all_bits - 2), all_bits))
    middle = [b for b in range(all_bits) if b != core and b not in first]
    groups = [first] + [middle[i : i + 2] for i in range(0, len(middle), 2)]
    bases = [[sum(1 << b for b in group[i:]) for i in range(len(group))] for group in groups]
    return bases, 1 << core


def group_masks(basis):
    masks = [0]
    for mask in basis:
        masks = masks + [m ^ mask for m in masks]
    return masks


def nearest_first(basis):
    return [basis[0] ^ basis[1], basis[0]] if len(basis) == 2 else basis


def swap(block, mask, count):
    return lax.ppermute(block, AXES, [(i, i ^ mask) for i in range(count)])


def swaps(block, masks, count):
    return [swap(block, m, count) for m in masks]


def forward(blocks):
    return blocks[:1] + blocks[:0:-1]


def place_mask(place, basis):
    total = jnp.zeros_like(place)
    for digit, mask in enumerate(basis):
        total = total ^ (((place >> digit) & 1) * mask)
    return total


def own_index():
    return lax.axis_index("exp") * lax.axis_size("hid") + lax.axis_index("hid")


def in_hbm(*arrays):
    return tuple(pltpu.with_memory_space_constraint(a, pltpu.HBM) for a in arrays)


def softmax_f32(values):
    raised = jnp.exp(values - jnp.max(values, axis=-1, keepdims=True))
    return raised / jnp.sum(raised, axis=-1, keepdims=True)


def prep_kernel(tokens_in, grad_in, logits_in, chosen_in, out_ref, logits_ref, chosen_ref, sems):
    tok, width = tokens_in.shape
    pairs = [
        (logits_in, logits_ref),
        (chosen_in, chosen_ref),
        (tokens_in, out_ref.at[0, :, 0:width]),
        (grad_in, out_ref.at[1, :, 0:width]),
    ]
    copies = [pltpu.make_async_copy(src, dst, sems.at[i]) for i, (src, dst) in enumerate(pairs)]
    for copy in copies:
        copy.start()
    copies[0].wait()
    copies[1].wait()
    logits = logits_ref[...]
    chosen = chosen_ref[...]
    experts = logits.shape[1]
    ids = lax.broadcasted_iota(jnp.int32, logits.shape, 1)
    hit = ids == chosen[:, 0:1]
    for k in range(1, chosen.shape[1]):
        hit = hit | (ids == chosen[:, k : k + 1])
    top = jnp.max(jnp.where(hit, logits, -jnp.inf), axis=1, keepdims=True)
    raised = jnp.where(hit, jnp.exp(jnp.minimum(logits - top, 0.0)), 0.0)
    parts = [raised / jnp.sum(raised, axis=1, keepdims=True)]
    rest = softmax_f32(logits)
    for _ in range(PIECES - 1):
        parts.append(rest)
        rest = rest - rest.astype(BF16).astype(F32)
    lanes = out_ref.shape[2] - width
    spare = lanes - PIECES * experts
    extras = jnp.concatenate(parts + ([jnp.zeros((tok, spare), F32)] if spare else []), axis=1)
    out_ref[0, :, width:] = extras.astype(BF16)
    out_ref[1, :, width:] = jnp.zeros((tok, lanes), BF16)
    copies[2].wait()
    copies[3].wait()


def hidden_parts(hidden):
    main = hidden // 256 * 256
    return [(0, main), (main, hidden)] if 0 < main < hidden else [(0, hidden)]


def load_kernel(chunks, block_in, gate_in, up_in, down_in, block_ref, pair_ref, down_ref, sems):
    copies = []

    def add(src, dst):
        copies.append(pltpu.make_async_copy(src, dst, sems.at[len(copies)]))

    hidden, width = down_ref.shape
    for c in range(chunks):
        part = pl.ds(c * (width // chunks), width // chunks)
        for first, last in hidden_parts(hidden):
            for k, ref in enumerate((gate_in, up_in)):
                to = 2 * first + k * (last - first)
                add(ref.at[0, part, first:last], pair_ref.at[part, to : to + last - first])
        part = pl.ds(c * (hidden // chunks), hidden // chunks)
        add(down_in.at[0, part, :], down_ref.at[part, :])
    add(block_in, block_ref)
    for copy in copies:
        copy.start()
    for copy in copies:
        copy.wait()


def join_kernel(*refs):
    blocks, out_ref, rows_ref = forward(refs[:-2]), refs[-2], refs[-1]
    count = len(blocks)
    tok = blocks[0].shape[1]
    for kind in range(2):
        for j, ref in enumerate(blocks):
            first = (kind * count + j) * tok
            rows_ref[first : first + tok, :] = ref[kind].astype(F32)
    out_ref[...] = rows_ref[...].astype(BF16)


def stack_kernel(*refs):
    out_ref = refs[-1]
    rows = refs[0].shape[0]
    for j, ref in enumerate(refs[:-1]):
        out_ref[j * rows : (j + 1) * rows, :] = ref[...]


def token_rows(refs, start, rows, group, kind, columns):
    parts = []
    for ref in refs:
        for j in range(rows // (2 * group)):
            first = start + (2 * j + kind) * group
            if not isinstance(first, int):
                first = pl.multiple_of(first, group)
            parts.append(ref[pl.ds(first, group), columns])
    return parts[0] if len(parts) == 1 else jnp.concatenate(parts, axis=0)


def put_scores(out_ref, scores_ref, width):
    rows = out_ref.shape[0]
    for c in range((out_ref.shape[1] - width) // LANES):
        out_ref[:, width + c * LANES : width + (c + 1) * LANES] = scores_ref[c * rows : (c + 1) * rows, :].astype(BF16)


def get_scores(in_ref, scores_ref, base, size, width):
    rows = in_ref.shape[0]
    for c in range(-(-size // rows)):
        here = min(rows, size - c * rows)
        tall = min(rows, -(-here // 16) * 16)
        block = in_ref[0:tall, width + c * LANES : width + (c + 1) * LANES].astype(F32)
        scores_ref[base + c * rows : base + c * rows + here, :] = block[:here]


def units_kernel(basis, group, tok, core_mask, blocks, *refs):
    own_refs, other_refs = forward(refs[:blocks]), forward(refs[blocks : 2 * blocks])
    pair_ref, down_ref, kept_ref, message_ref, pieces_ref, score_ref, padded_ref = refs[2 * blocks :]
    hidden, width = down_ref.shape
    rows, buf_width = own_refs[0].shape
    tokens = score_ref.shape[1]
    own = own_index()

    def terms(sets, start, step):
        act = token_rows(sets, start, step, group, 0, slice(None))
        count = act.shape[0]
        extras = act[:, width:].astype(F32)
        lane = lax.broadcasted_iota(jnp.int32, (count, buf_width - width), 1)
        column = jnp.sum(jnp.where(lane == own // 2, extras, 0.0), axis=1, keepdims=True)
        act = act[:, :width]
        cot = token_rows(sets, start, step, group, 1, slice(0, width))
        score = jnp.zeros((count, 1), F32)
        grads = []
        for first, last in hidden_parts(hidden):
            size = last - first
            pair = jnp.dot(act, pair_ref[:, 2 * first : 2 * last], preferred_element_type=F32)
            gate_pre = pair[:, :size]
            up_pre = pair[:, size:]
            back = lax.dot_general(cot, down_ref[first:last, :], NT, preferred_element_type=F32)
            sig = jax.nn.sigmoid(gate_pre)
            act_gate = gate_pre * sig
            score = score + jnp.sum(act_gate * up_pre * back, axis=1, keepdims=True)
            weighted = column * back
            grad_gate = weighted * up_pre * sig * (1.0 + gate_pre * (1.0 - sig))
            grad_up = weighted * act_gate
            grads += [grad_gate.astype(BF16), grad_up.astype(BF16)]
        grads = jnp.concatenate(grads, axis=1)
        return lax.dot_general(grads, pair_ref[...], NT, preferred_element_type=F32), score

    def in_order(score, place, swap_mask):
        token = lax.broadcasted_iota(jnp.int32, (score.shape[0], tokens), 1)
        whole = (place_mask(place // tok, basis) ^ (own ^ swap_mask)) * tok + place % tok
        return jnp.sum(jnp.where(whole == token, score, 0.0), axis=0, keepdims=True)

    half = blocks * rows // 2
    if 2 * half <= 128:
        total, score = terms(own_refs + other_refs, 0, rows)
        kept_ref[...] = total[:half]
        message_ref[:, 0:width] = total[half:].astype(BF16)
        row = lax.broadcasted_iota(jnp.int32, (2 * half, tokens), 0)
        score_ref[...] = in_order(score, row % half, jnp.where(row < half, 0, core_mask))
    else:
        step = min(rows, 128)
        score_ref[...] = jnp.zeros(score_ref.shape, F32)
        for out_ref, sets, swap_mask in ((kept_ref, own_refs, 0), (message_ref, other_refs, core_mask)):
            for j, ref in enumerate(sets):

                def one(index):
                    total, score = terms((ref,), index * step, step)
                    first = pl.multiple_of(j * (rows // 2) + index * (step // 2), step // 2)
                    out_ref[pl.ds(first, step // 2), 0:width] = total.astype(out_ref.dtype)
                    place = lax.broadcasted_iota(jnp.int32, (step // 2, tokens), 0) + first
                    score_ref[...] += in_order(score, place, swap_mask)

                pl.loop(0, rows // step)(one)

    lane_blocks = tokens // LANES
    padded_ref[...] = jnp.zeros(padded_ref.shape, F32)
    value = score_ref[...]
    for piece in range(SCORE_PIECES):
        rounded = value.astype(BF16).astype(F32)
        for b in range(lane_blocks):
            at = piece * lane_blocks + b
            padded_ref[at : at + 1, :] = rounded[:, b * LANES : (b + 1) * LANES]
        value = value - rounded
    pieces_ref[...] = padded_ref[0 : pieces_ref.shape[0], :]
    put_scores(message_ref, padded_ref, width)


def add_kernel(arrivals, positions, *refs):
    kept_ref, pieces_ref = refs[0], refs[1]
    arrived = refs[2 : 2 + arrivals]
    outs = refs[2 + arrivals :]
    next_kept_ref, next_pieces_ref = outs[0], outs[1]
    sends = outs[2 : 2 + len(positions)]
    total_ref, scores_ref = outs[2 + len(positions) :]
    width = kept_ref.shape[1]
    size = pieces_ref.shape[0]
    total = kept_ref[...]
    for ref in arrived:
        total = total + ref[:, 0:width].astype(F32)
    total_ref[...] = total
    if scores_ref.shape[0] > next_pieces_ref.shape[0]:
        scores_ref[...] = jnp.zeros(scores_ref.shape, F32)
    scores_ref[0:size, :] = pieces_ref[...]
    for j, ref in enumerate(arrived):
        get_scores(ref, scores_ref, (j + 1) * size, size, width)
    rows = next_kept_ref.shape[0]
    next_kept_ref[...] = total_ref[0:rows, :]
    next_pieces_ref[...] = scores_ref[0 : next_pieces_ref.shape[0], :]
    for j, ref in zip(positions, sends):
        ref[:, 0:width] = total_ref[j * rows : (j + 1) * rows, :].astype(BF16)
        put_scores(ref, scores_ref, width)


def table_kernel(basis, group, tok, core_mask, rows_out, blocks, after_ref, *refs):
    probs_ref, column_ref, mine_ref = refs[2 * blocks :]
    rows, buf_width = refs[0].shape
    half = blocks * rows // 2
    experts, tokens = probs_ref.shape
    lanes = -(-PIECES * experts // LANES) * LANES
    width = buf_width - lanes
    own = own_index()
    lane = lax.broadcasted_iota(jnp.int32, (experts, lanes), 1)
    ids = lax.broadcasted_iota(jnp.int32, (experts, lanes), 0)
    tally = jnp.zeros((experts, lanes), F32)
    for k in range(1, PIECES):
        tally = tally + jnp.where(lane == ids + k * experts, 1.0, 0.0)
    column = pl.multiple_of(own * rows_out // LANES * LANES, LANES)
    extras = jnp.zeros((tokens, lanes), F32)
    columns = jnp.zeros((tokens, LANES), F32)
    for index in range(2):
        sets = forward(refs[index * blocks : (index + 1) * blocks])
        row = lax.broadcasted_iota(jnp.int32, (half, tokens), 0)
        token = lax.broadcasted_iota(jnp.int32, (half, tokens), 1)
        whole = (place_mask(row // tok, basis) ^ (own ^ (core_mask if index else 0))) * tok + row % tok
        here = jnp.where(whole == token, 1.0, 0.0).astype(BF16)
        part = token_rows(sets, 0, rows, group, 0, slice(width, buf_width))
        extras = extras + lax.dot_general(here, part, TN, preferred_element_type=F32)
        part = token_rows(sets, 0, rows, group, 0, pl.ds(column, LANES))
        columns = columns + lax.dot_general(here, part, TN, preferred_element_type=F32)
    probs_ref[...] = lax.dot_general(tally.astype(BF16), extras.astype(BF16), NT, preferred_element_type=F32)
    column_ref[...] = columns.astype(BF16)
    row = lax.broadcasted_iota(jnp.int32, mine_ref.shape, 0)
    token = lax.broadcasted_iota(jnp.int32, mine_ref.shape, 1)
    mine_ref[...] = jnp.where((row < tok) & (token == own * tok + row), 1.0, 0.0).astype(BF16)


def final_kernel(arrivals, back_basis, *refs):
    probs_ref, column_ref, mine_ref, router_ref, kept_ref, pieces_ref = refs[:6]
    arrived = refs[6 : 6 + arrivals]
    x_out, grad_out, x_ref, grad_ref, scores_ref, sems = refs[6 + arrivals :]
    experts, width = router_ref.shape
    size = pieces_ref.shape[0]
    tok = kept_ref.shape[0]
    own = own_index()
    scores_ref[0:size, :] = pieces_ref[...]
    for j, ref in enumerate(arrived):
        get_scores(ref, scores_ref, (j + 1) * size, size, width)
    blocks = probs_ref.shape[1] // LANES
    wide = scores_ref.shape[0] // blocks
    sender = lax.broadcasted_iota(jnp.int32, (experts, wide), 1) // SCORE_PIECES
    ids = lax.broadcasted_iota(jnp.int32, (experts, wide), 0)
    pick = jnp.where(((place_mask(sender, back_basis) ^ own) >> 1) == ids, 1.0, 0.0).astype(BF16)
    parts = []
    for b in range(blocks):
        block = scores_ref[...] if blocks == 1 else scores_ref[pl.ds(b, wide, stride=blocks), :]
        parts.append(jnp.dot(pick, block.astype(BF16), preferred_element_type=F32))
    scores = parts[0] if blocks == 1 else jnp.concatenate(parts, axis=1)
    probs = probs_ref[...]
    mean = jnp.sum(probs * scores, axis=0, keepdims=True)
    logit_grad = (probs * (scores - mean)).astype(BF16)
    mine = lax.dot_general(mine_ref[...], logit_grad, NT, preferred_element_type=F32)
    part = jnp.dot(mine.astype(BF16), router_ref[...], preferred_element_type=F32)
    total = kept_ref[...]
    for ref in arrived:
        total = total + ref[:, 0:width].astype(F32)
    x_ref[...] = (total + part[:tok]).astype(BF16)
    x_copy = pltpu.make_async_copy(x_ref, x_out, sems.at[0])
    x_copy.start()
    grad = jnp.dot(logit_grad, column_ref[...], preferred_element_type=F32)
    rows_out = grad_ref.shape[1]
    first = own * rows_out % LANES
    grad_ref[...] = pltpu.roll(grad, (LANES - first) % LANES, 1)[:, :rows_out]
    grad_copy = pltpu.make_async_copy(grad_ref, grad_out, sems.at[1])
    grad_copy.start()
    x_copy.wait()
    grad_copy.wait()


def on_device(tokens, grad_out, router_logits, selected, router_w, w_gate, w_up, w_down):
    tok, width = tokens.shape
    experts = router_logits.shape[1]
    hidden = w_gate.shape[2]
    exp_size = lax.axis_size("exp")
    hid_size = lax.axis_size("hid")
    count = exp_size * hid_size
    half = count // 2
    groups, core_mask = stage_masks(exp_size, hid_size)
    basis = [m for group in groups for m in group]
    back_groups = [nearest_first(group) for group in groups[:0:-1]] + [groups[0]]
    back_basis = [core_mask] + [m for group in back_groups for m in group]
    token_count = count * tok
    lanes = -(-PIECES * experts // LANES) * LANES

    block = pl.pallas_call(
        prep_kernel,
        out_shape=jax.ShapeDtypeStruct((2, tok, width + lanes), BF16),
        in_specs=[HBM_SPEC] * 4,
        out_specs=VMEM_SPEC,
        scratch_shapes=[
            pltpu.VMEM(router_logits.shape, router_logits.dtype),
            pltpu.VMEM(selected.shape, selected.dtype),
            pltpu.SemaphoreType.DMA((4,)),
        ],
        compiler_params=PARAMS,
        name="prep",
    )(*in_hbm(tokens, grad_out, router_logits, selected))

    masks = group_masks(groups[0])
    blocks = [block] + swaps(block, masks[1:], count)
    group_rows = tok * len(blocks)
    block = pl.pallas_call(
        join_kernel,
        out_shape=jax.ShapeDtypeStruct((2 * group_rows, width + lanes), BF16),
        in_specs=[VMEM_SPEC] * len(blocks),
        out_specs=VMEM_SPEC,
        scratch_shapes=[pltpu.VMEM((2 * group_rows, width + lanes), F32)],
        compiler_params=PARAMS,
        name="join",
    )(*forward(blocks))
    for group in groups[1:-1]:
        blocks = [block] + swaps(block, group_masks(group)[1:], count)
        block = pl.pallas_call(
            stack_kernel,
            out_shape=jax.ShapeDtypeStruct((len(blocks) * block.shape[0], block.shape[1]), BF16),
            in_specs=[VMEM_SPEC] * len(blocks),
            out_specs=VMEM_SPEC,
            compiler_params=PARAMS,
            name="stack",
        )(*blocks)
    chunks = 4
    copied, pair, down = pl.pallas_call(
        functools.partial(load_kernel, chunks),
        out_shape=(
            pltpu.VMEM(block.shape, BF16),
            pltpu.VMEM((width, 2 * hidden), BF16),
            pltpu.VMEM((hidden, width), BF16),
        ),
        in_specs=[VMEM_SPEC] + [HBM_SPEC] * 3,
        out_specs=(VMEM_SPEC,) * 3,
        scratch_shapes=[pltpu.SemaphoreType.DMA(((2 * len(hidden_parts(hidden)) + 1) * chunks + 1,))],
        compiler_params=pltpu.CompilerParams(vmem_limit_bytes=4 * 2**20),
        cost_estimate=pl.CostEstimate(flops=0, bytes_accessed=6 * width * hidden * 2, transcendentals=0),
        name="load",
    )(block, *in_hbm(w_gate, w_up, w_down))
    masks = group_masks(groups[-1]) if len(groups) > 1 else [0]
    blocks = [block] + swaps(block, masks[1:], count)
    blocks = forward(blocks)
    blocks = blocks + [swap(b, core_mask, count) for b in [copied] + blocks[1:]]
    block_count = len(blocks) // 2

    unit_rows = SCORE_PIECES * token_count // LANES
    extra = -(-unit_rows // (half * tok)) * LANES
    kept, message, pieces = pl.pallas_call(
        functools.partial(units_kernel, basis, group_rows, tok, core_mask, block_count),
        out_shape=(
            jax.ShapeDtypeStruct((half * tok, width), F32),
            jax.ShapeDtypeStruct((half * tok, width + extra), BF16),
            jax.ShapeDtypeStruct((unit_rows, LANES), F32),
        ),
        in_specs=[VMEM_SPEC] * (len(blocks) + 2),
        out_specs=(VMEM_SPEC,) * 3,
        scratch_shapes=[
            pltpu.VMEM((1, token_count), F32),
            pltpu.VMEM((max(half * tok * extra // LANES, unit_rows), LANES), F32),
        ],
        compiler_params=PARAMS,
        cost_estimate=pl.CostEstimate(
            flops=10 * token_count * width * hidden,
            bytes_accessed=3 * width * hidden * 2 + 2 * token_count * width * 2,
            transcendentals=token_count * hidden,
        ),
        name="units",
    )(*blocks, pair, down)

    arrived = [swap(message, core_mask, count)]
    tables = None
    rows_out = width // count
    for group, back_group in zip(groups[::-1], back_groups):
        masks = group_masks(group)
        back_masks = group_masks(back_group)
        radix = len(masks)
        rows = kept.shape[0]
        next_rows = rows // radix
        size = pieces.shape[0] * (1 + len(arrived))
        extra = -(-size // next_rows) * LANES
        sends = [jax.ShapeDtypeStruct((next_rows, width + extra), BF16)] * (radix - 1)
        outs = pl.pallas_call(
            functools.partial(add_kernel, len(arrived), [masks.index(m) for m in back_masks[1:]]),
            out_shape=[
                jax.ShapeDtypeStruct((next_rows, width), F32),
                jax.ShapeDtypeStruct((size, LANES), F32),
            ]
            + sends,
            in_specs=[VMEM_SPEC] * (2 + len(arrived)),
            out_specs=[VMEM_SPEC] * (1 + radix),
            scratch_shapes=[
                pltpu.VMEM((rows, width), F32),
                pltpu.VMEM((max(next_rows * extra // LANES, size), LANES), F32),
            ],
            compiler_params=PARAMS,
            name="add",
        )(kept, pieces, *arrived)
        kept, pieces = outs[0], outs[1]
        if tables is None:
            tables = pl.pallas_call(
                functools.partial(table_kernel, basis, group_rows, tok, core_mask, rows_out, block_count),
                out_shape=(
                    jax.ShapeDtypeStruct((experts, token_count), F32),
                    jax.ShapeDtypeStruct((token_count, LANES), BF16),
                    jax.ShapeDtypeStruct((16, token_count), BF16),
                ),
                in_specs=[pl.BlockSpec(memory_space=pl.ANY)] + [VMEM_SPEC] * len(blocks),
                out_specs=(VMEM_SPEC,) * 3,
                compiler_params=PARAMS,
                cost_estimate=pl.CostEstimate(flops=10**9, bytes_accessed=10**6, transcendentals=0),
                name="tables",
            )(pieces, *blocks)
        arrived = [swap(piece, m, count) for piece, m in zip(outs[2:], back_masks[1:])]

    x_grad, grad = pl.pallas_call(
        functools.partial(final_kernel, len(arrived), back_basis),
        out_shape=(
            jax.ShapeDtypeStruct((tok, width), BF16),
            jax.ShapeDtypeStruct((experts, rows_out), F32),
        ),
        in_specs=[VMEM_SPEC] * (6 + len(arrived)),
        out_specs=(HBM_SPEC, HBM_SPEC),
        scratch_shapes=[
            pltpu.VMEM((tok, width), BF16),
            pltpu.VMEM((experts, rows_out), F32),
            pltpu.VMEM((pieces.shape[0] * (1 + len(arrived)), LANES), F32),
            pltpu.SemaphoreType.DMA((2,)),
        ],
        compiler_params=PARAMS,
        name="final",
    )(*tables, router_w.T, kept, pieces, *arrived)
    return (x_grad, grad.T)


def solution(mesh):
    rows = P(AXES, None)
    units = P(AXES, None, None)
    return jax.shard_map(
        on_device,
        mesh=mesh,
        in_specs=(rows, rows, rows, rows, P(), units, units, units),
        out_specs=(rows, rows),
        check_vma=False,
    )
```

```python
import functools

import jax
import jax.numpy as jnp
from jax import lax
from jax.experimental import pallas as pl
from jax.experimental.pallas import tpu as pltpu
from jax.sharding import PartitionSpec as P

AXES = ("exp", "hid")
LANES = 128
PIECES = 4
SCORE_PIECES = 2
VMEM_SPEC = pl.BlockSpec(memory_space=pltpu.VMEM)
HBM_SPEC = pl.BlockSpec(memory_space=pltpu.HBM)
F32 = jnp.float32
BF16 = jnp.bfloat16
NT = (((1,), (1,)), ((), ()))
TN = (((0,), (0,)), ((), ()))
PARAMS = pltpu.CompilerParams(vmem_limit_bytes=24 * 2**20)


def stage_masks(exp_size, hid_size):
    hid_bits = hid_size.bit_length() - 1
    all_bits = (exp_size * hid_size).bit_length() - 1
    core = hid_bits
    first = list(range(max(core + 1, all_bits - 2), all_bits))
    middle = [b for b in range(all_bits) if b != core and b not in first]
    groups = [first] + [middle[i : i + 2] for i in range(0, len(middle), 2)]
    bases = []
    for index, group in enumerate(groups):
        basis = [(sum(1 << b for b in group[i:]),) * 2 for i in range(len(group))]
        if index > 0 and len(group) == 2:
            basis[1] = (1 << group[1], 1 << group[0])
        bases.append(basis)
    return bases, core


def cross(a, b):
    return (a[0] ^ b[0], a[1] ^ b[1])


def group_masks(basis):
    masks = [(0, 0)]
    for mask in basis:
        masks = masks + [cross(m, mask) for m in masks]
    return masks


def last_first(basis):
    return [cross(basis[0], basis[1]), basis[1]] if len(basis) == 2 else basis


def swap(block, mask, count, core):
    return lax.ppermute(block, AXES, [(i, i ^ mask[i >> core & 1]) for i in range(count)])


def swaps(block, masks, count, core):
    return [swap(block, m, count, core) for m in masks]


def forward(blocks):
    return blocks[:1] + blocks[:0:-1]


def place_mask(place, basis, upper):
    total = jnp.zeros_like(place)
    for digit, (low, high) in enumerate(basis):
        mask = low if low == high else jnp.where(upper, high, low)
        total = total ^ (((place >> digit) & 1) * mask)
    return total


def own_index():
    return lax.axis_index("exp") * lax.axis_size("hid") + lax.axis_index("hid")


def in_hbm(*arrays):
    return tuple(pltpu.with_memory_space_constraint(a, pltpu.HBM) for a in arrays)


def softmax_f32(values):
    raised = jnp.exp(values - jnp.max(values, axis=-1, keepdims=True))
    return raised / jnp.sum(raised, axis=-1, keepdims=True)


def prep_kernel(tokens_in, grad_in, logits_in, chosen_in, out_ref, logits_ref, chosen_ref, sems):
    tok, width = tokens_in.shape
    pairs = [
        (logits_in, logits_ref),
        (chosen_in, chosen_ref),
        (tokens_in, out_ref.at[0, :, 0:width]),
        (grad_in, out_ref.at[1, :, 0:width]),
    ]
    copies = [pltpu.make_async_copy(src, dst, sems.at[i]) for i, (src, dst) in enumerate(pairs)]
    for copy in copies:
        copy.start()
    copies[0].wait()
    copies[1].wait()
    logits = logits_ref[...]
    chosen = chosen_ref[...]
    experts = logits.shape[1]
    ids = lax.broadcasted_iota(jnp.int32, logits.shape, 1)
    hit = ids == chosen[:, 0:1]
    for k in range(1, chosen.shape[1]):
        hit = hit | (ids == chosen[:, k : k + 1])
    top = jnp.max(jnp.where(hit, logits, -jnp.inf), axis=1, keepdims=True)
    raised = jnp.where(hit, jnp.exp(jnp.minimum(logits - top, 0.0)), 0.0)
    parts = [raised / jnp.sum(raised, axis=1, keepdims=True)]
    rest = softmax_f32(logits)
    for _ in range(PIECES - 1):
        parts.append(rest)
        rest = rest - rest.astype(BF16).astype(F32)
    lanes = out_ref.shape[2] - width
    spare = lanes - PIECES * experts
    extras = jnp.concatenate(parts + ([jnp.zeros((tok, spare), F32)] if spare else []), axis=1)
    out_ref[0, :, width:] = extras.astype(BF16)
    out_ref[1, :, width:] = jnp.zeros((tok, lanes), BF16)
    copies[2].wait()
    copies[3].wait()


def hidden_parts(hidden):
    main = hidden // 256 * 256
    return [(0, main), (main, hidden)] if 0 < main < hidden else [(0, hidden)]


def load_kernel(chunks, block_in, gate_in, up_in, down_in, block_ref, pair_ref, down_ref, sems):
    copies = []

    def add(src, dst):
        copies.append(pltpu.make_async_copy(src, dst, sems.at[len(copies)]))

    hidden, width = down_ref.shape
    for c in range(chunks):
        part = pl.ds(c * (width // chunks), width // chunks)
        for first, last in hidden_parts(hidden):
            for k, ref in enumerate((gate_in, up_in)):
                to = 2 * first + k * (last - first)
                add(ref.at[0, part, first:last], pair_ref.at[part, to : to + last - first])
        part = pl.ds(c * (hidden // chunks), hidden // chunks)
        add(down_in.at[0, part, :], down_ref.at[part, :])
    add(block_in, block_ref)
    for copy in copies:
        copy.start()
    for copy in copies:
        copy.wait()


def join_kernel(*refs):
    blocks, out_ref, rows_ref = forward(refs[:-2]), refs[-2], refs[-1]
    count = len(blocks)
    tok = blocks[0].shape[1]
    for kind in range(2):
        for j, ref in enumerate(blocks):
            first = (kind * count + j) * tok
            rows_ref[first : first + tok, :] = ref[kind].astype(F32)
    out_ref[...] = rows_ref[...].astype(BF16)


def stack_kernel(*refs):
    out_ref = refs[-1]
    rows = refs[0].shape[0]
    for j, ref in enumerate(refs[:-1]):
        out_ref[j * rows : (j + 1) * rows, :] = ref[...]


def token_rows(refs, start, rows, group, kind, columns):
    parts = []
    for ref in refs:
        for j in range(rows // (2 * group)):
            first = start + (2 * j + kind) * group
            if not isinstance(first, int):
                first = pl.multiple_of(first, group)
            parts.append(ref[pl.ds(first, group), columns])
    return parts[0] if len(parts) == 1 else jnp.concatenate(parts, axis=0)


def put_scores(out_ref, scores_ref, width):
    rows = out_ref.shape[0]
    for c in range((out_ref.shape[1] - width) // LANES):
        out_ref[:, width + c * LANES : width + (c + 1) * LANES] = scores_ref[c * rows : (c + 1) * rows, :].astype(BF16)


def get_scores(in_ref, scores_ref, base, size, width):
    rows = in_ref.shape[0]
    for c in range(-(-size // rows)):
        here = min(rows, size - c * rows)
        tall = min(rows, -(-here // 16) * 16)
        block = in_ref[0:tall, width + c * LANES : width + (c + 1) * LANES].astype(F32)
        scores_ref[base + c * rows : base + c * rows + here, :] = block[:here]


def units_kernel(basis, group, tok, core_mask, blocks, *refs):
    own_refs, other_refs = forward(refs[:blocks]), forward(refs[blocks : 2 * blocks])
    pair_ref, down_ref, kept_ref, message_ref, pieces_ref, score_ref, padded_ref = refs[2 * blocks :]
    hidden, width = down_ref.shape
    rows, buf_width = own_refs[0].shape
    tokens = score_ref.shape[1]
    own = own_index()

    def terms(sets, start, step):
        act = token_rows(sets, start, step, group, 0, slice(None))
        count = act.shape[0]
        extras = act[:, width:].astype(F32)
        lane = lax.broadcasted_iota(jnp.int32, (count, buf_width - width), 1)
        column = jnp.sum(jnp.where(lane == own // 2, extras, 0.0), axis=1, keepdims=True)
        act = act[:, :width]
        cot = token_rows(sets, start, step, group, 1, slice(0, width))
        score = jnp.zeros((count, 1), F32)
        grads = []
        for first, last in hidden_parts(hidden):
            size = last - first
            pair = jnp.dot(act, pair_ref[:, 2 * first : 2 * last], preferred_element_type=F32)
            gate_pre = pair[:, :size]
            up_pre = pair[:, size:]
            back = lax.dot_general(cot, down_ref[first:last, :], NT, preferred_element_type=F32)
            sig = jax.nn.sigmoid(gate_pre)
            act_gate = gate_pre * sig
            score = score + jnp.sum(act_gate * up_pre * back, axis=1, keepdims=True)
            weighted = column * back
            grad_gate = weighted * up_pre * sig * (1.0 + gate_pre * (1.0 - sig))
            grad_up = weighted * act_gate
            grads += [grad_gate.astype(BF16), grad_up.astype(BF16)]
        grads = jnp.concatenate(grads, axis=1)
        return lax.dot_general(grads, pair_ref[...], NT, preferred_element_type=F32), score

    def in_order(score, place, swap_mask):
        token = lax.broadcasted_iota(jnp.int32, (score.shape[0], tokens), 1)
        side = own ^ swap_mask
        whole = (place_mask(place // tok, basis, side & core_mask != 0) ^ side) * tok + place % tok
        return jnp.sum(jnp.where(whole == token, score, 0.0), axis=0, keepdims=True)

    half = blocks * rows // 2
    if 2 * half <= 128:
        total, score = terms(own_refs + other_refs, 0, rows)
        kept_ref[...] = total[:half]
        message_ref[:, 0:width] = total[half:].astype(BF16)
        row = lax.broadcasted_iota(jnp.int32, (2 * half, tokens), 0)
        score_ref[...] = in_order(score, row % half, jnp.where(row < half, 0, core_mask))
    else:
        step = min(rows, 128)
        score_ref[...] = jnp.zeros(score_ref.shape, F32)
        for out_ref, sets, swap_mask in ((kept_ref, own_refs, 0), (message_ref, other_refs, core_mask)):
            for j, ref in enumerate(sets):

                def one(index):
                    total, score = terms((ref,), index * step, step)
                    first = pl.multiple_of(j * (rows // 2) + index * (step // 2), step // 2)
                    out_ref[pl.ds(first, step // 2), 0:width] = total.astype(out_ref.dtype)
                    place = lax.broadcasted_iota(jnp.int32, (step // 2, tokens), 0) + first
                    score_ref[...] += in_order(score, place, swap_mask)

                pl.loop(0, rows // step)(one)

    lane_blocks = tokens // LANES
    padded_ref[...] = jnp.zeros(padded_ref.shape, F32)
    value = score_ref[...]
    for piece in range(SCORE_PIECES):
        rounded = value.astype(BF16).astype(F32)
        for b in range(lane_blocks):
            at = piece * lane_blocks + b
            padded_ref[at : at + 1, :] = rounded[:, b * LANES : (b + 1) * LANES]
        value = value - rounded
    pieces_ref[...] = padded_ref[0 : pieces_ref.shape[0], :]
    put_scores(message_ref, padded_ref, width)


def add_kernel(arrivals, positions, *refs):
    kept_ref, pieces_ref = refs[0], refs[1]
    arrived = refs[2 : 2 + arrivals]
    outs = refs[2 + arrivals :]
    next_kept_ref, next_pieces_ref = outs[0], outs[1]
    sends = outs[2 : 2 + len(positions)]
    total_ref, scores_ref = outs[2 + len(positions) :]
    width = kept_ref.shape[1]
    size = pieces_ref.shape[0]
    total = kept_ref[...]
    for ref in arrived:
        total = total + ref[:, 0:width].astype(F32)
    total_ref[...] = total
    if scores_ref.shape[0] > next_pieces_ref.shape[0]:
        scores_ref[...] = jnp.zeros(scores_ref.shape, F32)
    scores_ref[0:size, :] = pieces_ref[...]
    for j, ref in enumerate(arrived):
        get_scores(ref, scores_ref, (j + 1) * size, size, width)
    rows = next_kept_ref.shape[0]
    next_kept_ref[...] = total_ref[0:rows, :]
    next_pieces_ref[...] = scores_ref[0 : next_pieces_ref.shape[0], :]
    for j, ref in zip(positions, sends):
        ref[:, 0:width] = total_ref[j * rows : (j + 1) * rows, :].astype(BF16)
        put_scores(ref, scores_ref, width)


def table_kernel(basis, group, tok, core_mask, rows_out, blocks, after_ref, *refs):
    probs_ref, column_ref, mine_ref = refs[2 * blocks :]
    rows, buf_width = refs[0].shape
    half = blocks * rows // 2
    experts, tokens = probs_ref.shape
    lanes = -(-PIECES * experts // LANES) * LANES
    width = buf_width - lanes
    own = own_index()
    lane = lax.broadcasted_iota(jnp.int32, (experts, lanes), 1)
    ids = lax.broadcasted_iota(jnp.int32, (experts, lanes), 0)
    tally = jnp.zeros((experts, lanes), F32)
    for k in range(1, PIECES):
        tally = tally + jnp.where(lane == ids + k * experts, 1.0, 0.0)
    column = pl.multiple_of(own * rows_out // LANES * LANES, LANES)
    extras = jnp.zeros((tokens, lanes), F32)
    columns = jnp.zeros((tokens, LANES), F32)
    for index in range(2):
        sets = forward(refs[index * blocks : (index + 1) * blocks])
        row = lax.broadcasted_iota(jnp.int32, (half, tokens), 0)
        token = lax.broadcasted_iota(jnp.int32, (half, tokens), 1)
        side = own ^ (core_mask if index else 0)
        whole = (place_mask(row // tok, basis, side & core_mask != 0) ^ side) * tok + row % tok
        here = jnp.where(whole == token, 1.0, 0.0).astype(BF16)
        part = token_rows(sets, 0, rows, group, 0, slice(width, buf_width))
        extras = extras + lax.dot_general(here, part, TN, preferred_element_type=F32)
        part = token_rows(sets, 0, rows, group, 0, pl.ds(column, LANES))
        columns = columns + lax.dot_general(here, part, TN, preferred_element_type=F32)
    probs_ref[...] = lax.dot_general(tally.astype(BF16), extras.astype(BF16), NT, preferred_element_type=F32)
    column_ref[...] = columns.astype(BF16)
    row = lax.broadcasted_iota(jnp.int32, mine_ref.shape, 0)
    token = lax.broadcasted_iota(jnp.int32, mine_ref.shape, 1)
    mine_ref[...] = jnp.where((row < tok) & (token == own * tok + row), 1.0, 0.0).astype(BF16)


def final_kernel(arrivals, back_basis, core_mask, *refs):
    probs_ref, column_ref, mine_ref, router_ref, kept_ref, pieces_ref = refs[:6]
    arrived = refs[6 : 6 + arrivals]
    x_out, grad_out, x_ref, grad_ref, scores_ref, sems = refs[6 + arrivals :]
    experts, width = router_ref.shape
    size = pieces_ref.shape[0]
    tok = kept_ref.shape[0]
    own = own_index()
    scores_ref[0:size, :] = pieces_ref[...]
    for j, ref in enumerate(arrived):
        get_scores(ref, scores_ref, (j + 1) * size, size, width)
    blocks = probs_ref.shape[1] // LANES
    wide = scores_ref.shape[0] // blocks
    sender = lax.broadcasted_iota(jnp.int32, (experts, wide), 1) // SCORE_PIECES
    ids = lax.broadcasted_iota(jnp.int32, (experts, wide), 0)
    pick = jnp.where(((place_mask(sender, back_basis, own & core_mask != 0) ^ own) >> 1) == ids, 1.0, 0.0).astype(BF16)
    parts = []
    for b in range(blocks):
        block = scores_ref[...] if blocks == 1 else scores_ref[pl.ds(b, wide, stride=blocks), :]
        parts.append(jnp.dot(pick, block.astype(BF16), preferred_element_type=F32))
    scores = parts[0] if blocks == 1 else jnp.concatenate(parts, axis=1)
    probs = probs_ref[...]
    mean = jnp.sum(probs * scores, axis=0, keepdims=True)
    logit_grad = (probs * (scores - mean)).astype(BF16)
    mine = lax.dot_general(mine_ref[...], logit_grad, NT, preferred_element_type=F32)
    part = jnp.dot(mine.astype(BF16), router_ref[...], preferred_element_type=F32)
    total = kept_ref[...]
    for ref in arrived:
        total = total + ref[:, 0:width].astype(F32)
    x_ref[...] = (total + part[:tok]).astype(BF16)
    x_copy = pltpu.make_async_copy(x_ref, x_out, sems.at[0])
    x_copy.start()
    grad = jnp.dot(logit_grad, column_ref[...], preferred_element_type=F32)
    rows_out = grad_ref.shape[1]
    first = own * rows_out % LANES
    grad_ref[...] = pltpu.roll(grad, (LANES - first) % LANES, 1)[:, :rows_out]
    grad_copy = pltpu.make_async_copy(grad_ref, grad_out, sems.at[1])
    grad_copy.start()
    x_copy.wait()
    grad_copy.wait()


def on_device(tokens, grad_out, router_logits, selected, router_w, w_gate, w_up, w_down):
    tok, width = tokens.shape
    experts = router_logits.shape[1]
    hidden = w_gate.shape[2]
    exp_size = lax.axis_size("exp")
    hid_size = lax.axis_size("hid")
    count = exp_size * hid_size
    half = count // 2
    groups, core = stage_masks(exp_size, hid_size)
    core_mask = 1 << core
    basis = [m for group in groups for m in group]
    back_groups = [last_first(group) for group in groups[:0:-1]] + [groups[0]]
    core_pair = (core_mask, core_mask)
    back_basis = [core_pair] + [m for group in back_groups for m in group]
    token_count = count * tok
    lanes = -(-PIECES * experts // LANES) * LANES

    block = pl.pallas_call(
        prep_kernel,
        out_shape=jax.ShapeDtypeStruct((2, tok, width + lanes), BF16),
        in_specs=[HBM_SPEC] * 4,
        out_specs=VMEM_SPEC,
        scratch_shapes=[
            pltpu.VMEM(router_logits.shape, router_logits.dtype),
            pltpu.VMEM(selected.shape, selected.dtype),
            pltpu.SemaphoreType.DMA((4,)),
        ],
        compiler_params=PARAMS,
        name="prep",
    )(*in_hbm(tokens, grad_out, router_logits, selected))

    masks = group_masks(groups[0])
    blocks = [block] + swaps(block, masks[1:], count, core)
    group_rows = tok * len(blocks)
    block = pl.pallas_call(
        join_kernel,
        out_shape=jax.ShapeDtypeStruct((2 * group_rows, width + lanes), BF16),
        in_specs=[VMEM_SPEC] * len(blocks),
        out_specs=VMEM_SPEC,
        scratch_shapes=[pltpu.VMEM((2 * group_rows, width + lanes), F32)],
        compiler_params=PARAMS,
        name="join",
    )(*forward(blocks))
    for group in groups[1:-1]:
        blocks = [block] + swaps(block, group_masks(group)[1:], count, core)
        block = pl.pallas_call(
            stack_kernel,
            out_shape=jax.ShapeDtypeStruct((len(blocks) * block.shape[0], block.shape[1]), BF16),
            in_specs=[VMEM_SPEC] * len(blocks),
            out_specs=VMEM_SPEC,
            compiler_params=PARAMS,
            name="stack",
        )(*blocks)
    chunks = 4
    copied, pair, down = pl.pallas_call(
        functools.partial(load_kernel, chunks),
        out_shape=(
            pltpu.VMEM(block.shape, BF16),
            pltpu.VMEM((width, 2 * hidden), BF16),
            pltpu.VMEM((hidden, width), BF16),
        ),
        in_specs=[VMEM_SPEC] + [HBM_SPEC] * 3,
        out_specs=(VMEM_SPEC,) * 3,
        scratch_shapes=[pltpu.SemaphoreType.DMA(((2 * len(hidden_parts(hidden)) + 1) * chunks + 1,))],
        compiler_params=pltpu.CompilerParams(vmem_limit_bytes=4 * 2**20),
        cost_estimate=pl.CostEstimate(flops=0, bytes_accessed=6 * width * hidden * 2, transcendentals=0),
        name="load",
    )(block, *in_hbm(w_gate, w_up, w_down))
    masks = group_masks(groups[-1]) if len(groups) > 1 else [core_pair]
    blocks = [block] + swaps(block, masks[1:], count, core)
    blocks = forward(blocks)
    blocks = blocks + [swap(b, core_pair, count, core) for b in [copied] + blocks[1:]]
    block_count = len(blocks) // 2

    unit_rows = SCORE_PIECES * token_count // LANES
    extra = -(-unit_rows // (half * tok)) * LANES
    kept, message, pieces = pl.pallas_call(
        functools.partial(units_kernel, basis, group_rows, tok, core_mask, block_count),
        out_shape=(
            jax.ShapeDtypeStruct((half * tok, width), F32),
            jax.ShapeDtypeStruct((half * tok, width + extra), BF16),
            jax.ShapeDtypeStruct((unit_rows, LANES), F32),
        ),
        in_specs=[VMEM_SPEC] * (len(blocks) + 2),
        out_specs=(VMEM_SPEC,) * 3,
        scratch_shapes=[
            pltpu.VMEM((1, token_count), F32),
            pltpu.VMEM((max(half * tok * extra // LANES, unit_rows), LANES), F32),
        ],
        compiler_params=PARAMS,
        cost_estimate=pl.CostEstimate(
            flops=10 * token_count * width * hidden,
            bytes_accessed=3 * width * hidden * 2 + 2 * token_count * width * 2,
            transcendentals=token_count * hidden,
        ),
        name="units",
    )(*blocks, pair, down)

    arrived = [swap(message, core_pair, count, core)]
    tables = None
    rows_out = width // count
    for group, back_group in zip(groups[::-1], back_groups):
        masks = group_masks(group)
        back_masks = group_masks(back_group)
        radix = len(masks)
        rows = kept.shape[0]
        next_rows = rows // radix
        size = pieces.shape[0] * (1 + len(arrived))
        extra = -(-size // next_rows) * LANES
        sends = [jax.ShapeDtypeStruct((next_rows, width + extra), BF16)] * (radix - 1)
        outs = pl.pallas_call(
            functools.partial(add_kernel, len(arrived), [masks.index(m) for m in back_masks[1:]]),
            out_shape=[
                jax.ShapeDtypeStruct((next_rows, width), F32),
                jax.ShapeDtypeStruct((size, LANES), F32),
            ]
            + sends,
            in_specs=[VMEM_SPEC] * (2 + len(arrived)),
            out_specs=[VMEM_SPEC] * (1 + radix),
            scratch_shapes=[
                pltpu.VMEM((rows, width), F32),
                pltpu.VMEM((max(next_rows * extra // LANES, size), LANES), F32),
            ],
            compiler_params=PARAMS,
            name="add",
        )(kept, pieces, *arrived)
        kept, pieces = outs[0], outs[1]
        if tables is None:
            tables = pl.pallas_call(
                functools.partial(table_kernel, basis, group_rows, tok, core_mask, rows_out, block_count),
                out_shape=(
                    jax.ShapeDtypeStruct((experts, token_count), F32),
                    jax.ShapeDtypeStruct((token_count, LANES), BF16),
                    jax.ShapeDtypeStruct((16, token_count), BF16),
                ),
                in_specs=[pl.BlockSpec(memory_space=pl.ANY)] + [VMEM_SPEC] * len(blocks),
                out_specs=(VMEM_SPEC,) * 3,
                compiler_params=PARAMS,
                cost_estimate=pl.CostEstimate(flops=10**9, bytes_accessed=10**6, transcendentals=0),
                name="tables",
            )(pieces, *blocks)
        arrived = [swap(piece, m, count, core) for piece, m in zip(outs[2:], back_masks[1:])]

    x_grad, grad = pl.pallas_call(
        functools.partial(final_kernel, len(arrived), back_basis, core_mask),
        out_shape=(
            jax.ShapeDtypeStruct((tok, width), BF16),
            jax.ShapeDtypeStruct((experts, rows_out), F32),
        ),
        in_specs=[VMEM_SPEC] * (6 + len(arrived)),
        out_specs=(HBM_SPEC, HBM_SPEC),
        scratch_shapes=[
            pltpu.VMEM((tok, width), BF16),
            pltpu.VMEM((experts, rows_out), F32),
            pltpu.VMEM((pieces.shape[0] * (1 + len(arrived)), LANES), F32),
            pltpu.SemaphoreType.DMA((2,)),
        ],
        compiler_params=PARAMS,
        name="final",
    )(*tables, router_w.T, kept, pieces, *arrived)
    return (x_grad, grad.T)


def solution(mesh):
    rows = P(AXES, None)
    units = P(AXES, None, None)
    return jax.shard_map(
        on_device,
        mesh=mesh,
        in_specs=(rows, rows, rows, rows, P(), units, units, units),
        out_specs=(rows, rows),
        check_vma=False,
    )
```

```python
import functools

import jax
import jax.numpy as jnp
from jax import lax
from jax.experimental import pallas as pl
from jax.experimental.pallas import tpu as pltpu
from jax.sharding import PartitionSpec as P

AXES = ("exp", "hid")
LANES = 128
PIECES = 4
SCORE_PIECES = 2
VMEM_SPEC = pl.BlockSpec(memory_space=pltpu.VMEM)
HBM_SPEC = pl.BlockSpec(memory_space=pltpu.HBM)
F32 = jnp.float32
BF16 = jnp.bfloat16
NT = (((1,), (1,)), ((), ()))
TN = (((0,), (0,)), ((), ()))
PARAMS = pltpu.CompilerParams(vmem_limit_bytes=24 * 2**20)


def stage_masks(exp_size, hid_size):
    hid_bits = hid_size.bit_length() - 1
    all_bits = (exp_size * hid_size).bit_length() - 1
    core = hid_bits
    first = list(range(max(core + 1, all_bits - 2), all_bits))
    middle = [b for b in range(all_bits) if b != core and b not in first]
    groups = [first] + [middle[i : i + 2] for i in range(0, len(middle), 2)]
    bases = []
    for index, group in enumerate(groups):
        basis = [(sum(1 << b for b in group[i:]),) * 2 for i in range(len(group))]
        if index > 0 and len(group) == 2:
            basis[1] = (1 << group[1], 1 << group[0])
        bases.append(basis)
    return bases, core


def cross(a, b):
    return (a[0] ^ b[0], a[1] ^ b[1])


def group_masks(basis):
    masks = [(0, 0)]
    for mask in basis:
        masks = masks + [cross(m, mask) for m in masks]
    return masks


def near_first(basis):
    return [(m, m) for m in basis[1][::-1]] if len(basis) == 2 else basis


def swap(block, mask, count, core):
    return lax.ppermute(block, AXES, [(i, i ^ mask[i >> core & 1]) for i in range(count)])


def swaps(block, masks, count, core):
    return [swap(block, m, count, core) for m in masks]


def forward(blocks):
    return blocks[:1] + blocks[:0:-1]


def place_mask(place, basis, upper):
    total = jnp.zeros_like(place)
    for digit, (low, high) in enumerate(basis):
        mask = low if low == high else jnp.where(upper, high, low)
        total = total ^ (((place >> digit) & 1) * mask)
    return total


def own_index():
    return lax.axis_index("exp") * lax.axis_size("hid") + lax.axis_index("hid")


def in_hbm(*arrays):
    return tuple(pltpu.with_memory_space_constraint(a, pltpu.HBM) for a in arrays)


def softmax_f32(values):
    raised = jnp.exp(values - jnp.max(values, axis=-1, keepdims=True))
    return raised / jnp.sum(raised, axis=-1, keepdims=True)


def prep_kernel(tokens_in, grad_in, logits_in, chosen_in, out_ref, logits_ref, chosen_ref, sems):
    tok, width = tokens_in.shape
    pairs = [
        (logits_in, logits_ref),
        (chosen_in, chosen_ref),
        (tokens_in, out_ref.at[0, :, 0:width]),
        (grad_in, out_ref.at[1, :, 0:width]),
    ]
    copies = [pltpu.make_async_copy(src, dst, sems.at[i]) for i, (src, dst) in enumerate(pairs)]
    for copy in copies:
        copy.start()
    copies[0].wait()
    copies[1].wait()
    logits = logits_ref[...]
    chosen = chosen_ref[...]
    experts = logits.shape[1]
    ids = lax.broadcasted_iota(jnp.int32, logits.shape, 1)
    hit = ids == chosen[:, 0:1]
    for k in range(1, chosen.shape[1]):
        hit = hit | (ids == chosen[:, k : k + 1])
    top = jnp.max(jnp.where(hit, logits, -jnp.inf), axis=1, keepdims=True)
    raised = jnp.where(hit, jnp.exp(jnp.minimum(logits - top, 0.0)), 0.0)
    parts = [raised / jnp.sum(raised, axis=1, keepdims=True)]
    rest = softmax_f32(logits)
    for _ in range(PIECES - 1):
        parts.append(rest)
        rest = rest - rest.astype(BF16).astype(F32)
    lanes = out_ref.shape[2] - width
    spare = lanes - PIECES * experts
    extras = jnp.concatenate(parts + ([jnp.zeros((tok, spare), F32)] if spare else []), axis=1)
    out_ref[0, :, width:] = extras.astype(BF16)
    out_ref[1, :, width:] = jnp.zeros((tok, lanes), BF16)
    copies[2].wait()
    copies[3].wait()


def hidden_parts(hidden):
    main = hidden // 256 * 256
    return [(0, main), (main, hidden)] if 0 < main < hidden else [(0, hidden)]


def load_kernel(chunks, block_in, gate_in, up_in, down_in, block_ref, pair_ref, down_ref, sems):
    copies = []

    def add(src, dst):
        copies.append(pltpu.make_async_copy(src, dst, sems.at[len(copies)]))

    hidden, width = down_ref.shape
    for c in range(chunks):
        part = pl.ds(c * (width // chunks), width // chunks)
        for first, last in hidden_parts(hidden):
            for k, ref in enumerate((gate_in, up_in)):
                to = 2 * first + k * (last - first)
                add(ref.at[0, part, first:last], pair_ref.at[part, to : to + last - first])
        part = pl.ds(c * (hidden // chunks), hidden // chunks)
        add(down_in.at[0, part, :], down_ref.at[part, :])
    add(block_in, block_ref)
    for copy in copies:
        copy.start()
    for copy in copies:
        copy.wait()


def join_kernel(*refs):
    blocks, out_ref, rows_ref = forward(refs[:-2]), refs[-2], refs[-1]
    count = len(blocks)
    tok = blocks[0].shape[1]
    for kind in range(2):
        for j, ref in enumerate(blocks):
            first = (kind * count + j) * tok
            rows_ref[first : first + tok, :] = ref[kind].astype(F32)
    out_ref[...] = rows_ref[...].astype(BF16)


def stack_kernel(*refs):
    out_ref = refs[-1]
    rows = refs[0].shape[0]
    for j, ref in enumerate(refs[:-1]):
        out_ref[j * rows : (j + 1) * rows, :] = ref[...]


def token_rows(refs, start, rows, group, kind, columns):
    parts = []
    for ref in refs:
        for j in range(rows // (2 * group)):
            first = start + (2 * j + kind) * group
            if not isinstance(first, int):
                first = pl.multiple_of(first, group)
            parts.append(ref[pl.ds(first, group), columns])
    return parts[0] if len(parts) == 1 else jnp.concatenate(parts, axis=0)


def put_scores(out_ref, scores_ref, width):
    rows = out_ref.shape[0]
    for c in range((out_ref.shape[1] - width) // LANES):
        out_ref[:, width + c * LANES : width + (c + 1) * LANES] = scores_ref[c * rows : (c + 1) * rows, :].astype(BF16)


def get_scores(in_ref, scores_ref, base, size, width):
    rows = in_ref.shape[0]
    for c in range(-(-size // rows)):
        here = min(rows, size - c * rows)
        tall = min(rows, -(-here // 16) * 16)
        block = in_ref[0:tall, width + c * LANES : width + (c + 1) * LANES].astype(F32)
        scores_ref[base + c * rows : base + c * rows + here, :] = block[:here]


def units_kernel(basis, group, tok, core_mask, blocks, *refs):
    own_refs, other_refs = forward(refs[:blocks]), forward(refs[blocks : 2 * blocks])
    pair_ref, down_ref, kept_ref, message_ref, pieces_ref, score_ref, padded_ref = refs[2 * blocks :]
    hidden, width = down_ref.shape
    rows, buf_width = own_refs[0].shape
    tokens = score_ref.shape[1]
    own = own_index()

    def terms(sets, start, step):
        act = token_rows(sets, start, step, group, 0, slice(None))
        count = act.shape[0]
        extras = act[:, width:].astype(F32)
        lane = lax.broadcasted_iota(jnp.int32, (count, buf_width - width), 1)
        column = jnp.sum(jnp.where(lane == own // 2, extras, 0.0), axis=1, keepdims=True)
        act = act[:, :width]
        cot = token_rows(sets, start, step, group, 1, slice(0, width))
        score = jnp.zeros((count, 1), F32)
        grads = []
        for first, last in hidden_parts(hidden):
            size = last - first
            pair = jnp.dot(act, pair_ref[:, 2 * first : 2 * last], preferred_element_type=F32)
            gate_pre = pair[:, :size]
            up_pre = pair[:, size:]
            back = lax.dot_general(cot, down_ref[first:last, :], NT, preferred_element_type=F32)
            sig = jax.nn.sigmoid(gate_pre)
            act_gate = gate_pre * sig
            score = score + jnp.sum(act_gate * up_pre * back, axis=1, keepdims=True)
            weighted = column * back
            grad_gate = weighted * up_pre * sig * (1.0 + gate_pre * (1.0 - sig))
            grad_up = weighted * act_gate
            grads += [grad_gate.astype(BF16), grad_up.astype(BF16)]
        grads = jnp.concatenate(grads, axis=1)
        return lax.dot_general(grads, pair_ref[...], NT, preferred_element_type=F32), score

    def in_order(score, place, swap_mask):
        token = lax.broadcasted_iota(jnp.int32, (score.shape[0], tokens), 1)
        side = own ^ swap_mask
        whole = (place_mask(place // tok, basis, side & core_mask != 0) ^ side) * tok + place % tok
        return jnp.sum(jnp.where(whole == token, score, 0.0), axis=0, keepdims=True)

    half = blocks * rows // 2
    if 2 * half <= 128:
        total, score = terms(own_refs + other_refs, 0, rows)
        kept_ref[...] = total[:half]
        message_ref[:, 0:width] = total[half:].astype(BF16)
        row = lax.broadcasted_iota(jnp.int32, (2 * half, tokens), 0)
        score_ref[...] = in_order(score, row % half, jnp.where(row < half, 0, core_mask))
    else:
        step = min(rows, 128)
        score_ref[...] = jnp.zeros(score_ref.shape, F32)
        for out_ref, sets, swap_mask in ((kept_ref, own_refs, 0), (message_ref, other_refs, core_mask)):
            for j, ref in enumerate(sets):

                def one(index):
                    total, score = terms((ref,), index * step, step)
                    first = pl.multiple_of(j * (rows // 2) + index * (step // 2), step // 2)
                    out_ref[pl.ds(first, step // 2), 0:width] = total.astype(out_ref.dtype)
                    place = lax.broadcasted_iota(jnp.int32, (step // 2, tokens), 0) + first
                    score_ref[...] += in_order(score, place, swap_mask)

                pl.loop(0, rows // step)(one)

    lane_blocks = tokens // LANES
    padded_ref[...] = jnp.zeros(padded_ref.shape, F32)
    value = score_ref[...]
    for piece in range(SCORE_PIECES):
        rounded = value.astype(BF16).astype(F32)
        for b in range(lane_blocks):
            at = piece * lane_blocks + b
            padded_ref[at : at + 1, :] = rounded[:, b * LANES : (b + 1) * LANES]
        value = value - rounded
    pieces_ref[...] = padded_ref[0 : pieces_ref.shape[0], :]
    put_scores(message_ref, padded_ref, width)


def add_kernel(arrivals, positions, core_mask, *refs):
    kept_ref, pieces_ref = refs[0], refs[1]
    arrived = refs[2 : 2 + arrivals]
    outs = refs[2 + arrivals :]
    next_kept_ref, next_pieces_ref = outs[0], outs[1]
    sends = outs[2 : 2 + len(positions)]
    total_ref, scores_ref = outs[2 + len(positions) :]
    width = kept_ref.shape[1]
    size = pieces_ref.shape[0]
    total = kept_ref[...]
    for ref in arrived:
        total = total + ref[:, 0:width].astype(F32)
    total_ref[...] = total
    if scores_ref.shape[0] > next_pieces_ref.shape[0]:
        scores_ref[...] = jnp.zeros(scores_ref.shape, F32)
    scores_ref[0:size, :] = pieces_ref[...]
    for j, ref in enumerate(arrived):
        get_scores(ref, scores_ref, (j + 1) * size, size, width)
    rows = next_kept_ref.shape[0]
    next_kept_ref[...] = total_ref[0:rows, :]
    next_pieces_ref[...] = scores_ref[0 : next_pieces_ref.shape[0], :]
    upper = own_index() & core_mask != 0
    for (low, high), ref in zip(positions, sends):
        first = low * rows
        if low != high:
            first = pl.multiple_of(jnp.where(upper, high, low) * rows, rows)
        ref[:, 0:width] = total_ref[pl.ds(first, rows), :].astype(BF16)
        put_scores(ref, scores_ref, width)


def table_kernel(basis, group, tok, core_mask, rows_out, blocks, after_ref, *refs):
    probs_ref, column_ref, mine_ref = refs[2 * blocks :]
    rows, buf_width = refs[0].shape
    half = blocks * rows // 2
    experts, tokens = probs_ref.shape
    lanes = -(-PIECES * experts // LANES) * LANES
    width = buf_width - lanes
    own = own_index()
    lane = lax.broadcasted_iota(jnp.int32, (experts, lanes), 1)
    ids = lax.broadcasted_iota(jnp.int32, (experts, lanes), 0)
    tally = jnp.zeros((experts, lanes), F32)
    for k in range(1, PIECES):
        tally = tally + jnp.where(lane == ids + k * experts, 1.0, 0.0)
    column = pl.multiple_of(own * rows_out // LANES * LANES, LANES)
    extras = jnp.zeros((tokens, lanes), F32)
    columns = jnp.zeros((tokens, LANES), F32)
    for index in range(2):
        sets = forward(refs[index * blocks : (index + 1) * blocks])
        row = lax.broadcasted_iota(jnp.int32, (half, tokens), 0)
        token = lax.broadcasted_iota(jnp.int32, (half, tokens), 1)
        side = own ^ (core_mask if index else 0)
        whole = (place_mask(row // tok, basis, side & core_mask != 0) ^ side) * tok + row % tok
        here = jnp.where(whole == token, 1.0, 0.0).astype(BF16)
        part = token_rows(sets, 0, rows, group, 0, slice(width, buf_width))
        extras = extras + lax.dot_general(here, part, TN, preferred_element_type=F32)
        part = token_rows(sets, 0, rows, group, 0, pl.ds(column, LANES))
        columns = columns + lax.dot_general(here, part, TN, preferred_element_type=F32)
    probs_ref[...] = lax.dot_general(tally.astype(BF16), extras.astype(BF16), NT, preferred_element_type=F32)
    column_ref[...] = columns.astype(BF16)
    row = lax.broadcasted_iota(jnp.int32, mine_ref.shape, 0)
    token = lax.broadcasted_iota(jnp.int32, mine_ref.shape, 1)
    mine_ref[...] = jnp.where((row < tok) & (token == own * tok + row), 1.0, 0.0).astype(BF16)


def final_kernel(arrivals, back_basis, core_mask, *refs):
    probs_ref, column_ref, mine_ref, router_ref, kept_ref, pieces_ref = refs[:6]
    arrived = refs[6 : 6 + arrivals]
    x_out, grad_out, x_ref, grad_ref, scores_ref, sems = refs[6 + arrivals :]
    experts, width = router_ref.shape
    size = pieces_ref.shape[0]
    tok = kept_ref.shape[0]
    own = own_index()
    scores_ref[0:size, :] = pieces_ref[...]
    for j, ref in enumerate(arrived):
        get_scores(ref, scores_ref, (j + 1) * size, size, width)
    blocks = probs_ref.shape[1] // LANES
    wide = scores_ref.shape[0] // blocks
    sender = lax.broadcasted_iota(jnp.int32, (experts, wide), 1) // SCORE_PIECES
    ids = lax.broadcasted_iota(jnp.int32, (experts, wide), 0)
    pick = jnp.where(((place_mask(sender, back_basis, own & core_mask != 0) ^ own) >> 1) == ids, 1.0, 0.0).astype(BF16)
    parts = []
    for b in range(blocks):
        block = scores_ref[...] if blocks == 1 else scores_ref[pl.ds(b, wide, stride=blocks), :]
        parts.append(jnp.dot(pick, block.astype(BF16), preferred_element_type=F32))
    scores = parts[0] if blocks == 1 else jnp.concatenate(parts, axis=1)
    probs = probs_ref[...]
    mean = jnp.sum(probs * scores, axis=0, keepdims=True)
    logit_grad = (probs * (scores - mean)).astype(BF16)
    mine = lax.dot_general(mine_ref[...], logit_grad, NT, preferred_element_type=F32)
    part = jnp.dot(mine.astype(BF16), router_ref[...], preferred_element_type=F32)
    total = kept_ref[...]
    for ref in arrived:
        total = total + ref[:, 0:width].astype(F32)
    x_ref[...] = (total + part[:tok]).astype(BF16)
    x_copy = pltpu.make_async_copy(x_ref, x_out, sems.at[0])
    x_copy.start()
    grad = jnp.dot(logit_grad, column_ref[...], preferred_element_type=F32)
    rows_out = grad_ref.shape[1]
    first = own * rows_out % LANES
    grad_ref[...] = pltpu.roll(grad, (LANES - first) % LANES, 1)[:, :rows_out]
    grad_copy = pltpu.make_async_copy(grad_ref, grad_out, sems.at[1])
    grad_copy.start()
    x_copy.wait()
    grad_copy.wait()


def on_device(tokens, grad_out, router_logits, selected, router_w, w_gate, w_up, w_down):
    tok, width = tokens.shape
    experts = router_logits.shape[1]
    hidden = w_gate.shape[2]
    exp_size = lax.axis_size("exp")
    hid_size = lax.axis_size("hid")
    count = exp_size * hid_size
    half = count // 2
    groups, core = stage_masks(exp_size, hid_size)
    core_mask = 1 << core
    basis = [m for group in groups for m in group]
    back_groups = [near_first(group) for group in groups[:0:-1]] + [groups[0]]
    core_pair = (core_mask, core_mask)
    back_basis = [core_pair] + [m for group in back_groups for m in group]
    token_count = count * tok
    lanes = -(-PIECES * experts // LANES) * LANES

    block = pl.pallas_call(
        prep_kernel,
        out_shape=jax.ShapeDtypeStruct((2, tok, width + lanes), BF16),
        in_specs=[HBM_SPEC] * 4,
        out_specs=VMEM_SPEC,
        scratch_shapes=[
            pltpu.VMEM(router_logits.shape, router_logits.dtype),
            pltpu.VMEM(selected.shape, selected.dtype),
            pltpu.SemaphoreType.DMA((4,)),
        ],
        compiler_params=PARAMS,
        name="prep",
    )(*in_hbm(tokens, grad_out, router_logits, selected))

    masks = group_masks(groups[0])
    blocks = [block] + swaps(block, masks[1:], count, core)
    group_rows = tok * len(blocks)
    block = pl.pallas_call(
        join_kernel,
        out_shape=jax.ShapeDtypeStruct((2 * group_rows, width + lanes), BF16),
        in_specs=[VMEM_SPEC] * len(blocks),
        out_specs=VMEM_SPEC,
        scratch_shapes=[pltpu.VMEM((2 * group_rows, width + lanes), F32)],
        compiler_params=PARAMS,
        name="join",
    )(*forward(blocks))
    for group in groups[1:-1]:
        blocks = [block] + swaps(block, group_masks(group)[1:], count, core)
        block = pl.pallas_call(
            stack_kernel,
            out_shape=jax.ShapeDtypeStruct((len(blocks) * block.shape[0], block.shape[1]), BF16),
            in_specs=[VMEM_SPEC] * len(blocks),
            out_specs=VMEM_SPEC,
            compiler_params=PARAMS,
            name="stack",
        )(*blocks)
    chunks = 4
    copied, pair, down = pl.pallas_call(
        functools.partial(load_kernel, chunks),
        out_shape=(
            pltpu.VMEM(block.shape, BF16),
            pltpu.VMEM((width, 2 * hidden), BF16),
            pltpu.VMEM((hidden, width), BF16),
        ),
        in_specs=[VMEM_SPEC] + [HBM_SPEC] * 3,
        out_specs=(VMEM_SPEC,) * 3,
        scratch_shapes=[pltpu.SemaphoreType.DMA(((2 * len(hidden_parts(hidden)) + 1) * chunks + 1,))],
        compiler_params=pltpu.CompilerParams(vmem_limit_bytes=4 * 2**20),
        cost_estimate=pl.CostEstimate(flops=0, bytes_accessed=6 * width * hidden * 2, transcendentals=0),
        name="load",
    )(block, *in_hbm(w_gate, w_up, w_down))
    masks = group_masks(groups[-1]) if len(groups) > 1 else [core_pair]
    blocks = [block] + swaps(block, masks[1:], count, core)
    blocks = forward(blocks)
    blocks = blocks + [swap(b, core_pair, count, core) for b in [copied] + blocks[1:]]
    block_count = len(blocks) // 2

    unit_rows = SCORE_PIECES * token_count // LANES
    extra = -(-unit_rows // (half * tok)) * LANES
    kept, message, pieces = pl.pallas_call(
        functools.partial(units_kernel, basis, group_rows, tok, core_mask, block_count),
        out_shape=(
            jax.ShapeDtypeStruct((half * tok, width), F32),
            jax.ShapeDtypeStruct((half * tok, width + extra), BF16),
            jax.ShapeDtypeStruct((unit_rows, LANES), F32),
        ),
        in_specs=[VMEM_SPEC] * (len(blocks) + 2),
        out_specs=(VMEM_SPEC,) * 3,
        scratch_shapes=[
            pltpu.VMEM((1, token_count), F32),
            pltpu.VMEM((max(half * tok * extra // LANES, unit_rows), LANES), F32),
        ],
        compiler_params=PARAMS,
        cost_estimate=pl.CostEstimate(
            flops=10 * token_count * width * hidden,
            bytes_accessed=3 * width * hidden * 2 + 2 * token_count * width * 2,
            transcendentals=token_count * hidden,
        ),
        name="units",
    )(*blocks, pair, down)

    arrived = [swap(message, core_pair, count, core)]
    tables = None
    rows_out = width // count
    for group, back_group in zip(groups[::-1], back_groups):
        back_masks = group_masks(back_group)
        positions = [
            tuple([m[side] for m in group_masks(group)].index(mask[side]) for side in range(2)) for mask in back_masks[1:]
        ]
        radix = len(back_masks)
        rows = kept.shape[0]
        next_rows = rows // radix
        size = pieces.shape[0] * (1 + len(arrived))
        extra = -(-size // next_rows) * LANES
        sends = [jax.ShapeDtypeStruct((next_rows, width + extra), BF16)] * (radix - 1)
        outs = pl.pallas_call(
            functools.partial(add_kernel, len(arrived), positions, core_mask),
            out_shape=[
                jax.ShapeDtypeStruct((next_rows, width), F32),
                jax.ShapeDtypeStruct((size, LANES), F32),
            ]
            + sends,
            in_specs=[VMEM_SPEC] * (2 + len(arrived)),
            out_specs=[VMEM_SPEC] * (1 + radix),
            scratch_shapes=[
                pltpu.VMEM((rows, width), F32),
                pltpu.VMEM((max(next_rows * extra // LANES, size), LANES), F32),
            ],
            compiler_params=PARAMS,
            name="add",
        )(kept, pieces, *arrived)
        kept, pieces = outs[0], outs[1]
        if tables is None:
            tables = pl.pallas_call(
                functools.partial(table_kernel, basis, group_rows, tok, core_mask, rows_out, block_count),
                out_shape=(
                    jax.ShapeDtypeStruct((experts, token_count), F32),
                    jax.ShapeDtypeStruct((token_count, LANES), BF16),
                    jax.ShapeDtypeStruct((16, token_count), BF16),
                ),
                in_specs=[pl.BlockSpec(memory_space=pl.ANY)] + [VMEM_SPEC] * len(blocks),
                out_specs=(VMEM_SPEC,) * 3,
                compiler_params=PARAMS,
                cost_estimate=pl.CostEstimate(flops=10**9, bytes_accessed=10**6, transcendentals=0),
                name="tables",
            )(pieces, *blocks)
        arrived = [swap(piece, m, count, core) for piece, m in zip(outs[2:], back_masks[1:])]

    x_grad, grad = pl.pallas_call(
        functools.partial(final_kernel, len(arrived), back_basis, core_mask),
        out_shape=(
            jax.ShapeDtypeStruct((tok, width), BF16),
            jax.ShapeDtypeStruct((experts, rows_out), F32),
        ),
        in_specs=[VMEM_SPEC] * (6 + len(arrived)),
        out_specs=(HBM_SPEC, HBM_SPEC),
        scratch_shapes=[
            pltpu.VMEM((tok, width), BF16),
            pltpu.VMEM((experts, rows_out), F32),
            pltpu.VMEM((pieces.shape[0] * (1 + len(arrived)), LANES), F32),
            pltpu.SemaphoreType.DMA((2,)),
        ],
        compiler_params=PARAMS,
        name="final",
    )(*tables, router_w.T, kept, pieces, *arrived)
    return (x_grad, grad.T)


def solution(mesh):
    rows = P(AXES, None)
    units = P(AXES, None, None)
    return jax.shard_map(
        on_device,
        mesh=mesh,
        in_specs=(rows, rows, rows, rows, P(), units, units, units),
        out_specs=(rows, rows),
        check_vma=False,
    )
```

```python
import functools

import jax
import jax.numpy as jnp
from jax import lax
from jax.experimental import pallas as pl
from jax.experimental.pallas import tpu as pltpu
from jax.sharding import PartitionSpec as P

AXES = ("exp", "hid")
LANES = 128
PIECES = 4
SCORE_PIECES = 2
VMEM_SPEC = pl.BlockSpec(memory_space=pltpu.VMEM)
HBM_SPEC = pl.BlockSpec(memory_space=pltpu.HBM)
F32 = jnp.float32
BF16 = jnp.bfloat16
NT = (((1,), (1,)), ((), ()))
TN = (((0,), (0,)), ((), ()))
PARAMS = pltpu.CompilerParams(vmem_limit_bytes=24 * 2**20)


def stage_masks(exp_size, hid_size):
    hid_bits = hid_size.bit_length() - 1
    all_bits = (exp_size * hid_size).bit_length() - 1
    core = hid_bits
    first = list(range(max(core + 1, all_bits - 2), all_bits))
    middle = [b for b in range(all_bits) if b != core and b not in first]
    groups = [first] + [middle[i : i + 2] for i in range(0, len(middle), 2)]
    bases = [[(sum(1 << b for b in group[i:]),) * 2 for i in range(len(group))] for group in groups]
    bases[0] = bases[0][::-1]
    return bases, core


def cross(a, b):
    return (a[0] ^ b[0], a[1] ^ b[1])


def group_masks(basis):
    masks = [(0, 0)]
    for mask in basis:
        masks = masks + [cross(m, mask) for m in masks]
    return masks


def near_first(basis):
    return [cross(basis[0], basis[1]), basis[1]] if len(basis) == 2 else basis


def swap(block, mask, count, core):
    return lax.ppermute(block, AXES, [(i, i ^ mask[i >> core & 1]) for i in range(count)])


def swaps(block, masks, count, core):
    return [swap(block, m, count, core) for m in masks]


def forward(blocks):
    return blocks[:1] + blocks[:0:-1]


def place_mask(place, basis, upper):
    total = jnp.zeros_like(place)
    for digit, (low, high) in enumerate(basis):
        mask = low if low == high else jnp.where(upper, high, low)
        total = total ^ (((place >> digit) & 1) * mask)
    return total


def own_index():
    return lax.axis_index("exp") * lax.axis_size("hid") + lax.axis_index("hid")


def in_hbm(*arrays):
    return tuple(pltpu.with_memory_space_constraint(a, pltpu.HBM) for a in arrays)


def softmax_f32(values):
    raised = jnp.exp(values - jnp.max(values, axis=-1, keepdims=True))
    return raised / jnp.sum(raised, axis=-1, keepdims=True)


def prep_kernel(tokens_in, grad_in, logits_in, chosen_in, out_ref, logits_ref, chosen_ref, sems):
    tok, width = tokens_in.shape
    pairs = [
        (logits_in, logits_ref),
        (chosen_in, chosen_ref),
        (tokens_in, out_ref.at[0, :, 0:width]),
        (grad_in, out_ref.at[1, :, 0:width]),
    ]
    copies = [pltpu.make_async_copy(src, dst, sems.at[i]) for i, (src, dst) in enumerate(pairs)]
    for copy in copies:
        copy.start()
    copies[0].wait()
    copies[1].wait()
    logits = logits_ref[...]
    chosen = chosen_ref[...]
    experts = logits.shape[1]
    ids = lax.broadcasted_iota(jnp.int32, logits.shape, 1)
    hit = ids == chosen[:, 0:1]
    for k in range(1, chosen.shape[1]):
        hit = hit | (ids == chosen[:, k : k + 1])
    top = jnp.max(jnp.where(hit, logits, -jnp.inf), axis=1, keepdims=True)
    raised = jnp.where(hit, jnp.exp(jnp.minimum(logits - top, 0.0)), 0.0)
    parts = [raised / jnp.sum(raised, axis=1, keepdims=True)]
    rest = softmax_f32(logits)
    for _ in range(PIECES - 1):
        parts.append(rest)
        rest = rest - rest.astype(BF16).astype(F32)
    lanes = out_ref.shape[2] - width
    spare = lanes - PIECES * experts
    extras = jnp.concatenate(parts + ([jnp.zeros((tok, spare), F32)] if spare else []), axis=1)
    out_ref[0, :, width:] = extras.astype(BF16)
    out_ref[1, :, width:] = jnp.zeros((tok, lanes), BF16)
    copies[2].wait()
    copies[3].wait()


def hidden_parts(hidden):
    main = hidden // 256 * 256
    return [(0, main), (main, hidden)] if 0 < main < hidden else [(0, hidden)]


def load_kernel(chunks, block_in, gate_in, up_in, down_in, block_ref, pair_ref, down_ref, sems):
    copies = []

    def add(src, dst):
        copies.append(pltpu.make_async_copy(src, dst, sems.at[len(copies)]))

    hidden, width = down_ref.shape
    for c in range(chunks):
        part = pl.ds(c * (width // chunks), width // chunks)
        for first, last in hidden_parts(hidden):
            for k, ref in enumerate((gate_in, up_in)):
                to = 2 * first + k * (last - first)
                add(ref.at[0, part, first:last], pair_ref.at[part, to : to + last - first])
        part = pl.ds(c * (hidden // chunks), hidden // chunks)
        add(down_in.at[0, part, :], down_ref.at[part, :])
    add(block_in, block_ref)
    for copy in copies:
        copy.start()
    for copy in copies:
        copy.wait()


def join_kernel(*refs):
    blocks, out_ref, rows_ref = forward(refs[:-2]), refs[-2], refs[-1]
    count = len(blocks)
    tok = blocks[0].shape[1]
    for kind in range(2):
        for j, ref in enumerate(blocks):
            first = (kind * count + j) * tok
            rows_ref[first : first + tok, :] = ref[kind].astype(F32)
    out_ref[...] = rows_ref[...].astype(BF16)


def stack_kernel(*refs):
    out_ref = refs[-1]
    rows = refs[0].shape[0]
    for j, ref in enumerate(refs[:-1]):
        out_ref[j * rows : (j + 1) * rows, :] = ref[...]


def token_rows(refs, start, rows, group, kind, columns):
    parts = []
    for ref in refs:
        for j in range(rows // (2 * group)):
            first = start + (2 * j + kind) * group
            if not isinstance(first, int):
                first = pl.multiple_of(first, group)
            parts.append(ref[pl.ds(first, group), columns])
    return parts[0] if len(parts) == 1 else jnp.concatenate(parts, axis=0)


def put_scores(out_ref, scores_ref, width):
    rows = out_ref.shape[0]
    for c in range((out_ref.shape[1] - width) // LANES):
        out_ref[:, width + c * LANES : width + (c + 1) * LANES] = scores_ref[c * rows : (c + 1) * rows, :].astype(BF16)


def get_scores(in_ref, scores_ref, base, size, width):
    rows = in_ref.shape[0]
    for c in range(-(-size // rows)):
        here = min(rows, size - c * rows)
        tall = min(rows, -(-here // 16) * 16)
        block = in_ref[0:tall, width + c * LANES : width + (c + 1) * LANES].astype(F32)
        scores_ref[base + c * rows : base + c * rows + here, :] = block[:here]


def units_kernel(basis, group, tok, core_mask, blocks, *refs):
    own_refs, other_refs = forward(refs[:blocks]), forward(refs[blocks : 2 * blocks])
    pair_ref, down_ref, kept_ref, message_ref, pieces_ref, score_ref, padded_ref = refs[2 * blocks :]
    hidden, width = down_ref.shape
    rows, buf_width = own_refs[0].shape
    tokens = score_ref.shape[1]
    own = own_index()

    def terms(sets, start, step):
        act = token_rows(sets, start, step, group, 0, slice(None))
        count = act.shape[0]
        extras = act[:, width:].astype(F32)
        lane = lax.broadcasted_iota(jnp.int32, (count, buf_width - width), 1)
        column = jnp.sum(jnp.where(lane == own // 2, extras, 0.0), axis=1, keepdims=True)
        act = act[:, :width]
        cot = token_rows(sets, start, step, group, 1, slice(0, width))
        score = jnp.zeros((count, 1), F32)
        grads = []
        for first, last in hidden_parts(hidden):
            size = last - first
            pair = jnp.dot(act, pair_ref[:, 2 * first : 2 * last], preferred_element_type=F32)
            gate_pre = pair[:, :size]
            up_pre = pair[:, size:]
            back = lax.dot_general(cot, down_ref[first:last, :], NT, preferred_element_type=F32)
            sig = jax.nn.sigmoid(gate_pre)
            act_gate = gate_pre * sig
            score = score + jnp.sum(act_gate * up_pre * back, axis=1, keepdims=True)
            weighted = column * back
            grad_gate = weighted * up_pre * sig * (1.0 + gate_pre * (1.0 - sig))
            grad_up = weighted * act_gate
            grads += [grad_gate.astype(BF16), grad_up.astype(BF16)]
        grads = jnp.concatenate(grads, axis=1)
        return lax.dot_general(grads, pair_ref[...], NT, preferred_element_type=F32), score

    def in_order(score, place, swap_mask):
        token = lax.broadcasted_iota(jnp.int32, (score.shape[0], tokens), 1)
        side = own ^ swap_mask
        whole = (place_mask(place // tok, basis, side & core_mask != 0) ^ side) * tok + place % tok
        return jnp.sum(jnp.where(whole == token, score, 0.0), axis=0, keepdims=True)

    half = blocks * rows // 2
    if 2 * half <= 128:
        total, score = terms(own_refs + other_refs, 0, rows)
        kept_ref[...] = total[:half]
        message_ref[:, 0:width] = total[half:].astype(BF16)
        row = lax.broadcasted_iota(jnp.int32, (2 * half, tokens), 0)
        score_ref[...] = in_order(score, row % half, jnp.where(row < half, 0, core_mask))
    else:
        step = min(rows, 128)
        score_ref[...] = jnp.zeros(score_ref.shape, F32)
        for out_ref, sets, swap_mask in ((kept_ref, own_refs, 0), (message_ref, other_refs, core_mask)):
            for j, ref in enumerate(sets):

                def one(index):
                    total, score = terms((ref,), index * step, step)
                    first = pl.multiple_of(j * (rows // 2) + index * (step // 2), step // 2)
                    out_ref[pl.ds(first, step // 2), 0:width] = total.astype(out_ref.dtype)
                    place = lax.broadcasted_iota(jnp.int32, (step // 2, tokens), 0) + first
                    score_ref[...] += in_order(score, place, swap_mask)

                pl.loop(0, rows // step)(one)

    lane_blocks = tokens // LANES
    padded_ref[...] = jnp.zeros(padded_ref.shape, F32)
    value = score_ref[...]
    for piece in range(SCORE_PIECES):
        rounded = value.astype(BF16).astype(F32)
        for b in range(lane_blocks):
            at = piece * lane_blocks + b
            padded_ref[at : at + 1, :] = rounded[:, b * LANES : (b + 1) * LANES]
        value = value - rounded
    pieces_ref[...] = padded_ref[0 : pieces_ref.shape[0], :]
    put_scores(message_ref, padded_ref, width)


def add_kernel(arrivals, positions, core_mask, *refs):
    kept_ref, pieces_ref = refs[0], refs[1]
    arrived = refs[2 : 2 + arrivals]
    outs = refs[2 + arrivals :]
    next_kept_ref, next_pieces_ref = outs[0], outs[1]
    sends = outs[2 : 2 + len(positions)]
    total_ref, scores_ref = outs[2 + len(positions) :]
    width = kept_ref.shape[1]
    size = pieces_ref.shape[0]
    total = kept_ref[...]
    for ref in arrived:
        total = total + ref[:, 0:width].astype(F32)
    total_ref[...] = total
    if scores_ref.shape[0] > next_pieces_ref.shape[0]:
        scores_ref[...] = jnp.zeros(scores_ref.shape, F32)
    scores_ref[0:size, :] = pieces_ref[...]
    for j, ref in enumerate(arrived):
        get_scores(ref, scores_ref, (j + 1) * size, size, width)
    rows = next_kept_ref.shape[0]
    next_kept_ref[...] = total_ref[0:rows, :]
    next_pieces_ref[...] = scores_ref[0 : next_pieces_ref.shape[0], :]
    upper = own_index() & core_mask != 0
    for (low, high), ref in zip(positions, sends):
        first = low * rows
        if low != high:
            first = pl.multiple_of(jnp.where(upper, high, low) * rows, rows)
        ref[:, 0:width] = total_ref[pl.ds(first, rows), :].astype(BF16)
        put_scores(ref, scores_ref, width)


def table_kernel(basis, group, tok, core_mask, rows_out, blocks, after_ref, *refs):
    probs_ref, column_ref, mine_ref = refs[2 * blocks :]
    rows, buf_width = refs[0].shape
    half = blocks * rows // 2
    experts, tokens = probs_ref.shape
    lanes = -(-PIECES * experts // LANES) * LANES
    width = buf_width - lanes
    own = own_index()
    lane = lax.broadcasted_iota(jnp.int32, (experts, lanes), 1)
    ids = lax.broadcasted_iota(jnp.int32, (experts, lanes), 0)
    tally = jnp.zeros((experts, lanes), F32)
    for k in range(1, PIECES):
        tally = tally + jnp.where(lane == ids + k * experts, 1.0, 0.0)
    column = pl.multiple_of(own * rows_out // LANES * LANES, LANES)
    extras = jnp.zeros((tokens, lanes), F32)
    columns = jnp.zeros((tokens, LANES), F32)
    for index in range(2):
        sets = forward(refs[index * blocks : (index + 1) * blocks])
        row = lax.broadcasted_iota(jnp.int32, (half, tokens), 0)
        token = lax.broadcasted_iota(jnp.int32, (half, tokens), 1)
        side = own ^ (core_mask if index else 0)
        whole = (place_mask(row // tok, basis, side & core_mask != 0) ^ side) * tok + row % tok
        here = jnp.where(whole == token, 1.0, 0.0).astype(BF16)
        part = token_rows(sets, 0, rows, group, 0, slice(width, buf_width))
        extras = extras + lax.dot_general(here, part, TN, preferred_element_type=F32)
        part = token_rows(sets, 0, rows, group, 0, pl.ds(column, LANES))
        columns = columns + lax.dot_general(here, part, TN, preferred_element_type=F32)
    probs_ref[...] = lax.dot_general(tally.astype(BF16), extras.astype(BF16), NT, preferred_element_type=F32)
    column_ref[...] = columns.astype(BF16)
    row = lax.broadcasted_iota(jnp.int32, mine_ref.shape, 0)
    token = lax.broadcasted_iota(jnp.int32, mine_ref.shape, 1)
    mine_ref[...] = jnp.where((row < tok) & (token == own * tok + row), 1.0, 0.0).astype(BF16)


def final_kernel(arrivals, back_basis, core_mask, *refs):
    probs_ref, column_ref, mine_ref, router_ref, kept_ref, pieces_ref = refs[:6]
    arrived = refs[6 : 6 + arrivals]
    x_out, grad_out, x_ref, grad_ref, scores_ref, sems = refs[6 + arrivals :]
    experts, width = router_ref.shape
    size = pieces_ref.shape[0]
    tok = kept_ref.shape[0]
    own = own_index()
    scores_ref[0:size, :] = pieces_ref[...]
    for j, ref in enumerate(arrived):
        get_scores(ref, scores_ref, (j + 1) * size, size, width)
    blocks = probs_ref.shape[1] // LANES
    wide = scores_ref.shape[0] // blocks
    sender = lax.broadcasted_iota(jnp.int32, (experts, wide), 1) // SCORE_PIECES
    ids = lax.broadcasted_iota(jnp.int32, (experts, wide), 0)
    pick = jnp.where(((place_mask(sender, back_basis, own & core_mask != 0) ^ own) >> 1) == ids, 1.0, 0.0).astype(BF16)
    parts = []
    for b in range(blocks):
        block = scores_ref[...] if blocks == 1 else scores_ref[pl.ds(b, wide, stride=blocks), :]
        parts.append(jnp.dot(pick, block.astype(BF16), preferred_element_type=F32))
    scores = parts[0] if blocks == 1 else jnp.concatenate(parts, axis=1)
    probs = probs_ref[...]
    mean = jnp.sum(probs * scores, axis=0, keepdims=True)
    logit_grad = (probs * (scores - mean)).astype(BF16)
    mine = lax.dot_general(mine_ref[...], logit_grad, NT, preferred_element_type=F32)
    part = jnp.dot(mine.astype(BF16), router_ref[...], preferred_element_type=F32)
    total = kept_ref[...]
    for ref in arrived:
        total = total + ref[:, 0:width].astype(F32)
    x_ref[...] = (total + part[:tok]).astype(BF16)
    x_copy = pltpu.make_async_copy(x_ref, x_out, sems.at[0])
    x_copy.start()
    grad = jnp.dot(logit_grad, column_ref[...], preferred_element_type=F32)
    rows_out = grad_ref.shape[1]
    first = own * rows_out % LANES
    grad_ref[...] = pltpu.roll(grad, (LANES - first) % LANES, 1)[:, :rows_out]
    grad_copy = pltpu.make_async_copy(grad_ref, grad_out, sems.at[1])
    grad_copy.start()
    x_copy.wait()
    grad_copy.wait()


def on_device(tokens, grad_out, router_logits, selected, router_w, w_gate, w_up, w_down):
    tok, width = tokens.shape
    experts = router_logits.shape[1]
    hidden = w_gate.shape[2]
    exp_size = lax.axis_size("exp")
    hid_size = lax.axis_size("hid")
    count = exp_size * hid_size
    half = count // 2
    groups, core = stage_masks(exp_size, hid_size)
    core_mask = 1 << core
    basis = [m for group in groups for m in group]
    back_groups = [near_first(group) for group in groups[:0:-1]] + [groups[0][::-1]]
    core_pair = (core_mask, core_mask)
    back_basis = [core_pair] + [m for group in back_groups for m in group]
    token_count = count * tok
    lanes = -(-PIECES * experts // LANES) * LANES

    block = pl.pallas_call(
        prep_kernel,
        out_shape=jax.ShapeDtypeStruct((2, tok, width + lanes), BF16),
        in_specs=[HBM_SPEC] * 4,
        out_specs=VMEM_SPEC,
        scratch_shapes=[
            pltpu.VMEM(router_logits.shape, router_logits.dtype),
            pltpu.VMEM(selected.shape, selected.dtype),
            pltpu.SemaphoreType.DMA((4,)),
        ],
        compiler_params=PARAMS,
        name="prep",
    )(*in_hbm(tokens, grad_out, router_logits, selected))

    masks = group_masks(groups[0])
    blocks = [block] + swaps(block, masks[1:], count, core)
    group_rows = tok * len(blocks)
    block = pl.pallas_call(
        join_kernel,
        out_shape=jax.ShapeDtypeStruct((2 * group_rows, width + lanes), BF16),
        in_specs=[VMEM_SPEC] * len(blocks),
        out_specs=VMEM_SPEC,
        scratch_shapes=[pltpu.VMEM((2 * group_rows, width + lanes), F32)],
        compiler_params=PARAMS,
        name="join",
    )(*forward(blocks))
    for group in groups[1:-1]:
        blocks = [block] + swaps(block, group_masks(group)[1:], count, core)
        block = pl.pallas_call(
            stack_kernel,
            out_shape=jax.ShapeDtypeStruct((len(blocks) * block.shape[0], block.shape[1]), BF16),
            in_specs=[VMEM_SPEC] * len(blocks),
            out_specs=VMEM_SPEC,
            compiler_params=PARAMS,
            name="stack",
        )(*blocks)
    chunks = 4
    copied, pair, down = pl.pallas_call(
        functools.partial(load_kernel, chunks),
        out_shape=(
            pltpu.VMEM(block.shape, BF16),
            pltpu.VMEM((width, 2 * hidden), BF16),
            pltpu.VMEM((hidden, width), BF16),
        ),
        in_specs=[VMEM_SPEC] + [HBM_SPEC] * 3,
        out_specs=(VMEM_SPEC,) * 3,
        scratch_shapes=[pltpu.SemaphoreType.DMA(((2 * len(hidden_parts(hidden)) + 1) * chunks + 1,))],
        compiler_params=pltpu.CompilerParams(vmem_limit_bytes=4 * 2**20),
        cost_estimate=pl.CostEstimate(flops=0, bytes_accessed=6 * width * hidden * 2, transcendentals=0),
        name="load",
    )(block, *in_hbm(w_gate, w_up, w_down))
    masks = group_masks(groups[-1]) if len(groups) > 1 else [core_pair]
    blocks = [block] + swaps(block, masks[1:], count, core)
    blocks = forward(blocks)
    blocks = blocks + [swap(b, core_pair, count, core) for b in [copied] + blocks[1:]]
    block_count = len(blocks) // 2

    unit_rows = SCORE_PIECES * token_count // LANES
    extra = -(-unit_rows // (half * tok)) * LANES
    kept, message, pieces = pl.pallas_call(
        functools.partial(units_kernel, basis, group_rows, tok, core_mask, block_count),
        out_shape=(
            jax.ShapeDtypeStruct((half * tok, width), F32),
            jax.ShapeDtypeStruct((half * tok, width + extra), BF16),
            jax.ShapeDtypeStruct((unit_rows, LANES), F32),
        ),
        in_specs=[VMEM_SPEC] * (len(blocks) + 2),
        out_specs=(VMEM_SPEC,) * 3,
        scratch_shapes=[
            pltpu.VMEM((1, token_count), F32),
            pltpu.VMEM((max(half * tok * extra // LANES, unit_rows), LANES), F32),
        ],
        compiler_params=PARAMS,
        cost_estimate=pl.CostEstimate(
            flops=10 * token_count * width * hidden,
            bytes_accessed=3 * width * hidden * 2 + 2 * token_count * width * 2,
            transcendentals=token_count * hidden,
        ),
        name="units",
    )(*blocks, pair, down)

    arrived = [swap(message, core_pair, count, core)]
    tables = None
    rows_out = width // count
    for group, back_group in zip(groups[::-1], back_groups):
        back_masks = group_masks(back_group)
        positions = [
            tuple([m[side] for m in group_masks(group)].index(mask[side]) for side in range(2)) for mask in back_masks[1:]
        ]
        radix = len(back_masks)
        rows = kept.shape[0]
        next_rows = rows // radix
        size = pieces.shape[0] * (1 + len(arrived))
        extra = -(-size // next_rows) * LANES
        sends = [jax.ShapeDtypeStruct((next_rows, width + extra), BF16)] * (radix - 1)
        outs = pl.pallas_call(
            functools.partial(add_kernel, len(arrived), positions, core_mask),
            out_shape=[
                jax.ShapeDtypeStruct((next_rows, width), F32),
                jax.ShapeDtypeStruct((size, LANES), F32),
            ]
            + sends,
            in_specs=[VMEM_SPEC] * (2 + len(arrived)),
            out_specs=[VMEM_SPEC] * (1 + radix),
            scratch_shapes=[
                pltpu.VMEM((rows, width), F32),
                pltpu.VMEM((max(next_rows * extra // LANES, size), LANES), F32),
            ],
            compiler_params=PARAMS,
            name="add",
        )(kept, pieces, *arrived)
        kept, pieces = outs[0], outs[1]
        if tables is None:
            tables = pl.pallas_call(
                functools.partial(table_kernel, basis, group_rows, tok, core_mask, rows_out, block_count),
                out_shape=(
                    jax.ShapeDtypeStruct((experts, token_count), F32),
                    jax.ShapeDtypeStruct((token_count, LANES), BF16),
                    jax.ShapeDtypeStruct((16, token_count), BF16),
                ),
                in_specs=[pl.BlockSpec(memory_space=pl.ANY)] + [VMEM_SPEC] * len(blocks),
                out_specs=(VMEM_SPEC,) * 3,
                compiler_params=PARAMS,
                cost_estimate=pl.CostEstimate(flops=10**9, bytes_accessed=10**6, transcendentals=0),
                name="tables",
            )(pieces, *blocks)
        arrived = [swap(piece, m, count, core) for piece, m in zip(outs[2:], back_masks[1:])]

    x_grad, grad = pl.pallas_call(
        functools.partial(final_kernel, len(arrived), back_basis, core_mask),
        out_shape=(
            jax.ShapeDtypeStruct((tok, width), BF16),
            jax.ShapeDtypeStruct((experts, rows_out), F32),
        ),
        in_specs=[VMEM_SPEC] * (6 + len(arrived)),
        out_specs=(HBM_SPEC, HBM_SPEC),
        scratch_shapes=[
            pltpu.VMEM((tok, width), BF16),
            pltpu.VMEM((experts, rows_out), F32),
            pltpu.VMEM((pieces.shape[0] * (1 + len(arrived)), LANES), F32),
            pltpu.SemaphoreType.DMA((2,)),
        ],
        compiler_params=PARAMS,
        name="final",
    )(*tables, router_w.T, kept, pieces, *arrived)
    return (x_grad, grad.T)


def solution(mesh):
    rows = P(AXES, None)
    units = P(AXES, None, None)
    return jax.shard_map(
        on_device,
        mesh=mesh,
        in_specs=(rows, rows, rows, rows, P(), units, units, units),
        out_specs=(rows, rows),
        check_vma=False,
    )
```

```python
import functools

import jax
import jax.numpy as jnp
from jax import lax
from jax.experimental import pallas as pl
from jax.experimental.pallas import tpu as pltpu
from jax.sharding import PartitionSpec as P

AXES = ("exp", "hid")
LANES = 128
PIECES = 4
SCORE_PIECES = 2
VMEM_SPEC = pl.BlockSpec(memory_space=pltpu.VMEM)
HBM_SPEC = pl.BlockSpec(memory_space=pltpu.HBM)
F32 = jnp.float32
BF16 = jnp.bfloat16
NT = (((1,), (1,)), ((), ()))
TN = (((0,), (0,)), ((), ()))
PARAMS = pltpu.CompilerParams(vmem_limit_bytes=24 * 2**20)


def stage_masks(exp_size, hid_size):
    hid_bits = hid_size.bit_length() - 1
    all_bits = (exp_size * hid_size).bit_length() - 1
    core = hid_bits
    first = list(range(max(core + 1, all_bits - 2), all_bits))
    middle = [b for b in range(all_bits) if b != core and b not in first]
    groups = [first] + [middle[i : i + 2] for i in range(0, len(middle), 2)]
    bases = [[(sum(1 << b for b in group[i:]),) * 2 for i in range(len(group))] for group in groups]
    bases[0] = bases[0][::-1]
    return bases, core


def cross(a, b):
    return (a[0] ^ b[0], a[1] ^ b[1])


def group_masks(basis):
    masks = [(0, 0)]
    for mask in basis:
        masks = masks + [cross(m, mask) for m in masks]
    return masks


def near_first(basis):
    return [cross(basis[0], basis[1]), basis[1]] if len(basis) == 2 else basis


def swap(block, mask, count, core):
    return lax.ppermute(block, AXES, [(i, i ^ mask[i >> core & 1]) for i in range(count)])


def swaps(block, masks, count, core):
    return [swap(block, m, count, core) for m in masks]


def forward(blocks):
    return blocks[:1] + blocks[:0:-1]


def place_mask(place, basis, upper):
    total = jnp.zeros_like(place)
    for digit, (low, high) in enumerate(basis):
        mask = low if low == high else jnp.where(upper, high, low)
        total = total ^ (((place >> digit) & 1) * mask)
    return total


def own_index():
    return lax.axis_index("exp") * lax.axis_size("hid") + lax.axis_index("hid")


def in_hbm(*arrays):
    return tuple(pltpu.with_memory_space_constraint(a, pltpu.HBM) for a in arrays)


def piece_sum(experts, lanes, axis):
    shape = (lanes, experts) if axis == 0 else (experts, lanes)
    lane = lax.broadcasted_iota(jnp.int32, shape, axis)
    ids = lax.broadcasted_iota(jnp.int32, shape, 1 - axis)
    tally = jnp.zeros(shape, F32)
    for k in range(1, PIECES):
        tally = tally + jnp.where(lane == ids + k * experts, 1.0, 0.0)
    return tally.astype(BF16)


def combine_rows(extras, experts):
    hit = extras[:, :experts].astype(F32) > 0.5
    logits = jnp.dot(extras, piece_sum(experts, extras.shape[1], 0), preferred_element_type=F32)
    top = jnp.max(jnp.where(hit, logits, -jnp.inf), axis=1, keepdims=True)
    raised = jnp.where(hit, jnp.exp(jnp.minimum(logits - top, 0.0)), 0.0)
    return (raised / jnp.sum(raised, axis=1, keepdims=True)).astype(BF16).astype(F32)


def prep_kernel(tokens_in, grad_in, logits_in, chosen_in, out_ref, logits_ref, chosen_ref, sems):
    tok, width = tokens_in.shape
    pairs = [
        (logits_in, logits_ref),
        (chosen_in, chosen_ref),
        (tokens_in, out_ref.at[0, :, 0:width]),
        (grad_in, out_ref.at[1, :, 0:width]),
    ]
    copies = [pltpu.make_async_copy(src, dst, sems.at[i]) for i, (src, dst) in enumerate(pairs)]
    for copy in copies:
        copy.start()
    copies[0].wait()
    copies[1].wait()
    logits = logits_ref[...]
    chosen = chosen_ref[...]
    experts = logits.shape[1]
    ids = lax.broadcasted_iota(jnp.int32, logits.shape, 1)
    hit = ids == chosen[:, 0:1]
    for k in range(1, chosen.shape[1]):
        hit = hit | (ids == chosen[:, k : k + 1])
    parts = [jnp.where(hit, 1.0, 0.0)]
    rest = logits
    for _ in range(PIECES - 1):
        parts.append(rest)
        rest = rest - rest.astype(BF16).astype(F32)
    lanes = out_ref.shape[2] - width
    spare = lanes - PIECES * experts
    extras = jnp.concatenate(parts + ([jnp.zeros((tok, spare), F32)] if spare else []), axis=1)
    out_ref[0, :, width:] = extras.astype(BF16)
    out_ref[1, :, width:] = jnp.zeros((tok, lanes), BF16)
    copies[2].wait()
    copies[3].wait()


def hidden_parts(hidden):
    main = hidden // 256 * 256
    return [(0, main), (main, hidden)] if 0 < main < hidden else [(0, hidden)]


def load_kernel(chunks, block_in, gate_in, up_in, down_in, block_ref, pair_ref, down_ref, sems):
    copies = []

    def add(src, dst):
        copies.append(pltpu.make_async_copy(src, dst, sems.at[len(copies)]))

    hidden, width = down_ref.shape
    for c in range(chunks):
        part = pl.ds(c * (width // chunks), width // chunks)
        for first, last in hidden_parts(hidden):
            for k, ref in enumerate((gate_in, up_in)):
                to = 2 * first + k * (last - first)
                add(ref.at[0, part, first:last], pair_ref.at[part, to : to + last - first])
        part = pl.ds(c * (hidden // chunks), hidden // chunks)
        add(down_in.at[0, part, :], down_ref.at[part, :])
    add(block_in, block_ref)
    for copy in copies:
        copy.start()
    for copy in copies:
        copy.wait()


def join_kernel(*refs):
    blocks, out_ref, rows_ref = forward(refs[:-2]), refs[-2], refs[-1]
    count = len(blocks)
    tok = blocks[0].shape[1]
    for kind in range(2):
        for j, ref in enumerate(blocks):
            first = (kind * count + j) * tok
            rows_ref[first : first + tok, :] = ref[kind].astype(F32)
    out_ref[...] = rows_ref[...].astype(BF16)


def stack_kernel(*refs):
    out_ref = refs[-1]
    rows = refs[0].shape[0]
    for j, ref in enumerate(refs[:-1]):
        out_ref[j * rows : (j + 1) * rows, :] = ref[...]


def token_rows(refs, start, rows, group, kind, columns):
    parts = []
    for ref in refs:
        for j in range(rows // (2 * group)):
            first = start + (2 * j + kind) * group
            if not isinstance(first, int):
                first = pl.multiple_of(first, group)
            parts.append(ref[pl.ds(first, group), columns])
    return parts[0] if len(parts) == 1 else jnp.concatenate(parts, axis=0)


def put_scores(out_ref, scores_ref, width):
    rows = out_ref.shape[0]
    for c in range((out_ref.shape[1] - width) // LANES):
        out_ref[:, width + c * LANES : width + (c + 1) * LANES] = scores_ref[c * rows : (c + 1) * rows, :].astype(BF16)


def get_scores(in_ref, scores_ref, base, size, width):
    rows = in_ref.shape[0]
    for c in range(-(-size // rows)):
        here = min(rows, size - c * rows)
        tall = min(rows, -(-here // 16) * 16)
        block = in_ref[0:tall, width + c * LANES : width + (c + 1) * LANES].astype(F32)
        scores_ref[base + c * rows : base + c * rows + here, :] = block[:here]


def units_kernel(basis, group, tok, experts, core_mask, blocks, *refs):
    own_refs, other_refs = forward(refs[:blocks]), forward(refs[blocks : 2 * blocks])
    pair_ref, down_ref, kept_ref, message_ref, pieces_ref, score_ref, padded_ref = refs[2 * blocks :]
    hidden, width = down_ref.shape
    rows, buf_width = own_refs[0].shape
    tokens = score_ref.shape[1]
    own = own_index()

    def terms(sets, start, step):
        act = token_rows(sets, start, step, group, 0, slice(None))
        count = act.shape[0]
        combine = combine_rows(act[:, width:], experts)
        ids = lax.broadcasted_iota(jnp.int32, combine.shape, 1)
        column = jnp.sum(jnp.where(ids == own // 2, combine, 0.0), axis=1, keepdims=True)
        act = act[:, :width]
        cot = token_rows(sets, start, step, group, 1, slice(0, width))
        score = jnp.zeros((count, 1), F32)
        grads = []
        for first, last in hidden_parts(hidden):
            size = last - first
            pair = jnp.dot(act, pair_ref[:, 2 * first : 2 * last], preferred_element_type=F32)
            gate_pre = pair[:, :size]
            up_pre = pair[:, size:]
            back = lax.dot_general(cot, down_ref[first:last, :], NT, preferred_element_type=F32)
            sig = jax.nn.sigmoid(gate_pre)
            act_gate = gate_pre * sig
            score = score + jnp.sum(act_gate * up_pre * back, axis=1, keepdims=True)
            weighted = column * back
            grad_gate = weighted * up_pre * sig * (1.0 + gate_pre * (1.0 - sig))
            grad_up = weighted * act_gate
            grads += [grad_gate.astype(BF16), grad_up.astype(BF16)]
        grads = jnp.concatenate(grads, axis=1)
        return lax.dot_general(grads, pair_ref[...], NT, preferred_element_type=F32), score

    def in_order(score, place, swap_mask):
        token = lax.broadcasted_iota(jnp.int32, (score.shape[0], tokens), 1)
        side = own ^ swap_mask
        whole = (place_mask(place // tok, basis, side & core_mask != 0) ^ side) * tok + place % tok
        return jnp.sum(jnp.where(whole == token, score, 0.0), axis=0, keepdims=True)

    half = blocks * rows // 2
    if 2 * half <= 128:
        total, score = terms(own_refs + other_refs, 0, rows)
        kept_ref[...] = total[:half]
        message_ref[:, 0:width] = total[half:].astype(BF16)
        row = lax.broadcasted_iota(jnp.int32, (2 * half, tokens), 0)
        score_ref[...] = in_order(score, row % half, jnp.where(row < half, 0, core_mask))
    else:
        step = min(rows, 128)
        score_ref[...] = jnp.zeros(score_ref.shape, F32)
        for out_ref, sets, swap_mask in ((kept_ref, own_refs, 0), (message_ref, other_refs, core_mask)):
            for j, ref in enumerate(sets):

                def one(index):
                    total, score = terms((ref,), index * step, step)
                    first = pl.multiple_of(j * (rows // 2) + index * (step // 2), step // 2)
                    out_ref[pl.ds(first, step // 2), 0:width] = total.astype(out_ref.dtype)
                    place = lax.broadcasted_iota(jnp.int32, (step // 2, tokens), 0) + first
                    score_ref[...] += in_order(score, place, swap_mask)

                pl.loop(0, rows // step)(one)

    lane_blocks = tokens // LANES
    padded_ref[...] = jnp.zeros(padded_ref.shape, F32)
    value = score_ref[...]
    for piece in range(SCORE_PIECES):
        rounded = value.astype(BF16).astype(F32)
        for b in range(lane_blocks):
            at = piece * lane_blocks + b
            padded_ref[at : at + 1, :] = rounded[:, b * LANES : (b + 1) * LANES]
        value = value - rounded
    pieces_ref[...] = padded_ref[0 : pieces_ref.shape[0], :]
    put_scores(message_ref, padded_ref, width)


def add_kernel(arrivals, positions, core_mask, *refs):
    kept_ref, pieces_ref = refs[0], refs[1]
    arrived = refs[2 : 2 + arrivals]
    outs = refs[2 + arrivals :]
    next_kept_ref, next_pieces_ref = outs[0], outs[1]
    sends = outs[2 : 2 + len(positions)]
    total_ref, scores_ref = outs[2 + len(positions) :]
    width = kept_ref.shape[1]
    size = pieces_ref.shape[0]
    total = kept_ref[...]
    for ref in arrived:
        total = total + ref[:, 0:width].astype(F32)
    total_ref[...] = total
    if scores_ref.shape[0] > next_pieces_ref.shape[0]:
        scores_ref[...] = jnp.zeros(scores_ref.shape, F32)
    scores_ref[0:size, :] = pieces_ref[...]
    for j, ref in enumerate(arrived):
        get_scores(ref, scores_ref, (j + 1) * size, size, width)
    rows = next_kept_ref.shape[0]
    next_kept_ref[...] = total_ref[0:rows, :]
    next_pieces_ref[...] = scores_ref[0 : next_pieces_ref.shape[0], :]
    upper = own_index() & core_mask != 0
    for (low, high), ref in zip(positions, sends):
        first = low * rows
        if low != high:
            first = pl.multiple_of(jnp.where(upper, high, low) * rows, rows)
        ref[:, 0:width] = total_ref[pl.ds(first, rows), :].astype(BF16)
        put_scores(ref, scores_ref, width)


def table_kernel(basis, group, tok, core_mask, rows_out, blocks, after_ref, *refs):
    probs_ref, column_ref, mine_ref = refs[2 * blocks :]
    rows, buf_width = refs[0].shape
    half = blocks * rows // 2
    experts, tokens = probs_ref.shape
    lanes = -(-PIECES * experts // LANES) * LANES
    width = buf_width - lanes
    own = own_index()
    column = pl.multiple_of(own * rows_out // LANES * LANES, LANES)
    extras = jnp.zeros((tokens, lanes), F32)
    columns = jnp.zeros((tokens, LANES), F32)
    for index in range(2):
        sets = forward(refs[index * blocks : (index + 1) * blocks])
        row = lax.broadcasted_iota(jnp.int32, (half, tokens), 0)
        token = lax.broadcasted_iota(jnp.int32, (half, tokens), 1)
        side = own ^ (core_mask if index else 0)
        whole = (place_mask(row // tok, basis, side & core_mask != 0) ^ side) * tok + row % tok
        here = jnp.where(whole == token, 1.0, 0.0).astype(BF16)
        part = token_rows(sets, 0, rows, group, 0, slice(width, buf_width))
        extras = extras + lax.dot_general(here, part, TN, preferred_element_type=F32)
        part = token_rows(sets, 0, rows, group, 0, pl.ds(column, LANES))
        columns = columns + lax.dot_general(here, part, TN, preferred_element_type=F32)
    logits = lax.dot_general(piece_sum(experts, lanes, 1), extras.astype(BF16), NT, preferred_element_type=F32)
    raised = jnp.exp(logits - jnp.max(logits, axis=0, keepdims=True))
    probs_ref[...] = raised / jnp.sum(raised, axis=0, keepdims=True)
    column_ref[...] = columns.astype(BF16)
    row = lax.broadcasted_iota(jnp.int32, mine_ref.shape, 0)
    token = lax.broadcasted_iota(jnp.int32, mine_ref.shape, 1)
    mine_ref[...] = jnp.where((row < tok) & (token == own * tok + row), 1.0, 0.0).astype(BF16)


def final_kernel(arrivals, back_basis, core_mask, *refs):
    probs_ref, column_ref, mine_ref, router_ref, kept_ref, pieces_ref = refs[:6]
    arrived = refs[6 : 6 + arrivals]
    x_out, grad_out, x_ref, grad_ref, scores_ref, sems = refs[6 + arrivals :]
    experts, width = router_ref.shape
    size = pieces_ref.shape[0]
    tok = kept_ref.shape[0]
    own = own_index()
    scores_ref[0:size, :] = pieces_ref[...]
    for j, ref in enumerate(arrived):
        get_scores(ref, scores_ref, (j + 1) * size, size, width)
    blocks = probs_ref.shape[1] // LANES
    wide = scores_ref.shape[0] // blocks
    sender = lax.broadcasted_iota(jnp.int32, (experts, wide), 1) // SCORE_PIECES
    ids = lax.broadcasted_iota(jnp.int32, (experts, wide), 0)
    pick = jnp.where(((place_mask(sender, back_basis, own & core_mask != 0) ^ own) >> 1) == ids, 1.0, 0.0).astype(BF16)
    parts = []
    for b in range(blocks):
        block = scores_ref[...] if blocks == 1 else scores_ref[pl.ds(b, wide, stride=blocks), :]
        parts.append(jnp.dot(pick, block.astype(BF16), preferred_element_type=F32))
    scores = parts[0] if blocks == 1 else jnp.concatenate(parts, axis=1)
    probs = probs_ref[...]
    mean = jnp.sum(probs * scores, axis=0, keepdims=True)
    logit_grad = (probs * (scores - mean)).astype(BF16)
    mine = lax.dot_general(mine_ref[...], logit_grad, NT, preferred_element_type=F32)
    part = jnp.dot(mine.astype(BF16), router_ref[...], preferred_element_type=F32)
    total = kept_ref[...]
    for ref in arrived:
        total = total + ref[:, 0:width].astype(F32)
    x_ref[...] = (total + part[:tok]).astype(BF16)
    x_copy = pltpu.make_async_copy(x_ref, x_out, sems.at[0])
    x_copy.start()
    grad = jnp.dot(logit_grad, column_ref[...], preferred_element_type=F32)
    rows_out = grad_ref.shape[1]
    first = own * rows_out % LANES
    grad_ref[...] = pltpu.roll(grad, (LANES - first) % LANES, 1)[:, :rows_out]
    grad_copy = pltpu.make_async_copy(grad_ref, grad_out, sems.at[1])
    grad_copy.start()
    x_copy.wait()
    grad_copy.wait()


def on_device(tokens, grad_out, router_logits, selected, router_w, w_gate, w_up, w_down):
    tok, width = tokens.shape
    experts = router_logits.shape[1]
    hidden = w_gate.shape[2]
    exp_size = lax.axis_size("exp")
    hid_size = lax.axis_size("hid")
    count = exp_size * hid_size
    half = count // 2
    groups, core = stage_masks(exp_size, hid_size)
    core_mask = 1 << core
    basis = [m for group in groups for m in group]
    back_groups = [near_first(group) for group in groups[:0:-1]] + [groups[0]]
    core_pair = (core_mask, core_mask)
    back_basis = [core_pair] + [m for group in back_groups for m in group]
    token_count = count * tok
    lanes = -(-PIECES * experts // LANES) * LANES

    block = pl.pallas_call(
        prep_kernel,
        out_shape=jax.ShapeDtypeStruct((2, tok, width + lanes), BF16),
        in_specs=[HBM_SPEC] * 4,
        out_specs=VMEM_SPEC,
        scratch_shapes=[
            pltpu.VMEM(router_logits.shape, router_logits.dtype),
            pltpu.VMEM(selected.shape, selected.dtype),
            pltpu.SemaphoreType.DMA((4,)),
        ],
        compiler_params=PARAMS,
        name="prep",
    )(*in_hbm(tokens, grad_out, router_logits, selected))

    masks = group_masks(groups[0])
    blocks = [block] + swaps(block, masks[1:], count, core)
    group_rows = tok * len(blocks)
    block = pl.pallas_call(
        join_kernel,
        out_shape=jax.ShapeDtypeStruct((2 * group_rows, width + lanes), BF16),
        in_specs=[VMEM_SPEC] * len(blocks),
        out_specs=VMEM_SPEC,
        scratch_shapes=[pltpu.VMEM((2 * group_rows, width + lanes), F32)],
        compiler_params=PARAMS,
        name="join",
    )(*forward(blocks))
    for group in groups[1:-1]:
        blocks = [block] + swaps(block, group_masks(group)[1:], count, core)
        block = pl.pallas_call(
            stack_kernel,
            out_shape=jax.ShapeDtypeStruct((len(blocks) * block.shape[0], block.shape[1]), BF16),
            in_specs=[VMEM_SPEC] * len(blocks),
            out_specs=VMEM_SPEC,
            compiler_params=PARAMS,
            name="stack",
        )(*blocks)
    chunks = 4
    copied, pair, down = pl.pallas_call(
        functools.partial(load_kernel, chunks),
        out_shape=(
            pltpu.VMEM(block.shape, BF16),
            pltpu.VMEM((width, 2 * hidden), BF16),
            pltpu.VMEM((hidden, width), BF16),
        ),
        in_specs=[VMEM_SPEC] + [HBM_SPEC] * 3,
        out_specs=(VMEM_SPEC,) * 3,
        scratch_shapes=[pltpu.SemaphoreType.DMA(((2 * len(hidden_parts(hidden)) + 1) * chunks + 1,))],
        compiler_params=pltpu.CompilerParams(vmem_limit_bytes=4 * 2**20),
        cost_estimate=pl.CostEstimate(flops=0, bytes_accessed=6 * width * hidden * 2, transcendentals=0),
        name="load",
    )(block, *in_hbm(w_gate, w_up, w_down))
    masks = group_masks(groups[-1]) if len(groups) > 1 else [core_pair]
    blocks = [block] + swaps(block, masks[1:], count, core)
    blocks = forward(blocks)
    blocks = blocks + [swap(b, core_pair, count, core) for b in [copied] + blocks[1:]]
    block_count = len(blocks) // 2

    unit_rows = SCORE_PIECES * token_count // LANES
    extra = -(-unit_rows // (half * tok)) * LANES
    kept, message, pieces = pl.pallas_call(
        functools.partial(units_kernel, basis, group_rows, tok, experts, core_mask, block_count),
        out_shape=(
            jax.ShapeDtypeStruct((half * tok, width), F32),
            jax.ShapeDtypeStruct((half * tok, width + extra), BF16),
            jax.ShapeDtypeStruct((unit_rows, LANES), F32),
        ),
        in_specs=[VMEM_SPEC] * (len(blocks) + 2),
        out_specs=(VMEM_SPEC,) * 3,
        scratch_shapes=[
            pltpu.VMEM((1, token_count), F32),
            pltpu.VMEM((max(half * tok * extra // LANES, unit_rows), LANES), F32),
        ],
        compiler_params=PARAMS,
        cost_estimate=pl.CostEstimate(
            flops=10 * token_count * width * hidden,
            bytes_accessed=3 * width * hidden * 2 + 2 * token_count * width * 2,
            transcendentals=token_count * hidden,
        ),
        name="units",
    )(*blocks, pair, down)

    arrived = [swap(message, core_pair, count, core)]
    tables = None
    rows_out = width // count
    for group, back_group in zip(groups[::-1], back_groups):
        back_masks = group_masks(back_group)
        positions = [
            tuple([m[side] for m in group_masks(group)].index(mask[side]) for side in range(2)) for mask in back_masks[1:]
        ]
        radix = len(back_masks)
        rows = kept.shape[0]
        next_rows = rows // radix
        size = pieces.shape[0] * (1 + len(arrived))
        extra = -(-size // next_rows) * LANES
        sends = [jax.ShapeDtypeStruct((next_rows, width + extra), BF16)] * (radix - 1)
        outs = pl.pallas_call(
            functools.partial(add_kernel, len(arrived), positions, core_mask),
            out_shape=[
                jax.ShapeDtypeStruct((next_rows, width), F32),
                jax.ShapeDtypeStruct((size, LANES), F32),
            ]
            + sends,
            in_specs=[VMEM_SPEC] * (2 + len(arrived)),
            out_specs=[VMEM_SPEC] * (1 + radix),
            scratch_shapes=[
                pltpu.VMEM((rows, width), F32),
                pltpu.VMEM((max(next_rows * extra // LANES, size), LANES), F32),
            ],
            compiler_params=PARAMS,
            name="add",
        )(kept, pieces, *arrived)
        kept, pieces = outs[0], outs[1]
        if tables is None:
            tables = pl.pallas_call(
                functools.partial(table_kernel, basis, group_rows, tok, core_mask, rows_out, block_count),
                out_shape=(
                    jax.ShapeDtypeStruct((experts, token_count), F32),
                    jax.ShapeDtypeStruct((token_count, LANES), BF16),
                    jax.ShapeDtypeStruct((16, token_count), BF16),
                ),
                in_specs=[pl.BlockSpec(memory_space=pl.ANY)] + [VMEM_SPEC] * len(blocks),
                out_specs=(VMEM_SPEC,) * 3,
                compiler_params=PARAMS,
                cost_estimate=pl.CostEstimate(flops=10**9, bytes_accessed=10**6, transcendentals=0),
                name="tables",
            )(pieces, *blocks)
        arrived = [swap(piece, m, count, core) for piece, m in zip(outs[2:], back_masks[1:])]

    x_grad, grad = pl.pallas_call(
        functools.partial(final_kernel, len(arrived), back_basis, core_mask),
        out_shape=(
            jax.ShapeDtypeStruct((tok, width), BF16),
            jax.ShapeDtypeStruct((experts, rows_out), F32),
        ),
        in_specs=[VMEM_SPEC] * (6 + len(arrived)),
        out_specs=(HBM_SPEC, HBM_SPEC),
        scratch_shapes=[
            pltpu.VMEM((tok, width), BF16),
            pltpu.VMEM((experts, rows_out), F32),
            pltpu.VMEM((pieces.shape[0] * (1 + len(arrived)), LANES), F32),
            pltpu.SemaphoreType.DMA((2,)),
        ],
        compiler_params=PARAMS,
        name="final",
    )(*tables, router_w.T, kept, pieces, *arrived)
    return (x_grad, grad.T)


def solution(mesh):
    rows = P(AXES, None)
    units = P(AXES, None, None)
    return jax.shard_map(
        on_device,
        mesh=mesh,
        in_specs=(rows, rows, rows, rows, P(), units, units, units),
        out_specs=(rows, rows),
        check_vma=False,
    )
```

```python
import functools

import jax
import jax.numpy as jnp
from jax import lax
from jax.experimental import pallas as pl
from jax.experimental.pallas import tpu as pltpu
from jax.sharding import PartitionSpec as P

AXES = ("exp", "hid")
LANES = 128
PIECES = 4
SCORE_PIECES = 2
VMEM_SPEC = pl.BlockSpec(memory_space=pltpu.VMEM)
HBM_SPEC = pl.BlockSpec(memory_space=pltpu.HBM)
F32 = jnp.float32
BF16 = jnp.bfloat16
NT = (((1,), (1,)), ((), ()))
TN = (((0,), (0,)), ((), ()))
PARAMS = pltpu.CompilerParams(vmem_limit_bytes=24 * 2**20)


def stage_masks(exp_size, hid_size):
    hid_bits = hid_size.bit_length() - 1
    all_bits = (exp_size * hid_size).bit_length() - 1
    core = hid_bits
    first = list(range(max(core + 1, all_bits - 2), all_bits))
    middle = [b for b in range(all_bits) if b != core and b not in first]
    groups = [first] + [middle[i : i + 2] for i in range(0, len(middle), 2)]
    bases = [[(sum(1 << b for b in group[i:]),) * 2 for i in range(len(group))] for group in groups]
    bases[0] = bases[0][::-1]
    return bases, core


def cross(a, b):
    return (a[0] ^ b[0], a[1] ^ b[1])


def group_masks(basis):
    masks = [(0, 0)]
    for mask in basis:
        masks = masks + [cross(m, mask) for m in masks]
    return masks


def near_first(basis):
    return [cross(basis[0], basis[1]), basis[1]] if len(basis) == 2 else basis


def swap(block, mask, count, core):
    return lax.ppermute(block, AXES, [(i, i ^ mask[i >> core & 1]) for i in range(count)])


REDUCE_STEPS = ((1, 3, 0, 2), (3, 2, 1, 0), (2, 0, 3, 1))


def by_member(member, values):
    total = values[0]
    for k in range(1, len(values)):
        total = jnp.where(member == k, values[k], total)
    return total


def shift(block, step, count, low):
    return lax.ppermute(block, AXES, [(i, i ^ ((i >> low & 3) ^ step[i >> low & 3]) << low) for i in range(count)])


def swaps(block, masks, count, core):
    return [swap(block, m, count, core) for m in masks]


def forward(blocks):
    return blocks[:1] + blocks[:0:-1]


def place_mask(place, basis, upper):
    total = jnp.zeros_like(place)
    for digit, (low, high) in enumerate(basis):
        mask = low if low == high else jnp.where(upper, high, low)
        total = total ^ (((place >> digit) & 1) * mask)
    return total


def own_index():
    return lax.axis_index("exp") * lax.axis_size("hid") + lax.axis_index("hid")


def in_hbm(*arrays):
    return tuple(pltpu.with_memory_space_constraint(a, pltpu.HBM) for a in arrays)


def piece_sum(experts, lanes, axis):
    shape = (lanes, experts) if axis == 0 else (experts, lanes)
    lane = lax.broadcasted_iota(jnp.int32, shape, axis)
    ids = lax.broadcasted_iota(jnp.int32, shape, 1 - axis)
    tally = jnp.zeros(shape, F32)
    for k in range(1, PIECES):
        tally = tally + jnp.where(lane == ids + k * experts, 1.0, 0.0)
    return tally.astype(BF16)


def combine_rows(extras, experts):
    hit = extras[:, :experts].astype(F32) > 0.5
    logits = jnp.dot(extras, piece_sum(experts, extras.shape[1], 0), preferred_element_type=F32)
    top = jnp.max(jnp.where(hit, logits, -jnp.inf), axis=1, keepdims=True)
    raised = jnp.where(hit, jnp.exp(jnp.minimum(logits - top, 0.0)), 0.0)
    return (raised / jnp.sum(raised, axis=1, keepdims=True)).astype(BF16).astype(F32)


def prep_kernel(tokens_in, grad_in, logits_in, chosen_in, out_ref, logits_ref, chosen_ref, sems):
    tok, width = tokens_in.shape
    pairs = [
        (logits_in, logits_ref),
        (chosen_in, chosen_ref),
        (tokens_in, out_ref.at[0, :, 0:width]),
        (grad_in, out_ref.at[1, :, 0:width]),
    ]
    copies = [pltpu.make_async_copy(src, dst, sems.at[i]) for i, (src, dst) in enumerate(pairs)]
    for copy in copies:
        copy.start()
    copies[0].wait()
    copies[1].wait()
    logits = logits_ref[...]
    chosen = chosen_ref[...]
    experts = logits.shape[1]
    ids = lax.broadcasted_iota(jnp.int32, logits.shape, 1)
    hit = ids == chosen[:, 0:1]
    for k in range(1, chosen.shape[1]):
        hit = hit | (ids == chosen[:, k : k + 1])
    parts = [jnp.where(hit, 1.0, 0.0)]
    rest = logits
    for _ in range(PIECES - 1):
        parts.append(rest)
        rest = rest - rest.astype(BF16).astype(F32)
    lanes = out_ref.shape[2] - width
    spare = lanes - PIECES * experts
    extras = jnp.concatenate(parts + ([jnp.zeros((tok, spare), F32)] if spare else []), axis=1)
    out_ref[0, :, width:] = extras.astype(BF16)
    out_ref[1, :, width:] = jnp.zeros((tok, lanes), BF16)
    copies[2].wait()
    copies[3].wait()


def hidden_parts(hidden):
    main = hidden // 256 * 256
    return [(0, main), (main, hidden)] if 0 < main < hidden else [(0, hidden)]


def load_kernel(chunks, block_in, gate_in, up_in, down_in, block_ref, pair_ref, down_ref, sems):
    copies = []

    def add(src, dst):
        copies.append(pltpu.make_async_copy(src, dst, sems.at[len(copies)]))

    hidden, width = down_ref.shape
    for c in range(chunks):
        part = pl.ds(c * (width // chunks), width // chunks)
        for first, last in hidden_parts(hidden):
            for k, ref in enumerate((gate_in, up_in)):
                to = 2 * first + k * (last - first)
                add(ref.at[0, part, first:last], pair_ref.at[part, to : to + last - first])
        part = pl.ds(c * (hidden // chunks), hidden // chunks)
        add(down_in.at[0, part, :], down_ref.at[part, :])
    add(block_in, block_ref)
    for copy in copies:
        copy.start()
    for copy in copies:
        copy.wait()


def join_kernel(*refs):
    blocks, out_ref, rows_ref = forward(refs[:-2]), refs[-2], refs[-1]
    count = len(blocks)
    tok = blocks[0].shape[1]
    for kind in range(2):
        for j, ref in enumerate(blocks):
            first = (kind * count + j) * tok
            rows_ref[first : first + tok, :] = ref[kind].astype(F32)
    out_ref[...] = rows_ref[...].astype(BF16)


def stack_kernel(*refs):
    out_ref = refs[-1]
    rows = refs[0].shape[0]
    for j, ref in enumerate(refs[:-1]):
        out_ref[j * rows : (j + 1) * rows, :] = ref[...]


def token_rows(refs, start, rows, group, kind, columns):
    parts = []
    for ref in refs:
        for j in range(rows // (2 * group)):
            first = start + (2 * j + kind) * group
            if not isinstance(first, int):
                first = pl.multiple_of(first, group)
            parts.append(ref[pl.ds(first, group), columns])
    return parts[0] if len(parts) == 1 else jnp.concatenate(parts, axis=0)


def put_scores(out_ref, scores_ref, width):
    rows = out_ref.shape[0]
    for c in range((out_ref.shape[1] - width) // LANES):
        out_ref[:, width + c * LANES : width + (c + 1) * LANES] = scores_ref[c * rows : (c + 1) * rows, :].astype(BF16)


def get_scores(in_ref, scores_ref, base, size, width):
    rows = in_ref.shape[0]
    for c in range(-(-size // rows)):
        here = min(rows, size - c * rows)
        tall = min(rows, -(-here // 16) * 16)
        block = in_ref[0:tall, width + c * LANES : width + (c + 1) * LANES].astype(F32)
        scores_ref[base + c * rows : base + c * rows + here, :] = block[:here]


def units_kernel(basis, group, tok, experts, core_mask, blocks, *refs):
    own_refs, other_refs = forward(refs[:blocks]), forward(refs[blocks : 2 * blocks])
    pair_ref, down_ref, kept_ref, message_ref, pieces_ref, score_ref, padded_ref = refs[2 * blocks :]
    hidden, width = down_ref.shape
    rows, buf_width = own_refs[0].shape
    tokens = score_ref.shape[1]
    own = own_index()

    def terms(sets, start, step):
        act = token_rows(sets, start, step, group, 0, slice(None))
        count = act.shape[0]
        combine = combine_rows(act[:, width:], experts)
        ids = lax.broadcasted_iota(jnp.int32, combine.shape, 1)
        column = jnp.sum(jnp.where(ids == own // 2, combine, 0.0), axis=1, keepdims=True)
        act = act[:, :width]
        cot = token_rows(sets, start, step, group, 1, slice(0, width))
        score = jnp.zeros((count, 1), F32)
        grads = []
        for first, last in hidden_parts(hidden):
            size = last - first
            pair = jnp.dot(act, pair_ref[:, 2 * first : 2 * last], preferred_element_type=F32)
            gate_pre = pair[:, :size]
            up_pre = pair[:, size:]
            back = lax.dot_general(cot, down_ref[first:last, :], NT, preferred_element_type=F32)
            sig = jax.nn.sigmoid(gate_pre)
            act_gate = gate_pre * sig
            score = score + jnp.sum(act_gate * up_pre * back, axis=1, keepdims=True)
            weighted = column * back
            grad_gate = weighted * up_pre * sig * (1.0 + gate_pre * (1.0 - sig))
            grad_up = weighted * act_gate
            grads += [grad_gate.astype(BF16), grad_up.astype(BF16)]
        grads = jnp.concatenate(grads, axis=1)
        return lax.dot_general(grads, pair_ref[...], NT, preferred_element_type=F32), score

    def in_order(score, place, swap_mask):
        token = lax.broadcasted_iota(jnp.int32, (score.shape[0], tokens), 1)
        side = own ^ swap_mask
        whole = (place_mask(place // tok, basis, side & core_mask != 0) ^ side) * tok + place % tok
        return jnp.sum(jnp.where(whole == token, score, 0.0), axis=0, keepdims=True)

    half = blocks * rows // 2
    if 2 * half <= 128:
        total, score = terms(own_refs + other_refs, 0, rows)
        kept_ref[...] = total[:half]
        message_ref[:, 0:width] = total[half:].astype(BF16)
        row = lax.broadcasted_iota(jnp.int32, (2 * half, tokens), 0)
        score_ref[...] = in_order(score, row % half, jnp.where(row < half, 0, core_mask))
    else:
        step = min(rows, 128)
        score_ref[...] = jnp.zeros(score_ref.shape, F32)
        for out_ref, sets, swap_mask in ((kept_ref, own_refs, 0), (message_ref, other_refs, core_mask)):
            for j, ref in enumerate(sets):

                def one(index):
                    total, score = terms((ref,), index * step, step)
                    first = pl.multiple_of(j * (rows // 2) + index * (step // 2), step // 2)
                    out_ref[pl.ds(first, step // 2), 0:width] = total.astype(out_ref.dtype)
                    place = lax.broadcasted_iota(jnp.int32, (step // 2, tokens), 0) + first
                    score_ref[...] += in_order(score, place, swap_mask)

                pl.loop(0, rows // step)(one)

    lane_blocks = tokens // LANES
    padded_ref[...] = jnp.zeros(padded_ref.shape, F32)
    value = score_ref[...]
    for piece in range(SCORE_PIECES):
        rounded = value.astype(BF16).astype(F32)
        for b in range(lane_blocks):
            at = piece * lane_blocks + b
            padded_ref[at : at + 1, :] = rounded[:, b * LANES : (b + 1) * LANES]
        value = value - rounded
    pieces_ref[...] = padded_ref[0 : pieces_ref.shape[0], :]
    put_scores(message_ref, padded_ref, width)


def add_kernel(arrivals, positions, low, *refs):
    kept_ref, pieces_ref = refs[0], refs[1]
    arrived = refs[2 : 2 + arrivals]
    outs = refs[2 + arrivals :]
    next_kept_ref, next_pieces_ref = outs[0], outs[1]
    sends = outs[2 : 2 + len(positions)]
    total_ref, scores_ref = outs[2 + len(positions) :]
    width = kept_ref.shape[1]
    size = pieces_ref.shape[0]
    total = kept_ref[...]
    for ref in arrived:
        total = total + ref[:, 0:width].astype(F32)
    total_ref[...] = total
    if scores_ref.shape[0] > next_pieces_ref.shape[0]:
        scores_ref[...] = jnp.zeros(scores_ref.shape, F32)
    scores_ref[0:size, :] = pieces_ref[...]
    for j, ref in enumerate(arrived):
        get_scores(ref, scores_ref, (j + 1) * size, size, width)
    rows = next_kept_ref.shape[0]
    next_kept_ref[...] = total_ref[0:rows, :]
    next_pieces_ref[...] = scores_ref[0 : next_pieces_ref.shape[0], :]
    chunks = [total_ref[j * rows : (j + 1) * rows, :] for j in range(total_ref.shape[0] // rows)]
    member = own_index() >> low & 3
    for position, ref in zip(positions, sends):
        if isinstance(position, int):
            chunk = chunks[position]
        else:
            chunk = by_member(member, [chunks[p] for p in position])
        ref[:, 0:width] = chunk.astype(BF16)
        put_scores(ref, scores_ref, width)


def table_kernel(basis, group, tok, core_mask, rows_out, blocks, after_ref, *refs):
    probs_ref, column_ref, mine_ref = refs[2 * blocks :]
    rows, buf_width = refs[0].shape
    half = blocks * rows // 2
    experts, tokens = probs_ref.shape
    lanes = -(-PIECES * experts // LANES) * LANES
    width = buf_width - lanes
    own = own_index()
    column = pl.multiple_of(own * rows_out // LANES * LANES, LANES)
    extras = jnp.zeros((tokens, lanes), F32)
    columns = jnp.zeros((tokens, LANES), F32)
    for index in range(2):
        sets = forward(refs[index * blocks : (index + 1) * blocks])
        row = lax.broadcasted_iota(jnp.int32, (half, tokens), 0)
        token = lax.broadcasted_iota(jnp.int32, (half, tokens), 1)
        side = own ^ (core_mask if index else 0)
        whole = (place_mask(row // tok, basis, side & core_mask != 0) ^ side) * tok + row % tok
        here = jnp.where(whole == token, 1.0, 0.0).astype(BF16)
        part = token_rows(sets, 0, rows, group, 0, slice(width, buf_width))
        extras = extras + lax.dot_general(here, part, TN, preferred_element_type=F32)
        part = token_rows(sets, 0, rows, group, 0, pl.ds(column, LANES))
        columns = columns + lax.dot_general(here, part, TN, preferred_element_type=F32)
    logits = lax.dot_general(piece_sum(experts, lanes, 1), extras.astype(BF16), NT, preferred_element_type=F32)
    raised = jnp.exp(logits - jnp.max(logits, axis=0, keepdims=True))
    probs_ref[...] = raised / jnp.sum(raised, axis=0, keepdims=True)
    column_ref[...] = columns.astype(BF16)
    row = lax.broadcasted_iota(jnp.int32, mine_ref.shape, 0)
    token = lax.broadcasted_iota(jnp.int32, mine_ref.shape, 1)
    mine_ref[...] = jnp.where((row < tok) & (token == own * tok + row), 1.0, 0.0).astype(BF16)


def final_kernel(arrivals, back_basis, core_mask, low, *refs):
    probs_ref, column_ref, mine_ref, router_ref, kept_ref, pieces_ref = refs[:6]
    arrived = refs[6 : 6 + arrivals]
    x_out, grad_out, x_ref, grad_ref, scores_ref, sems = refs[6 + arrivals :]
    experts, width = router_ref.shape
    size = pieces_ref.shape[0]
    tok = kept_ref.shape[0]
    own = own_index()
    scores_ref[0:size, :] = pieces_ref[...]
    for j, ref in enumerate(arrived):
        get_scores(ref, scores_ref, (j + 1) * size, size, width)
    blocks = probs_ref.shape[1] // LANES
    wide = scores_ref.shape[0] // blocks
    sender = lax.broadcasted_iota(jnp.int32, (experts, wide), 1) // SCORE_PIECES
    ids = lax.broadcasted_iota(jnp.int32, (experts, wide), 0)
    mask = place_mask(sender, back_basis, own & core_mask != 0)
    if low is not None:
        member = own >> low & 3
        source = sender >> len(back_basis)
        for k, step in enumerate(REDUCE_STEPS):
            come = by_member(member, [d ^ step.index(d) for d in range(4)]) << low
            mask = mask ^ jnp.where(source == k + 1, come, 0)
    pick = jnp.where(((mask ^ own) >> 1) == ids, 1.0, 0.0).astype(BF16)
    parts = []
    for b in range(blocks):
        block = scores_ref[...] if blocks == 1 else scores_ref[pl.ds(b, wide, stride=blocks), :]
        parts.append(jnp.dot(pick, block.astype(BF16), preferred_element_type=F32))
    scores = parts[0] if blocks == 1 else jnp.concatenate(parts, axis=1)
    probs = probs_ref[...]
    mean = jnp.sum(probs * scores, axis=0, keepdims=True)
    logit_grad = (probs * (scores - mean)).astype(BF16)
    mine = lax.dot_general(mine_ref[...], logit_grad, NT, preferred_element_type=F32)
    part = jnp.dot(mine.astype(BF16), router_ref[...], preferred_element_type=F32)
    total = kept_ref[...]
    for ref in arrived:
        total = total + ref[:, 0:width].astype(F32)
    x_ref[...] = (total + part[:tok]).astype(BF16)
    x_copy = pltpu.make_async_copy(x_ref, x_out, sems.at[0])
    x_copy.start()
    grad = jnp.dot(logit_grad, column_ref[...], preferred_element_type=F32)
    rows_out = grad_ref.shape[1]
    first = own * rows_out % LANES
    grad_ref[...] = pltpu.roll(grad, (LANES - first) % LANES, 1)[:, :rows_out]
    grad_copy = pltpu.make_async_copy(grad_ref, grad_out, sems.at[1])
    grad_copy.start()
    x_copy.wait()
    grad_copy.wait()


def on_device(tokens, grad_out, router_logits, selected, router_w, w_gate, w_up, w_down):
    tok, width = tokens.shape
    experts = router_logits.shape[1]
    hidden = w_gate.shape[2]
    exp_size = lax.axis_size("exp")
    hid_size = lax.axis_size("hid")
    count = exp_size * hid_size
    half = count // 2
    groups, core = stage_masks(exp_size, hid_size)
    core_mask = 1 << core
    basis = [m for group in groups for m in group]
    back_groups = [near_first(group) for group in groups[:0:-1]] + [groups[0]]
    core_pair = (core_mask, core_mask)
    low = (count - 1).bit_length() - 2 if len(groups[0]) == 2 else None
    if low is not None:
        back_groups = back_groups[:-1]
    back_basis = [core_pair] + [m for group in back_groups for m in group]
    if low is not None:
        back_groups = back_groups + [None]
    token_count = count * tok
    lanes = -(-PIECES * experts // LANES) * LANES

    block = pl.pallas_call(
        prep_kernel,
        out_shape=jax.ShapeDtypeStruct((2, tok, width + lanes), BF16),
        in_specs=[HBM_SPEC] * 4,
        out_specs=VMEM_SPEC,
        scratch_shapes=[
            pltpu.VMEM(router_logits.shape, router_logits.dtype),
            pltpu.VMEM(selected.shape, selected.dtype),
            pltpu.SemaphoreType.DMA((4,)),
        ],
        compiler_params=PARAMS,
        name="prep",
    )(*in_hbm(tokens, grad_out, router_logits, selected))

    masks = group_masks(groups[0])
    blocks = [block] + swaps(block, masks[1:], count, core)
    group_rows = tok * len(blocks)
    block = pl.pallas_call(
        join_kernel,
        out_shape=jax.ShapeDtypeStruct((2 * group_rows, width + lanes), BF16),
        in_specs=[VMEM_SPEC] * len(blocks),
        out_specs=VMEM_SPEC,
        scratch_shapes=[pltpu.VMEM((2 * group_rows, width + lanes), F32)],
        compiler_params=PARAMS,
        name="join",
    )(*forward(blocks))
    for group in groups[1:-1]:
        blocks = [block] + swaps(block, group_masks(group)[1:], count, core)
        block = pl.pallas_call(
            stack_kernel,
            out_shape=jax.ShapeDtypeStruct((len(blocks) * block.shape[0], block.shape[1]), BF16),
            in_specs=[VMEM_SPEC] * len(blocks),
            out_specs=VMEM_SPEC,
            compiler_params=PARAMS,
            name="stack",
        )(*blocks)
    chunks = 4
    copied, pair, down = pl.pallas_call(
        functools.partial(load_kernel, chunks),
        out_shape=(
            pltpu.VMEM(block.shape, BF16),
            pltpu.VMEM((width, 2 * hidden), BF16),
            pltpu.VMEM((hidden, width), BF16),
        ),
        in_specs=[VMEM_SPEC] + [HBM_SPEC] * 3,
        out_specs=(VMEM_SPEC,) * 3,
        scratch_shapes=[pltpu.SemaphoreType.DMA(((2 * len(hidden_parts(hidden)) + 1) * chunks + 1,))],
        compiler_params=pltpu.CompilerParams(vmem_limit_bytes=4 * 2**20),
        cost_estimate=pl.CostEstimate(flops=0, bytes_accessed=6 * width * hidden * 2, transcendentals=0),
        name="load",
    )(block, *in_hbm(w_gate, w_up, w_down))
    masks = group_masks(groups[-1]) if len(groups) > 1 else [core_pair]
    blocks = [block] + swaps(block, masks[1:], count, core)
    blocks = forward(blocks)
    blocks = blocks + [swap(b, core_pair, count, core) for b in [copied] + blocks[1:]]
    block_count = len(blocks) // 2

    unit_rows = SCORE_PIECES * token_count // LANES
    extra = -(-unit_rows // (half * tok)) * LANES
    kept, message, pieces = pl.pallas_call(
        functools.partial(units_kernel, basis, group_rows, tok, experts, core_mask, block_count),
        out_shape=(
            jax.ShapeDtypeStruct((half * tok, width), F32),
            jax.ShapeDtypeStruct((half * tok, width + extra), BF16),
            jax.ShapeDtypeStruct((unit_rows, LANES), F32),
        ),
        in_specs=[VMEM_SPEC] * (len(blocks) + 2),
        out_specs=(VMEM_SPEC,) * 3,
        scratch_shapes=[
            pltpu.VMEM((1, token_count), F32),
            pltpu.VMEM((max(half * tok * extra // LANES, unit_rows), LANES), F32),
        ],
        compiler_params=PARAMS,
        cost_estimate=pl.CostEstimate(
            flops=10 * token_count * width * hidden,
            bytes_accessed=3 * width * hidden * 2 + 2 * token_count * width * 2,
            transcendentals=token_count * hidden,
        ),
        name="units",
    )(*blocks, pair, down)

    arrived = [swap(message, core_pair, count, core)]
    tables = None
    rows_out = width // count
    for group, back_group in zip(groups[::-1], back_groups):
        order = [m[0] for m in group_masks(group)]
        if back_group is None:
            positions = [[order.index((d ^ step[d]) << low) for d in range(4)] for step in REDUCE_STEPS]
        else:
            back_masks = group_masks(back_group)
            positions = [order.index(m[0]) for m in back_masks[1:]]
        radix = len(order)
        rows = kept.shape[0]
        next_rows = rows // radix
        size = pieces.shape[0] * (1 + len(arrived))
        extra = -(-size // next_rows) * LANES
        sends = [jax.ShapeDtypeStruct((next_rows, width + extra), BF16)] * (radix - 1)
        outs = pl.pallas_call(
            functools.partial(add_kernel, len(arrived), positions, low or 0),
            out_shape=[
                jax.ShapeDtypeStruct((next_rows, width), F32),
                jax.ShapeDtypeStruct((size, LANES), F32),
            ]
            + sends,
            in_specs=[VMEM_SPEC] * (2 + len(arrived)),
            out_specs=[VMEM_SPEC] * (1 + radix),
            scratch_shapes=[
                pltpu.VMEM((rows, width), F32),
                pltpu.VMEM((max(next_rows * extra // LANES, size), LANES), F32),
            ],
            compiler_params=PARAMS,
            name="add",
        )(kept, pieces, *arrived)
        kept, pieces = outs[0], outs[1]
        if tables is None:
            tables = pl.pallas_call(
                functools.partial(table_kernel, basis, group_rows, tok, core_mask, rows_out, block_count),
                out_shape=(
                    jax.ShapeDtypeStruct((experts, token_count), F32),
                    jax.ShapeDtypeStruct((token_count, LANES), BF16),
                    jax.ShapeDtypeStruct((16, token_count), BF16),
                ),
                in_specs=[pl.BlockSpec(memory_space=pl.ANY)] + [VMEM_SPEC] * len(blocks),
                out_specs=(VMEM_SPEC,) * 3,
                compiler_params=PARAMS,
                cost_estimate=pl.CostEstimate(flops=10**9, bytes_accessed=10**6, transcendentals=0),
                name="tables",
            )(pieces, *blocks)
        if back_group is None:
            arrived = [shift(piece, step, count, low) for piece, step in zip(outs[2:], REDUCE_STEPS)]
        else:
            arrived = [swap(piece, m, count, core) for piece, m in zip(outs[2:], back_masks[1:])]

    x_grad, grad = pl.pallas_call(
        functools.partial(final_kernel, len(arrived), back_basis, core_mask, low),
        out_shape=(
            jax.ShapeDtypeStruct((tok, width), BF16),
            jax.ShapeDtypeStruct((experts, rows_out), F32),
        ),
        in_specs=[VMEM_SPEC] * (6 + len(arrived)),
        out_specs=(HBM_SPEC, HBM_SPEC),
        scratch_shapes=[
            pltpu.VMEM((tok, width), BF16),
            pltpu.VMEM((experts, rows_out), F32),
            pltpu.VMEM((pieces.shape[0] * (1 + len(arrived)), LANES), F32),
            pltpu.SemaphoreType.DMA((2,)),
        ],
        compiler_params=PARAMS,
        name="final",
    )(*tables, router_w.T, kept, pieces, *arrived)
    return (x_grad, grad.T)


def solution(mesh):
    rows = P(AXES, None)
    units = P(AXES, None, None)
    return jax.shard_map(
        on_device,
        mesh=mesh,
        in_specs=(rows, rows, rows, rows, P(), units, units, units),
        out_specs=(rows, rows),
        check_vma=False,
    )
```

```python
import functools

import jax
import jax.numpy as jnp
from jax import lax
from jax.experimental import pallas as pl
from jax.experimental.pallas import tpu as pltpu
from jax.sharding import PartitionSpec as P

AXES = ("exp", "hid")
LANES = 128
PIECES = 4
SCORE_PIECES = 2
VMEM_SPEC = pl.BlockSpec(memory_space=pltpu.VMEM)
HBM_SPEC = pl.BlockSpec(memory_space=pltpu.HBM)
F32 = jnp.float32
BF16 = jnp.bfloat16
NT = (((1,), (1,)), ((), ()))
TN = (((0,), (0,)), ((), ()))
PARAMS = pltpu.CompilerParams(vmem_limit_bytes=24 * 2**20)


def stage_masks(exp_size, hid_size):
    hid_bits = hid_size.bit_length() - 1
    all_bits = (exp_size * hid_size).bit_length() - 1
    core = hid_bits
    first = list(range(max(core + 1, all_bits - 2), all_bits))
    middle = [b for b in range(all_bits) if b != core and b not in first]
    groups = [first] + [middle[i : i + 2] for i in range(0, len(middle), 2)]
    bases = [[(sum(1 << b for b in group[i:]),) * 2 for i in range(len(group))] for group in groups]
    bases[0] = bases[0][::-1]
    return bases, core


def cross(a, b):
    return (a[0] ^ b[0], a[1] ^ b[1])


def group_masks(basis):
    masks = [(0, 0)]
    for mask in basis:
        masks = masks + [cross(m, mask) for m in masks]
    return masks


def near_first(basis):
    return [cross(basis[0], basis[1]), basis[1]] if len(basis) == 2 else basis


def swap(block, mask, count, core):
    return lax.ppermute(block, AXES, [(i, i ^ mask[i >> core & 1]) for i in range(count)])


GATHER_STEPS = ((2, 3, 1, 0), (3, 2, 0, 1), (1, 0, 3, 2))
REDUCE_STEPS = ((1, 2, 3, 0), (2, 3, 0, 1), (3, 0, 1, 2))


def by_member(member, values):
    total = values[0]
    for k in range(1, len(values)):
        total = jnp.where(member == k, values[k], total)
    return total


def shift(block, step, count, low):
    return lax.ppermute(block, AXES, [(i, i ^ ((i >> low & 3) ^ step[i >> low & 3]) << low) for i in range(count)])


def swaps(block, masks, count, core):
    return [swap(block, m, count, core) for m in masks]


def forward(blocks):
    return blocks[:1] + blocks[:0:-1]


def place_mask(place, basis, upper):
    total = jnp.zeros_like(place)
    for digit, (low, high) in enumerate(basis):
        mask = low if low == high else jnp.where(upper, high, low)
        total = total ^ (((place >> digit) & 1) * mask)
    return total


def own_index():
    return lax.axis_index("exp") * lax.axis_size("hid") + lax.axis_index("hid")


def in_hbm(*arrays):
    return tuple(pltpu.with_memory_space_constraint(a, pltpu.HBM) for a in arrays)


def piece_sum(experts, lanes, axis):
    shape = (lanes, experts) if axis == 0 else (experts, lanes)
    lane = lax.broadcasted_iota(jnp.int32, shape, axis)
    ids = lax.broadcasted_iota(jnp.int32, shape, 1 - axis)
    tally = jnp.zeros(shape, F32)
    for k in range(1, PIECES):
        tally = tally + jnp.where(lane == ids + k * experts, 1.0, 0.0)
    return tally.astype(BF16)


def combine_rows(extras, experts):
    hit = extras[:, :experts].astype(F32) > 0.5
    logits = jnp.dot(extras, piece_sum(experts, extras.shape[1], 0), preferred_element_type=F32)
    top = jnp.max(jnp.where(hit, logits, -jnp.inf), axis=1, keepdims=True)
    raised = jnp.where(hit, jnp.exp(jnp.minimum(logits - top, 0.0)), 0.0)
    return (raised / jnp.sum(raised, axis=1, keepdims=True)).astype(BF16).astype(F32)


def prep_kernel(tokens_in, grad_in, logits_in, chosen_in, out_ref, logits_ref, chosen_ref, sems):
    tok, width = tokens_in.shape
    pairs = [
        (logits_in, logits_ref),
        (chosen_in, chosen_ref),
        (tokens_in, out_ref.at[0, :, 0:width]),
        (grad_in, out_ref.at[1, :, 0:width]),
    ]
    copies = [pltpu.make_async_copy(src, dst, sems.at[i]) for i, (src, dst) in enumerate(pairs)]
    for copy in copies:
        copy.start()
    copies[0].wait()
    copies[1].wait()
    logits = logits_ref[...]
    chosen = chosen_ref[...]
    experts = logits.shape[1]
    ids = lax.broadcasted_iota(jnp.int32, logits.shape, 1)
    hit = ids == chosen[:, 0:1]
    for k in range(1, chosen.shape[1]):
        hit = hit | (ids == chosen[:, k : k + 1])
    parts = [jnp.where(hit, 1.0, 0.0)]
    rest = logits
    for _ in range(PIECES - 1):
        parts.append(rest)
        rest = rest - rest.astype(BF16).astype(F32)
    lanes = out_ref.shape[2] - width
    spare = lanes - PIECES * experts
    extras = jnp.concatenate(parts + ([jnp.zeros((tok, spare), F32)] if spare else []), axis=1)
    out_ref[0, :, width:] = extras.astype(BF16)
    out_ref[1, :, width:] = jnp.zeros((tok, lanes), BF16)
    copies[2].wait()
    copies[3].wait()


def hidden_parts(hidden):
    main = hidden // 256 * 256
    return [(0, main), (main, hidden)] if 0 < main < hidden else [(0, hidden)]


def load_kernel(chunks, block_in, gate_in, up_in, down_in, block_ref, pair_ref, down_ref, sems):
    copies = []

    def add(src, dst):
        copies.append(pltpu.make_async_copy(src, dst, sems.at[len(copies)]))

    hidden, width = down_ref.shape
    for c in range(chunks):
        part = pl.ds(c * (width // chunks), width // chunks)
        for first, last in hidden_parts(hidden):
            for k, ref in enumerate((gate_in, up_in)):
                to = 2 * first + k * (last - first)
                add(ref.at[0, part, first:last], pair_ref.at[part, to : to + last - first])
        part = pl.ds(c * (hidden // chunks), hidden // chunks)
        add(down_in.at[0, part, :], down_ref.at[part, :])
    add(block_in, block_ref)
    for copy in copies:
        copy.start()
    for copy in copies:
        copy.wait()


def join_kernel(order, low, *refs):
    blocks, out_ref, rows_ref = forward(refs[:-2]), refs[-2], refs[-1]
    count = len(blocks)
    tok = blocks[0].shape[1]
    member = own_index() >> low & 3
    for kind in range(2):
        rows = [ref[kind].astype(F32) for ref in blocks]
        if order is not None:
            come = [[d ^ step.index(d) for d in range(4)] for step in GATHER_STEPS]
            places = [[[c[d] for c in come].index(mask) for d in range(4)] for mask in order[1:]]
            rows = rows[:1] + [by_member(member, [rows[1 + k] for k in place]) for place in places]
        for j, value in enumerate(rows):
            first = (kind * count + j) * tok
            rows_ref[first : first + tok, :] = value
    out_ref[...] = rows_ref[...].astype(BF16)


def stack_kernel(*refs):
    out_ref = refs[-1]
    rows = refs[0].shape[0]
    for j, ref in enumerate(refs[:-1]):
        out_ref[j * rows : (j + 1) * rows, :] = ref[...]


def token_rows(refs, start, rows, group, kind, columns):
    parts = []
    for ref in refs:
        for j in range(rows // (2 * group)):
            first = start + (2 * j + kind) * group
            if not isinstance(first, int):
                first = pl.multiple_of(first, group)
            parts.append(ref[pl.ds(first, group), columns])
    return parts[0] if len(parts) == 1 else jnp.concatenate(parts, axis=0)


def put_scores(out_ref, scores_ref, width):
    rows = out_ref.shape[0]
    for c in range((out_ref.shape[1] - width) // LANES):
        out_ref[:, width + c * LANES : width + (c + 1) * LANES] = scores_ref[c * rows : (c + 1) * rows, :].astype(BF16)


def get_scores(in_ref, scores_ref, base, size, width):
    rows = in_ref.shape[0]
    for c in range(-(-size // rows)):
        here = min(rows, size - c * rows)
        tall = min(rows, -(-here // 16) * 16)
        block = in_ref[0:tall, width + c * LANES : width + (c + 1) * LANES].astype(F32)
        scores_ref[base + c * rows : base + c * rows + here, :] = block[:here]


def units_kernel(basis, group, tok, experts, core_mask, blocks, *refs):
    own_refs, other_refs = forward(refs[:blocks]), forward(refs[blocks : 2 * blocks])
    pair_ref, down_ref, kept_ref, message_ref, pieces_ref, score_ref, padded_ref = refs[2 * blocks :]
    hidden, width = down_ref.shape
    rows, buf_width = own_refs[0].shape
    tokens = score_ref.shape[1]
    own = own_index()

    def terms(sets, start, step):
        act = token_rows(sets, start, step, group, 0, slice(None))
        count = act.shape[0]
        combine = combine_rows(act[:, width:], experts)
        ids = lax.broadcasted_iota(jnp.int32, combine.shape, 1)
        column = jnp.sum(jnp.where(ids == own // 2, combine, 0.0), axis=1, keepdims=True)
        act = act[:, :width]
        cot = token_rows(sets, start, step, group, 1, slice(0, width))
        score = jnp.zeros((count, 1), F32)
        grads = []
        for first, last in hidden_parts(hidden):
            size = last - first
            pair = jnp.dot(act, pair_ref[:, 2 * first : 2 * last], preferred_element_type=F32)
            gate_pre = pair[:, :size]
            up_pre = pair[:, size:]
            back = lax.dot_general(cot, down_ref[first:last, :], NT, preferred_element_type=F32)
            sig = jax.nn.sigmoid(gate_pre)
            act_gate = gate_pre * sig
            score = score + jnp.sum(act_gate * up_pre * back, axis=1, keepdims=True)
            weighted = column * back
            grad_gate = weighted * up_pre * sig * (1.0 + gate_pre * (1.0 - sig))
            grad_up = weighted * act_gate
            grads += [grad_gate.astype(BF16), grad_up.astype(BF16)]
        grads = jnp.concatenate(grads, axis=1)
        return lax.dot_general(grads, pair_ref[...], NT, preferred_element_type=F32), score

    def in_order(score, place, swap_mask):
        token = lax.broadcasted_iota(jnp.int32, (score.shape[0], tokens), 1)
        side = own ^ swap_mask
        whole = (place_mask(place // tok, basis, side & core_mask != 0) ^ side) * tok + place % tok
        return jnp.sum(jnp.where(whole == token, score, 0.0), axis=0, keepdims=True)

    half = blocks * rows // 2
    if 2 * half <= 128:
        total, score = terms(own_refs + other_refs, 0, rows)
        kept_ref[...] = total[:half]
        message_ref[:, 0:width] = total[half:].astype(BF16)
        row = lax.broadcasted_iota(jnp.int32, (2 * half, tokens), 0)
        score_ref[...] = in_order(score, row % half, jnp.where(row < half, 0, core_mask))
    else:
        step = min(rows, 128)
        score_ref[...] = jnp.zeros(score_ref.shape, F32)
        for out_ref, sets, swap_mask in ((kept_ref, own_refs, 0), (message_ref, other_refs, core_mask)):
            for j, ref in enumerate(sets):

                def one(index):
                    total, score = terms((ref,), index * step, step)
                    first = pl.multiple_of(j * (rows // 2) + index * (step // 2), step // 2)
                    out_ref[pl.ds(first, step // 2), 0:width] = total.astype(out_ref.dtype)
                    place = lax.broadcasted_iota(jnp.int32, (step // 2, tokens), 0) + first
                    score_ref[...] += in_order(score, place, swap_mask)

                pl.loop(0, rows // step)(one)

    lane_blocks = tokens // LANES
    padded_ref[...] = jnp.zeros(padded_ref.shape, F32)
    value = score_ref[...]
    for piece in range(SCORE_PIECES):
        rounded = value.astype(BF16).astype(F32)
        for b in range(lane_blocks):
            at = piece * lane_blocks + b
            padded_ref[at : at + 1, :] = rounded[:, b * LANES : (b + 1) * LANES]
        value = value - rounded
    pieces_ref[...] = padded_ref[0 : pieces_ref.shape[0], :]
    put_scores(message_ref, padded_ref, width)


def add_kernel(arrivals, positions, low, *refs):
    kept_ref, pieces_ref = refs[0], refs[1]
    arrived = refs[2 : 2 + arrivals]
    outs = refs[2 + arrivals :]
    next_kept_ref, next_pieces_ref = outs[0], outs[1]
    sends = outs[2 : 2 + len(positions)]
    total_ref, scores_ref = outs[2 + len(positions) :]
    width = kept_ref.shape[1]
    size = pieces_ref.shape[0]
    total = kept_ref[...]
    for ref in arrived:
        total = total + ref[:, 0:width].astype(F32)
    total_ref[...] = total
    if scores_ref.shape[0] > next_pieces_ref.shape[0]:
        scores_ref[...] = jnp.zeros(scores_ref.shape, F32)
    scores_ref[0:size, :] = pieces_ref[...]
    for j, ref in enumerate(arrived):
        get_scores(ref, scores_ref, (j + 1) * size, size, width)
    rows = next_kept_ref.shape[0]
    next_kept_ref[...] = total_ref[0:rows, :]
    next_pieces_ref[...] = scores_ref[0 : next_pieces_ref.shape[0], :]
    chunks = [total_ref[j * rows : (j + 1) * rows, :] for j in range(total_ref.shape[0] // rows)]
    member = own_index() >> low & 3
    for position, ref in zip(positions, sends):
        if isinstance(position, int):
            chunk = chunks[position]
        else:
            chunk = by_member(member, [chunks[p] for p in position])
        ref[:, 0:width] = chunk.astype(BF16)
        put_scores(ref, scores_ref, width)


def table_kernel(basis, group, tok, core_mask, rows_out, blocks, after_ref, *refs):
    probs_ref, column_ref, mine_ref = refs[2 * blocks :]
    rows, buf_width = refs[0].shape
    half = blocks * rows // 2
    experts, tokens = probs_ref.shape
    lanes = -(-PIECES * experts // LANES) * LANES
    width = buf_width - lanes
    own = own_index()
    column = pl.multiple_of(own * rows_out // LANES * LANES, LANES)
    extras = jnp.zeros((tokens, lanes), F32)
    columns = jnp.zeros((tokens, LANES), F32)
    for index in range(2):
        sets = forward(refs[index * blocks : (index + 1) * blocks])
        row = lax.broadcasted_iota(jnp.int32, (half, tokens), 0)
        token = lax.broadcasted_iota(jnp.int32, (half, tokens), 1)
        side = own ^ (core_mask if index else 0)
        whole = (place_mask(row // tok, basis, side & core_mask != 0) ^ side) * tok + row % tok
        here = jnp.where(whole == token, 1.0, 0.0).astype(BF16)
        part = token_rows(sets, 0, rows, group, 0, slice(width, buf_width))
        extras = extras + lax.dot_general(here, part, TN, preferred_element_type=F32)
        part = token_rows(sets, 0, rows, group, 0, pl.ds(column, LANES))
        columns = columns + lax.dot_general(here, part, TN, preferred_element_type=F32)
    logits = lax.dot_general(piece_sum(experts, lanes, 1), extras.astype(BF16), NT, preferred_element_type=F32)
    raised = jnp.exp(logits - jnp.max(logits, axis=0, keepdims=True))
    probs_ref[...] = raised / jnp.sum(raised, axis=0, keepdims=True)
    column_ref[...] = columns.astype(BF16)
    row = lax.broadcasted_iota(jnp.int32, mine_ref.shape, 0)
    token = lax.broadcasted_iota(jnp.int32, mine_ref.shape, 1)
    mine_ref[...] = jnp.where((row < tok) & (token == own * tok + row), 1.0, 0.0).astype(BF16)


def final_kernel(arrivals, back_basis, core_mask, low, *refs):
    probs_ref, column_ref, mine_ref, router_ref, kept_ref, pieces_ref = refs[:6]
    arrived = refs[6 : 6 + arrivals]
    x_out, grad_out, x_ref, grad_ref, scores_ref, sems = refs[6 + arrivals :]
    experts, width = router_ref.shape
    size = pieces_ref.shape[0]
    tok = kept_ref.shape[0]
    own = own_index()
    scores_ref[0:size, :] = pieces_ref[...]
    for j, ref in enumerate(arrived):
        get_scores(ref, scores_ref, (j + 1) * size, size, width)
    blocks = probs_ref.shape[1] // LANES
    wide = scores_ref.shape[0] // blocks
    sender = lax.broadcasted_iota(jnp.int32, (experts, wide), 1) // SCORE_PIECES
    ids = lax.broadcasted_iota(jnp.int32, (experts, wide), 0)
    mask = place_mask(sender, back_basis, own & core_mask != 0)
    if low is not None:
        member = own >> low & 3
        source = sender >> len(back_basis)
        for k, step in enumerate(REDUCE_STEPS):
            come = by_member(member, [d ^ step.index(d) for d in range(4)]) << low
            mask = mask ^ jnp.where(source == k + 1, come, 0)
    pick = jnp.where(((mask ^ own) >> 1) == ids, 1.0, 0.0).astype(BF16)
    parts = []
    for b in range(blocks):
        block = scores_ref[...] if blocks == 1 else scores_ref[pl.ds(b, wide, stride=blocks), :]
        parts.append(jnp.dot(pick, block.astype(BF16), preferred_element_type=F32))
    scores = parts[0] if blocks == 1 else jnp.concatenate(parts, axis=1)
    probs = probs_ref[...]
    mean = jnp.sum(probs * scores, axis=0, keepdims=True)
    logit_grad = (probs * (scores - mean)).astype(BF16)
    mine = lax.dot_general(mine_ref[...], logit_grad, NT, preferred_element_type=F32)
    part = jnp.dot(mine.astype(BF16), router_ref[...], preferred_element_type=F32)
    total = kept_ref[...]
    for ref in arrived:
        total = total + ref[:, 0:width].astype(F32)
    x_ref[...] = (total + part[:tok]).astype(BF16)
    x_copy = pltpu.make_async_copy(x_ref, x_out, sems.at[0])
    x_copy.start()
    grad = jnp.dot(logit_grad, column_ref[...], preferred_element_type=F32)
    rows_out = grad_ref.shape[1]
    first = own * rows_out % LANES
    grad_ref[...] = pltpu.roll(grad, (LANES - first) % LANES, 1)[:, :rows_out]
    grad_copy = pltpu.make_async_copy(grad_ref, grad_out, sems.at[1])
    grad_copy.start()
    x_copy.wait()
    grad_copy.wait()


def on_device(tokens, grad_out, router_logits, selected, router_w, w_gate, w_up, w_down):
    tok, width = tokens.shape
    experts = router_logits.shape[1]
    hidden = w_gate.shape[2]
    exp_size = lax.axis_size("exp")
    hid_size = lax.axis_size("hid")
    count = exp_size * hid_size
    half = count // 2
    groups, core = stage_masks(exp_size, hid_size)
    core_mask = 1 << core
    basis = [m for group in groups for m in group]
    back_groups = [near_first(group) for group in groups[:0:-1]] + [groups[0]]
    core_pair = (core_mask, core_mask)
    low = (count - 1).bit_length() - 2 if len(groups[0]) == 2 else None
    if low is not None:
        back_groups = back_groups[:-1]
    back_basis = [core_pair] + [m for group in back_groups for m in group]
    if low is not None:
        back_groups = back_groups + [None]
    token_count = count * tok
    lanes = -(-PIECES * experts // LANES) * LANES

    block = pl.pallas_call(
        prep_kernel,
        out_shape=jax.ShapeDtypeStruct((2, tok, width + lanes), BF16),
        in_specs=[HBM_SPEC] * 4,
        out_specs=VMEM_SPEC,
        scratch_shapes=[
            pltpu.VMEM(router_logits.shape, router_logits.dtype),
            pltpu.VMEM(selected.shape, selected.dtype),
            pltpu.SemaphoreType.DMA((4,)),
        ],
        compiler_params=PARAMS,
        name="prep",
    )(*in_hbm(tokens, grad_out, router_logits, selected))

    order = None
    if low is None:
        blocks = [block] + swaps(block, group_masks(groups[0])[1:], count, core)
    else:
        order = [m[0] >> low for m in group_masks(groups[0])]
        blocks = [block] + [shift(block, step, count, low) for step in GATHER_STEPS]
    group_rows = tok * len(blocks)
    block = pl.pallas_call(
        functools.partial(join_kernel, order, low or 0),
        out_shape=jax.ShapeDtypeStruct((2 * group_rows, width + lanes), BF16),
        in_specs=[VMEM_SPEC] * len(blocks),
        out_specs=VMEM_SPEC,
        scratch_shapes=[pltpu.VMEM((2 * group_rows, width + lanes), F32)],
        compiler_params=PARAMS,
        name="join",
    )(*forward(blocks))
    for group in groups[1:-1]:
        blocks = [block] + swaps(block, group_masks(group)[1:], count, core)
        block = pl.pallas_call(
            stack_kernel,
            out_shape=jax.ShapeDtypeStruct((len(blocks) * block.shape[0], block.shape[1]), BF16),
            in_specs=[VMEM_SPEC] * len(blocks),
            out_specs=VMEM_SPEC,
            compiler_params=PARAMS,
            name="stack",
        )(*blocks)
    chunks = 4
    copied, pair, down = pl.pallas_call(
        functools.partial(load_kernel, chunks),
        out_shape=(
            pltpu.VMEM(block.shape, BF16),
            pltpu.VMEM((width, 2 * hidden), BF16),
            pltpu.VMEM((hidden, width), BF16),
        ),
        in_specs=[VMEM_SPEC] + [HBM_SPEC] * 3,
        out_specs=(VMEM_SPEC,) * 3,
        scratch_shapes=[pltpu.SemaphoreType.DMA(((2 * len(hidden_parts(hidden)) + 1) * chunks + 1,))],
        compiler_params=pltpu.CompilerParams(vmem_limit_bytes=4 * 2**20),
        cost_estimate=pl.CostEstimate(flops=0, bytes_accessed=6 * width * hidden * 2, transcendentals=0),
        name="load",
    )(block, *in_hbm(w_gate, w_up, w_down))
    masks = group_masks(groups[-1]) if len(groups) > 1 else [core_pair]
    blocks = [block] + swaps(block, masks[1:], count, core)
    blocks = forward(blocks)
    blocks = blocks + [swap(b, core_pair, count, core) for b in [copied] + blocks[1:]]
    block_count = len(blocks) // 2

    unit_rows = SCORE_PIECES * token_count // LANES
    extra = -(-unit_rows // (half * tok)) * LANES
    kept, message, pieces = pl.pallas_call(
        functools.partial(units_kernel, basis, group_rows, tok, experts, core_mask, block_count),
        out_shape=(
            jax.ShapeDtypeStruct((half * tok, width), F32),
            jax.ShapeDtypeStruct((half * tok, width + extra), BF16),
            jax.ShapeDtypeStruct((unit_rows, LANES), F32),
        ),
        in_specs=[VMEM_SPEC] * (len(blocks) + 2),
        out_specs=(VMEM_SPEC,) * 3,
        scratch_shapes=[
            pltpu.VMEM((1, token_count), F32),
            pltpu.VMEM((max(half * tok * extra // LANES, unit_rows), LANES), F32),
        ],
        compiler_params=PARAMS,
        cost_estimate=pl.CostEstimate(
            flops=10 * token_count * width * hidden,
            bytes_accessed=3 * width * hidden * 2 + 2 * token_count * width * 2,
            transcendentals=token_count * hidden,
        ),
        name="units",
    )(*blocks, pair, down)

    arrived = [swap(message, core_pair, count, core)]
    tables = None
    rows_out = width // count
    for group, back_group in zip(groups[::-1], back_groups):
        order = [m[0] for m in group_masks(group)]
        if back_group is None:
            positions = [[order.index((d ^ step[d]) << low) for d in range(4)] for step in REDUCE_STEPS]
        else:
            back_masks = group_masks(back_group)
            positions = [order.index(m[0]) for m in back_masks[1:]]
        radix = len(order)
        rows = kept.shape[0]
        next_rows = rows // radix
        size = pieces.shape[0] * (1 + len(arrived))
        extra = -(-size // next_rows) * LANES
        sends = [jax.ShapeDtypeStruct((next_rows, width + extra), BF16)] * (radix - 1)
        outs = pl.pallas_call(
            functools.partial(add_kernel, len(arrived), positions, low or 0),
            out_shape=[
                jax.ShapeDtypeStruct((next_rows, width), F32),
                jax.ShapeDtypeStruct((size, LANES), F32),
            ]
            + sends,
            in_specs=[VMEM_SPEC] * (2 + len(arrived)),
            out_specs=[VMEM_SPEC] * (1 + radix),
            scratch_shapes=[
                pltpu.VMEM((rows, width), F32),
                pltpu.VMEM((max(next_rows * extra // LANES, size), LANES), F32),
            ],
            compiler_params=PARAMS,
            name="add",
        )(kept, pieces, *arrived)
        kept, pieces = outs[0], outs[1]
        if tables is None:
            tables = pl.pallas_call(
                functools.partial(table_kernel, basis, group_rows, tok, core_mask, rows_out, block_count),
                out_shape=(
                    jax.ShapeDtypeStruct((experts, token_count), F32),
                    jax.ShapeDtypeStruct((token_count, LANES), BF16),
                    jax.ShapeDtypeStruct((16, token_count), BF16),
                ),
                in_specs=[pl.BlockSpec(memory_space=pl.ANY)] + [VMEM_SPEC] * len(blocks),
                out_specs=(VMEM_SPEC,) * 3,
                compiler_params=PARAMS,
                cost_estimate=pl.CostEstimate(flops=10**9, bytes_accessed=10**6, transcendentals=0),
                name="tables",
            )(pieces, *blocks)
        if back_group is None:
            arrived = [shift(piece, step, count, low) for piece, step in zip(outs[2:], REDUCE_STEPS)]
        else:
            arrived = [swap(piece, m, count, core) for piece, m in zip(outs[2:], back_masks[1:])]

    x_grad, grad = pl.pallas_call(
        functools.partial(final_kernel, len(arrived), back_basis, core_mask, low),
        out_shape=(
            jax.ShapeDtypeStruct((tok, width), BF16),
            jax.ShapeDtypeStruct((experts, rows_out), F32),
        ),
        in_specs=[VMEM_SPEC] * (6 + len(arrived)),
        out_specs=(HBM_SPEC, HBM_SPEC),
        scratch_shapes=[
            pltpu.VMEM((tok, width), BF16),
            pltpu.VMEM((experts, rows_out), F32),
            pltpu.VMEM((pieces.shape[0] * (1 + len(arrived)), LANES), F32),
            pltpu.SemaphoreType.DMA((2,)),
        ],
        compiler_params=PARAMS,
        name="final",
    )(*tables, router_w.T, kept, pieces, *arrived)
    return (x_grad, grad.T)


def solution(mesh):
    rows = P(AXES, None)
    units = P(AXES, None, None)
    return jax.shard_map(
        on_device,
        mesh=mesh,
        in_specs=(rows, rows, rows, rows, P(), units, units, units),
        out_specs=(rows, rows),
        check_vma=False,
    )
```

```python
import functools

import jax
import jax.numpy as jnp
from jax import lax
from jax.experimental import pallas as pl
from jax.experimental.pallas import tpu as pltpu
from jax.sharding import PartitionSpec as P

AXES = ("exp", "hid")
LANES = 128
PIECES = 4
SCORE_PIECES = 2
VMEM_SPEC = pl.BlockSpec(memory_space=pltpu.VMEM)
HBM_SPEC = pl.BlockSpec(memory_space=pltpu.HBM)
F32 = jnp.float32
BF16 = jnp.bfloat16
NT = (((1,), (1,)), ((), ()))
TN = (((0,), (0,)), ((), ()))
PARAMS = pltpu.CompilerParams(vmem_limit_bytes=24 * 2**20)


def stage_masks(exp_size, hid_size):
    hid_bits = hid_size.bit_length() - 1
    all_bits = (exp_size * hid_size).bit_length() - 1
    core = hid_bits
    first = list(range(max(core + 1, all_bits - 2), all_bits))
    middle = [b for b in range(all_bits) if b != core and b not in first]
    groups = [first] + [middle[i : i + 2] for i in range(0, len(middle), 2)]
    bases = [[(sum(1 << b for b in group[i:]),) * 2 for i in range(len(group))] for group in groups]
    bases[0] = bases[0][::-1]
    return bases, core


def cross(a, b):
    return (a[0] ^ b[0], a[1] ^ b[1])


def group_masks(basis):
    masks = [(0, 0)]
    for mask in basis:
        masks = masks + [cross(m, mask) for m in masks]
    return masks


def near_first(basis):
    return [cross(basis[0], basis[1]), basis[1]] if len(basis) == 2 else basis


def swap(block, mask, count, core):
    return lax.ppermute(block, AXES, [(i, i ^ mask[i >> core & 1]) for i in range(count)])


GATHER_STEPS = ((2, 3, 1, 0), (3, 2, 0, 1), (1, 0, 3, 2))
REDUCE_STEPS = (
    (1, 2, None, 0),
    (2, None, 0, 1),
    (3, 0, 1, 2),
    (None, 3, None, None),
    (None, None, 3, None),
)


def by_member(member, values):
    total = values[0]
    for k in range(1, len(values)):
        total = jnp.where(member == k, values[k], total)
    return total


def shift(block, step, count, low):
    pairs = [(i, step[i >> low & 3]) for i in range(count)]
    return lax.ppermute(block, AXES, [(i, i & ~(3 << low) | to << low) for i, to in pairs if to is not None])


def mask_from(step, member):
    return member ^ step.index(member) if member in step else 0


def swaps(block, masks, count, core):
    return [swap(block, m, count, core) for m in masks]


def forward(blocks):
    return blocks[:1] + blocks[:0:-1]


def place_mask(place, basis, upper):
    total = jnp.zeros_like(place)
    for digit, (low, high) in enumerate(basis):
        mask = low if low == high else jnp.where(upper, high, low)
        total = total ^ (((place >> digit) & 1) * mask)
    return total


def own_index():
    return lax.axis_index("exp") * lax.axis_size("hid") + lax.axis_index("hid")


def in_hbm(*arrays):
    return tuple(pltpu.with_memory_space_constraint(a, pltpu.HBM) for a in arrays)


def piece_sum(experts, lanes, axis):
    shape = (lanes, experts) if axis == 0 else (experts, lanes)
    lane = lax.broadcasted_iota(jnp.int32, shape, axis)
    ids = lax.broadcasted_iota(jnp.int32, shape, 1 - axis)
    tally = jnp.zeros(shape, F32)
    for k in range(1, PIECES):
        tally = tally + jnp.where(lane == ids + k * experts, 1.0, 0.0)
    return tally.astype(BF16)


def combine_rows(extras, experts):
    hit = extras[:, :experts].astype(F32) > 0.5
    logits = jnp.dot(extras, piece_sum(experts, extras.shape[1], 0), preferred_element_type=F32)
    top = jnp.max(jnp.where(hit, logits, -jnp.inf), axis=1, keepdims=True)
    raised = jnp.where(hit, jnp.exp(jnp.minimum(logits - top, 0.0)), 0.0)
    return (raised / jnp.sum(raised, axis=1, keepdims=True)).astype(BF16).astype(F32)


def prep_kernel(tokens_in, grad_in, logits_in, chosen_in, out_ref, logits_ref, chosen_ref, sems):
    tok, width = tokens_in.shape
    pairs = [
        (logits_in, logits_ref),
        (chosen_in, chosen_ref),
        (tokens_in, out_ref.at[0, :, 0:width]),
        (grad_in, out_ref.at[1, :, 0:width]),
    ]
    copies = [pltpu.make_async_copy(src, dst, sems.at[i]) for i, (src, dst) in enumerate(pairs)]
    for copy in copies:
        copy.start()
    copies[0].wait()
    copies[1].wait()
    logits = logits_ref[...]
    chosen = chosen_ref[...]
    experts = logits.shape[1]
    ids = lax.broadcasted_iota(jnp.int32, logits.shape, 1)
    hit = ids == chosen[:, 0:1]
    for k in range(1, chosen.shape[1]):
        hit = hit | (ids == chosen[:, k : k + 1])
    parts = [jnp.where(hit, 1.0, 0.0)]
    rest = logits
    for _ in range(PIECES - 1):
        parts.append(rest)
        rest = rest - rest.astype(BF16).astype(F32)
    lanes = out_ref.shape[2] - width
    spare = lanes - PIECES * experts
    extras = jnp.concatenate(parts + ([jnp.zeros((tok, spare), F32)] if spare else []), axis=1)
    out_ref[0, :, width:] = extras.astype(BF16)
    out_ref[1, :, width:] = jnp.zeros((tok, lanes), BF16)
    copies[2].wait()
    copies[3].wait()


def hidden_parts(hidden):
    main = hidden // 256 * 256
    return [(0, main), (main, hidden)] if 0 < main < hidden else [(0, hidden)]


def load_kernel(chunks, block_in, gate_in, up_in, down_in, block_ref, pair_ref, down_ref, sems):
    copies = []

    def add(src, dst):
        copies.append(pltpu.make_async_copy(src, dst, sems.at[len(copies)]))

    hidden, width = down_ref.shape
    for c in range(chunks):
        part = pl.ds(c * (width // chunks), width // chunks)
        for first, last in hidden_parts(hidden):
            for k, ref in enumerate((gate_in, up_in)):
                to = 2 * first + k * (last - first)
                add(ref.at[0, part, first:last], pair_ref.at[part, to : to + last - first])
        part = pl.ds(c * (hidden // chunks), hidden // chunks)
        add(down_in.at[0, part, :], down_ref.at[part, :])
    add(block_in, block_ref)
    for copy in copies:
        copy.start()
    for copy in copies:
        copy.wait()


def join_kernel(order, low, *refs):
    blocks, out_ref, rows_ref = forward(refs[:-2]), refs[-2], refs[-1]
    count = len(blocks)
    tok = blocks[0].shape[1]
    member = own_index() >> low & 3
    for kind in range(2):
        rows = [ref[kind].astype(F32) for ref in blocks]
        if order is not None:
            come = [[mask_from(step, d) for d in range(4)] for step in GATHER_STEPS]
            places = [[[c[d] for c in come].index(mask) for d in range(4)] for mask in order[1:]]
            rows = rows[:1] + [by_member(member, [rows[1 + k] for k in place]) for place in places]
        for j, value in enumerate(rows):
            first = (kind * count + j) * tok
            rows_ref[first : first + tok, :] = value
    out_ref[...] = rows_ref[...].astype(BF16)


def stack_kernel(*refs):
    out_ref = refs[-1]
    rows = refs[0].shape[0]
    for j, ref in enumerate(refs[:-1]):
        out_ref[j * rows : (j + 1) * rows, :] = ref[...]


def token_rows(refs, start, rows, group, kind, columns):
    parts = []
    for ref in refs:
        for j in range(rows // (2 * group)):
            first = start + (2 * j + kind) * group
            if not isinstance(first, int):
                first = pl.multiple_of(first, group)
            parts.append(ref[pl.ds(first, group), columns])
    return parts[0] if len(parts) == 1 else jnp.concatenate(parts, axis=0)


def put_scores(out_ref, scores_ref, width):
    rows = out_ref.shape[0]
    for c in range((out_ref.shape[1] - width) // LANES):
        out_ref[:, width + c * LANES : width + (c + 1) * LANES] = scores_ref[c * rows : (c + 1) * rows, :].astype(BF16)


def get_scores(in_ref, scores_ref, base, size, width):
    rows = in_ref.shape[0]
    for c in range(-(-size // rows)):
        here = min(rows, size - c * rows)
        tall = min(rows, -(-here // 16) * 16)
        block = in_ref[0:tall, width + c * LANES : width + (c + 1) * LANES].astype(F32)
        scores_ref[base + c * rows : base + c * rows + here, :] = block[:here]


def units_kernel(basis, group, tok, experts, core_mask, blocks, *refs):
    own_refs, other_refs = forward(refs[:blocks]), forward(refs[blocks : 2 * blocks])
    pair_ref, down_ref, kept_ref, message_ref, pieces_ref, score_ref, padded_ref = refs[2 * blocks :]
    hidden, width = down_ref.shape
    rows, buf_width = own_refs[0].shape
    tokens = score_ref.shape[1]
    own = own_index()

    def terms(sets, start, step):
        act = token_rows(sets, start, step, group, 0, slice(None))
        count = act.shape[0]
        combine = combine_rows(act[:, width:], experts)
        ids = lax.broadcasted_iota(jnp.int32, combine.shape, 1)
        column = jnp.sum(jnp.where(ids == own // 2, combine, 0.0), axis=1, keepdims=True)
        act = act[:, :width]
        cot = token_rows(sets, start, step, group, 1, slice(0, width))
        score = jnp.zeros((count, 1), F32)
        grads = []
        for first, last in hidden_parts(hidden):
            size = last - first
            pair = jnp.dot(act, pair_ref[:, 2 * first : 2 * last], preferred_element_type=F32)
            gate_pre = pair[:, :size]
            up_pre = pair[:, size:]
            back = lax.dot_general(cot, down_ref[first:last, :], NT, preferred_element_type=F32)
            sig = jax.nn.sigmoid(gate_pre)
            act_gate = gate_pre * sig
            score = score + jnp.sum(act_gate * up_pre * back, axis=1, keepdims=True)
            weighted = column * back
            grad_gate = weighted * up_pre * sig * (1.0 + gate_pre * (1.0 - sig))
            grad_up = weighted * act_gate
            grads += [grad_gate.astype(BF16), grad_up.astype(BF16)]
        grads = jnp.concatenate(grads, axis=1)
        return lax.dot_general(grads, pair_ref[...], NT, preferred_element_type=F32), score

    def in_order(score, place, swap_mask):
        token = lax.broadcasted_iota(jnp.int32, (score.shape[0], tokens), 1)
        side = own ^ swap_mask
        whole = (place_mask(place // tok, basis, side & core_mask != 0) ^ side) * tok + place % tok
        return jnp.sum(jnp.where(whole == token, score, 0.0), axis=0, keepdims=True)

    half = blocks * rows // 2
    if 2 * half <= 128:
        total, score = terms(own_refs + other_refs, 0, rows)
        kept_ref[...] = total[:half]
        message_ref[:, 0:width] = total[half:].astype(BF16)
        row = lax.broadcasted_iota(jnp.int32, (2 * half, tokens), 0)
        score_ref[...] = in_order(score, row % half, jnp.where(row < half, 0, core_mask))
    else:
        step = min(rows, 128)
        score_ref[...] = jnp.zeros(score_ref.shape, F32)
        for out_ref, sets, swap_mask in ((kept_ref, own_refs, 0), (message_ref, other_refs, core_mask)):
            for j, ref in enumerate(sets):

                def one(index):
                    total, score = terms((ref,), index * step, step)
                    first = pl.multiple_of(j * (rows // 2) + index * (step // 2), step // 2)
                    out_ref[pl.ds(first, step // 2), 0:width] = total.astype(out_ref.dtype)
                    place = lax.broadcasted_iota(jnp.int32, (step // 2, tokens), 0) + first
                    score_ref[...] += in_order(score, place, swap_mask)

                pl.loop(0, rows // step)(one)

    lane_blocks = tokens // LANES
    padded_ref[...] = jnp.zeros(padded_ref.shape, F32)
    value = score_ref[...]
    for piece in range(SCORE_PIECES):
        rounded = value.astype(BF16).astype(F32)
        for b in range(lane_blocks):
            at = piece * lane_blocks + b
            padded_ref[at : at + 1, :] = rounded[:, b * LANES : (b + 1) * LANES]
        value = value - rounded
    pieces_ref[...] = padded_ref[0 : pieces_ref.shape[0], :]
    put_scores(message_ref, padded_ref, width)


def add_kernel(arrivals, positions, low, *refs):
    kept_ref, pieces_ref = refs[0], refs[1]
    arrived = refs[2 : 2 + arrivals]
    outs = refs[2 + arrivals :]
    next_kept_ref, next_pieces_ref = outs[0], outs[1]
    sends = outs[2 : 2 + len(positions)]
    total_ref, scores_ref = outs[2 + len(positions) :]
    width = kept_ref.shape[1]
    size = pieces_ref.shape[0]
    total = kept_ref[...]
    for ref in arrived:
        total = total + ref[:, 0:width].astype(F32)
    total_ref[...] = total
    if scores_ref.shape[0] > next_pieces_ref.shape[0]:
        scores_ref[...] = jnp.zeros(scores_ref.shape, F32)
    scores_ref[0:size, :] = pieces_ref[...]
    for j, ref in enumerate(arrived):
        get_scores(ref, scores_ref, (j + 1) * size, size, width)
    rows = next_kept_ref.shape[0]
    next_kept_ref[...] = total_ref[0:rows, :]
    next_pieces_ref[...] = scores_ref[0 : next_pieces_ref.shape[0], :]
    chunks = [total_ref[j * rows : (j + 1) * rows, :] for j in range(total_ref.shape[0] // rows)]
    member = own_index() >> low & 3
    for position, ref in zip(positions, sends):
        if isinstance(position, int):
            chunk = chunks[position]
        else:
            chunk = by_member(member, [chunks[p] for p in position])
        ref[:, 0:width] = chunk.astype(BF16)
        put_scores(ref, scores_ref, width)


def table_kernel(basis, group, tok, core_mask, rows_out, blocks, after_ref, *refs):
    probs_ref, column_ref, mine_ref = refs[2 * blocks :]
    rows, buf_width = refs[0].shape
    half = blocks * rows // 2
    experts, tokens = probs_ref.shape
    lanes = -(-PIECES * experts // LANES) * LANES
    width = buf_width - lanes
    own = own_index()
    column = pl.multiple_of(own * rows_out // LANES * LANES, LANES)
    extras = jnp.zeros((tokens, lanes), F32)
    columns = jnp.zeros((tokens, LANES), F32)
    for index in range(2):
        sets = forward(refs[index * blocks : (index + 1) * blocks])
        row = lax.broadcasted_iota(jnp.int32, (half, tokens), 0)
        token = lax.broadcasted_iota(jnp.int32, (half, tokens), 1)
        side = own ^ (core_mask if index else 0)
        whole = (place_mask(row // tok, basis, side & core_mask != 0) ^ side) * tok + row % tok
        here = jnp.where(whole == token, 1.0, 0.0).astype(BF16)
        part = token_rows(sets, 0, rows, group, 0, slice(width, buf_width))
        extras = extras + lax.dot_general(here, part, TN, preferred_element_type=F32)
        part = token_rows(sets, 0, rows, group, 0, pl.ds(column, LANES))
        columns = columns + lax.dot_general(here, part, TN, preferred_element_type=F32)
    logits = lax.dot_general(piece_sum(experts, lanes, 1), extras.astype(BF16), NT, preferred_element_type=F32)
    raised = jnp.exp(logits - jnp.max(logits, axis=0, keepdims=True))
    probs_ref[...] = raised / jnp.sum(raised, axis=0, keepdims=True)
    column_ref[...] = columns.astype(BF16)
    row = lax.broadcasted_iota(jnp.int32, mine_ref.shape, 0)
    token = lax.broadcasted_iota(jnp.int32, mine_ref.shape, 1)
    mine_ref[...] = jnp.where((row < tok) & (token == own * tok + row), 1.0, 0.0).astype(BF16)


def final_kernel(arrivals, back_basis, core_mask, low, *refs):
    probs_ref, column_ref, mine_ref, router_ref, kept_ref, pieces_ref = refs[:6]
    arrived = refs[6 : 6 + arrivals]
    x_out, grad_out, x_ref, grad_ref, scores_ref, sems = refs[6 + arrivals :]
    experts, width = router_ref.shape
    size = pieces_ref.shape[0]
    tok = kept_ref.shape[0]
    own = own_index()
    scores_ref[0:size, :] = pieces_ref[...]
    for j, ref in enumerate(arrived):
        get_scores(ref, scores_ref, (j + 1) * size, size, width)
    blocks = probs_ref.shape[1] // LANES
    wide = scores_ref.shape[0] // blocks
    sender = lax.broadcasted_iota(jnp.int32, (experts, wide), 1) // SCORE_PIECES
    ids = lax.broadcasted_iota(jnp.int32, (experts, wide), 0)
    mask = place_mask(sender, back_basis, own & core_mask != 0)
    if low is not None:
        member = own >> low & 3
        source = sender >> len(back_basis)
        for k, step in enumerate(REDUCE_STEPS):
            come = by_member(member, [mask_from(step, d) for d in range(4)]) << low
            mask = mask ^ jnp.where(source == k + 1, come, 0)
    pick = jnp.where(((mask ^ own) >> 1) == ids, 1.0, 0.0).astype(BF16)
    parts = []
    for b in range(blocks):
        block = scores_ref[...] if blocks == 1 else scores_ref[pl.ds(b, wide, stride=blocks), :]
        parts.append(jnp.dot(pick, block.astype(BF16), preferred_element_type=F32))
    scores = parts[0] if blocks == 1 else jnp.concatenate(parts, axis=1)
    probs = probs_ref[...]
    mean = jnp.sum(probs * scores, axis=0, keepdims=True)
    logit_grad = (probs * (scores - mean)).astype(BF16)
    mine = lax.dot_general(mine_ref[...], logit_grad, NT, preferred_element_type=F32)
    part = jnp.dot(mine.astype(BF16), router_ref[...], preferred_element_type=F32)
    total = kept_ref[...]
    for ref in arrived:
        total = total + ref[:, 0:width].astype(F32)
    x_ref[...] = (total + part[:tok]).astype(BF16)
    x_copy = pltpu.make_async_copy(x_ref, x_out, sems.at[0])
    x_copy.start()
    grad = jnp.dot(logit_grad, column_ref[...], preferred_element_type=F32)
    rows_out = grad_ref.shape[1]
    first = own * rows_out % LANES
    grad_ref[...] = pltpu.roll(grad, (LANES - first) % LANES, 1)[:, :rows_out]
    grad_copy = pltpu.make_async_copy(grad_ref, grad_out, sems.at[1])
    grad_copy.start()
    x_copy.wait()
    grad_copy.wait()


def on_device(tokens, grad_out, router_logits, selected, router_w, w_gate, w_up, w_down):
    tok, width = tokens.shape
    experts = router_logits.shape[1]
    hidden = w_gate.shape[2]
    exp_size = lax.axis_size("exp")
    hid_size = lax.axis_size("hid")
    count = exp_size * hid_size
    half = count // 2
    groups, core = stage_masks(exp_size, hid_size)
    core_mask = 1 << core
    basis = [m for group in groups for m in group]
    back_groups = [near_first(group) for group in groups[:0:-1]] + [groups[0]]
    core_pair = (core_mask, core_mask)
    low = (count - 1).bit_length() - 2 if len(groups[0]) == 2 else None
    if low is not None:
        back_groups = back_groups[:-1]
    back_basis = [core_pair] + [m for group in back_groups for m in group]
    if low is not None:
        back_groups = back_groups + [None]
    token_count = count * tok
    lanes = -(-PIECES * experts // LANES) * LANES

    block = pl.pallas_call(
        prep_kernel,
        out_shape=jax.ShapeDtypeStruct((2, tok, width + lanes), BF16),
        in_specs=[HBM_SPEC] * 4,
        out_specs=VMEM_SPEC,
        scratch_shapes=[
            pltpu.VMEM(router_logits.shape, router_logits.dtype),
            pltpu.VMEM(selected.shape, selected.dtype),
            pltpu.SemaphoreType.DMA((4,)),
        ],
        compiler_params=PARAMS,
        name="prep",
    )(*in_hbm(tokens, grad_out, router_logits, selected))

    order = None
    if low is None:
        blocks = [block] + swaps(block, group_masks(groups[0])[1:], count, core)
    else:
        order = [m[0] >> low for m in group_masks(groups[0])]
        blocks = [block] + [shift(block, step, count, low) for step in GATHER_STEPS]
    group_rows = tok * len(blocks)
    block = pl.pallas_call(
        functools.partial(join_kernel, order, low or 0),
        out_shape=jax.ShapeDtypeStruct((2 * group_rows, width + lanes), BF16),
        in_specs=[VMEM_SPEC] * len(blocks),
        out_specs=VMEM_SPEC,
        scratch_shapes=[pltpu.VMEM((2 * group_rows, width + lanes), F32)],
        compiler_params=PARAMS,
        name="join",
    )(*forward(blocks))
    for group in groups[1:-1]:
        blocks = [block] + swaps(block, group_masks(group)[1:], count, core)
        block = pl.pallas_call(
            stack_kernel,
            out_shape=jax.ShapeDtypeStruct((len(blocks) * block.shape[0], block.shape[1]), BF16),
            in_specs=[VMEM_SPEC] * len(blocks),
            out_specs=VMEM_SPEC,
            compiler_params=PARAMS,
            name="stack",
        )(*blocks)
    chunks = 4
    copied, pair, down = pl.pallas_call(
        functools.partial(load_kernel, chunks),
        out_shape=(
            pltpu.VMEM(block.shape, BF16),
            pltpu.VMEM((width, 2 * hidden), BF16),
            pltpu.VMEM((hidden, width), BF16),
        ),
        in_specs=[VMEM_SPEC] + [HBM_SPEC] * 3,
        out_specs=(VMEM_SPEC,) * 3,
        scratch_shapes=[pltpu.SemaphoreType.DMA(((2 * len(hidden_parts(hidden)) + 1) * chunks + 1,))],
        compiler_params=pltpu.CompilerParams(vmem_limit_bytes=4 * 2**20),
        cost_estimate=pl.CostEstimate(flops=0, bytes_accessed=6 * width * hidden * 2, transcendentals=0),
        name="load",
    )(block, *in_hbm(w_gate, w_up, w_down))
    masks = group_masks(groups[-1]) if len(groups) > 1 else [core_pair]
    blocks = [block] + swaps(block, masks[1:], count, core)
    blocks = forward(blocks)
    blocks = blocks + [swap(b, core_pair, count, core) for b in [copied] + blocks[1:]]
    block_count = len(blocks) // 2

    unit_rows = SCORE_PIECES * token_count // LANES
    extra = -(-unit_rows // (half * tok)) * LANES
    kept, message, pieces = pl.pallas_call(
        functools.partial(units_kernel, basis, group_rows, tok, experts, core_mask, block_count),
        out_shape=(
            jax.ShapeDtypeStruct((half * tok, width), F32),
            jax.ShapeDtypeStruct((half * tok, width + extra), BF16),
            jax.ShapeDtypeStruct((unit_rows, LANES), F32),
        ),
        in_specs=[VMEM_SPEC] * (len(blocks) + 2),
        out_specs=(VMEM_SPEC,) * 3,
        scratch_shapes=[
            pltpu.VMEM((1, token_count), F32),
            pltpu.VMEM((max(half * tok * extra // LANES, unit_rows), LANES), F32),
        ],
        compiler_params=PARAMS,
        cost_estimate=pl.CostEstimate(
            flops=10 * token_count * width * hidden,
            bytes_accessed=3 * width * hidden * 2 + 2 * token_count * width * 2,
            transcendentals=token_count * hidden,
        ),
        name="units",
    )(*blocks, pair, down)

    arrived = [swap(message, core_pair, count, core)]
    tables = None
    rows_out = width // count
    for group, back_group in zip(groups[::-1], back_groups):
        order = [m[0] for m in group_masks(group)]
        if back_group is None:
            positions = [[order.index((d ^ (d if to is None else to)) << low) for d, to in enumerate(step)] for step in REDUCE_STEPS]
        else:
            back_masks = group_masks(back_group)
            positions = [order.index(m[0]) for m in back_masks[1:]]
        radix = len(order)
        rows = kept.shape[0]
        next_rows = rows // radix
        size = pieces.shape[0] * (1 + len(arrived))
        extra = -(-size // next_rows) * LANES
        sends = [jax.ShapeDtypeStruct((next_rows, width + extra), BF16)] * len(positions)
        outs = pl.pallas_call(
            functools.partial(add_kernel, len(arrived), positions, low or 0),
            out_shape=[
                jax.ShapeDtypeStruct((next_rows, width), F32),
                jax.ShapeDtypeStruct((size, LANES), F32),
            ]
            + sends,
            in_specs=[VMEM_SPEC] * (2 + len(arrived)),
            out_specs=[VMEM_SPEC] * (2 + len(positions)),
            scratch_shapes=[
                pltpu.VMEM((rows, width), F32),
                pltpu.VMEM((max(next_rows * extra // LANES, size), LANES), F32),
            ],
            compiler_params=PARAMS,
            name="add",
        )(kept, pieces, *arrived)
        kept, pieces = outs[0], outs[1]
        if tables is None:
            tables = pl.pallas_call(
                functools.partial(table_kernel, basis, group_rows, tok, core_mask, rows_out, block_count),
                out_shape=(
                    jax.ShapeDtypeStruct((experts, token_count), F32),
                    jax.ShapeDtypeStruct((token_count, LANES), BF16),
                    jax.ShapeDtypeStruct((16, token_count), BF16),
                ),
                in_specs=[pl.BlockSpec(memory_space=pl.ANY)] + [VMEM_SPEC] * len(blocks),
                out_specs=(VMEM_SPEC,) * 3,
                compiler_params=PARAMS,
                cost_estimate=pl.CostEstimate(flops=10**9, bytes_accessed=10**6, transcendentals=0),
                name="tables",
            )(pieces, *blocks)
        if back_group is None:
            arrived = [shift(piece, step, count, low) for piece, step in zip(outs[2:], REDUCE_STEPS)]
        else:
            arrived = [swap(piece, m, count, core) for piece, m in zip(outs[2:], back_masks[1:])]

    x_grad, grad = pl.pallas_call(
        functools.partial(final_kernel, len(arrived), back_basis, core_mask, low),
        out_shape=(
            jax.ShapeDtypeStruct((tok, width), BF16),
            jax.ShapeDtypeStruct((experts, rows_out), F32),
        ),
        in_specs=[VMEM_SPEC] * (6 + len(arrived)),
        out_specs=(HBM_SPEC, HBM_SPEC),
        scratch_shapes=[
            pltpu.VMEM((tok, width), BF16),
            pltpu.VMEM((experts, rows_out), F32),
            pltpu.VMEM((pieces.shape[0] * (1 + len(arrived)), LANES), F32),
            pltpu.SemaphoreType.DMA((2,)),
        ],
        compiler_params=PARAMS,
        name="final",
    )(*tables, router_w.T, kept, pieces, *arrived)
    return (x_grad, grad.T)


def solution(mesh):
    rows = P(AXES, None)
    units = P(AXES, None, None)
    return jax.shard_map(
        on_device,
        mesh=mesh,
        in_specs=(rows, rows, rows, rows, P(), units, units, units),
        out_specs=(rows, rows),
        check_vma=False,
    )
```

```python
import functools

import jax
import jax.numpy as jnp
from jax import lax
from jax.experimental import pallas as pl
from jax.experimental.pallas import tpu as pltpu
from jax.sharding import PartitionSpec as P

AXES = ("exp", "hid")
LANES = 128
PIECES = 4
SCORE_PIECES = 2
VMEM_SPEC = pl.BlockSpec(memory_space=pltpu.VMEM)
HBM_SPEC = pl.BlockSpec(memory_space=pltpu.HBM)
F32 = jnp.float32
BF16 = jnp.bfloat16
NT = (((1,), (1,)), ((), ()))
TN = (((0,), (0,)), ((), ()))
PARAMS = pltpu.CompilerParams(vmem_limit_bytes=24 * 2**20)


def stage_masks(exp_size, hid_size):
    hid_bits = hid_size.bit_length() - 1
    all_bits = (exp_size * hid_size).bit_length() - 1
    core = hid_bits
    first = list(range(max(core + 1, all_bits - 2), all_bits))
    middle = [b for b in range(all_bits) if b != core and b not in first]
    groups = [first] + [middle[i : i + 2] for i in range(0, len(middle), 2)]
    bases = [[(sum(1 << b for b in group[i:]),) * 2 for i in range(len(group))] for group in groups]
    bases[0] = bases[0][::-1]
    return bases, core


def cross(a, b):
    return (a[0] ^ b[0], a[1] ^ b[1])


def group_masks(basis):
    masks = [(0, 0)]
    for mask in basis:
        masks = masks + [cross(m, mask) for m in masks]
    return masks


def near_first(basis):
    return [cross(basis[0], basis[1]), basis[1]] if len(basis) == 2 else basis


def swap(block, mask, count, core):
    return lax.ppermute(block, AXES, [(i, i ^ mask[i >> core & 1]) for i in range(count)])


GATHER_STEPS = ((2, 3, 1, 0), (3, 2, 0, 1), (1, 0, 3, 2))
REDUCE_STEPS = ((1, 3, 0, 2), (3, 2, 1, 0), (2, 0, 3, 1))


def by_member(member, values):
    total = values[0]
    for k in range(1, len(values)):
        total = jnp.where(member == k, values[k], total)
    return total


def shift(block, step, count, low):
    return lax.ppermute(block, AXES, [(i, i ^ ((i >> low & 3) ^ step[i >> low & 3]) << low) for i in range(count)])


def swaps(block, masks, count, core):
    return [swap(block, m, count, core) for m in masks]


def forward(blocks):
    return blocks[:1] + blocks[:0:-1]


def place_mask(place, basis, upper):
    total = jnp.zeros_like(place)
    for digit, (low, high) in enumerate(basis):
        mask = low if low == high else jnp.where(upper, high, low)
        total = total ^ (((place >> digit) & 1) * mask)
    return total


def own_index():
    return lax.axis_index("exp") * lax.axis_size("hid") + lax.axis_index("hid")


def in_hbm(*arrays):
    return tuple(pltpu.with_memory_space_constraint(a, pltpu.HBM) for a in arrays)


def piece_sum(experts, lanes, axis):
    shape = (lanes, experts) if axis == 0 else (experts, lanes)
    lane = lax.broadcasted_iota(jnp.int32, shape, axis)
    ids = lax.broadcasted_iota(jnp.int32, shape, 1 - axis)
    tally = jnp.zeros(shape, F32)
    for k in range(1, PIECES):
        tally = tally + jnp.where(lane == ids + k * experts, 1.0, 0.0)
    return tally.astype(BF16)


def combine_rows(extras, experts):
    hit = extras[:, :experts].astype(F32) > 0.5
    logits = jnp.dot(extras, piece_sum(experts, extras.shape[1], 0), preferred_element_type=F32)
    top = jnp.max(jnp.where(hit, logits, -jnp.inf), axis=1, keepdims=True)
    raised = jnp.where(hit, jnp.exp(jnp.minimum(logits - top, 0.0)), 0.0)
    return (raised / jnp.sum(raised, axis=1, keepdims=True)).astype(BF16).astype(F32)


def prep_kernel(tokens_in, grad_in, logits_in, chosen_in, out_ref, logits_ref, chosen_ref, sems):
    tok, width = tokens_in.shape
    pairs = [
        (logits_in, logits_ref),
        (chosen_in, chosen_ref),
        (tokens_in, out_ref.at[0, :, 0:width]),
        (grad_in, out_ref.at[1, :, 0:width]),
    ]
    copies = [pltpu.make_async_copy(src, dst, sems.at[i]) for i, (src, dst) in enumerate(pairs)]
    for copy in copies:
        copy.start()
    copies[0].wait()
    copies[1].wait()
    logits = logits_ref[...]
    chosen = chosen_ref[...]
    experts = logits.shape[1]
    ids = lax.broadcasted_iota(jnp.int32, logits.shape, 1)
    hit = ids == chosen[:, 0:1]
    for k in range(1, chosen.shape[1]):
        hit = hit | (ids == chosen[:, k : k + 1])
    parts = [jnp.where(hit, 1.0, 0.0)]
    rest = logits
    for _ in range(PIECES - 1):
        parts.append(rest)
        rest = rest - rest.astype(BF16).astype(F32)
    lanes = out_ref.shape[2] - width
    spare = lanes - PIECES * experts
    extras = jnp.concatenate(parts + ([jnp.zeros((tok, spare), F32)] if spare else []), axis=1)
    out_ref[0, :, width:] = extras.astype(BF16)
    out_ref[1, :, width:] = jnp.zeros((tok, lanes), BF16)
    copies[2].wait()
    copies[3].wait()


def hidden_parts(hidden):
    main = hidden // 256 * 256
    return [(0, main), (main, hidden)] if 0 < main < hidden else [(0, hidden)]


def load_kernel(chunks, block_in, gate_in, up_in, down_in, block_ref, pair_ref, down_ref, sems):
    copies = []

    def add(src, dst):
        copies.append(pltpu.make_async_copy(src, dst, sems.at[len(copies)]))

    hidden, width = down_ref.shape
    for c in range(chunks):
        part = pl.ds(c * (width // chunks), width // chunks)
        for first, last in hidden_parts(hidden):
            for k, ref in enumerate((gate_in, up_in)):
                to = 2 * first + k * (last - first)
                add(ref.at[0, part, first:last], pair_ref.at[part, to : to + last - first])
        part = pl.ds(c * (hidden // chunks), hidden // chunks)
        add(down_in.at[0, part, :], down_ref.at[part, :])
    add(block_in, block_ref)
    for copy in copies:
        copy.start()
    for copy in copies:
        copy.wait()


def join_kernel(order, low, *refs):
    blocks, out_ref, rows_ref = forward(refs[:-2]), refs[-2], refs[-1]
    count = len(blocks)
    tok = blocks[0].shape[1]
    member = own_index() >> low & 3
    for kind in range(2):
        rows = [ref[kind].astype(F32) for ref in blocks]
        if order is not None:
            come = [[d ^ step.index(d) for d in range(4)] for step in GATHER_STEPS]
            places = [[[c[d] for c in come].index(mask) for d in range(4)] for mask in order[1:]]
            rows = rows[:1] + [by_member(member, [rows[1 + k] for k in place]) for place in places]
        for j, value in enumerate(rows):
            first = (kind * count + j) * tok
            rows_ref[first : first + tok, :] = value
    out_ref[...] = rows_ref[...].astype(BF16)


def stack_kernel(*refs):
    out_ref = refs[-1]
    rows = refs[0].shape[0]
    for j, ref in enumerate(refs[:-1]):
        out_ref[j * rows : (j + 1) * rows, :] = ref[...]


def token_rows(refs, start, rows, group, kind, columns):
    parts = []
    for ref in refs:
        for j in range(rows // (2 * group)):
            first = start + (2 * j + kind) * group
            if not isinstance(first, int):
                first = pl.multiple_of(first, group)
            parts.append(ref[pl.ds(first, group), columns])
    return parts[0] if len(parts) == 1 else jnp.concatenate(parts, axis=0)


def put_scores(out_ref, scores_ref, width):
    rows = out_ref.shape[0]
    for c in range((out_ref.shape[1] - width) // LANES):
        out_ref[:, width + c * LANES : width + (c + 1) * LANES] = scores_ref[c * rows : (c + 1) * rows, :].astype(BF16)


def get_scores(in_ref, scores_ref, base, size, width):
    rows = in_ref.shape[0]
    for c in range(-(-size // rows)):
        here = min(rows, size - c * rows)
        tall = min(rows, -(-here // 16) * 16)
        block = in_ref[0:tall, width + c * LANES : width + (c + 1) * LANES].astype(F32)
        scores_ref[base + c * rows : base + c * rows + here, :] = block[:here]


def units_kernel(basis, group, tok, experts, core_mask, blocks, *refs):
    own_refs, other_refs = forward(refs[:blocks]), forward(refs[blocks : 2 * blocks])
    pair_ref, down_ref, kept_ref, message_ref, pieces_ref, score_ref, padded_ref = refs[2 * blocks :]
    hidden, width = down_ref.shape
    rows, buf_width = own_refs[0].shape
    tokens = score_ref.shape[1]
    own = own_index()

    def terms(sets, start, step):
        act = token_rows(sets, start, step, group, 0, slice(None))
        count = act.shape[0]
        combine = combine_rows(act[:, width:], experts)
        ids = lax.broadcasted_iota(jnp.int32, combine.shape, 1)
        column = jnp.sum(jnp.where(ids == own // 2, combine, 0.0), axis=1, keepdims=True)
        act = act[:, :width]
        cot = token_rows(sets, start, step, group, 1, slice(0, width))
        score = jnp.zeros((count, 1), F32)
        grads = []
        for first, last in hidden_parts(hidden):
            size = last - first
            pair = jnp.dot(act, pair_ref[:, 2 * first : 2 * last], preferred_element_type=F32)
            gate_pre = pair[:, :size]
            up_pre = pair[:, size:]
            back = lax.dot_general(cot, down_ref[first:last, :], NT, preferred_element_type=F32)
            sig = jax.nn.sigmoid(gate_pre)
            act_gate = gate_pre * sig
            score = score + jnp.sum(act_gate * up_pre * back, axis=1, keepdims=True)
            weighted = column * back
            grad_gate = weighted * up_pre * sig * (1.0 + gate_pre * (1.0 - sig))
            grad_up = weighted * act_gate
            grads += [grad_gate.astype(BF16), grad_up.astype(BF16)]
        grads = jnp.concatenate(grads, axis=1)
        return lax.dot_general(grads, pair_ref[...], NT, preferred_element_type=F32), score

    def in_order(score, place, swap_mask):
        token = lax.broadcasted_iota(jnp.int32, (score.shape[0], tokens), 1)
        side = own ^ swap_mask
        whole = (place_mask(place // tok, basis, side & core_mask != 0) ^ side) * tok + place % tok
        return jnp.sum(jnp.where(whole == token, score, 0.0), axis=0, keepdims=True)

    half = blocks * rows // 2
    if 2 * half <= 128:
        total, score = terms(own_refs + other_refs, 0, rows)
        kept_ref[...] = total[:half]
        message_ref[:, 0:width] = total[half:].astype(BF16)
        row = lax.broadcasted_iota(jnp.int32, (2 * half, tokens), 0)
        score_ref[...] = in_order(score, row % half, jnp.where(row < half, 0, core_mask))
    else:
        step = min(rows, 128)
        score_ref[...] = jnp.zeros(score_ref.shape, F32)
        for out_ref, sets, swap_mask in ((kept_ref, own_refs, 0), (message_ref, other_refs, core_mask)):
            for j, ref in enumerate(sets):

                def one(index):
                    total, score = terms((ref,), index * step, step)
                    first = pl.multiple_of(j * (rows // 2) + index * (step // 2), step // 2)
                    out_ref[pl.ds(first, step // 2), 0:width] = total.astype(out_ref.dtype)
                    place = lax.broadcasted_iota(jnp.int32, (step // 2, tokens), 0) + first
                    score_ref[...] += in_order(score, place, swap_mask)

                pl.loop(0, rows // step)(one)

    lane_blocks = tokens // LANES
    padded_ref[...] = jnp.zeros(padded_ref.shape, F32)
    value = score_ref[...]
    for piece in range(SCORE_PIECES):
        rounded = value.astype(BF16).astype(F32)
        for b in range(lane_blocks):
            at = piece * lane_blocks + b
            padded_ref[at : at + 1, :] = rounded[:, b * LANES : (b + 1) * LANES]
        value = value - rounded
    pieces_ref[...] = padded_ref[0 : pieces_ref.shape[0], :]
    put_scores(message_ref, padded_ref, width)


def add_kernel(arrivals, positions, low, *refs):
    kept_ref, pieces_ref = refs[0], refs[1]
    arrived = refs[2 : 2 + arrivals]
    outs = refs[2 + arrivals :]
    next_kept_ref, next_pieces_ref = outs[0], outs[1]
    sends = outs[2 : 2 + len(positions)]
    total_ref, scores_ref = outs[2 + len(positions) :]
    width = kept_ref.shape[1]
    size = pieces_ref.shape[0]
    total = kept_ref[...]
    for ref in arrived:
        total = total + ref[:, 0:width].astype(F32)
    total_ref[...] = total
    if scores_ref.shape[0] > next_pieces_ref.shape[0]:
        scores_ref[...] = jnp.zeros(scores_ref.shape, F32)
    scores_ref[0:size, :] = pieces_ref[...]
    for j, ref in enumerate(arrived):
        get_scores(ref, scores_ref, (j + 1) * size, size, width)
    rows = next_kept_ref.shape[0]
    next_kept_ref[...] = total_ref[0:rows, :]
    next_pieces_ref[...] = scores_ref[0 : next_pieces_ref.shape[0], :]
    chunks = [total_ref[j * rows : (j + 1) * rows, :] for j in range(total_ref.shape[0] // rows)]
    member = own_index() >> low & 3
    for position, ref in zip(positions, sends):
        if isinstance(position, int):
            chunk = chunks[position]
        else:
            chunk = by_member(member, [chunks[p] for p in position])
        ref[:, 0:width] = chunk.astype(BF16)
        put_scores(ref, scores_ref, width)


def table_kernel(basis, group, tok, core_mask, rows_out, blocks, after_ref, *refs):
    probs_ref, column_ref, mine_ref = refs[2 * blocks :]
    rows, buf_width = refs[0].shape
    half = blocks * rows // 2
    experts, tokens = probs_ref.shape
    lanes = -(-PIECES * experts // LANES) * LANES
    width = buf_width - lanes
    own = own_index()
    column = pl.multiple_of(own * rows_out // LANES * LANES, LANES)
    extras = jnp.zeros((tokens, lanes), F32)
    columns = jnp.zeros((tokens, LANES), F32)
    for index in range(2):
        sets = forward(refs[index * blocks : (index + 1) * blocks])
        row = lax.broadcasted_iota(jnp.int32, (half, tokens), 0)
        token = lax.broadcasted_iota(jnp.int32, (half, tokens), 1)
        side = own ^ (core_mask if index else 0)
        whole = (place_mask(row // tok, basis, side & core_mask != 0) ^ side) * tok + row % tok
        here = jnp.where(whole == token, 1.0, 0.0).astype(BF16)
        part = token_rows(sets, 0, rows, group, 0, slice(width, buf_width))
        extras = extras + lax.dot_general(here, part, TN, preferred_element_type=F32)
        part = token_rows(sets, 0, rows, group, 0, pl.ds(column, LANES))
        columns = columns + lax.dot_general(here, part, TN, preferred_element_type=F32)
    logits = lax.dot_general(piece_sum(experts, lanes, 1), extras.astype(BF16), NT, preferred_element_type=F32)
    raised = jnp.exp(logits - jnp.max(logits, axis=0, keepdims=True))
    probs_ref[...] = raised / jnp.sum(raised, axis=0, keepdims=True)
    column_ref[...] = columns.astype(BF16)
    row = lax.broadcasted_iota(jnp.int32, mine_ref.shape, 0)
    token = lax.broadcasted_iota(jnp.int32, mine_ref.shape, 1)
    mine_ref[...] = jnp.where((row < tok) & (token == own * tok + row), 1.0, 0.0).astype(BF16)


def final_kernel(arrivals, back_basis, core_mask, low, *refs):
    probs_ref, column_ref, mine_ref, router_ref, kept_ref, pieces_ref = refs[:6]
    arrived = refs[6 : 6 + arrivals]
    x_out, grad_out, x_ref, grad_ref, scores_ref, sems = refs[6 + arrivals :]
    experts, width = router_ref.shape
    size = pieces_ref.shape[0]
    tok = kept_ref.shape[0]
    own = own_index()
    scores_ref[0:size, :] = pieces_ref[...]
    for j, ref in enumerate(arrived):
        get_scores(ref, scores_ref, (j + 1) * size, size, width)
    blocks = probs_ref.shape[1] // LANES
    wide = scores_ref.shape[0] // blocks
    sender = lax.broadcasted_iota(jnp.int32, (experts, wide), 1) // SCORE_PIECES
    ids = lax.broadcasted_iota(jnp.int32, (experts, wide), 0)
    mask = place_mask(sender, back_basis, own & core_mask != 0)
    if low is not None:
        member = own >> low & 3
        source = sender >> len(back_basis)
        for k, step in enumerate(REDUCE_STEPS):
            come = by_member(member, [d ^ step.index(d) for d in range(4)]) << low
            mask = mask ^ jnp.where(source == k + 1, come, 0)
    pick = jnp.where(((mask ^ own) >> 1) == ids, 1.0, 0.0).astype(BF16)
    parts = []
    for b in range(blocks):
        block = scores_ref[...] if blocks == 1 else scores_ref[pl.ds(b, wide, stride=blocks), :]
        parts.append(jnp.dot(pick, block.astype(BF16), preferred_element_type=F32))
    scores = parts[0] if blocks == 1 else jnp.concatenate(parts, axis=1)
    probs = probs_ref[...]
    mean = jnp.sum(probs * scores, axis=0, keepdims=True)
    logit_grad = (probs * (scores - mean)).astype(BF16)
    mine = lax.dot_general(mine_ref[...], logit_grad, NT, preferred_element_type=F32)
    part = jnp.dot(mine.astype(BF16), router_ref[...], preferred_element_type=F32)
    total = kept_ref[...]
    for ref in arrived:
        total = total + ref[:, 0:width].astype(F32)
    x_ref[...] = (total + part[:tok]).astype(BF16)
    x_copy = pltpu.make_async_copy(x_ref, x_out, sems.at[0])
    x_copy.start()
    grad = jnp.dot(logit_grad, column_ref[...], preferred_element_type=F32)
    rows_out = grad_ref.shape[1]
    first = own * rows_out % LANES
    grad_ref[...] = pltpu.roll(grad, (LANES - first) % LANES, 1)[:, :rows_out]
    grad_copy = pltpu.make_async_copy(grad_ref, grad_out, sems.at[1])
    grad_copy.start()
    x_copy.wait()
    grad_copy.wait()


def on_device(tokens, grad_out, router_logits, selected, router_w, w_gate, w_up, w_down):
    tok, width = tokens.shape
    experts = router_logits.shape[1]
    hidden = w_gate.shape[2]
    exp_size = lax.axis_size("exp")
    hid_size = lax.axis_size("hid")
    count = exp_size * hid_size
    half = count // 2
    groups, core = stage_masks(exp_size, hid_size)
    core_mask = 1 << core
    basis = [m for group in groups for m in group]
    back_groups = [near_first(group) for group in groups[:0:-1]] + [groups[0]]
    core_pair = (core_mask, core_mask)
    low = (count - 1).bit_length() - 2 if len(groups[0]) == 2 else None
    if low is not None:
        back_groups = back_groups[:-1]
    back_basis = [core_pair] + [m for group in back_groups for m in group]
    if low is not None:
        back_groups = back_groups + [None]
    token_count = count * tok
    lanes = -(-PIECES * experts // LANES) * LANES

    block = pl.pallas_call(
        prep_kernel,
        out_shape=jax.ShapeDtypeStruct((2, tok, width + lanes), BF16),
        in_specs=[HBM_SPEC] * 4,
        out_specs=VMEM_SPEC,
        scratch_shapes=[
            pltpu.VMEM(router_logits.shape, router_logits.dtype),
            pltpu.VMEM(selected.shape, selected.dtype),
            pltpu.SemaphoreType.DMA((4,)),
        ],
        compiler_params=PARAMS,
        name="prep",
    )(*in_hbm(tokens, grad_out, router_logits, selected))

    order = None
    if low is None:
        blocks = [block] + swaps(block, group_masks(groups[0])[1:], count, core)
    else:
        order = [m[0] >> low for m in group_masks(groups[0])]
        blocks = [block] + [shift(block, step, count, low) for step in GATHER_STEPS]
    group_rows = tok * len(blocks)
    block = pl.pallas_call(
        functools.partial(join_kernel, order, low or 0),
        out_shape=jax.ShapeDtypeStruct((2 * group_rows, width + lanes), BF16),
        in_specs=[VMEM_SPEC] * len(blocks),
        out_specs=VMEM_SPEC,
        scratch_shapes=[pltpu.VMEM((2 * group_rows, width + lanes), F32)],
        compiler_params=PARAMS,
        name="join",
    )(*forward(blocks))
    for group in groups[1:-1]:
        blocks = [block] + swaps(block, group_masks(group)[1:], count, core)
        block = pl.pallas_call(
            stack_kernel,
            out_shape=jax.ShapeDtypeStruct((len(blocks) * block.shape[0], block.shape[1]), BF16),
            in_specs=[VMEM_SPEC] * len(blocks),
            out_specs=VMEM_SPEC,
            compiler_params=PARAMS,
            name="stack",
        )(*blocks)
    chunks = 4
    copied, pair, down = pl.pallas_call(
        functools.partial(load_kernel, chunks),
        out_shape=(
            pltpu.VMEM(block.shape, BF16),
            pltpu.VMEM((width, 2 * hidden), BF16),
            pltpu.VMEM((hidden, width), BF16),
        ),
        in_specs=[VMEM_SPEC] + [HBM_SPEC] * 3,
        out_specs=(VMEM_SPEC,) * 3,
        scratch_shapes=[pltpu.SemaphoreType.DMA(((2 * len(hidden_parts(hidden)) + 1) * chunks + 1,))],
        compiler_params=pltpu.CompilerParams(vmem_limit_bytes=4 * 2**20),
        cost_estimate=pl.CostEstimate(flops=0, bytes_accessed=6 * width * hidden * 2, transcendentals=0),
        name="load",
    )(block, *in_hbm(w_gate, w_up, w_down))
    masks = group_masks(groups[-1]) if len(groups) > 1 else [core_pair]
    blocks = [block] + swaps(block, masks[1:], count, core)
    blocks = forward(blocks)
    blocks = blocks + [swap(b, core_pair, count, core) for b in [copied] + blocks[1:]]
    block_count = len(blocks) // 2

    unit_rows = SCORE_PIECES * token_count // LANES
    extra = -(-unit_rows // (half * tok)) * LANES
    kept, message, pieces = pl.pallas_call(
        functools.partial(units_kernel, basis, group_rows, tok, experts, core_mask, block_count),
        out_shape=(
            jax.ShapeDtypeStruct((half * tok, width), F32),
            jax.ShapeDtypeStruct((half * tok, width + extra), BF16),
            jax.ShapeDtypeStruct((unit_rows, LANES), F32),
        ),
        in_specs=[VMEM_SPEC] * (len(blocks) + 2),
        out_specs=(VMEM_SPEC,) * 3,
        scratch_shapes=[
            pltpu.VMEM((1, token_count), F32),
            pltpu.VMEM((max(half * tok * extra // LANES, unit_rows), LANES), F32),
        ],
        compiler_params=PARAMS,
        cost_estimate=pl.CostEstimate(
            flops=10 * token_count * width * hidden,
            bytes_accessed=3 * width * hidden * 2 + 2 * token_count * width * 2,
            transcendentals=token_count * hidden,
        ),
        name="units",
    )(*blocks, pair, down)

    arrived = [swap(message, core_pair, count, core)]
    tables = None
    rows_out = width // count
    for group, back_group in zip(groups[::-1], back_groups):
        order = [m[0] for m in group_masks(group)]
        if back_group is None:
            positions = [[order.index((d ^ step[d]) << low) for d in range(4)] for step in REDUCE_STEPS]
        else:
            back_masks = group_masks(back_group)
            positions = [order.index(m[0]) for m in back_masks[1:]]
        radix = len(order)
        rows = kept.shape[0]
        next_rows = rows // radix
        size = pieces.shape[0] * (1 + len(arrived))
        extra = -(-size // next_rows) * LANES
        sends = [jax.ShapeDtypeStruct((next_rows, width + extra), BF16)] * (radix - 1)
        outs = pl.pallas_call(
            functools.partial(add_kernel, len(arrived), positions, low or 0),
            out_shape=[
                jax.ShapeDtypeStruct((next_rows, width), F32),
                jax.ShapeDtypeStruct((size, LANES), F32),
            ]
            + sends,
            in_specs=[VMEM_SPEC] * (2 + len(arrived)),
            out_specs=[VMEM_SPEC] * (1 + radix),
            scratch_shapes=[
                pltpu.VMEM((rows, width), F32),
                pltpu.VMEM((max(next_rows * extra // LANES, size), LANES), F32),
            ],
            compiler_params=PARAMS,
            name="add",
        )(kept, pieces, *arrived)
        kept, pieces = outs[0], outs[1]
        if tables is None:
            tables = pl.pallas_call(
                functools.partial(table_kernel, basis, group_rows, tok, core_mask, rows_out, block_count),
                out_shape=(
                    jax.ShapeDtypeStruct((experts, token_count), F32),
                    jax.ShapeDtypeStruct((token_count, LANES), BF16),
                    jax.ShapeDtypeStruct((16, token_count), BF16),
                ),
                in_specs=[pl.BlockSpec(memory_space=pl.ANY)] + [VMEM_SPEC] * len(blocks),
                out_specs=(VMEM_SPEC,) * 3,
                compiler_params=PARAMS,
                cost_estimate=pl.CostEstimate(flops=10**9, bytes_accessed=10**6, transcendentals=0),
                name="tables",
            )(pieces, *blocks)
        if back_group is None:
            arrived = [shift(piece, step, count, low) for piece, step in zip(outs[2:], REDUCE_STEPS)]
        else:
            arrived = [swap(piece, m, count, core) for piece, m in zip(outs[2:], back_masks[1:])]

    x_grad, grad = pl.pallas_call(
        functools.partial(final_kernel, len(arrived), back_basis, core_mask, low),
        out_shape=(
            jax.ShapeDtypeStruct((tok, width), BF16),
            jax.ShapeDtypeStruct((experts, rows_out), F32),
        ),
        in_specs=[VMEM_SPEC] * (6 + len(arrived)),
        out_specs=(HBM_SPEC, HBM_SPEC),
        scratch_shapes=[
            pltpu.VMEM((tok, width), BF16),
            pltpu.VMEM((experts, rows_out), F32),
            pltpu.VMEM((pieces.shape[0] * (1 + len(arrived)), LANES), F32),
            pltpu.SemaphoreType.DMA((2,)),
        ],
        compiler_params=PARAMS,
        name="final",
    )(*tables, router_w.T, kept, pieces, *arrived)
    return (x_grad, grad.T)


def solution(mesh):
    rows = P(AXES, None)
    units = P(AXES, None, None)
    return jax.shard_map(
        on_device,
        mesh=mesh,
        in_specs=(rows, rows, rows, rows, P(), units, units, units),
        out_specs=(rows, rows),
        check_vma=False,
    )
```

```python
import functools

import jax
import jax.numpy as jnp
from jax import lax
from jax.experimental import pallas as pl
from jax.experimental.pallas import tpu as pltpu
from jax.sharding import PartitionSpec as P

AXES = ("exp", "hid")
LANES = 128
PIECES = 4
SCORE_PIECES = 2
VMEM_SPEC = pl.BlockSpec(memory_space=pltpu.VMEM)
HBM_SPEC = pl.BlockSpec(memory_space=pltpu.HBM)
F32 = jnp.float32
BF16 = jnp.bfloat16
NT = (((1,), (1,)), ((), ()))
TN = (((0,), (0,)), ((), ()))
PARAMS = pltpu.CompilerParams(vmem_limit_bytes=24 * 2**20)


def stage_masks(exp_size, hid_size):
    hid_bits = hid_size.bit_length() - 1
    all_bits = (exp_size * hid_size).bit_length() - 1
    core = hid_bits
    first = list(range(max(core + 1, all_bits - 2), all_bits))
    middle = [b for b in range(all_bits) if b != core and b not in first]
    groups = [first] + [middle[i : i + 2] for i in range(0, len(middle), 2)]
    bases = [[(sum(1 << b for b in group[i:]),) * 2 for i in range(len(group))] for group in groups]
    bases[0] = bases[0][::-1]
    return bases, core


def cross(a, b):
    return (a[0] ^ b[0], a[1] ^ b[1])


def group_masks(basis):
    masks = [(0, 0)]
    for mask in basis:
        masks = masks + [cross(m, mask) for m in masks]
    return masks


def near_first(basis):
    return [cross(basis[0], basis[1]), basis[1]] if len(basis) == 2 else basis


def swap(block, mask, count, core):
    return lax.ppermute(block, AXES, [(i, i ^ mask[i >> core & 1]) for i in range(count)])


REDUCE_STEPS = ((1, 3, 0, 2), (3, 2, 1, 0), (2, 0, 3, 1))


def by_member(member, values):
    total = values[0]
    for k in range(1, len(values)):
        total = jnp.where(member == k, values[k], total)
    return total


def shift(block, step, count, low):
    return lax.ppermute(block, AXES, [(i, i ^ ((i >> low & 3) ^ step[i >> low & 3]) << low) for i in range(count)])


def swaps(block, masks, count, core):
    return [swap(block, m, count, core) for m in masks]


def forward(blocks):
    return blocks[:1] + blocks[:0:-1]


def place_mask(place, basis, upper):
    total = jnp.zeros_like(place)
    for digit, (low, high) in enumerate(basis):
        mask = low if low == high else jnp.where(upper, high, low)
        total = total ^ (((place >> digit) & 1) * mask)
    return total


def own_index():
    return lax.axis_index("exp") * lax.axis_size("hid") + lax.axis_index("hid")


def in_hbm(*arrays):
    return tuple(pltpu.with_memory_space_constraint(a, pltpu.HBM) for a in arrays)


def piece_sum(experts, lanes, axis):
    shape = (lanes, experts) if axis == 0 else (experts, lanes)
    lane = lax.broadcasted_iota(jnp.int32, shape, axis)
    ids = lax.broadcasted_iota(jnp.int32, shape, 1 - axis)
    tally = jnp.zeros(shape, F32)
    for k in range(1, PIECES):
        tally = tally + jnp.where(lane == ids + k * experts, 1.0, 0.0)
    return tally.astype(BF16)


def combine_rows(extras, experts):
    hit = extras[:, :experts].astype(F32) > 0.5
    logits = jnp.dot(extras, piece_sum(experts, extras.shape[1], 0), preferred_element_type=F32)
    top = jnp.max(jnp.where(hit, logits, -jnp.inf), axis=1, keepdims=True)
    raised = jnp.where(hit, jnp.exp(jnp.minimum(logits - top, 0.0)), 0.0)
    return (raised / jnp.sum(raised, axis=1, keepdims=True)).astype(BF16).astype(F32)


def prep_kernel(tokens_in, grad_in, logits_in, chosen_in, out_ref, logits_ref, chosen_ref, sems):
    tok, width = tokens_in.shape
    pairs = [
        (logits_in, logits_ref),
        (chosen_in, chosen_ref),
        (tokens_in, out_ref.at[0, :, 0:width]),
        (grad_in, out_ref.at[1, :, 0:width]),
    ]
    copies = [pltpu.make_async_copy(src, dst, sems.at[i]) for i, (src, dst) in enumerate(pairs)]
    for copy in copies:
        copy.start()
    copies[0].wait()
    copies[1].wait()
    logits = logits_ref[...]
    chosen = chosen_ref[...]
    experts = logits.shape[1]
    ids = lax.broadcasted_iota(jnp.int32, logits.shape, 1)
    hit = ids == chosen[:, 0:1]
    for k in range(1, chosen.shape[1]):
        hit = hit | (ids == chosen[:, k : k + 1])
    parts = [jnp.where(hit, 1.0, 0.0)]
    rest = logits
    for _ in range(PIECES - 1):
        parts.append(rest)
        rest = rest - rest.astype(BF16).astype(F32)
    lanes = out_ref.shape[2] - width
    spare = lanes - PIECES * experts
    extras = jnp.concatenate(parts + ([jnp.zeros((tok, spare), F32)] if spare else []), axis=1)
    out_ref[0, :, width:] = extras.astype(BF16)
    out_ref[1, :, width:] = jnp.zeros((tok, lanes), BF16)
    copies[2].wait()
    copies[3].wait()


def hidden_parts(hidden):
    main = hidden // 256 * 256
    return [(0, main), (main, hidden)] if 0 < main < hidden else [(0, hidden)]


def load_kernel(chunks, block_in, gate_in, up_in, down_in, block_ref, pair_ref, down_ref, sems):
    copies = []

    def add(src, dst):
        copies.append(pltpu.make_async_copy(src, dst, sems.at[len(copies)]))

    hidden, width = down_ref.shape
    for c in range(chunks):
        part = pl.ds(c * (width // chunks), width // chunks)
        for first, last in hidden_parts(hidden):
            for k, ref in enumerate((gate_in, up_in)):
                to = 2 * first + k * (last - first)
                add(ref.at[0, part, first:last], pair_ref.at[part, to : to + last - first])
        part = pl.ds(c * (hidden // chunks), hidden // chunks)
        add(down_in.at[0, part, :], down_ref.at[part, :])
    add(block_in, block_ref)
    for copy in copies:
        copy.start()
    for copy in copies:
        copy.wait()


def join_kernel(*refs):
    blocks, out_ref, rows_ref = forward(refs[:-2]), refs[-2], refs[-1]
    count = len(blocks)
    tok = blocks[0].shape[1]
    for kind in range(2):
        for j, ref in enumerate(blocks):
            first = (kind * count + j) * tok
            rows_ref[first : first + tok, :] = ref[kind].astype(F32)
    out_ref[...] = rows_ref[...].astype(BF16)


def stack_kernel(*refs):
    out_ref = refs[-1]
    rows = refs[0].shape[0]
    for j, ref in enumerate(refs[:-1]):
        out_ref[j * rows : (j + 1) * rows, :] = ref[...]


def token_rows(refs, start, rows, group, kind, columns):
    parts = []
    for ref in refs:
        for j in range(rows // (2 * group)):
            first = start + (2 * j + kind) * group
            if not isinstance(first, int):
                first = pl.multiple_of(first, group)
            parts.append(ref[pl.ds(first, group), columns])
    return parts[0] if len(parts) == 1 else jnp.concatenate(parts, axis=0)


def put_scores(out_ref, scores_ref, width):
    rows = out_ref.shape[0]
    for c in range((out_ref.shape[1] - width) // LANES):
        out_ref[:, width + c * LANES : width + (c + 1) * LANES] = scores_ref[c * rows : (c + 1) * rows, :].astype(BF16)


def get_scores(in_ref, scores_ref, base, size, width):
    rows = in_ref.shape[0]
    for c in range(-(-size // rows)):
        here = min(rows, size - c * rows)
        tall = min(rows, -(-here // 16) * 16)
        block = in_ref[0:tall, width + c * LANES : width + (c + 1) * LANES].astype(F32)
        scores_ref[base + c * rows : base + c * rows + here, :] = block[:here]


def units_kernel(basis, group, tok, experts, core_mask, blocks, *refs):
    own_refs, other_refs = forward(refs[:blocks]), forward(refs[blocks : 2 * blocks])
    pair_ref, down_ref, kept_ref, message_ref, pieces_ref, score_ref, padded_ref = refs[2 * blocks :]
    hidden, width = down_ref.shape
    rows, buf_width = own_refs[0].shape
    tokens = score_ref.shape[1]
    own = own_index()

    def terms(sets, start, step):
        act = token_rows(sets, start, step, group, 0, slice(None))
        count = act.shape[0]
        combine = combine_rows(act[:, width:], experts)
        ids = lax.broadcasted_iota(jnp.int32, combine.shape, 1)
        column = jnp.sum(jnp.where(ids == own // 2, combine, 0.0), axis=1, keepdims=True)
        act = act[:, :width]
        cot = token_rows(sets, start, step, group, 1, slice(0, width))
        score = jnp.zeros((count, 1), F32)
        grads = []
        for first, last in hidden_parts(hidden):
            size = last - first
            pair = jnp.dot(act, pair_ref[:, 2 * first : 2 * last], preferred_element_type=F32)
            gate_pre = pair[:, :size]
            up_pre = pair[:, size:]
            back = lax.dot_general(cot, down_ref[first:last, :], NT, preferred_element_type=F32)
            sig = jax.nn.sigmoid(gate_pre)
            act_gate = gate_pre * sig
            score = score + jnp.sum(act_gate * up_pre * back, axis=1, keepdims=True)
            weighted = column * back
            grad_gate = weighted * up_pre * sig * (1.0 + gate_pre * (1.0 - sig))
            grad_up = weighted * act_gate
            grads += [grad_gate.astype(BF16), grad_up.astype(BF16)]
        return jnp.concatenate(grads, axis=1), score

    def back_product(grads):
        return lax.dot_general(grads, pair_ref[...], NT, preferred_element_type=F32)

    def in_order(score, place, swap_mask):
        token = lax.broadcasted_iota(jnp.int32, (score.shape[0], tokens), 1)
        side = own ^ swap_mask
        whole = (place_mask(place // tok, basis, side & core_mask != 0) ^ side) * tok + place % tok
        return jnp.sum(jnp.where(whole == token, score, 0.0), axis=0, keepdims=True)

    def send_scores():
        lane_blocks = tokens // LANES
        padded_ref[...] = jnp.zeros(padded_ref.shape, F32)
        value = score_ref[...]
        for piece in range(SCORE_PIECES):
            rounded = value.astype(BF16).astype(F32)
            for b in range(lane_blocks):
                at = piece * lane_blocks + b
                padded_ref[at : at + 1, :] = rounded[:, b * LANES : (b + 1) * LANES]
            value = value - rounded
        pieces_ref[...] = padded_ref[0 : pieces_ref.shape[0], :]
        put_scores(message_ref, padded_ref, width)

    half = blocks * rows // 2
    if 2 * half <= 128:
        grads, score = terms(own_refs + other_refs, 0, rows)
        row = lax.broadcasted_iota(jnp.int32, (2 * half, tokens), 0)
        score_ref[...] = in_order(score, row % half, jnp.where(row < half, 0, core_mask))
        send_scores()
        total = back_product(grads)
        kept_ref[...] = total[:half]
        message_ref[:, 0:width] = total[half:].astype(BF16)
    else:
        step = min(rows, 128)
        score_ref[...] = jnp.zeros(score_ref.shape, F32)
        for out_ref, sets, swap_mask in ((kept_ref, own_refs, 0), (message_ref, other_refs, core_mask)):
            for j, ref in enumerate(sets):

                def one(index):
                    grads, score = terms((ref,), index * step, step)
                    total = back_product(grads)
                    first = pl.multiple_of(j * (rows // 2) + index * (step // 2), step // 2)
                    out_ref[pl.ds(first, step // 2), 0:width] = total.astype(out_ref.dtype)
                    place = lax.broadcasted_iota(jnp.int32, (step // 2, tokens), 0) + first
                    score_ref[...] += in_order(score, place, swap_mask)

                pl.loop(0, rows // step)(one)

        send_scores()


def add_kernel(arrivals, positions, low, *refs):
    kept_ref, pieces_ref = refs[0], refs[1]
    arrived = refs[2 : 2 + arrivals]
    outs = refs[2 + arrivals :]
    next_kept_ref, next_pieces_ref = outs[0], outs[1]
    sends = outs[2 : 2 + len(positions)]
    total_ref, scores_ref = outs[2 + len(positions) :]
    width = kept_ref.shape[1]
    size = pieces_ref.shape[0]
    total = kept_ref[...]
    for ref in arrived:
        total = total + ref[:, 0:width].astype(F32)
    total_ref[...] = total
    if scores_ref.shape[0] > next_pieces_ref.shape[0]:
        scores_ref[...] = jnp.zeros(scores_ref.shape, F32)
    scores_ref[0:size, :] = pieces_ref[...]
    for j, ref in enumerate(arrived):
        get_scores(ref, scores_ref, (j + 1) * size, size, width)
    rows = next_kept_ref.shape[0]
    next_kept_ref[...] = total_ref[0:rows, :]
    next_pieces_ref[...] = scores_ref[0 : next_pieces_ref.shape[0], :]
    chunks = [total_ref[j * rows : (j + 1) * rows, :] for j in range(total_ref.shape[0] // rows)]
    member = own_index() >> low & 3
    for position, ref in zip(positions, sends):
        if isinstance(position, int):
            chunk = chunks[position]
        else:
            chunk = by_member(member, [chunks[p] for p in position])
        ref[:, 0:width] = chunk.astype(BF16)
        put_scores(ref, scores_ref, width)


def table_kernel(basis, back_basis, low, group, tok, core_mask, rows_out, blocks, after_ref, *refs):
    probs_ref, column_ref, mine_ref, pick_ref = refs[2 * blocks :]
    rows, buf_width = refs[0].shape
    half = blocks * rows // 2
    experts, tokens = probs_ref.shape
    lanes = -(-PIECES * experts // LANES) * LANES
    width = buf_width - lanes
    own = own_index()
    column = pl.multiple_of(own * rows_out // LANES * LANES, LANES)
    extras = jnp.zeros((tokens, lanes), F32)
    columns = jnp.zeros((tokens, LANES), F32)
    for index in range(2):
        sets = forward(refs[index * blocks : (index + 1) * blocks])
        row = lax.broadcasted_iota(jnp.int32, (half, tokens), 0)
        token = lax.broadcasted_iota(jnp.int32, (half, tokens), 1)
        side = own ^ (core_mask if index else 0)
        whole = (place_mask(row // tok, basis, side & core_mask != 0) ^ side) * tok + row % tok
        here = jnp.where(whole == token, 1.0, 0.0).astype(BF16)
        part = token_rows(sets, 0, rows, group, 0, slice(width, buf_width))
        extras = extras + lax.dot_general(here, part, TN, preferred_element_type=F32)
        part = token_rows(sets, 0, rows, group, 0, pl.ds(column, LANES))
        columns = columns + lax.dot_general(here, part, TN, preferred_element_type=F32)
    logits = lax.dot_general(piece_sum(experts, lanes, 1), extras.astype(BF16), NT, preferred_element_type=F32)
    raised = jnp.exp(logits - jnp.max(logits, axis=0, keepdims=True))
    probs_ref[...] = raised / jnp.sum(raised, axis=0, keepdims=True)
    column_ref[...] = columns.astype(BF16)
    row = lax.broadcasted_iota(jnp.int32, mine_ref.shape, 0)
    token = lax.broadcasted_iota(jnp.int32, mine_ref.shape, 1)
    mine_ref[...] = jnp.where((row < tok) & (token == own * tok + row), 1.0, 0.0).astype(BF16)
    wide = pick_ref.shape[1]
    sender = lax.broadcasted_iota(jnp.int32, (experts, wide), 1) // SCORE_PIECES
    ids = lax.broadcasted_iota(jnp.int32, (experts, wide), 0)
    mask = place_mask(sender, back_basis, own & core_mask != 0)
    if low is not None:
        member = own >> low & 3
        source = sender >> len(back_basis)
        for k, step in enumerate(REDUCE_STEPS):
            come = by_member(member, [d ^ step.index(d) for d in range(4)]) << low
            mask = mask ^ jnp.where(source == k + 1, come, 0)
    pick_ref[...] = jnp.where(((mask ^ own) >> 1) == ids, 1.0, 0.0).astype(BF16)


def final_kernel(arrivals, *refs):
    probs_ref, column_ref, mine_ref, pick_ref, router_ref, kept_ref, pieces_ref = refs[:7]
    arrived = refs[7 : 7 + arrivals]
    x_out, grad_out, x_ref, grad_ref, scores_ref, sems = refs[7 + arrivals :]
    experts, width = router_ref.shape
    size = pieces_ref.shape[0]
    tok = kept_ref.shape[0]
    own = own_index()
    scores_ref[0:size, :] = pieces_ref[...]
    for j, ref in enumerate(arrived):
        get_scores(ref, scores_ref, (j + 1) * size, size, width)
    blocks = probs_ref.shape[1] // LANES
    wide = scores_ref.shape[0] // blocks
    parts = []
    for b in range(blocks):
        block = scores_ref[...] if blocks == 1 else scores_ref[pl.ds(b, wide, stride=blocks), :]
        parts.append(jnp.dot(pick_ref[...], block.astype(BF16), preferred_element_type=F32))
    scores = parts[0] if blocks == 1 else jnp.concatenate(parts, axis=1)
    probs = probs_ref[...]
    mean = jnp.sum(probs * scores, axis=0, keepdims=True)
    logit_grad = (probs * (scores - mean)).astype(BF16)
    mine = lax.dot_general(mine_ref[...], logit_grad, NT, preferred_element_type=F32)
    part = jnp.dot(mine.astype(BF16), router_ref[...], preferred_element_type=F32)
    total = kept_ref[...]
    for ref in arrived:
        total = total + ref[:, 0:width].astype(F32)
    x_ref[...] = (total + part[:tok]).astype(BF16)
    x_copy = pltpu.make_async_copy(x_ref, x_out, sems.at[0])
    x_copy.start()
    grad = jnp.dot(logit_grad, column_ref[...], preferred_element_type=F32)
    rows_out = grad_ref.shape[1]
    first = own * rows_out % LANES
    grad_ref[...] = pltpu.roll(grad, (LANES - first) % LANES, 1)[:, :rows_out]
    grad_copy = pltpu.make_async_copy(grad_ref, grad_out, sems.at[1])
    grad_copy.start()
    x_copy.wait()
    grad_copy.wait()


def on_device(tokens, grad_out, router_logits, selected, router_w, w_gate, w_up, w_down):
    tok, width = tokens.shape
    experts = router_logits.shape[1]
    hidden = w_gate.shape[2]
    exp_size = lax.axis_size("exp")
    hid_size = lax.axis_size("hid")
    count = exp_size * hid_size
    half = count // 2
    groups, core = stage_masks(exp_size, hid_size)
    core_mask = 1 << core
    basis = [m for group in groups for m in group]
    back_groups = [near_first(group) for group in groups[:0:-1]] + [groups[0]]
    core_pair = (core_mask, core_mask)
    low = (count - 1).bit_length() - 2 if len(groups[0]) == 2 else None
    if low is not None:
        back_groups = back_groups[:-1]
    back_basis = [core_pair] + [m for group in back_groups for m in group]
    if low is not None:
        back_groups = back_groups + [None]
    token_count = count * tok
    lanes = -(-PIECES * experts // LANES) * LANES

    block = pl.pallas_call(
        prep_kernel,
        out_shape=jax.ShapeDtypeStruct((2, tok, width + lanes), BF16),
        in_specs=[HBM_SPEC] * 4,
        out_specs=VMEM_SPEC,
        scratch_shapes=[
            pltpu.VMEM(router_logits.shape, router_logits.dtype),
            pltpu.VMEM(selected.shape, selected.dtype),
            pltpu.SemaphoreType.DMA((4,)),
        ],
        compiler_params=PARAMS,
        name="prep",
    )(*in_hbm(tokens, grad_out, router_logits, selected))

    masks = group_masks(groups[0])
    blocks = [block] + swaps(block, masks[1:], count, core)
    group_rows = tok * len(blocks)
    block = pl.pallas_call(
        join_kernel,
        out_shape=jax.ShapeDtypeStruct((2 * group_rows, width + lanes), BF16),
        in_specs=[VMEM_SPEC] * len(blocks),
        out_specs=VMEM_SPEC,
        scratch_shapes=[pltpu.VMEM((2 * group_rows, width + lanes), F32)],
        compiler_params=PARAMS,
        name="join",
    )(*forward(blocks))
    for group in groups[1:-1]:
        blocks = [block] + swaps(block, group_masks(group)[1:], count, core)
        block = pl.pallas_call(
            stack_kernel,
            out_shape=jax.ShapeDtypeStruct((len(blocks) * block.shape[0], block.shape[1]), BF16),
            in_specs=[VMEM_SPEC] * len(blocks),
            out_specs=VMEM_SPEC,
            compiler_params=PARAMS,
            name="stack",
        )(*blocks)
    chunks = 4
    copied, pair, down = pl.pallas_call(
        functools.partial(load_kernel, chunks),
        out_shape=(
            pltpu.VMEM(block.shape, BF16),
            pltpu.VMEM((width, 2 * hidden), BF16),
            pltpu.VMEM((hidden, width), BF16),
        ),
        in_specs=[VMEM_SPEC] + [HBM_SPEC] * 3,
        out_specs=(VMEM_SPEC,) * 3,
        scratch_shapes=[pltpu.SemaphoreType.DMA(((2 * len(hidden_parts(hidden)) + 1) * chunks + 1,))],
        compiler_params=pltpu.CompilerParams(vmem_limit_bytes=4 * 2**20),
        cost_estimate=pl.CostEstimate(flops=0, bytes_accessed=6 * width * hidden * 2, transcendentals=0),
        name="load",
    )(block, *in_hbm(w_gate, w_up, w_down))
    masks = group_masks(groups[-1]) if len(groups) > 1 else [core_pair]
    blocks = [block] + swaps(block, masks[1:], count, core)
    blocks = forward(blocks)
    blocks = blocks + [swap(b, core_pair, count, core) for b in [copied] + blocks[1:]]
    block_count = len(blocks) // 2

    unit_rows = SCORE_PIECES * token_count // LANES
    extra = -(-unit_rows // (half * tok)) * LANES
    kept, message, pieces = pl.pallas_call(
        functools.partial(units_kernel, basis, group_rows, tok, experts, core_mask, block_count),
        out_shape=(
            jax.ShapeDtypeStruct((half * tok, width), F32),
            jax.ShapeDtypeStruct((half * tok, width + extra), BF16),
            jax.ShapeDtypeStruct((unit_rows, LANES), F32),
        ),
        in_specs=[VMEM_SPEC] * (len(blocks) + 2),
        out_specs=(VMEM_SPEC,) * 3,
        scratch_shapes=[
            pltpu.VMEM((1, token_count), F32),
            pltpu.VMEM((max(half * tok * extra // LANES, unit_rows), LANES), F32),
        ],
        compiler_params=PARAMS,
        cost_estimate=pl.CostEstimate(
            flops=10 * token_count * width * hidden,
            bytes_accessed=3 * width * hidden * 2 + 2 * token_count * width * 2,
            transcendentals=token_count * hidden,
        ),
        name="units",
    )(*blocks, pair, down)

    arrived = [swap(message, core_pair, count, core)]
    tables = None
    rows_out = width // count
    for group, back_group in zip(groups[::-1], back_groups):
        order = [m[0] for m in group_masks(group)]
        if back_group is None:
            positions = [[order.index((d ^ step[d]) << low) for d in range(4)] for step in REDUCE_STEPS]
        else:
            back_masks = group_masks(back_group)
            positions = [order.index(m[0]) for m in back_masks[1:]]
        radix = len(order)
        rows = kept.shape[0]
        next_rows = rows // radix
        size = pieces.shape[0] * (1 + len(arrived))
        extra = -(-size // next_rows) * LANES
        sends = [jax.ShapeDtypeStruct((next_rows, width + extra), BF16)] * (radix - 1)
        outs = pl.pallas_call(
            functools.partial(add_kernel, len(arrived), positions, low or 0),
            out_shape=[
                jax.ShapeDtypeStruct((next_rows, width), F32),
                jax.ShapeDtypeStruct((size, LANES), F32),
            ]
            + sends,
            in_specs=[VMEM_SPEC] * (2 + len(arrived)),
            out_specs=[VMEM_SPEC] * (1 + radix),
            scratch_shapes=[
                pltpu.VMEM((rows, width), F32),
                pltpu.VMEM((max(next_rows * extra // LANES, size), LANES), F32),
            ],
            compiler_params=PARAMS,
            name="add",
        )(kept, pieces, *arrived)
        kept, pieces = outs[0], outs[1]
        if tables is None:
            tables = pl.pallas_call(
                functools.partial(table_kernel, basis, back_basis, low, group_rows, tok, core_mask, rows_out, block_count),
                out_shape=(
                    jax.ShapeDtypeStruct((experts, token_count), F32),
                    jax.ShapeDtypeStruct((token_count, LANES), BF16),
                    jax.ShapeDtypeStruct((16, token_count), BF16),
                    jax.ShapeDtypeStruct((experts, SCORE_PIECES * count), BF16),
                ),
                in_specs=[pl.BlockSpec(memory_space=pl.ANY)] + [VMEM_SPEC] * len(blocks),
                out_specs=(VMEM_SPEC,) * 4,
                compiler_params=PARAMS,
                cost_estimate=pl.CostEstimate(flops=10**9, bytes_accessed=10**6, transcendentals=0),
                name="tables",
            )(pieces, *blocks)
        if back_group is None:
            arrived = [shift(piece, step, count, low) for piece, step in zip(outs[2:], REDUCE_STEPS)]
        else:
            arrived = [swap(piece, m, count, core) for piece, m in zip(outs[2:], back_masks[1:])]

    x_grad, grad = pl.pallas_call(
        functools.partial(final_kernel, len(arrived)),
        out_shape=(
            jax.ShapeDtypeStruct((tok, width), BF16),
            jax.ShapeDtypeStruct((experts, rows_out), F32),
        ),
        in_specs=[VMEM_SPEC] * (7 + len(arrived)),
        out_specs=(HBM_SPEC, HBM_SPEC),
        scratch_shapes=[
            pltpu.VMEM((tok, width), BF16),
            pltpu.VMEM((experts, rows_out), F32),
            pltpu.VMEM((pieces.shape[0] * (1 + len(arrived)), LANES), F32),
            pltpu.SemaphoreType.DMA((2,)),
        ],
        compiler_params=PARAMS,
        name="final",
    )(*tables, router_w.T, kept, pieces, *arrived)
    return (x_grad, grad.T)


def solution(mesh):
    rows = P(AXES, None)
    units = P(AXES, None, None)
    return jax.shard_map(
        on_device,
        mesh=mesh,
        in_specs=(rows, rows, rows, rows, P(), units, units, units),
        out_specs=(rows, rows),
        check_vma=False,
    )
```

```python
import functools

import jax
import jax.numpy as jnp
from jax import lax
from jax.experimental import pallas as pl
from jax.experimental.pallas import tpu as pltpu
from jax.sharding import PartitionSpec as P

AXES = ("exp", "hid")
LANES = 128
PIECES = 4
SCORE_PIECES = 2
VMEM_SPEC = pl.BlockSpec(memory_space=pltpu.VMEM)
HBM_SPEC = pl.BlockSpec(memory_space=pltpu.HBM)
F32 = jnp.float32
BF16 = jnp.bfloat16
NT = (((1,), (1,)), ((), ()))
TN = (((0,), (0,)), ((), ()))
PARAMS = pltpu.CompilerParams(vmem_limit_bytes=24 * 2**20)


def stage_masks(exp_size, hid_size):
    hid_bits = hid_size.bit_length() - 1
    all_bits = (exp_size * hid_size).bit_length() - 1
    core = hid_bits
    first = list(range(max(core + 1, all_bits - 2), all_bits))
    middle = [b for b in range(all_bits) if b != core and b not in first]
    groups = [first] + [middle[i : i + 2] for i in range(0, len(middle), 2)]
    bases = [[(sum(1 << b for b in group[: len(group) - i]),) * 2 for i in range(len(group))] for group in groups]
    bases[0] = [(sum(1 << b for b in first[i:]),) * 2 for i in range(len(first))][::-1]
    return bases, core


def cross(a, b):
    return (a[0] ^ b[0], a[1] ^ b[1])


def group_masks(basis):
    masks = [(0, 0)]
    for mask in basis:
        masks = masks + [cross(m, mask) for m in masks]
    return masks


def near_first(basis):
    return [cross(basis[0], basis[1]), basis[1]] if len(basis) == 2 else basis


def swap(block, mask, count, core):
    return lax.ppermute(block, AXES, [(i, i ^ mask[i >> core & 1]) for i in range(count)])


REDUCE_STEPS = ((1, 3, 0, 2), (3, 2, 1, 0), (2, 0, 3, 1))


def by_member(member, values):
    total = values[0]
    for k in range(1, len(values)):
        total = jnp.where(member == k, values[k], total)
    return total


def shift(block, step, count, low):
    return lax.ppermute(block, AXES, [(i, i ^ ((i >> low & 3) ^ step[i >> low & 3]) << low) for i in range(count)])


def swaps(block, masks, count, core):
    return [swap(block, m, count, core) for m in masks]


def forward(blocks):
    return blocks[:1] + blocks[:0:-1]


def place_mask(place, basis, upper):
    total = jnp.zeros_like(place)
    for digit, (low, high) in enumerate(basis):
        mask = low if low == high else jnp.where(upper, high, low)
        total = total ^ (((place >> digit) & 1) * mask)
    return total


def own_index():
    return lax.axis_index("exp") * lax.axis_size("hid") + lax.axis_index("hid")


def in_hbm(*arrays):
    return tuple(pltpu.with_memory_space_constraint(a, pltpu.HBM) for a in arrays)


def piece_sum(experts, lanes, axis):
    shape = (lanes, experts) if axis == 0 else (experts, lanes)
    lane = lax.broadcasted_iota(jnp.int32, shape, axis)
    ids = lax.broadcasted_iota(jnp.int32, shape, 1 - axis)
    tally = jnp.zeros(shape, F32)
    for k in range(1, PIECES):
        tally = tally + jnp.where(lane == ids + k * experts, 1.0, 0.0)
    return tally.astype(BF16)


def combine_rows(extras, experts):
    hit = extras[:, :experts].astype(F32) > 0.5
    logits = jnp.dot(extras, piece_sum(experts, extras.shape[1], 0), preferred_element_type=F32)
    top = jnp.max(jnp.where(hit, logits, -jnp.inf), axis=1, keepdims=True)
    raised = jnp.where(hit, jnp.exp(jnp.minimum(logits - top, 0.0)), 0.0)
    return (raised / jnp.sum(raised, axis=1, keepdims=True)).astype(BF16).astype(F32)


def prep_kernel(tokens_in, grad_in, logits_in, chosen_in, out_ref, logits_ref, chosen_ref, sems):
    tok, width = tokens_in.shape
    pairs = [
        (logits_in, logits_ref),
        (chosen_in, chosen_ref),
        (tokens_in, out_ref.at[0, :, 0:width]),
        (grad_in, out_ref.at[1, :, 0:width]),
    ]
    copies = [pltpu.make_async_copy(src, dst, sems.at[i]) for i, (src, dst) in enumerate(pairs)]
    for copy in copies:
        copy.start()
    copies[0].wait()
    copies[1].wait()
    logits = logits_ref[...]
    chosen = chosen_ref[...]
    experts = logits.shape[1]
    ids = lax.broadcasted_iota(jnp.int32, logits.shape, 1)
    hit = ids == chosen[:, 0:1]
    for k in range(1, chosen.shape[1]):
        hit = hit | (ids == chosen[:, k : k + 1])
    parts = [jnp.where(hit, 1.0, 0.0)]
    rest = logits
    for _ in range(PIECES - 1):
        parts.append(rest)
        rest = rest - rest.astype(BF16).astype(F32)
    lanes = out_ref.shape[2] - width
    spare = lanes - PIECES * experts
    extras = jnp.concatenate(parts + ([jnp.zeros((tok, spare), F32)] if spare else []), axis=1)
    out_ref[0, :, width:] = extras.astype(BF16)
    out_ref[1, :, width:] = jnp.zeros((tok, lanes), BF16)
    copies[2].wait()
    copies[3].wait()


def hidden_parts(hidden):
    main = hidden // 256 * 256
    return [(0, main), (main, hidden)] if 0 < main < hidden else [(0, hidden)]


def load_kernel(chunks, block_in, gate_in, up_in, down_in, block_ref, pair_ref, down_ref, sems):
    copies = []

    def add(src, dst):
        copies.append(pltpu.make_async_copy(src, dst, sems.at[len(copies)]))

    hidden, width = down_ref.shape
    for c in range(chunks):
        part = pl.ds(c * (width // chunks), width // chunks)
        for first, last in hidden_parts(hidden):
            for k, ref in enumerate((gate_in, up_in)):
                to = 2 * first + k * (last - first)
                add(ref.at[0, part, first:last], pair_ref.at[part, to : to + last - first])
        part = pl.ds(c * (hidden // chunks), hidden // chunks)
        add(down_in.at[0, part, :], down_ref.at[part, :])
    add(block_in, block_ref)
    for copy in copies:
        copy.start()
    for copy in copies:
        copy.wait()


def join_kernel(*refs):
    blocks, out_ref, rows_ref = forward(refs[:-2]), refs[-2], refs[-1]
    count = len(blocks)
    tok = blocks[0].shape[1]
    for kind in range(2):
        for j, ref in enumerate(blocks):
            first = (kind * count + j) * tok
            rows_ref[first : first + tok, :] = ref[kind].astype(F32)
    out_ref[...] = rows_ref[...].astype(BF16)


def stack_kernel(*refs):
    out_ref = refs[-1]
    rows = refs[0].shape[0]
    for j, ref in enumerate(refs[:-1]):
        out_ref[j * rows : (j + 1) * rows, :] = ref[...]


def token_rows(refs, start, rows, group, kind, columns):
    parts = []
    for ref in refs:
        for j in range(rows // (2 * group)):
            first = start + (2 * j + kind) * group
            if not isinstance(first, int):
                first = pl.multiple_of(first, group)
            parts.append(ref[pl.ds(first, group), columns])
    return parts[0] if len(parts) == 1 else jnp.concatenate(parts, axis=0)


def put_scores(out_ref, scores_ref, width):
    rows = out_ref.shape[0]
    for c in range((out_ref.shape[1] - width) // LANES):
        out_ref[:, width + c * LANES : width + (c + 1) * LANES] = scores_ref[c * rows : (c + 1) * rows, :].astype(BF16)


def get_scores(in_ref, scores_ref, base, size, width):
    rows = in_ref.shape[0]
    for c in range(-(-size // rows)):
        here = min(rows, size - c * rows)
        tall = min(rows, -(-here // 16) * 16)
        block = in_ref[0:tall, width + c * LANES : width + (c + 1) * LANES].astype(F32)
        scores_ref[base + c * rows : base + c * rows + here, :] = block[:here]


def units_kernel(basis, group, tok, experts, core_mask, blocks, *refs):
    own_refs, other_refs = forward(refs[:blocks]), forward(refs[blocks : 2 * blocks])
    pair_ref, down_ref, kept_ref, message_ref, pieces_ref, score_ref, padded_ref = refs[2 * blocks :]
    hidden, width = down_ref.shape
    rows, buf_width = own_refs[0].shape
    tokens = score_ref.shape[1]
    own = own_index()

    def terms(sets, start, step):
        act = token_rows(sets, start, step, group, 0, slice(None))
        count = act.shape[0]
        combine = combine_rows(act[:, width:], experts)
        ids = lax.broadcasted_iota(jnp.int32, combine.shape, 1)
        column = jnp.sum(jnp.where(ids == own // 2, combine, 0.0), axis=1, keepdims=True)
        act = act[:, :width]
        cot = token_rows(sets, start, step, group, 1, slice(0, width))
        score = jnp.zeros((count, 1), F32)
        grads = []
        for first, last in hidden_parts(hidden):
            size = last - first
            pair = jnp.dot(act, pair_ref[:, 2 * first : 2 * last], preferred_element_type=F32)
            gate_pre = pair[:, :size]
            up_pre = pair[:, size:]
            back = lax.dot_general(cot, down_ref[first:last, :], NT, preferred_element_type=F32)
            sig = jax.nn.sigmoid(gate_pre)
            act_gate = gate_pre * sig
            score = score + jnp.sum(act_gate * up_pre * back, axis=1, keepdims=True)
            weighted = column * back
            grad_gate = weighted * up_pre * sig * (1.0 + gate_pre * (1.0 - sig))
            grad_up = weighted * act_gate
            grads += [grad_gate.astype(BF16), grad_up.astype(BF16)]
        return jnp.concatenate(grads, axis=1), score

    def back_product(grads):
        return lax.dot_general(grads, pair_ref[...], NT, preferred_element_type=F32)

    def in_order(score, place, swap_mask):
        token = lax.broadcasted_iota(jnp.int32, (score.shape[0], tokens), 1)
        side = own ^ swap_mask
        whole = (place_mask(place // tok, basis, side & core_mask != 0) ^ side) * tok + place % tok
        return jnp.sum(jnp.where(whole == token, score, 0.0), axis=0, keepdims=True)

    def send_scores():
        lane_blocks = tokens // LANES
        padded_ref[...] = jnp.zeros(padded_ref.shape, F32)
        value = score_ref[...]
        for piece in range(SCORE_PIECES):
            rounded = value.astype(BF16).astype(F32)
            for b in range(lane_blocks):
                at = piece * lane_blocks + b
                padded_ref[at : at + 1, :] = rounded[:, b * LANES : (b + 1) * LANES]
            value = value - rounded
        pieces_ref[...] = padded_ref[0 : pieces_ref.shape[0], :]
        put_scores(message_ref, padded_ref, width)

    half = blocks * rows // 2
    if 2 * half <= 128:
        grads, score = terms(own_refs + other_refs, 0, rows)
        row = lax.broadcasted_iota(jnp.int32, (2 * half, tokens), 0)
        score_ref[...] = in_order(score, row % half, jnp.where(row < half, 0, core_mask))
        send_scores()
        total = back_product(grads)
        kept_ref[...] = total[:half]
        message_ref[:, 0:width] = total[half:].astype(BF16)
    else:
        step = min(rows, 128)
        score_ref[...] = jnp.zeros(score_ref.shape, F32)
        for out_ref, sets, swap_mask in ((kept_ref, own_refs, 0), (message_ref, other_refs, core_mask)):
            for j, ref in enumerate(sets):

                def one(index):
                    grads, score = terms((ref,), index * step, step)
                    total = back_product(grads)
                    first = pl.multiple_of(j * (rows // 2) + index * (step // 2), step // 2)
                    out_ref[pl.ds(first, step // 2), 0:width] = total.astype(out_ref.dtype)
                    place = lax.broadcasted_iota(jnp.int32, (step // 2, tokens), 0) + first
                    score_ref[...] += in_order(score, place, swap_mask)

                pl.loop(0, rows // step)(one)

        send_scores()


def add_kernel(arrivals, positions, low, *refs):
    kept_ref, pieces_ref = refs[0], refs[1]
    arrived = refs[2 : 2 + arrivals]
    outs = refs[2 + arrivals :]
    next_kept_ref, next_pieces_ref = outs[0], outs[1]
    sends = outs[2 : 2 + len(positions)]
    total_ref, scores_ref = outs[2 + len(positions) :]
    width = kept_ref.shape[1]
    size = pieces_ref.shape[0]
    total = kept_ref[...]
    for ref in arrived:
        total = total + ref[:, 0:width].astype(F32)
    total_ref[...] = total
    if scores_ref.shape[0] > next_pieces_ref.shape[0]:
        scores_ref[...] = jnp.zeros(scores_ref.shape, F32)
    scores_ref[0:size, :] = pieces_ref[...]
    for j, ref in enumerate(arrived):
        get_scores(ref, scores_ref, (j + 1) * size, size, width)
    rows = next_kept_ref.shape[0]
    next_kept_ref[...] = total_ref[0:rows, :]
    next_pieces_ref[...] = scores_ref[0 : next_pieces_ref.shape[0], :]
    chunks = [total_ref[j * rows : (j + 1) * rows, :] for j in range(total_ref.shape[0] // rows)]
    member = own_index() >> low & 3
    for position, ref in zip(positions, sends):
        if isinstance(position, int):
            chunk = chunks[position]
        else:
            chunk = by_member(member, [chunks[p] for p in position])
        ref[:, 0:width] = chunk.astype(BF16)
        put_scores(ref, scores_ref, width)


def table_kernel(basis, back_basis, low, group, tok, core_mask, rows_out, blocks, after_ref, *refs):
    probs_ref, column_ref, mine_ref, pick_ref = refs[2 * blocks :]
    rows, buf_width = refs[0].shape
    half = blocks * rows // 2
    experts, tokens = probs_ref.shape
    lanes = -(-PIECES * experts // LANES) * LANES
    width = buf_width - lanes
    own = own_index()
    column = pl.multiple_of(own * rows_out // LANES * LANES, LANES)
    extras = jnp.zeros((tokens, lanes), F32)
    columns = jnp.zeros((tokens, LANES), F32)
    for index in range(2):
        sets = forward(refs[index * blocks : (index + 1) * blocks])
        row = lax.broadcasted_iota(jnp.int32, (half, tokens), 0)
        token = lax.broadcasted_iota(jnp.int32, (half, tokens), 1)
        side = own ^ (core_mask if index else 0)
        whole = (place_mask(row // tok, basis, side & core_mask != 0) ^ side) * tok + row % tok
        here = jnp.where(whole == token, 1.0, 0.0).astype(BF16)
        part = token_rows(sets, 0, rows, group, 0, slice(width, buf_width))
        extras = extras + lax.dot_general(here, part, TN, preferred_element_type=F32)
        part = token_rows(sets, 0, rows, group, 0, pl.ds(column, LANES))
        columns = columns + lax.dot_general(here, part, TN, preferred_element_type=F32)
    logits = lax.dot_general(piece_sum(experts, lanes, 1), extras.astype(BF16), NT, preferred_element_type=F32)
    raised = jnp.exp(logits - jnp.max(logits, axis=0, keepdims=True))
    probs_ref[...] = raised / jnp.sum(raised, axis=0, keepdims=True)
    column_ref[...] = columns.astype(BF16)
    row = lax.broadcasted_iota(jnp.int32, mine_ref.shape, 0)
    token = lax.broadcasted_iota(jnp.int32, mine_ref.shape, 1)
    mine_ref[...] = jnp.where((row < tok) & (token == own * tok + row), 1.0, 0.0).astype(BF16)
    wide = pick_ref.shape[1]
    sender = lax.broadcasted_iota(jnp.int32, (experts, wide), 1) // SCORE_PIECES
    ids = lax.broadcasted_iota(jnp.int32, (experts, wide), 0)
    mask = place_mask(sender, back_basis, own & core_mask != 0)
    if low is not None:
        member = own >> low & 3
        source = sender >> len(back_basis)
        for k, step in enumerate(REDUCE_STEPS):
            come = by_member(member, [d ^ step.index(d) for d in range(4)]) << low
            mask = mask ^ jnp.where(source == k + 1, come, 0)
    pick_ref[...] = jnp.where(((mask ^ own) >> 1) == ids, 1.0, 0.0).astype(BF16)


def final_kernel(arrivals, *refs):
    probs_ref, column_ref, mine_ref, pick_ref, router_ref, kept_ref, pieces_ref = refs[:7]
    arrived = refs[7 : 7 + arrivals]
    x_out, grad_out, x_ref, grad_ref, scores_ref, sems = refs[7 + arrivals :]
    experts, width = router_ref.shape
    size = pieces_ref.shape[0]
    tok = kept_ref.shape[0]
    own = own_index()
    scores_ref[0:size, :] = pieces_ref[...]
    for j, ref in enumerate(arrived):
        get_scores(ref, scores_ref, (j + 1) * size, size, width)
    blocks = probs_ref.shape[1] // LANES
    wide = scores_ref.shape[0] // blocks
    parts = []
    for b in range(blocks):
        block = scores_ref[...] if blocks == 1 else scores_ref[pl.ds(b, wide, stride=blocks), :]
        parts.append(jnp.dot(pick_ref[...], block.astype(BF16), preferred_element_type=F32))
    scores = parts[0] if blocks == 1 else jnp.concatenate(parts, axis=1)
    probs = probs_ref[...]
    mean = jnp.sum(probs * scores, axis=0, keepdims=True)
    logit_grad = (probs * (scores - mean)).astype(BF16)
    mine = lax.dot_general(mine_ref[...], logit_grad, NT, preferred_element_type=F32)
    part = jnp.dot(mine.astype(BF16), router_ref[...], preferred_element_type=F32)
    total = kept_ref[...]
    for ref in arrived:
        total = total + ref[:, 0:width].astype(F32)
    x_ref[...] = (total + part[:tok]).astype(BF16)
    x_copy = pltpu.make_async_copy(x_ref, x_out, sems.at[0])
    x_copy.start()
    grad = jnp.dot(logit_grad, column_ref[...], preferred_element_type=F32)
    rows_out = grad_ref.shape[1]
    first = own * rows_out % LANES
    grad_ref[...] = pltpu.roll(grad, (LANES - first) % LANES, 1)[:, :rows_out]
    grad_copy = pltpu.make_async_copy(grad_ref, grad_out, sems.at[1])
    grad_copy.start()
    x_copy.wait()
    grad_copy.wait()


def on_device(tokens, grad_out, router_logits, selected, router_w, w_gate, w_up, w_down):
    tok, width = tokens.shape
    experts = router_logits.shape[1]
    hidden = w_gate.shape[2]
    exp_size = lax.axis_size("exp")
    hid_size = lax.axis_size("hid")
    count = exp_size * hid_size
    half = count // 2
    groups, core = stage_masks(exp_size, hid_size)
    core_mask = 1 << core
    basis = [m for group in groups for m in group]
    back_groups = [near_first(group) for group in groups[:0:-1]] + [groups[0]]
    core_pair = (core_mask, core_mask)
    low = (count - 1).bit_length() - 2 if len(groups[0]) == 2 else None
    if low is not None:
        back_groups = back_groups[:-1]
    back_basis = [core_pair] + [m for group in back_groups for m in group]
    if low is not None:
        back_groups = back_groups + [None]
    token_count = count * tok
    lanes = -(-PIECES * experts // LANES) * LANES

    block = pl.pallas_call(
        prep_kernel,
        out_shape=jax.ShapeDtypeStruct((2, tok, width + lanes), BF16),
        in_specs=[HBM_SPEC] * 4,
        out_specs=VMEM_SPEC,
        scratch_shapes=[
            pltpu.VMEM(router_logits.shape, router_logits.dtype),
            pltpu.VMEM(selected.shape, selected.dtype),
            pltpu.SemaphoreType.DMA((4,)),
        ],
        compiler_params=PARAMS,
        name="prep",
    )(*in_hbm(tokens, grad_out, router_logits, selected))

    masks = group_masks(groups[0])
    blocks = [block] + swaps(block, masks[1:], count, core)
    group_rows = tok * len(blocks)
    block = pl.pallas_call(
        join_kernel,
        out_shape=jax.ShapeDtypeStruct((2 * group_rows, width + lanes), BF16),
        in_specs=[VMEM_SPEC] * len(blocks),
        out_specs=VMEM_SPEC,
        scratch_shapes=[pltpu.VMEM((2 * group_rows, width + lanes), F32)],
        compiler_params=PARAMS,
        name="join",
    )(*forward(blocks))
    for group in groups[1:-1]:
        blocks = [block] + swaps(block, group_masks(group)[1:], count, core)
        block = pl.pallas_call(
            stack_kernel,
            out_shape=jax.ShapeDtypeStruct((len(blocks) * block.shape[0], block.shape[1]), BF16),
            in_specs=[VMEM_SPEC] * len(blocks),
            out_specs=VMEM_SPEC,
            compiler_params=PARAMS,
            name="stack",
        )(*blocks)
    chunks = 4
    copied, pair, down = pl.pallas_call(
        functools.partial(load_kernel, chunks),
        out_shape=(
            pltpu.VMEM(block.shape, BF16),
            pltpu.VMEM((width, 2 * hidden), BF16),
            pltpu.VMEM((hidden, width), BF16),
        ),
        in_specs=[VMEM_SPEC] + [HBM_SPEC] * 3,
        out_specs=(VMEM_SPEC,) * 3,
        scratch_shapes=[pltpu.SemaphoreType.DMA(((2 * len(hidden_parts(hidden)) + 1) * chunks + 1,))],
        compiler_params=pltpu.CompilerParams(vmem_limit_bytes=4 * 2**20),
        cost_estimate=pl.CostEstimate(flops=0, bytes_accessed=6 * width * hidden * 2, transcendentals=0),
        name="load",
    )(block, *in_hbm(w_gate, w_up, w_down))
    masks = group_masks(groups[-1]) if len(groups) > 1 else [core_pair]
    blocks = [block] + swaps(block, masks[1:], count, core)
    blocks = forward(blocks)
    blocks = blocks + [swap(b, core_pair, count, core) for b in [copied] + blocks[1:]]
    block_count = len(blocks) // 2

    unit_rows = SCORE_PIECES * token_count // LANES
    extra = -(-unit_rows // (half * tok)) * LANES
    kept, message, pieces = pl.pallas_call(
        functools.partial(units_kernel, basis, group_rows, tok, experts, core_mask, block_count),
        out_shape=(
            jax.ShapeDtypeStruct((half * tok, width), F32),
            jax.ShapeDtypeStruct((half * tok, width + extra), BF16),
            jax.ShapeDtypeStruct((unit_rows, LANES), F32),
        ),
        in_specs=[VMEM_SPEC] * (len(blocks) + 2),
        out_specs=(VMEM_SPEC,) * 3,
        scratch_shapes=[
            pltpu.VMEM((1, token_count), F32),
            pltpu.VMEM((max(half * tok * extra // LANES, unit_rows), LANES), F32),
        ],
        compiler_params=PARAMS,
        cost_estimate=pl.CostEstimate(
            flops=10 * token_count * width * hidden,
            bytes_accessed=3 * width * hidden * 2 + 2 * token_count * width * 2,
            transcendentals=token_count * hidden,
        ),
        name="units",
    )(*blocks, pair, down)

    arrived = [swap(message, core_pair, count, core)]
    tables = None
    rows_out = width // count
    for group, back_group in zip(groups[::-1], back_groups):
        order = [m[0] for m in group_masks(group)]
        if back_group is None:
            positions = [[order.index((d ^ step[d]) << low) for d in range(4)] for step in REDUCE_STEPS]
        else:
            back_masks = group_masks(back_group)
            positions = [order.index(m[0]) for m in back_masks[1:]]
        radix = len(order)
        rows = kept.shape[0]
        next_rows = rows // radix
        size = pieces.shape[0] * (1 + len(arrived))
        extra = -(-size // next_rows) * LANES
        sends = [jax.ShapeDtypeStruct((next_rows, width + extra), BF16)] * (radix - 1)
        outs = pl.pallas_call(
            functools.partial(add_kernel, len(arrived), positions, low or 0),
            out_shape=[
                jax.ShapeDtypeStruct((next_rows, width), F32),
                jax.ShapeDtypeStruct((size, LANES), F32),
            ]
            + sends,
            in_specs=[VMEM_SPEC] * (2 + len(arrived)),
            out_specs=[VMEM_SPEC] * (1 + radix),
            scratch_shapes=[
                pltpu.VMEM((rows, width), F32),
                pltpu.VMEM((max(next_rows * extra // LANES, size), LANES), F32),
            ],
            compiler_params=PARAMS,
            name="add",
        )(kept, pieces, *arrived)
        kept, pieces = outs[0], outs[1]
        if tables is None:
            tables = pl.pallas_call(
                functools.partial(table_kernel, basis, back_basis, low, group_rows, tok, core_mask, rows_out, block_count),
                out_shape=(
                    jax.ShapeDtypeStruct((experts, token_count), F32),
                    jax.ShapeDtypeStruct((token_count, LANES), BF16),
                    jax.ShapeDtypeStruct((16, token_count), BF16),
                    jax.ShapeDtypeStruct((experts, SCORE_PIECES * count), BF16),
                ),
                in_specs=[pl.BlockSpec(memory_space=pl.ANY)] + [VMEM_SPEC] * len(blocks),
                out_specs=(VMEM_SPEC,) * 4,
                compiler_params=PARAMS,
                cost_estimate=pl.CostEstimate(flops=10**9, bytes_accessed=10**6, transcendentals=0),
                name="tables",
            )(pieces, *blocks)
        if back_group is None:
            arrived = [shift(piece, step, count, low) for piece, step in zip(outs[2:], REDUCE_STEPS)]
        else:
            arrived = [swap(piece, m, count, core) for piece, m in zip(outs[2:], back_masks[1:])]

    x_grad, grad = pl.pallas_call(
        functools.partial(final_kernel, len(arrived)),
        out_shape=(
            jax.ShapeDtypeStruct((tok, width), BF16),
            jax.ShapeDtypeStruct((experts, rows_out), F32),
        ),
        in_specs=[VMEM_SPEC] * (7 + len(arrived)),
        out_specs=(HBM_SPEC, HBM_SPEC),
        scratch_shapes=[
            pltpu.VMEM((tok, width), BF16),
            pltpu.VMEM((experts, rows_out), F32),
            pltpu.VMEM((pieces.shape[0] * (1 + len(arrived)), LANES), F32),
            pltpu.SemaphoreType.DMA((2,)),
        ],
        compiler_params=PARAMS,
        name="final",
    )(*tables, router_w.T, kept, pieces, *arrived)
    return (x_grad, grad.T)


def solution(mesh):
    rows = P(AXES, None)
    units = P(AXES, None, None)
    return jax.shard_map(
        on_device,
        mesh=mesh,
        in_specs=(rows, rows, rows, rows, P(), units, units, units),
        out_specs=(rows, rows),
        check_vma=False,
    )
```

```python
import functools

import jax
import jax.numpy as jnp
from jax import lax
from jax.experimental import pallas as pl
from jax.experimental.pallas import tpu as pltpu
from jax.sharding import PartitionSpec as P

AXES = ("exp", "hid")
LANES = 128
PIECES = 4
SCORE_PIECES = 2
VMEM_SPEC = pl.BlockSpec(memory_space=pltpu.VMEM)
HBM_SPEC = pl.BlockSpec(memory_space=pltpu.HBM)
F32 = jnp.float32
BF16 = jnp.bfloat16
NT = (((1,), (1,)), ((), ()))
TN = (((0,), (0,)), ((), ()))
PARAMS = pltpu.CompilerParams(vmem_limit_bytes=24 * 2**20)


def stage_masks(exp_size, hid_size):
    hid_bits = hid_size.bit_length() - 1
    all_bits = (exp_size * hid_size).bit_length() - 1
    core = hid_bits
    first = list(range(max(core + 1, all_bits - 2), all_bits))
    middle = [b for b in range(all_bits) if b != core and b not in first]
    groups = [first] + [middle[i : i + 2] for i in range(0, len(middle), 2)]
    bases = [[(sum(1 << b for b in group[: len(group) - i]),) * 2 for i in range(len(group))] for group in groups]
    bases[0] = [(sum(1 << b for b in first[i:]),) * 2 for i in range(len(first))][::-1]
    return bases, core


def cross(a, b):
    return (a[0] ^ b[0], a[1] ^ b[1])


def group_masks(basis):
    masks = [(0, 0)]
    for mask in basis:
        masks = masks + [cross(m, mask) for m in masks]
    return masks


def near_first(basis):
    return [basis[1], cross(basis[0], basis[1])] if len(basis) == 2 else basis


def swap(block, mask, count, core):
    return lax.ppermute(block, AXES, [(i, i ^ mask[i >> core & 1]) for i in range(count)])


REDUCE_STEPS = ((1, 3, 0, 2), (3, 2, 1, 0), (2, 0, 3, 1))


def by_member(member, values):
    total = values[0]
    for k in range(1, len(values)):
        total = jnp.where(member == k, values[k], total)
    return total


def shift(block, step, count, low):
    return lax.ppermute(block, AXES, [(i, i ^ ((i >> low & 3) ^ step[i >> low & 3]) << low) for i in range(count)])


def swaps(block, masks, count, core):
    return [swap(block, m, count, core) for m in masks]


def forward(blocks):
    return blocks[:1] + blocks[:0:-1]


def place_mask(place, basis, upper):
    total = jnp.zeros_like(place)
    for digit, (low, high) in enumerate(basis):
        mask = low if low == high else jnp.where(upper, high, low)
        total = total ^ (((place >> digit) & 1) * mask)
    return total


def own_index():
    return lax.axis_index("exp") * lax.axis_size("hid") + lax.axis_index("hid")


def in_hbm(*arrays):
    return tuple(pltpu.with_memory_space_constraint(a, pltpu.HBM) for a in arrays)


def piece_sum(experts, lanes, axis):
    shape = (lanes, experts) if axis == 0 else (experts, lanes)
    lane = lax.broadcasted_iota(jnp.int32, shape, axis)
    ids = lax.broadcasted_iota(jnp.int32, shape, 1 - axis)
    tally = jnp.zeros(shape, F32)
    for k in range(1, PIECES):
        tally = tally + jnp.where(lane == ids + k * experts, 1.0, 0.0)
    return tally.astype(BF16)


def combine_rows(extras, experts):
    hit = extras[:, :experts].astype(F32) > 0.5
    logits = jnp.dot(extras, piece_sum(experts, extras.shape[1], 0), preferred_element_type=F32)
    top = jnp.max(jnp.where(hit, logits, -jnp.inf), axis=1, keepdims=True)
    raised = jnp.where(hit, jnp.exp(jnp.minimum(logits - top, 0.0)), 0.0)
    return (raised / jnp.sum(raised, axis=1, keepdims=True)).astype(BF16).astype(F32)


def prep_kernel(tokens_in, grad_in, logits_in, chosen_in, out_ref, logits_ref, chosen_ref, sems):
    tok, width = tokens_in.shape
    pairs = [
        (logits_in, logits_ref),
        (chosen_in, chosen_ref),
        (tokens_in, out_ref.at[0, :, 0:width]),
        (grad_in, out_ref.at[1, :, 0:width]),
    ]
    copies = [pltpu.make_async_copy(src, dst, sems.at[i]) for i, (src, dst) in enumerate(pairs)]
    for copy in copies:
        copy.start()
    copies[0].wait()
    copies[1].wait()
    logits = logits_ref[...]
    chosen = chosen_ref[...]
    experts = logits.shape[1]
    ids = lax.broadcasted_iota(jnp.int32, logits.shape, 1)
    hit = ids == chosen[:, 0:1]
    for k in range(1, chosen.shape[1]):
        hit = hit | (ids == chosen[:, k : k + 1])
    parts = [jnp.where(hit, 1.0, 0.0)]
    rest = logits
    for _ in range(PIECES - 1):
        parts.append(rest)
        rest = rest - rest.astype(BF16).astype(F32)
    lanes = out_ref.shape[2] - width
    spare = lanes - PIECES * experts
    extras = jnp.concatenate(parts + ([jnp.zeros((tok, spare), F32)] if spare else []), axis=1)
    out_ref[0, :, width:] = extras.astype(BF16)
    out_ref[1, :, width:] = jnp.zeros((tok, lanes), BF16)
    copies[2].wait()
    copies[3].wait()


def hidden_parts(hidden):
    main = hidden // 256 * 256
    return [(0, main), (main, hidden)] if 0 < main < hidden else [(0, hidden)]


def load_kernel(chunks, block_in, gate_in, up_in, down_in, block_ref, pair_ref, down_ref, sems):
    copies = []

    def add(src, dst):
        copies.append(pltpu.make_async_copy(src, dst, sems.at[len(copies)]))

    hidden, width = down_ref.shape
    for c in range(chunks):
        part = pl.ds(c * (width // chunks), width // chunks)
        for first, last in hidden_parts(hidden):
            for k, ref in enumerate((gate_in, up_in)):
                to = 2 * first + k * (last - first)
                add(ref.at[0, part, first:last], pair_ref.at[part, to : to + last - first])
        part = pl.ds(c * (hidden // chunks), hidden // chunks)
        add(down_in.at[0, part, :], down_ref.at[part, :])
    add(block_in, block_ref)
    for copy in copies:
        copy.start()
    for copy in copies:
        copy.wait()


def join_kernel(*refs):
    blocks, out_ref, rows_ref = forward(refs[:-2]), refs[-2], refs[-1]
    count = len(blocks)
    tok = blocks[0].shape[1]
    for kind in range(2):
        for j, ref in enumerate(blocks):
            first = (kind * count + j) * tok
            rows_ref[first : first + tok, :] = ref[kind].astype(F32)
    out_ref[...] = rows_ref[...].astype(BF16)


def stack_kernel(*refs):
    out_ref = refs[-1]
    rows = refs[0].shape[0]
    for j, ref in enumerate(refs[:-1]):
        out_ref[j * rows : (j + 1) * rows, :] = ref[...]


def token_rows(refs, start, rows, group, kind, columns):
    parts = []
    for ref in refs:
        for j in range(rows // (2 * group)):
            first = start + (2 * j + kind) * group
            if not isinstance(first, int):
                first = pl.multiple_of(first, group)
            parts.append(ref[pl.ds(first, group), columns])
    return parts[0] if len(parts) == 1 else jnp.concatenate(parts, axis=0)


def put_scores(out_ref, scores_ref, width):
    rows = out_ref.shape[0]
    for c in range((out_ref.shape[1] - width) // LANES):
        out_ref[:, width + c * LANES : width + (c + 1) * LANES] = scores_ref[c * rows : (c + 1) * rows, :].astype(BF16)


def get_scores(in_ref, scores_ref, base, size, width):
    rows = in_ref.shape[0]
    for c in range(-(-size // rows)):
        here = min(rows, size - c * rows)
        tall = min(rows, -(-here // 16) * 16)
        block = in_ref[0:tall, width + c * LANES : width + (c + 1) * LANES].astype(F32)
        scores_ref[base + c * rows : base + c * rows + here, :] = block[:here]


def units_kernel(basis, group, tok, experts, core_mask, blocks, *refs):
    own_refs, other_refs = forward(refs[:blocks]), forward(refs[blocks : 2 * blocks])
    pair_ref, down_ref, kept_ref, message_ref, pieces_ref, score_ref, padded_ref = refs[2 * blocks :]
    hidden, width = down_ref.shape
    rows, buf_width = own_refs[0].shape
    tokens = score_ref.shape[1]
    own = own_index()

    def terms(sets, start, step):
        act = token_rows(sets, start, step, group, 0, slice(None))
        count = act.shape[0]
        combine = combine_rows(act[:, width:], experts)
        ids = lax.broadcasted_iota(jnp.int32, combine.shape, 1)
        column = jnp.sum(jnp.where(ids == own // 2, combine, 0.0), axis=1, keepdims=True)
        act = act[:, :width]
        cot = token_rows(sets, start, step, group, 1, slice(0, width))
        score = jnp.zeros((count, 1), F32)
        grads = []
        for first, last in hidden_parts(hidden):
            size = last - first
            pair = jnp.dot(act, pair_ref[:, 2 * first : 2 * last], preferred_element_type=F32)
            gate_pre = pair[:, :size]
            up_pre = pair[:, size:]
            back = lax.dot_general(cot, down_ref[first:last, :], NT, preferred_element_type=F32)
            sig = jax.nn.sigmoid(gate_pre)
            act_gate = gate_pre * sig
            score = score + jnp.sum(act_gate * up_pre * back, axis=1, keepdims=True)
            weighted = column * back
            grad_gate = weighted * up_pre * sig * (1.0 + gate_pre * (1.0 - sig))
            grad_up = weighted * act_gate
            grads += [grad_gate.astype(BF16), grad_up.astype(BF16)]
        return jnp.concatenate(grads, axis=1), score

    def back_product(grads):
        return lax.dot_general(grads, pair_ref[...], NT, preferred_element_type=F32)

    def in_order(score, place, swap_mask):
        token = lax.broadcasted_iota(jnp.int32, (score.shape[0], tokens), 1)
        side = own ^ swap_mask
        whole = (place_mask(place // tok, basis, side & core_mask != 0) ^ side) * tok + place % tok
        return jnp.sum(jnp.where(whole == token, score, 0.0), axis=0, keepdims=True)

    def send_scores():
        lane_blocks = tokens // LANES
        padded_ref[...] = jnp.zeros(padded_ref.shape, F32)
        value = score_ref[...]
        for piece in range(SCORE_PIECES):
            rounded = value.astype(BF16).astype(F32)
            for b in range(lane_blocks):
                at = piece * lane_blocks + b
                padded_ref[at : at + 1, :] = rounded[:, b * LANES : (b + 1) * LANES]
            value = value - rounded
        pieces_ref[...] = padded_ref[0 : pieces_ref.shape[0], :]
        put_scores(message_ref, padded_ref, width)

    half = blocks * rows // 2
    if 2 * half <= 128:
        grads, score = terms(own_refs + other_refs, 0, rows)
        row = lax.broadcasted_iota(jnp.int32, (2 * half, tokens), 0)
        score_ref[...] = in_order(score, row % half, jnp.where(row < half, 0, core_mask))
        send_scores()
        total = back_product(grads)
        kept_ref[...] = total[:half]
        message_ref[:, 0:width] = total[half:].astype(BF16)
    else:
        step = min(rows, 128)
        score_ref[...] = jnp.zeros(score_ref.shape, F32)
        for out_ref, sets, swap_mask in ((kept_ref, own_refs, 0), (message_ref, other_refs, core_mask)):
            for j, ref in enumerate(sets):

                def one(index):
                    grads, score = terms((ref,), index * step, step)
                    total = back_product(grads)
                    first = pl.multiple_of(j * (rows // 2) + index * (step // 2), step // 2)
                    out_ref[pl.ds(first, step // 2), 0:width] = total.astype(out_ref.dtype)
                    place = lax.broadcasted_iota(jnp.int32, (step // 2, tokens), 0) + first
                    score_ref[...] += in_order(score, place, swap_mask)

                pl.loop(0, rows // step)(one)

        send_scores()


def add_kernel(arrivals, positions, low, *refs):
    kept_ref, pieces_ref = refs[0], refs[1]
    arrived = refs[2 : 2 + arrivals]
    outs = refs[2 + arrivals :]
    next_kept_ref, next_pieces_ref = outs[0], outs[1]
    sends = outs[2 : 2 + len(positions)]
    total_ref, scores_ref = outs[2 + len(positions) :]
    width = kept_ref.shape[1]
    size = pieces_ref.shape[0]
    total = kept_ref[...]
    for ref in arrived:
        total = total + ref[:, 0:width].astype(F32)
    total_ref[...] = total
    if scores_ref.shape[0] > next_pieces_ref.shape[0]:
        scores_ref[...] = jnp.zeros(scores_ref.shape, F32)
    scores_ref[0:size, :] = pieces_ref[...]
    for j, ref in enumerate(arrived):
        get_scores(ref, scores_ref, (j + 1) * size, size, width)
    rows = next_kept_ref.shape[0]
    next_kept_ref[...] = total_ref[0:rows, :]
    next_pieces_ref[...] = scores_ref[0 : next_pieces_ref.shape[0], :]
    chunks = [total_ref[j * rows : (j + 1) * rows, :] for j in range(total_ref.shape[0] // rows)]
    member = own_index() >> low & 3
    for position, ref in zip(positions, sends):
        if isinstance(position, int):
            chunk = chunks[position]
        else:
            chunk = by_member(member, [chunks[p] for p in position])
        ref[:, 0:width] = chunk.astype(BF16)
        put_scores(ref, scores_ref, width)


def table_kernel(basis, back_basis, low, group, tok, core_mask, rows_out, blocks, after_ref, *refs):
    probs_ref, column_ref, mine_ref, pick_ref = refs[2 * blocks :]
    rows, buf_width = refs[0].shape
    half = blocks * rows // 2
    experts, tokens = probs_ref.shape
    lanes = -(-PIECES * experts // LANES) * LANES
    width = buf_width - lanes
    own = own_index()
    column = pl.multiple_of(own * rows_out // LANES * LANES, LANES)
    extras = jnp.zeros((tokens, lanes), F32)
    columns = jnp.zeros((tokens, LANES), F32)
    for index in range(2):
        sets = forward(refs[index * blocks : (index + 1) * blocks])
        row = lax.broadcasted_iota(jnp.int32, (half, tokens), 0)
        token = lax.broadcasted_iota(jnp.int32, (half, tokens), 1)
        side = own ^ (core_mask if index else 0)
        whole = (place_mask(row // tok, basis, side & core_mask != 0) ^ side) * tok + row % tok
        here = jnp.where(whole == token, 1.0, 0.0).astype(BF16)
        part = token_rows(sets, 0, rows, group, 0, slice(width, buf_width))
        extras = extras + lax.dot_general(here, part, TN, preferred_element_type=F32)
        part = token_rows(sets, 0, rows, group, 0, pl.ds(column, LANES))
        columns = columns + lax.dot_general(here, part, TN, preferred_element_type=F32)
    logits = lax.dot_general(piece_sum(experts, lanes, 1), extras.astype(BF16), NT, preferred_element_type=F32)
    raised = jnp.exp(logits - jnp.max(logits, axis=0, keepdims=True))
    probs_ref[...] = raised / jnp.sum(raised, axis=0, keepdims=True)
    column_ref[...] = columns.astype(BF16)
    row = lax.broadcasted_iota(jnp.int32, mine_ref.shape, 0)
    token = lax.broadcasted_iota(jnp.int32, mine_ref.shape, 1)
    mine_ref[...] = jnp.where((row < tok) & (token == own * tok + row), 1.0, 0.0).astype(BF16)
    wide = pick_ref.shape[1]
    sender = lax.broadcasted_iota(jnp.int32, (experts, wide), 1) // SCORE_PIECES
    ids = lax.broadcasted_iota(jnp.int32, (experts, wide), 0)
    mask = place_mask(sender, back_basis, own & core_mask != 0)
    if low is not None:
        member = own >> low & 3
        source = sender >> len(back_basis)
        for k, step in enumerate(REDUCE_STEPS):
            come = by_member(member, [d ^ step.index(d) for d in range(4)]) << low
            mask = mask ^ jnp.where(source == k + 1, come, 0)
    pick_ref[...] = jnp.where(((mask ^ own) >> 1) == ids, 1.0, 0.0).astype(BF16)


def final_kernel(arrivals, *refs):
    probs_ref, column_ref, mine_ref, pick_ref, router_ref, kept_ref, pieces_ref = refs[:7]
    arrived = refs[7 : 7 + arrivals]
    x_out, grad_out, x_ref, grad_ref, scores_ref, sems = refs[7 + arrivals :]
    experts, width = router_ref.shape
    size = pieces_ref.shape[0]
    tok = kept_ref.shape[0]
    own = own_index()
    scores_ref[0:size, :] = pieces_ref[...]
    for j, ref in enumerate(arrived):
        get_scores(ref, scores_ref, (j + 1) * size, size, width)
    blocks = probs_ref.shape[1] // LANES
    wide = scores_ref.shape[0] // blocks
    parts = []
    for b in range(blocks):
        block = scores_ref[...] if blocks == 1 else scores_ref[pl.ds(b, wide, stride=blocks), :]
        parts.append(jnp.dot(pick_ref[...], block.astype(BF16), preferred_element_type=F32))
    scores = parts[0] if blocks == 1 else jnp.concatenate(parts, axis=1)
    probs = probs_ref[...]
    mean = jnp.sum(probs * scores, axis=0, keepdims=True)
    logit_grad = (probs * (scores - mean)).astype(BF16)
    mine = lax.dot_general(mine_ref[...], logit_grad, NT, preferred_element_type=F32)
    part = jnp.dot(mine.astype(BF16), router_ref[...], preferred_element_type=F32)
    total = kept_ref[...]
    for ref in arrived:
        total = total + ref[:, 0:width].astype(F32)
    x_ref[...] = (total + part[:tok]).astype(BF16)
    x_copy = pltpu.make_async_copy(x_ref, x_out, sems.at[0])
    x_copy.start()
    grad = jnp.dot(logit_grad, column_ref[...], preferred_element_type=F32)
    rows_out = grad_ref.shape[1]
    first = own * rows_out % LANES
    grad_ref[...] = pltpu.roll(grad, (LANES - first) % LANES, 1)[:, :rows_out]
    grad_copy = pltpu.make_async_copy(grad_ref, grad_out, sems.at[1])
    grad_copy.start()
    x_copy.wait()
    grad_copy.wait()


def on_device(tokens, grad_out, router_logits, selected, router_w, w_gate, w_up, w_down):
    tok, width = tokens.shape
    experts = router_logits.shape[1]
    hidden = w_gate.shape[2]
    exp_size = lax.axis_size("exp")
    hid_size = lax.axis_size("hid")
    count = exp_size * hid_size
    half = count // 2
    groups, core = stage_masks(exp_size, hid_size)
    core_mask = 1 << core
    basis = [m for group in groups for m in group]
    back_groups = [near_first(group) for group in groups[:0:-1]] + [groups[0]]
    core_pair = (core_mask, core_mask)
    low = (count - 1).bit_length() - 2 if len(groups[0]) == 2 else None
    if low is not None:
        back_groups = back_groups[:-1]
    back_basis = [core_pair] + [m for group in back_groups for m in group]
    if low is not None:
        back_groups = back_groups + [None]
    token_count = count * tok
    lanes = -(-PIECES * experts // LANES) * LANES

    block = pl.pallas_call(
        prep_kernel,
        out_shape=jax.ShapeDtypeStruct((2, tok, width + lanes), BF16),
        in_specs=[HBM_SPEC] * 4,
        out_specs=VMEM_SPEC,
        scratch_shapes=[
            pltpu.VMEM(router_logits.shape, router_logits.dtype),
            pltpu.VMEM(selected.shape, selected.dtype),
            pltpu.SemaphoreType.DMA((4,)),
        ],
        compiler_params=PARAMS,
        name="prep",
    )(*in_hbm(tokens, grad_out, router_logits, selected))

    masks = group_masks(groups[0])
    blocks = [block] + swaps(block, masks[1:], count, core)
    group_rows = tok * len(blocks)
    block = pl.pallas_call(
        join_kernel,
        out_shape=jax.ShapeDtypeStruct((2 * group_rows, width + lanes), BF16),
        in_specs=[VMEM_SPEC] * len(blocks),
        out_specs=VMEM_SPEC,
        scratch_shapes=[pltpu.VMEM((2 * group_rows, width + lanes), F32)],
        compiler_params=PARAMS,
        name="join",
    )(*forward(blocks))
    for group in groups[1:-1]:
        blocks = [block] + swaps(block, group_masks(group)[1:], count, core)
        block = pl.pallas_call(
            stack_kernel,
            out_shape=jax.ShapeDtypeStruct((len(blocks) * block.shape[0], block.shape[1]), BF16),
            in_specs=[VMEM_SPEC] * len(blocks),
            out_specs=VMEM_SPEC,
            compiler_params=PARAMS,
            name="stack",
        )(*blocks)
    chunks = 4
    copied, pair, down = pl.pallas_call(
        functools.partial(load_kernel, chunks),
        out_shape=(
            pltpu.VMEM(block.shape, BF16),
            pltpu.VMEM((width, 2 * hidden), BF16),
            pltpu.VMEM((hidden, width), BF16),
        ),
        in_specs=[VMEM_SPEC] + [HBM_SPEC] * 3,
        out_specs=(VMEM_SPEC,) * 3,
        scratch_shapes=[pltpu.SemaphoreType.DMA(((2 * len(hidden_parts(hidden)) + 1) * chunks + 1,))],
        compiler_params=pltpu.CompilerParams(vmem_limit_bytes=4 * 2**20),
        cost_estimate=pl.CostEstimate(flops=0, bytes_accessed=6 * width * hidden * 2, transcendentals=0),
        name="load",
    )(block, *in_hbm(w_gate, w_up, w_down))
    masks = group_masks(groups[-1]) if len(groups) > 1 else [core_pair]
    blocks = [block] + swaps(block, masks[1:], count, core)
    blocks = forward(blocks)
    blocks = blocks + [swap(b, core_pair, count, core) for b in [copied] + blocks[1:]]
    block_count = len(blocks) // 2

    unit_rows = SCORE_PIECES * token_count // LANES
    extra = -(-unit_rows // (half * tok)) * LANES
    kept, message, pieces = pl.pallas_call(
        functools.partial(units_kernel, basis, group_rows, tok, experts, core_mask, block_count),
        out_shape=(
            jax.ShapeDtypeStruct((half * tok, width), F32),
            jax.ShapeDtypeStruct((half * tok, width + extra), BF16),
            jax.ShapeDtypeStruct((unit_rows, LANES), F32),
        ),
        in_specs=[VMEM_SPEC] * (len(blocks) + 2),
        out_specs=(VMEM_SPEC,) * 3,
        scratch_shapes=[
            pltpu.VMEM((1, token_count), F32),
            pltpu.VMEM((max(half * tok * extra // LANES, unit_rows), LANES), F32),
        ],
        compiler_params=PARAMS,
        cost_estimate=pl.CostEstimate(
            flops=10 * token_count * width * hidden,
            bytes_accessed=3 * width * hidden * 2 + 2 * token_count * width * 2,
            transcendentals=token_count * hidden,
        ),
        name="units",
    )(*blocks, pair, down)

    arrived = [swap(message, core_pair, count, core)]
    tables = None
    rows_out = width // count
    for group, back_group in zip(groups[::-1], back_groups):
        order = [m[0] for m in group_masks(group)]
        if back_group is None:
            positions = [[order.index((d ^ step[d]) << low) for d in range(4)] for step in REDUCE_STEPS]
        else:
            back_masks = group_masks(back_group)
            positions = [order.index(m[0]) for m in back_masks[1:]]
        radix = len(order)
        rows = kept.shape[0]
        next_rows = rows // radix
        size = pieces.shape[0] * (1 + len(arrived))
        extra = -(-size // next_rows) * LANES
        sends = [jax.ShapeDtypeStruct((next_rows, width + extra), BF16)] * (radix - 1)
        outs = pl.pallas_call(
            functools.partial(add_kernel, len(arrived), positions, low or 0),
            out_shape=[
                jax.ShapeDtypeStruct((next_rows, width), F32),
                jax.ShapeDtypeStruct((size, LANES), F32),
            ]
            + sends,
            in_specs=[VMEM_SPEC] * (2 + len(arrived)),
            out_specs=[VMEM_SPEC] * (1 + radix),
            scratch_shapes=[
                pltpu.VMEM((rows, width), F32),
                pltpu.VMEM((max(next_rows * extra // LANES, size), LANES), F32),
            ],
            compiler_params=PARAMS,
            name="add",
        )(kept, pieces, *arrived)
        kept, pieces = outs[0], outs[1]
        if tables is None:
            tables = pl.pallas_call(
                functools.partial(table_kernel, basis, back_basis, low, group_rows, tok, core_mask, rows_out, block_count),
                out_shape=(
                    jax.ShapeDtypeStruct((experts, token_count), F32),
                    jax.ShapeDtypeStruct((token_count, LANES), BF16),
                    jax.ShapeDtypeStruct((16, token_count), BF16),
                    jax.ShapeDtypeStruct((experts, SCORE_PIECES * count), BF16),
                ),
                in_specs=[pl.BlockSpec(memory_space=pl.ANY)] + [VMEM_SPEC] * len(blocks),
                out_specs=(VMEM_SPEC,) * 4,
                compiler_params=PARAMS,
                cost_estimate=pl.CostEstimate(flops=10**9, bytes_accessed=10**6, transcendentals=0),
                name="tables",
            )(pieces, *blocks)
        if back_group is None:
            arrived = [shift(piece, step, count, low) for piece, step in zip(outs[2:], REDUCE_STEPS)]
        else:
            arrived = [swap(piece, m, count, core) for piece, m in zip(outs[2:], back_masks[1:])]

    x_grad, grad = pl.pallas_call(
        functools.partial(final_kernel, len(arrived)),
        out_shape=(
            jax.ShapeDtypeStruct((tok, width), BF16),
            jax.ShapeDtypeStruct((experts, rows_out), F32),
        ),
        in_specs=[VMEM_SPEC] * (7 + len(arrived)),
        out_specs=(HBM_SPEC, HBM_SPEC),
        scratch_shapes=[
            pltpu.VMEM((tok, width), BF16),
            pltpu.VMEM((experts, rows_out), F32),
            pltpu.VMEM((pieces.shape[0] * (1 + len(arrived)), LANES), F32),
            pltpu.SemaphoreType.DMA((2,)),
        ],
        compiler_params=PARAMS,
        name="final",
    )(*tables, router_w.T, kept, pieces, *arrived)
    return (x_grad, grad.T)


def solution(mesh):
    rows = P(AXES, None)
    units = P(AXES, None, None)
    return jax.shard_map(
        on_device,
        mesh=mesh,
        in_specs=(rows, rows, rows, rows, P(), units, units, units),
        out_specs=(rows, rows),
        check_vma=False,
    )
```

```python
import functools

import jax
import jax.numpy as jnp
from jax import lax
from jax.experimental import pallas as pl
from jax.experimental.pallas import tpu as pltpu
from jax.sharding import PartitionSpec as P

AXES = ("exp", "hid")
LANES = 128
PIECES = 4
SCORE_PIECES = 2
VMEM_SPEC = pl.BlockSpec(memory_space=pltpu.VMEM)
HBM_SPEC = pl.BlockSpec(memory_space=pltpu.HBM)
F32 = jnp.float32
BF16 = jnp.bfloat16
NT = (((1,), (1,)), ((), ()))
TN = (((0,), (0,)), ((), ()))
PARAMS = pltpu.CompilerParams(vmem_limit_bytes=24 * 2**20)


def stage_masks(exp_size, hid_size):
    hid_bits = hid_size.bit_length() - 1
    all_bits = (exp_size * hid_size).bit_length() - 1
    core = hid_bits
    first = list(range(max(core + 1, all_bits - 2), all_bits))
    middle = [b for b in range(all_bits) if b != core and b not in first]
    groups = [first] + [middle[i : i + 2] for i in range(0, len(middle), 2)]
    bases = [[(sum(1 << b for b in group[i:]),) * 2 for i in range(len(group))] for group in groups]
    bases[0] = bases[0][::-1]
    return bases, core


def cross(a, b):
    return (a[0] ^ b[0], a[1] ^ b[1])


def group_masks(basis):
    masks = [(0, 0)]
    for mask in basis:
        masks = masks + [cross(m, mask) for m in masks]
    return masks


def near_first(basis):
    return [cross(basis[0], basis[1]), basis[1]] if len(basis) == 2 else basis


def swap(block, mask, count, core):
    return lax.ppermute(block, AXES, [(i, i ^ mask[i >> core & 1]) for i in range(count)])


REDUCE_STEPS = ((1, 3, 0, 2), (3, 2, 1, 0), (2, 0, 3, 1))


def by_member(member, values):
    total = values[0]
    for k in range(1, len(values)):
        total = jnp.where(member == k, values[k], total)
    return total


def shift(block, step, count, low):
    return lax.ppermute(block, AXES, [(i, i ^ ((i >> low & 3) ^ step[i >> low & 3]) << low) for i in range(count)])


def swaps(block, masks, count, core):
    return [swap(block, m, count, core) for m in masks]


def forward(blocks):
    return blocks[:1] + blocks[:0:-1]


def place_mask(place, basis, upper):
    total = jnp.zeros_like(place)
    for digit, (low, high) in enumerate(basis):
        mask = low if low == high else jnp.where(upper, high, low)
        total = total ^ (((place >> digit) & 1) * mask)
    return total


def own_index():
    return lax.axis_index("exp") * lax.axis_size("hid") + lax.axis_index("hid")


def in_hbm(*arrays):
    return tuple(pltpu.with_memory_space_constraint(a, pltpu.HBM) for a in arrays)


def piece_sum(experts, lanes, axis):
    shape = (lanes, experts) if axis == 0 else (experts, lanes)
    lane = lax.broadcasted_iota(jnp.int32, shape, axis)
    ids = lax.broadcasted_iota(jnp.int32, shape, 1 - axis)
    tally = jnp.zeros(shape, F32)
    for k in range(1, PIECES):
        tally = tally + jnp.where(lane == ids + k * experts, 1.0, 0.0)
    return tally.astype(BF16)


def combine_rows(extras, experts):
    hit = extras[:, :experts].astype(F32) > 0.5
    logits = jnp.dot(extras, piece_sum(experts, extras.shape[1], 0), preferred_element_type=F32)
    top = jnp.max(jnp.where(hit, logits, -jnp.inf), axis=1, keepdims=True)
    raised = jnp.where(hit, jnp.exp(jnp.minimum(logits - top, 0.0)), 0.0)
    return (raised / jnp.sum(raised, axis=1, keepdims=True)).astype(BF16).astype(F32)


def prep_kernel(tokens_in, grad_in, logits_in, chosen_in, out_ref, logits_ref, chosen_ref, sems):
    tok, width = tokens_in.shape
    pairs = [
        (logits_in, logits_ref),
        (chosen_in, chosen_ref),
        (tokens_in, out_ref.at[0, :, 0:width]),
        (grad_in, out_ref.at[1, :, 0:width]),
    ]
    copies = [pltpu.make_async_copy(src, dst, sems.at[i]) for i, (src, dst) in enumerate(pairs)]
    for copy in copies:
        copy.start()
    copies[0].wait()
    copies[1].wait()
    logits = logits_ref[...]
    chosen = chosen_ref[...]
    experts = logits.shape[1]
    ids = lax.broadcasted_iota(jnp.int32, logits.shape, 1)
    hit = ids == chosen[:, 0:1]
    for k in range(1, chosen.shape[1]):
        hit = hit | (ids == chosen[:, k : k + 1])
    parts = [jnp.where(hit, 1.0, 0.0)]
    rest = logits
    for _ in range(PIECES - 1):
        parts.append(rest)
        rest = rest - rest.astype(BF16).astype(F32)
    lanes = out_ref.shape[2] - width
    spare = lanes - PIECES * experts
    extras = jnp.concatenate(parts + ([jnp.zeros((tok, spare), F32)] if spare else []), axis=1)
    out_ref[0, :, width:] = extras.astype(BF16)
    out_ref[1, :, width:] = jnp.zeros((tok, lanes), BF16)
    copies[2].wait()
    copies[3].wait()


def hidden_parts(hidden):
    main = hidden // 256 * 256
    return [(0, main), (main, hidden)] if 0 < main < hidden else [(0, hidden)]


def load_kernel(chunks, block_in, gate_in, up_in, down_in, block_ref, pair_ref, down_ref, sems):
    copies = []

    def add(src, dst):
        copies.append(pltpu.make_async_copy(src, dst, sems.at[len(copies)]))

    hidden, width = down_ref.shape
    for c in range(chunks):
        part = pl.ds(c * (width // chunks), width // chunks)
        for first, last in hidden_parts(hidden):
            for k, ref in enumerate((gate_in, up_in)):
                to = 2 * first + k * (last - first)
                add(ref.at[0, part, first:last], pair_ref.at[part, to : to + last - first])
        part = pl.ds(c * (hidden // chunks), hidden // chunks)
        add(down_in.at[0, part, :], down_ref.at[part, :])
    add(block_in, block_ref)
    for copy in copies:
        copy.start()
    for copy in copies:
        copy.wait()


def join_kernel(*refs):
    blocks, out_ref, rows_ref = forward(refs[:-2]), refs[-2], refs[-1]
    count = len(blocks)
    tok = blocks[0].shape[1]
    for kind in range(2):
        for j, ref in enumerate(blocks):
            first = (kind * count + j) * tok
            rows_ref[first : first + tok, :] = ref[kind].astype(F32)
    out_ref[...] = rows_ref[...].astype(BF16)


def stack_kernel(*refs):
    out_ref = refs[-1]
    rows = refs[0].shape[0]
    for j, ref in enumerate(refs[:-1]):
        out_ref[j * rows : (j + 1) * rows, :] = ref[...]


def token_rows(refs, start, rows, group, kind, columns):
    parts = []
    for ref in refs:
        for j in range(rows // (2 * group)):
            first = start + (2 * j + kind) * group
            if not isinstance(first, int):
                first = pl.multiple_of(first, group)
            parts.append(ref[pl.ds(first, group), columns])
    return parts[0] if len(parts) == 1 else jnp.concatenate(parts, axis=0)


def put_scores(out_ref, scores_ref, width):
    rows = out_ref.shape[0]
    for c in range((out_ref.shape[1] - width) // LANES):
        out_ref[:, width + c * LANES : width + (c + 1) * LANES] = scores_ref[c * rows : (c + 1) * rows, :].astype(BF16)


def get_scores(in_ref, scores_ref, base, size, width):
    rows = in_ref.shape[0]
    for c in range(-(-size // rows)):
        here = min(rows, size - c * rows)
        tall = min(rows, -(-here // 16) * 16)
        block = in_ref[0:tall, width + c * LANES : width + (c + 1) * LANES].astype(F32)
        scores_ref[base + c * rows : base + c * rows + here, :] = block[:here]


def units_kernel(basis, group, tok, experts, core_mask, blocks, *refs):
    own_refs, other_refs = forward(refs[:blocks]), forward(refs[blocks : 2 * blocks])
    pair_ref, down_ref, kept_ref, message_ref, pieces_ref, score_ref, padded_ref = refs[2 * blocks :]
    hidden, width = down_ref.shape
    rows, buf_width = own_refs[0].shape
    tokens = score_ref.shape[1]
    own = own_index()

    def terms(sets, start, step):
        act = token_rows(sets, start, step, group, 0, slice(None))
        count = act.shape[0]
        combine = combine_rows(act[:, width:], experts)
        ids = lax.broadcasted_iota(jnp.int32, combine.shape, 1)
        column = jnp.sum(jnp.where(ids == own // 2, combine, 0.0), axis=1, keepdims=True)
        act = act[:, :width]
        cot = token_rows(sets, start, step, group, 1, slice(0, width))
        score = jnp.zeros((count, 1), F32)
        grads = []
        for first, last in hidden_parts(hidden):
            size = last - first
            pair = jnp.dot(act, pair_ref[:, 2 * first : 2 * last], preferred_element_type=F32)
            gate_pre = pair[:, :size]
            up_pre = pair[:, size:]
            back = lax.dot_general(cot, down_ref[first:last, :], NT, preferred_element_type=F32)
            sig = jax.nn.sigmoid(gate_pre)
            act_gate = gate_pre * sig
            score = score + jnp.sum(act_gate * up_pre * back, axis=1, keepdims=True)
            weighted = column * back
            grad_gate = weighted * up_pre * sig * (1.0 + gate_pre * (1.0 - sig))
            grad_up = weighted * act_gate
            grads += [grad_gate.astype(BF16), grad_up.astype(BF16)]
        return jnp.concatenate(grads, axis=1), score

    def back_product(grads):
        return lax.dot_general(grads, pair_ref[...], NT, preferred_element_type=F32)

    def in_order(score, place, swap_mask):
        token = lax.broadcasted_iota(jnp.int32, (score.shape[0], tokens), 1)
        side = own ^ swap_mask
        whole = (place_mask(place // tok, basis, side & core_mask != 0) ^ side) * tok + place % tok
        return jnp.sum(jnp.where(whole == token, score, 0.0), axis=0, keepdims=True)

    def send_scores():
        lane_blocks = tokens // LANES
        padded_ref[...] = jnp.zeros(padded_ref.shape, F32)
        value = score_ref[...]
        for piece in range(SCORE_PIECES):
            rounded = value.astype(BF16).astype(F32)
            for b in range(lane_blocks):
                at = piece * lane_blocks + b
                padded_ref[at : at + 1, :] = rounded[:, b * LANES : (b + 1) * LANES]
            value = value - rounded
        pieces_ref[...] = padded_ref[0 : pieces_ref.shape[0], :]
        put_scores(message_ref, padded_ref, width)

    half = blocks * rows // 2
    if 2 * half <= 128:
        grads, score = terms(own_refs + other_refs, 0, rows)
        row = lax.broadcasted_iota(jnp.int32, (2 * half, tokens), 0)
        score_ref[...] = in_order(score, row % half, jnp.where(row < half, 0, core_mask))
        send_scores()
        total = back_product(grads)
        kept_ref[...] = total[:half]
        message_ref[:, 0:width] = total[half:].astype(BF16)
    else:
        step = min(rows, 128)
        score_ref[...] = jnp.zeros(score_ref.shape, F32)
        for out_ref, sets, swap_mask in ((kept_ref, own_refs, 0), (message_ref, other_refs, core_mask)):
            for j, ref in enumerate(sets):

                def one(index):
                    grads, score = terms((ref,), index * step, step)
                    total = back_product(grads)
                    first = pl.multiple_of(j * (rows // 2) + index * (step // 2), step // 2)
                    out_ref[pl.ds(first, step // 2), 0:width] = total.astype(out_ref.dtype)
                    place = lax.broadcasted_iota(jnp.int32, (step // 2, tokens), 0) + first
                    score_ref[...] += in_order(score, place, swap_mask)

                pl.loop(0, rows // step)(one)

        send_scores()


def add_kernel(arrivals, positions, low, *refs):
    kept_ref, pieces_ref = refs[0], refs[1]
    arrived = refs[2 : 2 + arrivals]
    outs = refs[2 + arrivals :]
    next_kept_ref, next_pieces_ref = outs[0], outs[1]
    sends = outs[2 : 2 + len(positions)]
    total_ref, scores_ref = outs[2 + len(positions) :]
    width = kept_ref.shape[1]
    size = pieces_ref.shape[0]
    total = kept_ref[...]
    for ref in arrived:
        total = total + ref[:, 0:width].astype(F32)
    total_ref[...] = total
    if scores_ref.shape[0] > next_pieces_ref.shape[0]:
        scores_ref[...] = jnp.zeros(scores_ref.shape, F32)
    scores_ref[0:size, :] = pieces_ref[...]
    for j, ref in enumerate(arrived):
        get_scores(ref, scores_ref, (j + 1) * size, size, width)
    rows = next_kept_ref.shape[0]
    next_kept_ref[...] = total_ref[0:rows, :]
    next_pieces_ref[...] = scores_ref[0 : next_pieces_ref.shape[0], :]
    chunks = [total_ref[j * rows : (j + 1) * rows, :] for j in range(total_ref.shape[0] // rows)]
    member = own_index() >> low & 3
    for position, ref in zip(positions, sends):
        if isinstance(position, int):
            chunk = chunks[position]
        else:
            chunk = by_member(member, [chunks[p] for p in position])
        ref[:, 0:width] = chunk.astype(BF16)
        put_scores(ref, scores_ref, width)


def table_kernel(basis, back_basis, low, group, tok, core_mask, rows_out, blocks, after_ref, *refs):
    probs_ref, column_ref, mine_ref, pick_ref = refs[2 * blocks :]
    rows, buf_width = refs[0].shape
    half = blocks * rows // 2
    experts, tokens = probs_ref.shape
    lanes = -(-PIECES * experts // LANES) * LANES
    width = buf_width - lanes
    own = own_index()
    column = pl.multiple_of(own * rows_out // LANES * LANES, LANES)
    extras = jnp.zeros((tokens, lanes), F32)
    columns = jnp.zeros((tokens, LANES), F32)
    for index in range(2):
        sets = forward(refs[index * blocks : (index + 1) * blocks])
        row = lax.broadcasted_iota(jnp.int32, (half, tokens), 0)
        token = lax.broadcasted_iota(jnp.int32, (half, tokens), 1)
        side = own ^ (core_mask if index else 0)
        whole = (place_mask(row // tok, basis, side & core_mask != 0) ^ side) * tok + row % tok
        here = jnp.where(whole == token, 1.0, 0.0).astype(BF16)
        part = token_rows(sets, 0, rows, group, 0, slice(width, buf_width))
        extras = extras + lax.dot_general(here, part, TN, preferred_element_type=F32)
        part = token_rows(sets, 0, rows, group, 0, pl.ds(column, LANES))
        columns = columns + lax.dot_general(here, part, TN, preferred_element_type=F32)
    logits = lax.dot_general(piece_sum(experts, lanes, 1), extras.astype(BF16), NT, preferred_element_type=F32)
    raised = jnp.exp(logits - jnp.max(logits, axis=0, keepdims=True))
    probs_ref[...] = raised / jnp.sum(raised, axis=0, keepdims=True)
    column_ref[...] = columns.astype(BF16)
    row = lax.broadcasted_iota(jnp.int32, mine_ref.shape, 0)
    token = lax.broadcasted_iota(jnp.int32, mine_ref.shape, 1)
    mine_ref[...] = jnp.where((row < tok) & (token == own * tok + row), 1.0, 0.0).astype(BF16)
    wide = pick_ref.shape[1]
    sender = lax.broadcasted_iota(jnp.int32, (experts, wide), 1) // SCORE_PIECES
    ids = lax.broadcasted_iota(jnp.int32, (experts, wide), 0)
    mask = place_mask(sender, back_basis, own & core_mask != 0)
    if low is not None:
        member = own >> low & 3
        source = sender >> len(back_basis)
        for k, step in enumerate(REDUCE_STEPS):
            come = by_member(member, [d ^ step.index(d) for d in range(4)]) << low
            mask = mask ^ jnp.where(source == k + 1, come, 0)
    pick_ref[...] = jnp.where(((mask ^ own) >> 1) == ids, 1.0, 0.0).astype(BF16)


def final_kernel(arrivals, *refs):
    probs_ref, column_ref, mine_ref, pick_ref, router_ref, kept_ref, pieces_ref = refs[:7]
    arrived = refs[7 : 7 + arrivals]
    x_out, grad_out, x_ref, grad_ref, scores_ref, sems = refs[7 + arrivals :]
    experts, width = router_ref.shape
    size = pieces_ref.shape[0]
    tok = kept_ref.shape[0]
    own = own_index()
    scores_ref[0:size, :] = pieces_ref[...]
    for j, ref in enumerate(arrived):
        get_scores(ref, scores_ref, (j + 1) * size, size, width)
    blocks = probs_ref.shape[1] // LANES
    wide = scores_ref.shape[0] // blocks
    parts = []
    for b in range(blocks):
        block = scores_ref[...] if blocks == 1 else scores_ref[pl.ds(b, wide, stride=blocks), :]
        parts.append(jnp.dot(pick_ref[...], block.astype(BF16), preferred_element_type=F32))
    scores = parts[0] if blocks == 1 else jnp.concatenate(parts, axis=1)
    probs = probs_ref[...]
    mean = jnp.sum(probs * scores, axis=0, keepdims=True)
    logit_grad = (probs * (scores - mean)).astype(BF16)
    mine = lax.dot_general(mine_ref[...], logit_grad, NT, preferred_element_type=F32)
    grad = jnp.dot(logit_grad, column_ref[...], preferred_element_type=F32)
    rows_out = grad_ref.shape[1]
    first = own * rows_out % LANES
    grad_ref[...] = pltpu.roll(grad, (LANES - first) % LANES, 1)[:, :rows_out]
    grad_copy = pltpu.make_async_copy(grad_ref, grad_out, sems.at[1])
    grad_copy.start()
    part = jnp.dot(mine.astype(BF16), router_ref[...], preferred_element_type=F32)
    total = kept_ref[...]
    for ref in arrived:
        total = total + ref[:, 0:width].astype(F32)
    x_ref[...] = (total + part[:tok]).astype(BF16)
    x_copy = pltpu.make_async_copy(x_ref, x_out, sems.at[0])
    x_copy.start()
    x_copy.wait()
    grad_copy.wait()


def on_device(tokens, grad_out, router_logits, selected, router_w, w_gate, w_up, w_down):
    tok, width = tokens.shape
    experts = router_logits.shape[1]
    hidden = w_gate.shape[2]
    exp_size = lax.axis_size("exp")
    hid_size = lax.axis_size("hid")
    count = exp_size * hid_size
    half = count // 2
    groups, core = stage_masks(exp_size, hid_size)
    core_mask = 1 << core
    basis = [m for group in groups for m in group]
    back_groups = [near_first(group) for group in groups[:0:-1]] + [groups[0]]
    core_pair = (core_mask, core_mask)
    low = (count - 1).bit_length() - 2 if len(groups[0]) == 2 else None
    if low is not None:
        back_groups = back_groups[:-1]
    back_basis = [core_pair] + [m for group in back_groups for m in group]
    if low is not None:
        back_groups = back_groups + [None]
    token_count = count * tok
    lanes = -(-PIECES * experts // LANES) * LANES

    block = pl.pallas_call(
        prep_kernel,
        out_shape=jax.ShapeDtypeStruct((2, tok, width + lanes), BF16),
        in_specs=[HBM_SPEC] * 4,
        out_specs=VMEM_SPEC,
        scratch_shapes=[
            pltpu.VMEM(router_logits.shape, router_logits.dtype),
            pltpu.VMEM(selected.shape, selected.dtype),
            pltpu.SemaphoreType.DMA((4,)),
        ],
        compiler_params=PARAMS,
        name="prep",
    )(*in_hbm(tokens, grad_out, router_logits, selected))

    masks = group_masks(groups[0])
    blocks = [block] + swaps(block, masks[1:], count, core)
    group_rows = tok * len(blocks)
    block = pl.pallas_call(
        join_kernel,
        out_shape=jax.ShapeDtypeStruct((2 * group_rows, width + lanes), BF16),
        in_specs=[VMEM_SPEC] * len(blocks),
        out_specs=VMEM_SPEC,
        scratch_shapes=[pltpu.VMEM((2 * group_rows, width + lanes), F32)],
        compiler_params=PARAMS,
        name="join",
    )(*forward(blocks))
    for group in groups[1:-1]:
        blocks = [block] + swaps(block, group_masks(group)[1:], count, core)
        block = pl.pallas_call(
            stack_kernel,
            out_shape=jax.ShapeDtypeStruct((len(blocks) * block.shape[0], block.shape[1]), BF16),
            in_specs=[VMEM_SPEC] * len(blocks),
            out_specs=VMEM_SPEC,
            compiler_params=PARAMS,
            name="stack",
        )(*blocks)
    chunks = 4
    copied, pair, down = pl.pallas_call(
        functools.partial(load_kernel, chunks),
        out_shape=(
            pltpu.VMEM(block.shape, BF16),
            pltpu.VMEM((width, 2 * hidden), BF16),
            pltpu.VMEM((hidden, width), BF16),
        ),
        in_specs=[VMEM_SPEC] + [HBM_SPEC] * 3,
        out_specs=(VMEM_SPEC,) * 3,
        scratch_shapes=[pltpu.SemaphoreType.DMA(((2 * len(hidden_parts(hidden)) + 1) * chunks + 1,))],
        compiler_params=pltpu.CompilerParams(vmem_limit_bytes=4 * 2**20),
        cost_estimate=pl.CostEstimate(flops=0, bytes_accessed=6 * width * hidden * 2, transcendentals=0),
        name="load",
    )(block, *in_hbm(w_gate, w_up, w_down))
    masks = group_masks(groups[-1]) if len(groups) > 1 else [core_pair]
    blocks = [block] + swaps(block, masks[1:], count, core)
    blocks = forward(blocks)
    blocks = blocks + [swap(b, core_pair, count, core) for b in [copied] + blocks[1:]]
    block_count = len(blocks) // 2

    unit_rows = SCORE_PIECES * token_count // LANES
    extra = -(-unit_rows // (half * tok)) * LANES
    kept, message, pieces = pl.pallas_call(
        functools.partial(units_kernel, basis, group_rows, tok, experts, core_mask, block_count),
        out_shape=(
            jax.ShapeDtypeStruct((half * tok, width), F32),
            jax.ShapeDtypeStruct((half * tok, width + extra), BF16),
            jax.ShapeDtypeStruct((unit_rows, LANES), F32),
        ),
        in_specs=[VMEM_SPEC] * (len(blocks) + 2),
        out_specs=(VMEM_SPEC,) * 3,
        scratch_shapes=[
            pltpu.VMEM((1, token_count), F32),
            pltpu.VMEM((max(half * tok * extra // LANES, unit_rows), LANES), F32),
        ],
        compiler_params=PARAMS,
        cost_estimate=pl.CostEstimate(
            flops=10 * token_count * width * hidden,
            bytes_accessed=3 * width * hidden * 2 + 2 * token_count * width * 2,
            transcendentals=token_count * hidden,
        ),
        name="units",
    )(*blocks, pair, down)

    arrived = [swap(message, core_pair, count, core)]
    tables = None
    rows_out = width // count
    for group, back_group in zip(groups[::-1], back_groups):
        order = [m[0] for m in group_masks(group)]
        if back_group is None:
            positions = [[order.index((d ^ step[d]) << low) for d in range(4)] for step in REDUCE_STEPS]
        else:
            back_masks = group_masks(back_group)
            positions = [order.index(m[0]) for m in back_masks[1:]]
        radix = len(order)
        rows = kept.shape[0]
        next_rows = rows // radix
        size = pieces.shape[0] * (1 + len(arrived))
        extra = -(-size // next_rows) * LANES
        sends = [jax.ShapeDtypeStruct((next_rows, width + extra), BF16)] * (radix - 1)
        outs = pl.pallas_call(
            functools.partial(add_kernel, len(arrived), positions, low or 0),
            out_shape=[
                jax.ShapeDtypeStruct((next_rows, width), F32),
                jax.ShapeDtypeStruct((size, LANES), F32),
            ]
            + sends,
            in_specs=[VMEM_SPEC] * (2 + len(arrived)),
            out_specs=[VMEM_SPEC] * (1 + radix),
            scratch_shapes=[
                pltpu.VMEM((rows, width), F32),
                pltpu.VMEM((max(next_rows * extra // LANES, size), LANES), F32),
            ],
            compiler_params=PARAMS,
            name="add",
        )(kept, pieces, *arrived)
        kept, pieces = outs[0], outs[1]
        if tables is None:
            tables = pl.pallas_call(
                functools.partial(table_kernel, basis, back_basis, low, group_rows, tok, core_mask, rows_out, block_count),
                out_shape=(
                    jax.ShapeDtypeStruct((experts, token_count), F32),
                    jax.ShapeDtypeStruct((token_count, LANES), BF16),
                    jax.ShapeDtypeStruct((16, token_count), BF16),
                    jax.ShapeDtypeStruct((experts, SCORE_PIECES * count), BF16),
                ),
                in_specs=[pl.BlockSpec(memory_space=pl.ANY)] + [VMEM_SPEC] * len(blocks),
                out_specs=(VMEM_SPEC,) * 4,
                compiler_params=PARAMS,
                cost_estimate=pl.CostEstimate(flops=10**9, bytes_accessed=10**6, transcendentals=0),
                name="tables",
            )(pieces, *blocks)
        if back_group is None:
            arrived = [shift(piece, step, count, low) for piece, step in zip(outs[2:], REDUCE_STEPS)]
        else:
            arrived = [swap(piece, m, count, core) for piece, m in zip(outs[2:], back_masks[1:])]

    x_grad, grad = pl.pallas_call(
        functools.partial(final_kernel, len(arrived)),
        out_shape=(
            jax.ShapeDtypeStruct((tok, width), BF16),
            jax.ShapeDtypeStruct((experts, rows_out), F32),
        ),
        in_specs=[VMEM_SPEC] * (7 + len(arrived)),
        out_specs=(HBM_SPEC, HBM_SPEC),
        scratch_shapes=[
            pltpu.VMEM((tok, width), BF16),
            pltpu.VMEM((experts, rows_out), F32),
            pltpu.VMEM((pieces.shape[0] * (1 + len(arrived)), LANES), F32),
            pltpu.SemaphoreType.DMA((2,)),
        ],
        compiler_params=PARAMS,
        name="final",
    )(*tables, router_w.T, kept, pieces, *arrived)
    return (x_grad, grad.T)


def solution(mesh):
    rows = P(AXES, None)
    units = P(AXES, None, None)
    return jax.shard_map(
        on_device,
        mesh=mesh,
        in_specs=(rows, rows, rows, rows, P(), units, units, units),
        out_specs=(rows, rows),
        check_vma=False,
    )
```
